32 devices in a mesh: seq: 8 (over y, x, core), batch: 4 (over z).
Axes of the slice: x: 2, y: 2, z: 4, core: 2. Of those that a mesh axis runs over, the one named last changes fastest.
Arguments:
- token_ids: int32 [4, 1024], P('batch', 'seq'), may hold values from 0 to 50303
- pos_weights: int32 [4, 1024], P('batch', 'seq'), may hold values from 1 to 4, as said below
- pad_lengths: int32 [4], P('batch'), may hold values from 0 to 511, as said below
- embed_in: bfloat16 [50304, 1024], P('batch'), may hold values from -20 to 20
- w_qkv: bfloat16 [1024, 3072], P(('seq', 'batch')), may hold values from -0.1875 to 0.1875
- w_out: bfloat16 [1024, 1024], P(('seq', 'batch')), may hold values from -1.5 to 1.5
- w_fc: bfloat16 [1024, 4096], P(('seq', 'batch')), may hold values from -0.1875 to 0.1875
- w_proj: bfloat16 [4096, 1024], P(('seq', 'batch')), may hold values from -0.1875 to 0.1875
- norm_gains: float32 [3, 1024], replicated, may hold values from 0.5 to 1.5
- layer_biases: float32 [5, 1024], replicated, may hold values from -1.2 to 1.2
- wide_bias: float32 [7168], replicated, may hold values from -1.2 to 1.2
- unembed: bfloat16 [50304, 1024], P('batch'), may hold values from -0.375 to 0.375
- trans_weight: float32 [2, 1024, 1024], P(None, 'seq'), may hold values from -0.1875 to 0.1875
- trans_bias: float32 [2, 1024], P(None, 'seq'), may hold values from -0.6 to 0.6
- mom1_weight: float32 [2, 1024, 1024], P(None, 'seq'), may hold values from -4.5553006e-07 to 4.5553006e-07
- mom2_weight: float32 [2, 1024, 1024], P(None, 'seq'), may hold values from 4.7637196e-16 to 1.9054879e-15
- mom1_bias: float32 [2, 1024], P(None, 'seq'), may hold values from -1.3803941e-06 to 1.3803941e-06
- mom2_bias: float32 [2, 1024], P(None, 'seq'), may hold values from 4.7637196e-16 to 1.9054879e-15
Outputs:
- loss_sum: float32 [], replicated
- token_count: float32 [], replicated
- grad_norm: float32 [], replicated
- new_mom1_weight: float32 [2, 1024, 1024], P(None, 'seq')
- new_mom2_weight: float32 [2, 1024, 1024], P(None, 'seq')
- new_trans_weight: float32 [2, 1024, 1024], P(None, 'seq')
- new_mom1_bias: float32 [2, 1024], P(None, 'seq')
- new_mom2_bias: float32 [2, 1024], P(None, 'seq')
- new_trans_bias: float32 [2, 1024], P(None, 'seq')
The draws below stay inside these ranges and needn't reach their ends.
Inputs may be any that keep to these rules, and one draw needn't show every extreme that they name: `pos_weights`: 1 at positions before 128; from 128 on 2 to 4. `pad_lengths`: under half of 1024; one sequence has none, another has the most.
All inputs are finite; a program needn't handle non-finite values.
Results may differ from the reference program's by a relative error of at most 0.014.
Values may be sent and summed in bfloat16 or wider, within the bound.
A program may use at most 384 MiB of HBM per device.

```python
import math
import jax
import jax.numpy as jnp
import numpy as np
from jax import lax

D = 1024
FF = 4096
HEAD_DIM = 64
VOCAB = 50304
ROT = 16
PREFIX = 128
STEP = 10
LENGTH = 1024
SEQS = 4


def draw_pos_weights(key, part):
    key = jax.random.fold_in(key, 11)
    extra = jax.random.randint(key, (SEQS, LENGTH), 0, 2)
    places = jnp.arange(LENGTH, dtype=jnp.int32)[None, :]
    later_weight = 2 + 2 * places // LENGTH + extra
    return jnp.where(places < PREFIX, 1, later_weight).astype(jnp.int32)


def draw_pad_lengths(key, part):
    key = jax.random.fold_in(key, 12)
    first_key, second_key, third_key = jax.random.split(key, 3)
    padding = jax.random.randint(first_key, (SEQS,), 0, LENGTH // 2)
    chosen = jax.random.randint(second_key, (), 0, SEQS)
    longest = (chosen + jax.random.randint(third_key, (), 1, SEQS)) % SEQS
    rows = jnp.arange(SEQS)
    padding = jnp.where(rows == longest, LENGTH // 2 - 1, padding)
    return jnp.where(rows == chosen, 0, padding).astype(jnp.int32)


def draw_embed_in(key, part):
    key = jax.random.fold_in(key, 13)
    column_ramp = jnp.arange(D, dtype=jnp.float32) / (D - 1)
    random_part = jnp.clip(jax.random.normal(key, (VOCAB, D), jnp.float32), -4.0, 4.0)
    scaling = 3.0 ** column_ramp
    return (random_part * scaling[None, :]).astype(jnp.bfloat16)


def draw_unembed(key, part):
    key = jax.random.fold_in(key, 14)
    row_ramp = jnp.arange(VOCAB, dtype=jnp.float32) / (VOCAB - 1)
    random_part = jnp.clip(jax.random.normal(key, (VOCAB, D), jnp.float32), -4.0, 4.0)
    scaling = 1.0 + 2.0 * row_ramp
    return (random_part * scaling[:, None] / D ** 0.5).astype(jnp.bfloat16)


def set_ends(result, stream_key, low, top_value):
    place = [jax.random.randint(jax.random.fold_in(stream_key, axis), (), 0, length) for axis, length in enumerate(result.shape)]
    main_axis = result.shape.index(max(result.shape))
    neighbour = place[:main_axis] + [(place[main_axis] + 1) % result.shape[main_axis]] + place[main_axis + 1:]
    return result.at[tuple(place)].set(low).at[tuple(neighbour)].set(top_value)


def block_scale(stream_key, dims, pieces, least, largest):
    def one(position, shards_of):
        draws = jax.random.uniform(jax.random.fold_in(jax.random.fold_in(stream_key, 6), position), (shards_of,), jnp.float32, least / len(pieces), largest / len(pieces))
        return jnp.repeat(jnp.exp(draws), dims[position] // shards_of).reshape((-1,) + (1,) * (len(dims) - position - 1))

    loudness = one(*pieces[0])
    for cut in pieces[1:]:
        loudness = loudness * one(*cut)
    return loudness


def cumulative_ranks(number_of, skew):
    weights = [(1 << 20) // math.isqrt(rank ** skew) + 1 for rank in range(1, number_of + 1)]
    spread = 1 + sum(weights) // (1 << 30)
    return np.cumsum(np.array([max(1, weight // spread) for weight in weights]))


def ranked(own_key, dims, amount, skew):
    table = cumulative_ranks(amount, skew)
    lot = jax.random.randint(jax.random.fold_in(own_key, 1), dims, 0, int(table[amount - 1]))
    standing = jnp.searchsorted(jnp.asarray(table, jnp.int32), lot, side="right")
    return jax.random.permutation(jax.random.fold_in(own_key, 2), amount)[standing].astype(jnp.int32)


def noise(own_key, extent, scale, most, cuts=(), held_as=jnp.bfloat16):
    drawn = jax.random.normal(own_key, extent, jnp.float32) * scale
    if len(cuts) > 0:
        drawn = block_scale(own_key, extent, cuts, -0.22, 0.18) * drawn
    return jnp.clip(drawn, min=-most, max=most).astype(held_as)


def setup_inputs(seed: int = 0) -> dict:
    key_of = jax.random.split(jax.random.key(seed), 19)
    token_ids = set_ends(ranked(key_of[0], (SEQS, LENGTH), VOCAB, 2), jax.random.fold_in(key_of[0], 3), 0, VOCAB - 1).astype(jnp.int32)
    pos_weights = draw_pos_weights(jax.random.fold_in(key_of[18], 71), 0)
    pad_lengths = draw_pad_lengths(jax.random.fold_in(key_of[18], 71), 0)
    embed_in = draw_embed_in(jax.random.fold_in(key_of[18], 71), 0)
    w_qkv = noise(key_of[4], (D, 3 * D), D ** -0.5, 0.1875, ((0, 32),))
    w_out = noise(key_of[5], (D, D), (D // 64) ** -0.5, 1.5, ((0, 32),))
    w_fc = noise(key_of[6], (D, FF), D ** -0.5, 0.1875, ((0, 32),))
    w_proj = noise(key_of[7], (FF, D), (FF // 4) ** -0.5, 0.1875, ((0, 32),))
    norm_gains = jnp.clip(1.0 + 0.1 * jax.random.normal(key_of[8], (3, D), jnp.float32), 0.5, 1.5)
    layer_biases = noise(key_of[9], (5, D), 0.2, 1.2, (), jnp.float32)
    wide_bias = noise(key_of[10], (3 * D + FF,), 0.2, 1.2, (), jnp.float32)
    unembed = draw_unembed(jax.random.fold_in(key_of[18], 71), 0)
    trans_weight = noise(key_of[12], (2, D, D), D ** -0.5, 0.1875, ((1, 8),), jnp.float32)
    trans_bias = noise(key_of[13], (2, D), 0.1, 0.6, ((1, 8),), jnp.float32)
    mom1_weight = noise(key_of[14], (2, D, D), (0.11 * 0.001 / (2 * D * D + 2 * D) ** 0.5), 4.55530056342468e-07, ((1, 8),), jnp.float32)
    mom2_weight = jnp.clip(jnp.exp(math.log(1.905487859242116e-15) - 1.3862944 * jax.random.uniform(key_of[15], (2, D, D), jnp.float32) ** block_scale(key_of[15], (2, D, D), ((1, 8),), -0.2, 0.2)), 4.76371964810529e-16, 1.905487859242116e-15)
    mom1_bias = noise(key_of[16], (2, D), (0.33 * 0.001 / (2 * D * D + 2 * D) ** 0.5), 1.380394110128691e-06, ((1, 8),), jnp.float32)
    mom2_bias = jnp.clip(jnp.exp(math.log(1.905487859242116e-15) - 1.3862944 * jax.random.uniform(key_of[17], (2, D), jnp.float32) ** block_scale(key_of[17], (2, D), ((1, 8),), -0.2, 0.2)), 4.76371964810529e-16, 1.905487859242116e-15)
    return dict(token_ids=token_ids, pos_weights=pos_weights, pad_lengths=pad_lengths, embed_in=embed_in, w_qkv=w_qkv, w_out=w_out, w_fc=w_fc, w_proj=w_proj, norm_gains=norm_gains, layer_biases=layer_biases, wide_bias=wide_bias, unembed=unembed, trans_weight=trans_weight, trans_bias=trans_bias, mom1_weight=mom1_weight, mom2_weight=mom2_weight, mom1_bias=mom1_bias, mom2_bias=mom2_bias)


@jax.custom_vjp
def low(v):
    return lax.optimization_barrier(v.astype(jnp.bfloat16)).astype(jnp.float32)

@jax.custom_vjp
def low_back(v):
    return v

def low_keep(v):
    return (low(v), None)

def low_pass(kept, grad):
    return (grad,)

def back_keep(v):
    return (v, None)

def back_low(kept, grad):
    return (low(grad),)
low.defvjp(low_keep, low_pass)
low_back.defvjp(back_keep, back_low)
norm_eps = 1e-05
clip_max = 0.001
beta_one = 0.9
beta_two = 0.999
learn_rate = 0.03
decay_rate = 0.01
adam_eps = 1e-08
highest = lax.Precision.HIGHEST

def normalize(values, gain_row, offset_row):
    average = lax.optimization_barrier(jnp.mean(values, axis=-1, keepdims=True))
    centered = values - average
    variance = lax.optimization_barrier(jnp.mean(centered * centered, axis=-1, keepdims=True))
    return centered * lax.rsqrt(variance + norm_eps) * gain_row + offset_row

def rotate(vectors, places):
    half_rot = ROT // 2
    frequency = 10000.0 ** (-2.0 * jnp.arange(half_rot, dtype=jnp.float32) / ROT)
    angles = places.astype(jnp.float32)[:, None] * frequency[None, :]
    cosine = jnp.cos(angles)[:, None, :]
    sine = jnp.sin(angles)[:, None, :]
    lower_part = vectors[..., :half_rot]
    upper_part = vectors[..., half_rot:ROT]
    return jnp.concatenate([lower_part * cosine - upper_part * sine, upper_part * cosine + lower_part * sine, vectors[..., ROT:]], axis=-1)

def adam_update(weight, gradient, earlier, later):
    earlier = beta_one * earlier + (1.0 - beta_one) * gradient
    later = beta_two * later + (1.0 - beta_two) * gradient * gradient
    update = earlier / (1.0 - beta_one ** STEP) / (jnp.sqrt(later / (1.0 - beta_two ** STEP)) + adam_eps)
    return (earlier, later, weight * (1.0 - learn_rate * decay_rate) - learn_rate * update)

def frozen_layer(token_row, embed, matrices, norm_gains, layer_biases, wide_bias):
    joined_w, out_w, fc_w, proj_w = matrices
    width = embed.shape[1]
    head_count = width // HEAD_DIM
    places = jnp.arange(LENGTH, dtype=jnp.int32)
    stream0 = jnp.take(embed, token_row, axis=0)
    x_attn = low(normalize(stream0, norm_gains[0], layer_biases[0]))
    x_mlp = low(normalize(stream0, norm_gains[1], layer_biases[1]))
    joined = (jnp.dot(x_attn, joined_w, precision=highest) + wide_bias[:3 * width]).reshape(LENGTH, 3, head_count, HEAD_DIM)
    queries = low(rotate(joined[:, 0], places))
    key_rows = low(rotate(joined[:, 1], places))
    value_rows = low(joined[:, 2])
    size = 512 if LENGTH % 512 == 0 else LENGTH

    def query_block(offset):
        block_q = lax.dynamic_slice_in_dim(queries, offset, size, 0)
        scores = jnp.einsum('qhd,khd->hqk', block_q, key_rows, precision=highest) * HEAD_DIM ** (-0.5)
        allowed = places[None, :] <= (offset + jnp.arange(size, dtype=jnp.int32))[:, None]
        scores = jnp.where(allowed[None], scores, -1e+30)
        peak = lax.optimization_barrier(jnp.max(scores, axis=-1, keepdims=True))
        exponent = jnp.where(allowed[None], jnp.exp(scores - peak), 0.0)
        mixed = jnp.einsum('hqk,khd->qhd', low(exponent), value_rows, precision=highest)
        return low((mixed / jnp.transpose(lax.optimization_barrier(jnp.sum(exponent, axis=-1)))[:, :, None]).reshape(size, width))
    offsets = jnp.arange(LENGTH // size, dtype=jnp.int32) * size
    attended = lax.map(query_block, offsets).reshape(LENGTH, width)
    attn = jnp.dot(attended, out_w, precision=highest) + layer_biases[2]
    hidden = low(jax.nn.gelu(jnp.dot(x_mlp, fc_w, precision=highest) + wide_bias[3 * width:], approximate=False))
    mlp = jnp.dot(hidden, proj_w, precision=highest) + layer_biases[3]
    return (stream0, stream0 + attn + mlp)

def reference(token_ids, pos_weights, pad_lengths, embed_in, w_qkv, w_out, w_fc, w_proj, norm_gains, layer_biases, wide_bias, unembed, trans_weight, trans_bias, mom1_weight, mom2_weight, mom1_bias, mom2_bias):
    embed = embed_in.astype(jnp.float32)
    table = unembed.astype(jnp.float32)
    matrices = tuple((matrix.astype(jnp.float32) for matrix in (w_qkv, w_out, w_fc, w_proj)))
    streams0, streams1 = lax.map(lambda token_row: frozen_layer(token_row, embed, matrices, norm_gains, layer_biases, wide_bias), token_ids)
    places = jnp.arange(LENGTH, dtype=jnp.int32)
    living = places[None, :] < (LENGTH - pad_lengths)[:, None]
    token_weight = jnp.where(living, pos_weights, 0).astype(jnp.float32)
    token_count = jnp.sum(token_weight)
    flat_rows = SEQS * LENGTH
    size = 512 if flat_rows % 512 == 0 else flat_rows
    count_blocks = flat_rows // size
    width = embed.shape[1]
    blocks0 = streams0.reshape(count_blocks, size, width)
    blocks1 = streams1.reshape(count_blocks, size, width)
    weight_blocks = token_weight.reshape(count_blocks, size)
    gain_final = norm_gains[2]
    offset_final = layer_biases[4]

    def loss_fn(trans_w, trans_b):
        trans_low = low(trans_w)

        def block_loss(block_args):
            base0, base1, weight_row = block_args
            model_state = low(normalize(base1, gain_final, offset_final))
            model_logits = jnp.dot(model_state, table.T, precision=highest)
            model_lse = jax.nn.logsumexp(model_logits, axis=-1)
            model_probs = jnp.exp(model_logits - model_lse[:, None])
            summed = jnp.zeros((), jnp.float32)
            for index, (stream, stream_low) in enumerate(((base0, base0), (base1, low(base1)))):
                projected = low_back(jnp.dot(stream_low, trans_low[index], precision=highest))
                state = low(normalize(stream + projected + trans_b[index], gain_final, offset_final))
                probe_logits = low_back(jnp.dot(state, table.T, precision=highest))
                probe_lse = jax.nn.logsumexp(probe_logits, axis=-1)
                diverge = lax.optimization_barrier(jnp.sum(model_probs * (model_logits - probe_logits), axis=-1)) - model_lse + probe_lse
                summed = summed + jnp.sum(weight_row * diverge)
            return summed
        return jnp.sum(lax.map(jax.checkpoint(block_loss), (blocks0, blocks1, weight_blocks)))
    loss_sum, pull_back = jax.vjp(loss_fn, trans_weight, trans_bias)
    grad_w, grad_b = pull_back(1.0 / token_count)
    grad_norm = jnp.sqrt(jnp.sum(grad_w * grad_w) + jnp.sum(grad_b * grad_b))
    factor = jnp.minimum(1.0, clip_max / (grad_norm + 1e-06))
    first_w, second_w, new_w = adam_update(trans_weight, grad_w * factor, mom1_weight, mom2_weight)
    first_b, second_b, new_b = adam_update(trans_bias, grad_b * factor, mom1_bias, mom2_bias)
    return (loss_sum, token_count, grad_norm, first_w, second_w, new_w, first_b, second_b, new_b)
```

```python
import functools

import jax
import jax.numpy as jnp
from jax import lax
from jax.experimental import pallas as pl
from jax.experimental.pallas import tpu as pltpu
from jax.sharding import PartitionSpec as P

HEAD_DIM = 64
ROT = 16
STEP = 10


VOCAB_TILE = 1280
LANES = 128
NEGATIVE = -1e30
VMEM_BYTES = 60 * 1024 * 1024
norm_eps = 1e-05
clip_max = 0.001
beta_one = 0.9
beta_two = 0.999
learn_rate = 0.03
decay_rate = 0.01
adam_eps = 1e-08


def merged(part, axis, combine):
    gathered = jax.tree.map(lambda a: lax.all_gather(a, axis), part)

    def take(source):
        return jax.tree.map(lambda a: lax.dynamic_index_in_dim(a, source, 0, False), gathered)

    return lax.fori_loop(
        1, lax.axis_size(axis), lambda source, state: combine(state, take(source)), take(0)
    )


def normalize(values, gain_row, offset_row):
    average = jnp.mean(values, axis=-1, keepdims=True)
    centered = values - average
    variance = jnp.mean(centered * centered, axis=-1, keepdims=True)
    return centered * lax.rsqrt(variance + norm_eps) * gain_row + offset_row


def norm_back(values, upstream, gain_row):
    average = jnp.mean(values, axis=-1, keepdims=True)
    centered = values - average
    variance = jnp.mean(centered * centered, axis=-1, keepdims=True)
    inverse = lax.rsqrt(variance + norm_eps)
    unit = centered * inverse
    scaled = upstream * gain_row
    return (
        scaled
        - jnp.mean(scaled, axis=-1, keepdims=True)
        - unit * jnp.mean(scaled * unit, axis=-1, keepdims=True)
    ) * inverse


def rotate(vectors, places):
    half_rot = ROT // 2
    frequency = 10000.0 ** (-2.0 * jnp.arange(half_rot, dtype=jnp.float32) / ROT)
    angles = places.astype(jnp.float32)[:, None] * frequency[None, :]
    cosine = jnp.cos(angles)[:, None, :]
    sine = jnp.sin(angles)[:, None, :]
    lower_part = vectors[..., :half_rot]
    upper_part = vectors[..., half_rot:ROT]
    return jnp.concatenate(
        [
            lower_part * cosine - upper_part * sine,
            upper_part * cosine + lower_part * sine,
            vectors[..., ROT:],
        ],
        axis=-1,
    )


def adam_update(weight, gradient, earlier, later):
    earlier = beta_one * earlier + (1.0 - beta_one) * gradient
    later = beta_two * later + (1.0 - beta_two) * gradient * gradient
    update = (
        earlier / (1.0 - beta_one**STEP) / (jnp.sqrt(later / (1.0 - beta_two**STEP)) + adam_eps)
    )
    return (earlier, later, weight * (1.0 - learn_rate * decay_rate) - learn_rate * update)


def forward_kernel(vocab, states_ref, table_ref, exps_ref, cols_ref, sums_ref, cross_ref, left, right, peak):
    tile = pl.program_id(0)
    rows = states_ref.shape[1]
    width = table_ref.shape[0]
    chunk = left.shape[0] // 3
    group = 16
    piece = 256
    limit = vocab - tile * width
    last = vocab - (pl.cdiv(vocab, width) - 1) * width
    lane = lax.broadcasted_iota(jnp.int32, (group, LANES), 1)

    @pl.when(tile == 0)
    def _():
        peak[...] = jnp.full_like(peak, NEGATIVE)
        cols_ref[...] = jnp.zeros_like(cols_ref)
        sums_ref[...] = jnp.zeros_like(sums_ref)
        cross_ref[...] = jnp.zeros_like(cross_ref)

    def multiply(index, target, start):
        table = table_ref[start : start + piece, :]
        for state in range(3):
            target[state * chunk : (state + 1) * chunk, start : start + piece] = lax.dot_general(
                states_ref[state, index * chunk : (index + 1) * chunk, :],
                table,
                (((1,), (1,)), ((), ())),
                preferred_element_type=jnp.float32,
            )

    def reduce_rows(index, source, part):
        begin = index * chunk + part * group
        span = slice(begin, begin + group)

        def logits(state, block):
            value = source[
                state * chunk + part * group : state * chunk + (part + 1) * group,
                block * LANES : (block + 1) * LANES,
            ]
            if (block + 1) * LANES > last:
                value = jnp.where(lane + block * LANES < limit, value, NEGATIVE)
            return value

        blocks = width // LANES
        tops = []
        totals = []
        for state in range(3):
            top = logits(state, 0)
            for block in range(1, blocks):
                top = jnp.maximum(top, logits(state, block))
            before = peak[state, span, :]
            now = jnp.maximum(before, jnp.max(top, axis=-1, keepdims=True))
            peak[state, span, :] = now
            cols_ref[state, span, :] = jnp.where(lane == tile, now, cols_ref[state, span, :])
            fade = jnp.exp(before - now)
            tops.append(now)
            totals.append(sums_ref[state, span, :] * fade)
            if state == 0:
                crossing = [cross_ref[other, span, :] * fade for other in range(2)]
        for block in range(blocks):
            place = slice(block * LANES, (block + 1) * LANES)
            base = logits(0, block)
            base_exp = jnp.exp(base - tops[0])
            totals[0] += base_exp
            exps_ref[0, 0, span, place] = base_exp.astype(jnp.bfloat16)
            for state in range(1, 3):
                value = logits(state, block)
                value_exp = jnp.exp(value - tops[state])
                totals[state] += value_exp
                exps_ref[0, state, span, place] = value_exp.astype(jnp.bfloat16)
                crossing[state - 1] += base_exp * (base - value)
        for state in range(3):
            sums_ref[state, span, :] = totals[state]
        for other in range(2):
            cross_ref[other, span, :] = crossing[other]

    count = rows // chunk
    groups = chunk // group
    pieces = width // piece
    buffers = (left, right)
    for index in range(count + 1):
        done = 0
        for step in range(pieces):
            if index < count:
                multiply(index, buffers[index % 2], step * piece)
            if index > 0:
                upto = (step + 1) * groups // pieces
                for part in range(done, upto):
                    reduce_rows(index - 1, buffers[(index - 1) % 2], part)
                done = upto


def vocab_forward(states, table):
    _, rows, depth = states.shape
    vocab = table.shape[0]
    tiles = pl.cdiv(vocab, VOCAB_TILE)
    chunk = 128
    stat = lambda count: pl.BlockSpec((count, rows, LANES), lambda i: (0, 0, 0))
    return pl.pallas_call(
        functools.partial(forward_kernel, vocab),
        grid=(tiles,),
        in_specs=[
            pl.BlockSpec((3, rows, depth), lambda i: (0, 0, 0)),
            pl.BlockSpec((VOCAB_TILE, depth), lambda i: (i, 0)),
        ],
        out_specs=[
            pl.BlockSpec((1, 3, rows, VOCAB_TILE), lambda i: (i, 0, 0, 0)),
            stat(3),
            stat(3),
            stat(2),
        ],
        out_shape=[
            jax.ShapeDtypeStruct((tiles, 3, rows, VOCAB_TILE), jnp.bfloat16),
            jax.ShapeDtypeStruct((3, rows, LANES), jnp.float32),
            jax.ShapeDtypeStruct((3, rows, LANES), jnp.float32),
            jax.ShapeDtypeStruct((2, rows, LANES), jnp.float32),
        ],
        scratch_shapes=[
            pltpu.VMEM((3 * chunk, VOCAB_TILE), jnp.float32),
            pltpu.VMEM((3 * chunk, VOCAB_TILE), jnp.float32),
            pltpu.VMEM((3, rows, LANES), jnp.float32),
        ],
        compiler_params=pltpu.CompilerParams(vmem_limit_bytes=VMEM_BYTES),
        cost_estimate=pl.CostEstimate(
            flops=6 * rows * depth * vocab,
            bytes_accessed=2 * vocab * (depth + 3 * rows),
            transcendentals=3 * rows * vocab,
        ),
        name="vocab_forward",
    )(states, table)


def backward_kernel(vocab, exps_ref, scales_ref, table_ref, out_ref, left, right, tail):
    tile = pl.program_id(0)
    rows = exps_ref.shape[2]
    width, depth = table_ref.shape
    chunk = left.shape[0] // 2
    group = 16
    piece = 256
    limit = vocab - tile * width
    last = vocab - (pl.cdiv(vocab, width) - 1) * width
    whole = last // piece * piece
    lane = lax.broadcasted_iota(jnp.int32, (group, LANES), 1)

    @pl.when(tile == 0)
    def _():
        out_ref[...] = jnp.zeros_like(out_ref)

    below = lax.broadcasted_iota(jnp.int32, (width - whole, depth), 0) + whole < limit
    tail[...] = jnp.where(below, table_ref[whole:, :], jnp.zeros((), tail.dtype))

    def differences(index, target, part):
        begin = index * chunk + part * group
        span = slice(begin, begin + group)
        factors = [
            jnp.sum(jnp.where(lane == tile, scales_ref[state, span, :], 0.0), axis=-1, keepdims=True)
            for state in range(3)
        ]
        factors = [jnp.broadcast_to(factor, (group, LANES)) for factor in factors]
        for block in range(width // LANES):
            place = slice(block * LANES, (block + 1) * LANES)
            base = exps_ref[0, 0, span, place].astype(jnp.float32) * factors[0]
            for state in range(1, 3):
                value = exps_ref[0, state, span, place].astype(jnp.float32) * factors[state]
                target[
                    (state - 1) * chunk + part * group : (state - 1) * chunk + (part + 1) * group, place
                ] = (value - base).astype(jnp.bfloat16)

    def multiply(index, source, start):
        place = slice(start, start + piece)
        span = slice(index * chunk, (index + 1) * chunk)
        part = jnp.dot(
            source[:, whole:], tail[:, place], preferred_element_type=jnp.float32
        )
        if whole > 0:
            part += jnp.dot(
                source[:, :whole], table_ref[:whole, place], preferred_element_type=jnp.float32
            )
        for probe in range(2):
            out_ref[probe, span, place] += part[probe * chunk : (probe + 1) * chunk]

    count = rows // chunk
    groups = chunk // group
    pieces = depth // piece
    buffers = (left, right)
    for index in range(count + 1):
        done = 0
        for step in range(pieces):
            if index > 0:
                multiply(index - 1, buffers[(index - 1) % 2], step * piece)
            if index < count:
                upto = (step + 1) * groups // pieces
                for part in range(done, upto):
                    differences(index, buffers[index % 2], part)
                done = upto


def vocab_backward(exps, scales, table):
    tiles, _, rows, _ = exps.shape
    vocab, depth = table.shape
    chunk = 256
    last = vocab - (tiles - 1) * VOCAB_TILE
    return pl.pallas_call(
        functools.partial(backward_kernel, vocab),
        grid=(tiles,),
        in_specs=[
            pl.BlockSpec((1, 3, rows, VOCAB_TILE), lambda i: (i, 0, 0, 0)),
            pl.BlockSpec((3, rows, LANES), lambda i: (0, 0, 0)),
            pl.BlockSpec((VOCAB_TILE, depth), lambda i: (i, 0)),
        ],
        out_specs=pl.BlockSpec((2, rows, depth), lambda i: (0, 0, 0)),
        out_shape=jax.ShapeDtypeStruct((2, rows, depth), jnp.float32),
        scratch_shapes=[
            pltpu.VMEM((2 * chunk, VOCAB_TILE), jnp.bfloat16),
            pltpu.VMEM((2 * chunk, VOCAB_TILE), jnp.bfloat16),
            pltpu.VMEM((VOCAB_TILE - last // 256 * 256, depth), jnp.bfloat16),
        ],
        compiler_params=pltpu.CompilerParams(vmem_limit_bytes=VMEM_BYTES),
        cost_estimate=pl.CostEstimate(
            flops=4 * rows * depth * vocab,
            bytes_accessed=2 * vocab * (depth + 3 * rows),
            transcendentals=0,
        ),
        name="vocab_backward",
    )(exps, scales, table)


def body(
    token_ids,
    pos_weights,
    pad_lengths,
    embed_in,
    w_qkv,
    w_out,
    w_fc,
    w_proj,
    norm_gains,
    layer_biases,
    wide_bias,
    unembed,
    trans_weight,
    trans_bias,
    mom1_weight,
    mom2_weight,
    mom1_bias,
    mom2_bias,
):
    tok_rows = token_ids.shape[1]
    width = embed_in.shape[1]
    vocab_rows = unembed.shape[0]
    n_seq = lax.axis_size("seq")
    batch_index = lax.axis_index("batch")
    seq_index = lax.axis_index("seq")
    all_ids, all_weights, all_padding = (
        lax.all_gather(token_ids, "batch", axis=0, tiled=True),
        lax.all_gather(pos_weights, "batch", axis=0, tiled=True),
        lax.all_gather(pad_lengths, "batch", axis=0, tiled=True),
    )
    local_places = seq_index * tok_rows + jnp.arange(tok_rows, dtype=jnp.int32)
    living = local_places[None, :] < (tok_rows * n_seq - all_padding)[:, None]
    weight_all = jnp.where(living, all_weights, 0).astype(jnp.float32)
    weight_own = lax.dynamic_slice_in_dim(weight_all, batch_index, 1, 0)[0]
    token_count = lax.psum(jnp.sum(weight_own), ("seq", "batch"))
    flat_ids = all_ids.reshape(-1)
    vocab_start = batch_index * vocab_rows
    wanted = flat_ids - vocab_start
    inside = (wanted >= 0) & (wanted < vocab_rows)
    picked = jnp.take(embed_in, jnp.clip(wanted, 0, vocab_rows - 1), axis=0)
    stream0 = lax.psum_scatter(
        jnp.where(inside[:, None], picked.astype(jnp.float32), 0.0).astype(jnp.bfloat16),
        "batch",
        scatter_dimension=0,
        tiled=True,
    ).astype(jnp.float32)
    joined_w, out_w, fc_w, proj_w = (
        lax.all_gather(w_qkv, ("seq", "batch"), axis=0, tiled=True),
        lax.all_gather(w_out, ("seq", "batch"), axis=0, tiled=True),
        lax.all_gather(w_fc, ("seq", "batch"), axis=0, tiled=True),
        lax.all_gather(w_proj, ("seq", "batch"), axis=0, tiled=True),
    )
    trans_full, bias_full = (
        lax.all_gather(trans_weight.astype(jnp.bfloat16), "seq", axis=1, tiled=True).astype(
            trans_weight.dtype
        ),
        lax.all_gather(trans_bias.astype(jnp.bfloat16), "seq", axis=1, tiled=True).astype(
            trans_bias.dtype
        ),
    )
    head_count = width // HEAD_DIM
    x_attn = normalize(stream0, norm_gains[0], layer_biases[0]).astype(jnp.bfloat16)
    x_mlp = normalize(stream0, norm_gains[1], layer_biases[1]).astype(jnp.bfloat16)
    joined = (
        jnp.dot(x_attn, joined_w, preferred_element_type=jnp.float32) + wide_bias[: 3 * width]
    ).reshape(tok_rows, 3, head_count, HEAD_DIM)
    queries = rotate(joined[:, 0], local_places).astype(jnp.bfloat16)
    key_rows = rotate(joined[:, 1], local_places).astype(jnp.bfloat16).reshape(tok_rows, width)
    value_rows = joined[:, 2].astype(jnp.bfloat16).reshape(tok_rows, width)
    peaks = jnp.full((head_count, tok_rows), -1e30, jnp.float32)
    key_part = lax.all_gather(key_rows, "seq", axis=0, tiled=True).reshape(-1, head_count, HEAD_DIM)
    value_part = lax.all_gather(value_rows, "seq", axis=0, tiled=True).reshape(
        -1, head_count, HEAD_DIM
    )
    scores = jnp.einsum(
        "qhd,khd->hqk", queries, key_part, preferred_element_type=jnp.float32
    ) * HEAD_DIM ** (-0.5)
    key_places = jnp.arange(key_part.shape[0], dtype=jnp.int32)
    allowed = (key_places[None, :] <= local_places[:, None])[None]
    scores = jnp.where(allowed, scores, -1e30)
    new_peaks = jnp.maximum(peaks, jnp.max(scores, axis=-1))
    exponent = jnp.where(allowed, jnp.exp(scores - new_peaks[..., None]), 0.0)
    weighted = jnp.einsum(
        "hqk,khd->hqd",
        exponent.astype(jnp.bfloat16),
        value_part,
        preferred_element_type=jnp.float32,
    )
    weighted, peaks, summed = (weighted, new_peaks, jnp.sum(exponent, axis=-1))
    attended = (
        jnp.transpose(weighted / summed[..., None], (1, 0, 2))
        .reshape(tok_rows, width)
        .astype(jnp.bfloat16)
    )
    attn = jnp.dot(attended, out_w, preferred_element_type=jnp.float32) + layer_biases[2]
    hidden = jax.nn.gelu(
        jnp.dot(x_mlp, fc_w, preferred_element_type=jnp.float32) + wide_bias[3 * width :],
        approximate=False,
    ).astype(jnp.bfloat16)
    stream1 = (
        stream0
        + attn
        + jnp.dot(hidden, proj_w, preferred_element_type=jnp.float32)
        + layer_biases[3]
    )
    gain_final = norm_gains[2]
    offset_final = layer_biases[4]
    probe_in = (stream0, stream1)
    probe_low = (stream0.astype(jnp.bfloat16), stream1.astype(jnp.bfloat16))
    trans_low = trans_full.astype(jnp.bfloat16)
    translated = [
        probe_in[index]
        + jnp.dot(probe_low[index], trans_low[index], preferred_element_type=jnp.float32)
        + bias_full[index]
        for index in range(2)
    ]
    states = jnp.stack(
        [
            normalize(stream1, gain_final, offset_final),
            normalize(translated[0], gain_final, offset_final),
            normalize(translated[1], gain_final, offset_final),
        ]
    ).astype(jnp.bfloat16)
    gathered = lax.all_gather(states, "batch", axis=1, tiled=True)
    all_rows = gathered.shape[1]

    exps, peak_cols, sums_lane, cross_lane = vocab_forward(gathered, unembed)
    tiles = exps.shape[0]
    peak_all = peak_cols[:, :, tiles - 1]
    sums_all = jnp.sum(sums_lane, axis=-1)
    cross_all = jnp.sum(cross_lane, axis=-1)

    def combine(earlier, later):
        peak_a, sums_a, cross_a = earlier
        peak_b, sums_b, cross_b = later
        peak_new = jnp.maximum(peak_a, peak_b)
        factor_a = jnp.exp(peak_a - peak_new)
        factor_b = jnp.exp(peak_b - peak_new)
        return (
            peak_new,
            sums_a * factor_a + sums_b * factor_b,
            cross_a * factor_a[0] + cross_b * factor_b[0],
        )

    peak_all, sums_all, cross_all = merged((peak_all, sums_all, cross_all), "batch", combine)
    log_totals = peak_all + jnp.log(sums_all)
    diverge = cross_all / sums_all[0] - log_totals[0] + log_totals[1:]
    diverge_own = lax.dynamic_slice_in_dim(diverge, batch_index * tok_rows, tok_rows, 1)
    loss_local = jnp.sum(weight_own * (diverge_own[0] + diverge_own[1]))
    token_coef = weight_all.reshape(-1) / token_count
    scales = token_coef[None, :, None] * jnp.exp(peak_cols - log_totals[:, :, None])
    partial = vocab_backward(exps, scales, unembed)
    dstates = (
        lax.psum_scatter(
            jnp.transpose(partial, (1, 0, 2)).reshape(all_rows, 2 * width).astype(jnp.bfloat16),
            "batch",
            scatter_dimension=0,
            tiled=True,
        )
        .astype(jnp.float32)
        .reshape(tok_rows, 2, width)
    )
    grad_w_list = []
    grad_b_list = []
    for index in range(2):
        delta = norm_back(translated[index], dstates[:, index], gain_final)
        grad_w_list.append(
            jnp.einsum(
                "td,te->de",
                probe_low[index],
                delta.astype(jnp.bfloat16),
                preferred_element_type=jnp.float32,
            )
        )
        grad_b_list.append(jnp.sum(delta, axis=0))
    grad_w = jnp.stack(grad_w_list)
    grad_b = jnp.stack(grad_b_list)
    grad_w, grad_b = (
        lax.psum(grad_w.astype(jnp.bfloat16), "batch").astype(jnp.float32),
        lax.psum(grad_b.astype(jnp.bfloat16), "batch").astype(jnp.float32),
    )
    grad_w, grad_b = (
        lax.psum_scatter(
            grad_w.astype(jnp.bfloat16), "seq", scatter_dimension=1, tiled=True
        ).astype(jnp.float32),
        lax.psum_scatter(
            grad_b.astype(jnp.bfloat16), "seq", scatter_dimension=1, tiled=True
        ).astype(jnp.float32),
    )
    squares = jnp.sum(grad_w * grad_w) + jnp.sum(grad_b * grad_b)
    first_copy = (batch_index == 0).astype(jnp.float32)
    loss_sum, norm_square = lax.psum((loss_local, squares * first_copy), ("seq", "batch"))
    grad_norm = jnp.sqrt(norm_square)
    factor = jnp.minimum(1.0, clip_max / (grad_norm + 1e-06))
    first_w, second_w, new_w = adam_update(trans_weight, grad_w * factor, mom1_weight, mom2_weight)
    first_b, second_b, new_b = adam_update(trans_bias, grad_b * factor, mom1_bias, mom2_bias)
    return (loss_sum, token_count, grad_norm, first_w, second_w, new_w, first_b, second_b, new_b)


def solution(mesh):
    return jax.shard_map(
        body,
        mesh=mesh,
        in_specs=(
            P("batch", "seq"),
            P("batch", "seq"),
            P("batch"),
            P("batch", None),
            P(("seq", "batch"), None),
            P(("seq", "batch"), None),
            P(("seq", "batch"), None),
            P(("seq", "batch"), None),
            P(),
            P(),
            P(),
            P("batch", None),
            P(None, "seq", None),
            P(None, "seq"),
            P(None, "seq", None),
            P(None, "seq", None),
            P(None, "seq"),
            P(None, "seq"),
        ),
        out_specs=(
            P(),
            P(),
            P(),
            P(None, "seq", None),
            P(None, "seq", None),
            P(None, "seq", None),
            P(None, "seq"),
            P(None, "seq"),
            P(None, "seq"),
        ),
        check_vma=False,
    )
```

```python
import functools

import jax
import jax.numpy as jnp
from jax import lax
from jax.experimental import pallas as pl
from jax.experimental.pallas import tpu as pltpu
from jax.sharding import PartitionSpec as P

HEAD_DIM = 64
ROT = 16
STEP = 10


VOCAB_TILE = 1280
LANES = 128
NEGATIVE = -1e30
VMEM_BYTES = 60 * 1024 * 1024
norm_eps = 1e-05
clip_max = 0.001
beta_one = 0.9
beta_two = 0.999
learn_rate = 0.03
decay_rate = 0.01
adam_eps = 1e-08


def merged(part, axis, combine):
    gathered = jax.tree.map(lambda a: lax.all_gather(a, axis), part)

    def take(source):
        return jax.tree.map(lambda a: lax.dynamic_index_in_dim(a, source, 0, False), gathered)

    return lax.fori_loop(
        1, lax.axis_size(axis), lambda source, state: combine(state, take(source)), take(0)
    )


def normalize(values, gain_row, offset_row):
    average = jnp.mean(values, axis=-1, keepdims=True)
    centered = values - average
    variance = jnp.mean(centered * centered, axis=-1, keepdims=True)
    return centered * lax.rsqrt(variance + norm_eps) * gain_row + offset_row


def norm_back(values, upstream, gain_row):
    average = jnp.mean(values, axis=-1, keepdims=True)
    centered = values - average
    variance = jnp.mean(centered * centered, axis=-1, keepdims=True)
    inverse = lax.rsqrt(variance + norm_eps)
    unit = centered * inverse
    scaled = upstream * gain_row
    return (
        scaled
        - jnp.mean(scaled, axis=-1, keepdims=True)
        - unit * jnp.mean(scaled * unit, axis=-1, keepdims=True)
    ) * inverse


def rotate(vectors, places):
    half_rot = ROT // 2
    frequency = 10000.0 ** (-2.0 * jnp.arange(half_rot, dtype=jnp.float32) / ROT)
    angles = places.astype(jnp.float32)[:, None] * frequency[None, :]
    cosine = jnp.cos(angles)[:, None, :]
    sine = jnp.sin(angles)[:, None, :]
    lower_part = vectors[..., :half_rot]
    upper_part = vectors[..., half_rot:ROT]
    return jnp.concatenate(
        [
            lower_part * cosine - upper_part * sine,
            upper_part * cosine + lower_part * sine,
            vectors[..., ROT:],
        ],
        axis=-1,
    )


def adam_update(weight, gradient, earlier, later):
    earlier = beta_one * earlier + (1.0 - beta_one) * gradient
    later = beta_two * later + (1.0 - beta_two) * gradient * gradient
    update = (
        earlier / (1.0 - beta_one**STEP) / (jnp.sqrt(later / (1.0 - beta_two**STEP)) + adam_eps)
    )
    return (earlier, later, weight * (1.0 - learn_rate * decay_rate) - learn_rate * update)


def forward_kernel(vocab, states_ref, table_ref, first_ref, second_ref, peaks_ref, sums_ref, cross_ref, turned, left, right, peak):
    step = pl.program_id(0)
    steps = pl.num_programs(0) - 1
    width = table_ref.shape[0]
    half = left.shape[1] // 3
    group = 16
    last = vocab - (pl.cdiv(vocab, width) - 1) * width
    row = lax.broadcasted_iota(jnp.int32, (group, LANES), 0)

    def reset(part):
        span = slice(part * half, (part + 1) * half)
        peak[:, span] = jnp.full((8, half), NEGATIVE, jnp.float32)
        sums_ref[:, :, span] = jnp.zeros((3, 8, half), jnp.float32)
        cross_ref[:, :, span] = jnp.zeros((2, 8, half), jnp.float32)

    @pl.when(step == 0)
    def _():
        reset(0)
        for state in range(3):
            for part in range(2):
                turned[part, :, state * half : (state + 1) * half] = jnp.transpose(
                    states_ref[state, part * half : (part + 1) * half, :]
                )

    @pl.when(step <= 1)
    def _():
        reset(1)

    def multiply(part, target, state):
        place = slice(state * half, (state + 1) * half)
        target[:, place] = jnp.dot(
            table_ref[...], turned[part, :, place], preferred_element_type=jnp.float32
        )

    def units(part, source, target, tile):
        limit = vocab - tile * width
        blocks = width // group
        result = []
        for lanes in range(half // LANES):
            span = slice(part * half + lanes * LANES, part * half + (lanes + 1) * LANES)
            local = slice(lanes * LANES, (lanes + 1) * LANES)
            held = {}

            def logits(state, block, lanes=lanes):
                begin = state * half + lanes * LANES
                value = source[block * group : (block + 1) * group, begin : begin + LANES]
                if (block + 1) * group > last:
                    value = jnp.where(row + block * group < limit, value, NEGATIVE)
                return value

            def tops(span=span, held=held, logits=logits):
                held["top"], held["sum"], held["cross"] = [], [], []
                for state in range(3):
                    top = logits(state, 0)
                    for block in range(1, blocks):
                        top = jnp.maximum(top, logits(state, block))
                    before = peak[state : state + 1, span]
                    now = jnp.maximum(before, jnp.max(top, axis=0, keepdims=True))
                    peak[state : state + 1, span] = now
                    peaks_ref[pl.ds(tile, 1), state, span] = now
                    fade = jnp.exp(before - now)
                    held["top"].append(jnp.broadcast_to(now, (group, LANES)))
                    held["sum"].append(sums_ref[state, :, span] * fade)
                    if state == 0:
                        held["cross"] = [cross_ref[other, :, span] * fade for other in range(2)]

            def fold(value):
                return value[:8] + value[8:]

            def powers(begin, end, held=held, logits=logits, local=local, fold=fold):
                for block in range(begin, end):
                    place = slice(block * group, (block + 1) * group)
                    base = logits(0, block)
                    base_exp = jnp.exp(base - held["top"][0])
                    held["sum"][0] += fold(base_exp)
                    target[0, 0, place, local] = base_exp.astype(jnp.bfloat16)
                    for state in range(1, 3):
                        value = logits(state, block)
                        value_exp = jnp.exp(value - held["top"][state])
                        held["sum"][state] += fold(value_exp)
                        target[0, state, place, local] = value_exp.astype(jnp.bfloat16)
                        held["cross"][state - 1] += fold(base_exp * (base - value))

            def finish(span=span, held=held):
                for state in range(3):
                    sums_ref[state, :, span] = held["sum"][state]
                for other in range(2):
                    cross_ref[other, :, span] = held["cross"][other]

            result.append(tops)
            cuts = 5
            for cut in range(cuts):
                result.append(
                    functools.partial(powers, cut * blocks // cuts, (cut + 1) * blocks // cuts)
                )
            result.append(finish)
        return result

    def stage(part, target, work):
        done = 0
        for state in range(3):
            multiply(part, target, state)
            upto = (state + 1) * len(work) // 3
            for unit in work[done:upto]:
                unit()
            done = upto

    before = jnp.maximum(step - 1, 0)

    @pl.when(step < steps)
    def _():
        stage(0, left, units(1, right, second_ref, before))
        stage(1, right, units(0, left, first_ref, step))

    @pl.when(step == steps)
    def _():
        for unit in units(1, right, second_ref, before):
            unit()


def vocab_forward(states, table):
    _, rows, depth = states.shape
    vocab = table.shape[0]
    tiles = pl.cdiv(vocab, VOCAB_TILE)
    half = rows // 2
    kept = jax.ShapeDtypeStruct((tiles, 3, VOCAB_TILE, half), jnp.bfloat16)
    block = (1, 3, VOCAB_TILE, half)
    whole = lambda *shape: pl.BlockSpec(shape, lambda i: (0,) * len(shape))
    return pl.pallas_call(
        functools.partial(forward_kernel, vocab),
        grid=(tiles + 1,),
        in_specs=[
            whole(3, rows, depth),
            pl.BlockSpec((VOCAB_TILE, depth), lambda i: (jnp.minimum(i, tiles - 1), 0)),
        ],
        out_specs=[
            pl.BlockSpec(block, lambda i: (jnp.minimum(i, tiles - 1), 0, 0, 0)),
            pl.BlockSpec(block, lambda i: (jnp.maximum(i - 1, 0), 0, 0, 0)),
            whole(tiles, 3, rows),
            whole(3, 8, rows),
            whole(2, 8, rows),
        ],
        out_shape=[
            kept,
            kept,
            jax.ShapeDtypeStruct((tiles, 3, rows), jnp.float32),
            jax.ShapeDtypeStruct((3, 8, rows), jnp.float32),
            jax.ShapeDtypeStruct((2, 8, rows), jnp.float32),
        ],
        scratch_shapes=[
            pltpu.VMEM((2, depth, 3 * half), jnp.bfloat16),
            pltpu.VMEM((VOCAB_TILE, 3 * half), jnp.float32),
            pltpu.VMEM((VOCAB_TILE, 3 * half), jnp.float32),
            pltpu.VMEM((8, rows), jnp.float32),
        ],
        compiler_params=pltpu.CompilerParams(vmem_limit_bytes=VMEM_BYTES),
        cost_estimate=pl.CostEstimate(
            flops=6 * rows * depth * vocab,
            bytes_accessed=2 * vocab * (depth + 3 * rows),
            transcendentals=3 * rows * vocab,
        ),
        name="vocab_forward",
    )(states, table)


def backward_kernel(vocab, first_ref, second_ref, scales_ref, table_ref, out_ref, left, right, tail):
    step = pl.program_id(0)
    tiles = pl.num_programs(0) - 1
    width, depth = table_ref.shape
    half = first_ref.shape[3]
    piece = 256
    last = vocab - (pl.cdiv(vocab, width) - 1) * width
    whole = last // piece * piece
    tile = jnp.maximum(step - 1, 0)
    limit = vocab - tile * width

    def units(part, source, target, index):
        result = []

        def turn(lanes, block):
            begin = part * half + lanes * LANES
            span = slice(begin, begin + LANES)
            place = slice(block * LANES, (block + 1) * LANES)
            local = slice(lanes * LANES, (lanes + 1) * LANES)
            factors = scales_ref[pl.ds(index, 1), :, span][0]
            base = source[0, 0, place, local].astype(jnp.float32) * factors[0:1]
            for state in range(1, 3):
                value = source[0, state, place, local].astype(jnp.float32) * factors[state : state + 1]
                first = (state - 1) * half + lanes * LANES
                target[first : first + LANES, place] = jnp.transpose(
                    (value - base).astype(jnp.bfloat16)
                )

        for lanes in range(half // LANES):
            for block in range(width // LANES):
                result.append(functools.partial(turn, lanes, block))
        return result

    def multiply(part, source, start):
        place = slice(start, start + piece)
        span = slice(part * half, (part + 1) * half)
        partial = jnp.dot(source[:, whole:], tail[:, place], preferred_element_type=jnp.float32)
        if whole > 0:
            partial += jnp.dot(
                source[:, :whole], table_ref[:whole, place], preferred_element_type=jnp.float32
            )
        for probe in range(2):
            out_ref[probe, span, place] += partial[probe * half : (probe + 1) * half]

    def stage(part, source, work):
        done = 0
        pieces = depth // piece
        for index in range(pieces):
            multiply(part, source, index * piece)
            upto = (index + 1) * len(work) // pieces
            for unit in work[done:upto]:
                unit()
            done = upto

    ahead = jnp.minimum(step, tiles - 1)

    @pl.when(step == 0)
    def _():
        out_ref[...] = jnp.zeros_like(out_ref)
        for unit in units(0, first_ref, left, ahead):
            unit()

    @pl.when(step > 0)
    def _():
        below = lax.broadcasted_iota(jnp.int32, (width - whole, depth), 0) + whole < limit
        tail[...] = jnp.where(below, table_ref[whole:, :], jnp.zeros((), tail.dtype))
        stage(0, left, units(1, second_ref, right, tile))
        stage(1, right, units(0, first_ref, left, ahead))


def vocab_backward(first, second, scales, table):
    tiles, _, _, half = first.shape
    vocab, depth = table.shape
    rows = 2 * half
    last = vocab - (tiles - 1) * VOCAB_TILE
    block = (1, 3, VOCAB_TILE, half)
    return pl.pallas_call(
        functools.partial(backward_kernel, vocab),
        grid=(tiles + 1,),
        in_specs=[
            pl.BlockSpec(block, lambda i: (jnp.minimum(i, tiles - 1), 0, 0, 0)),
            pl.BlockSpec(block, lambda i: (jnp.maximum(i - 1, 0), 0, 0, 0)),
            pl.BlockSpec((tiles, 3, rows), lambda i: (0, 0, 0)),
            pl.BlockSpec((VOCAB_TILE, depth), lambda i: (jnp.maximum(i - 1, 0), 0)),
        ],
        out_specs=pl.BlockSpec((2, rows, depth), lambda i: (0, 0, 0)),
        out_shape=jax.ShapeDtypeStruct((2, rows, depth), jnp.float32),
        scratch_shapes=[
            pltpu.VMEM((2 * half, VOCAB_TILE), jnp.bfloat16),
            pltpu.VMEM((2 * half, VOCAB_TILE), jnp.bfloat16),
            pltpu.VMEM((VOCAB_TILE - last // 256 * 256, depth), jnp.bfloat16),
        ],
        compiler_params=pltpu.CompilerParams(vmem_limit_bytes=VMEM_BYTES),
        cost_estimate=pl.CostEstimate(
            flops=4 * rows * depth * vocab,
            bytes_accessed=2 * vocab * (depth + 3 * rows),
            transcendentals=0,
        ),
        name="vocab_backward",
    )(first, second, scales, table)


def body(
    token_ids,
    pos_weights,
    pad_lengths,
    embed_in,
    w_qkv,
    w_out,
    w_fc,
    w_proj,
    norm_gains,
    layer_biases,
    wide_bias,
    unembed,
    trans_weight,
    trans_bias,
    mom1_weight,
    mom2_weight,
    mom1_bias,
    mom2_bias,
):
    tok_rows = token_ids.shape[1]
    width = embed_in.shape[1]
    vocab_rows = unembed.shape[0]
    n_seq = lax.axis_size("seq")
    batch_index = lax.axis_index("batch")
    seq_index = lax.axis_index("seq")
    all_ids, all_weights, all_padding = (
        lax.all_gather(token_ids, "batch", axis=0, tiled=True),
        lax.all_gather(pos_weights, "batch", axis=0, tiled=True),
        lax.all_gather(pad_lengths, "batch", axis=0, tiled=True),
    )
    local_places = seq_index * tok_rows + jnp.arange(tok_rows, dtype=jnp.int32)
    living = local_places[None, :] < (tok_rows * n_seq - all_padding)[:, None]
    weight_all = jnp.where(living, all_weights, 0).astype(jnp.float32)
    weight_own = lax.dynamic_slice_in_dim(weight_all, batch_index, 1, 0)[0]
    token_count = lax.psum(jnp.sum(weight_own), ("seq", "batch"))
    flat_ids = all_ids.reshape(-1)
    vocab_start = batch_index * vocab_rows
    wanted = flat_ids - vocab_start
    inside = (wanted >= 0) & (wanted < vocab_rows)
    picked = jnp.take(embed_in, jnp.clip(wanted, 0, vocab_rows - 1), axis=0)
    stream0 = lax.psum_scatter(
        jnp.where(inside[:, None], picked.astype(jnp.float32), 0.0).astype(jnp.bfloat16),
        "batch",
        scatter_dimension=0,
        tiled=True,
    ).astype(jnp.float32)
    joined_w, out_w, fc_w, proj_w = (
        lax.all_gather(w_qkv, ("seq", "batch"), axis=0, tiled=True),
        lax.all_gather(w_out, ("seq", "batch"), axis=0, tiled=True),
        lax.all_gather(w_fc, ("seq", "batch"), axis=0, tiled=True),
        lax.all_gather(w_proj, ("seq", "batch"), axis=0, tiled=True),
    )
    trans_full, bias_full = (
        lax.all_gather(trans_weight.astype(jnp.bfloat16), "seq", axis=1, tiled=True).astype(
            trans_weight.dtype
        ),
        lax.all_gather(trans_bias.astype(jnp.bfloat16), "seq", axis=1, tiled=True).astype(
            trans_bias.dtype
        ),
    )
    head_count = width // HEAD_DIM
    x_attn = normalize(stream0, norm_gains[0], layer_biases[0]).astype(jnp.bfloat16)
    x_mlp = normalize(stream0, norm_gains[1], layer_biases[1]).astype(jnp.bfloat16)
    joined = (
        jnp.dot(x_attn, joined_w, preferred_element_type=jnp.float32) + wide_bias[: 3 * width]
    ).reshape(tok_rows, 3, head_count, HEAD_DIM)
    queries = rotate(joined[:, 0], local_places).astype(jnp.bfloat16)
    key_rows = rotate(joined[:, 1], local_places).astype(jnp.bfloat16).reshape(tok_rows, width)
    value_rows = joined[:, 2].astype(jnp.bfloat16).reshape(tok_rows, width)
    peaks = jnp.full((head_count, tok_rows), -1e30, jnp.float32)
    key_part = lax.all_gather(key_rows, "seq", axis=0, tiled=True).reshape(-1, head_count, HEAD_DIM)
    value_part = lax.all_gather(value_rows, "seq", axis=0, tiled=True).reshape(
        -1, head_count, HEAD_DIM
    )
    scores = jnp.einsum(
        "qhd,khd->hqk", queries, key_part, preferred_element_type=jnp.float32
    ) * HEAD_DIM ** (-0.5)
    key_places = jnp.arange(key_part.shape[0], dtype=jnp.int32)
    allowed = (key_places[None, :] <= local_places[:, None])[None]
    scores = jnp.where(allowed, scores, -1e30)
    new_peaks = jnp.maximum(peaks, jnp.max(scores, axis=-1))
    exponent = jnp.where(allowed, jnp.exp(scores - new_peaks[..., None]), 0.0)
    weighted = jnp.einsum(
        "hqk,khd->hqd",
        exponent.astype(jnp.bfloat16),
        value_part,
        preferred_element_type=jnp.float32,
    )
    weighted, peaks, summed = (weighted, new_peaks, jnp.sum(exponent, axis=-1))
    attended = (
        jnp.transpose(weighted / summed[..., None], (1, 0, 2))
        .reshape(tok_rows, width)
        .astype(jnp.bfloat16)
    )
    attn = jnp.dot(attended, out_w, preferred_element_type=jnp.float32) + layer_biases[2]
    hidden = jax.nn.gelu(
        jnp.dot(x_mlp, fc_w, preferred_element_type=jnp.float32) + wide_bias[3 * width :],
        approximate=False,
    ).astype(jnp.bfloat16)
    stream1 = (
        stream0
        + attn
        + jnp.dot(hidden, proj_w, preferred_element_type=jnp.float32)
        + layer_biases[3]
    )
    gain_final = norm_gains[2]
    offset_final = layer_biases[4]
    probe_in = (stream0, stream1)
    probe_low = (stream0.astype(jnp.bfloat16), stream1.astype(jnp.bfloat16))
    trans_low = trans_full.astype(jnp.bfloat16)
    translated = [
        probe_in[index]
        + jnp.dot(probe_low[index], trans_low[index], preferred_element_type=jnp.float32)
        + bias_full[index]
        for index in range(2)
    ]
    states = jnp.stack(
        [
            normalize(stream1, gain_final, offset_final),
            normalize(translated[0], gain_final, offset_final),
            normalize(translated[1], gain_final, offset_final),
        ]
    ).astype(jnp.bfloat16)
    gathered = lax.all_gather(states, "batch", axis=1, tiled=True)
    all_rows = gathered.shape[1]

    first, second, peaks, sums_part, cross_part = vocab_forward(gathered, unembed)
    peak_all = peaks[-1]
    sums_all = jnp.sum(sums_part, axis=1)
    cross_all = jnp.sum(cross_part, axis=1)

    def combine(earlier, later):
        peak_a, sums_a, cross_a = earlier
        peak_b, sums_b, cross_b = later
        peak_new = jnp.maximum(peak_a, peak_b)
        factor_a = jnp.exp(peak_a - peak_new)
        factor_b = jnp.exp(peak_b - peak_new)
        return (
            peak_new,
            sums_a * factor_a + sums_b * factor_b,
            cross_a * factor_a[0] + cross_b * factor_b[0],
        )

    peak_all, sums_all, cross_all = merged((peak_all, sums_all, cross_all), "batch", combine)
    log_totals = peak_all + jnp.log(sums_all)
    diverge = cross_all / sums_all[0] - log_totals[0] + log_totals[1:]
    diverge_own = lax.dynamic_slice_in_dim(diverge, batch_index * tok_rows, tok_rows, 1)
    loss_local = jnp.sum(weight_own * (diverge_own[0] + diverge_own[1]))
    token_coef = weight_all.reshape(-1) / token_count
    scales = token_coef[None, None, :] * jnp.exp(peaks - log_totals[None])
    partial = vocab_backward(first, second, scales, unembed)
    dstates = (
        lax.psum_scatter(
            jnp.transpose(partial, (1, 0, 2)).reshape(all_rows, 2 * width).astype(jnp.bfloat16),
            "batch",
            scatter_dimension=0,
            tiled=True,
        )
        .astype(jnp.float32)
        .reshape(tok_rows, 2, width)
    )
    grad_w_list = []
    grad_b_list = []
    for index in range(2):
        delta = norm_back(translated[index], dstates[:, index], gain_final)
        grad_w_list.append(
            jnp.einsum(
                "td,te->de",
                probe_low[index],
                delta.astype(jnp.bfloat16),
                preferred_element_type=jnp.float32,
            )
        )
        grad_b_list.append(jnp.sum(delta, axis=0))
    grad_w = jnp.stack(grad_w_list)
    grad_b = jnp.stack(grad_b_list)
    grad_w, grad_b = (
        lax.psum(grad_w.astype(jnp.bfloat16), "batch").astype(jnp.float32),
        lax.psum(grad_b.astype(jnp.bfloat16), "batch").astype(jnp.float32),
    )
    grad_w, grad_b = (
        lax.psum_scatter(
            grad_w.astype(jnp.bfloat16), "seq", scatter_dimension=1, tiled=True
        ).astype(jnp.float32),
        lax.psum_scatter(
            grad_b.astype(jnp.bfloat16), "seq", scatter_dimension=1, tiled=True
        ).astype(jnp.float32),
    )
    squares = jnp.sum(grad_w * grad_w) + jnp.sum(grad_b * grad_b)
    first_copy = (batch_index == 0).astype(jnp.float32)
    loss_sum, norm_square = lax.psum((loss_local, squares * first_copy), ("seq", "batch"))
    grad_norm = jnp.sqrt(norm_square)
    factor = jnp.minimum(1.0, clip_max / (grad_norm + 1e-06))
    first_w, second_w, new_w = adam_update(trans_weight, grad_w * factor, mom1_weight, mom2_weight)
    first_b, second_b, new_b = adam_update(trans_bias, grad_b * factor, mom1_bias, mom2_bias)
    return (loss_sum, token_count, grad_norm, first_w, second_w, new_w, first_b, second_b, new_b)


def solution(mesh):
    return jax.shard_map(
        body,
        mesh=mesh,
        in_specs=(
            P("batch", "seq"),
            P("batch", "seq"),
            P("batch"),
            P("batch", None),
            P(("seq", "batch"), None),
            P(("seq", "batch"), None),
            P(("seq", "batch"), None),
            P(("seq", "batch"), None),
            P(),
            P(),
            P(),
            P("batch", None),
            P(None, "seq", None),
            P(None, "seq"),
            P(None, "seq", None),
            P(None, "seq", None),
            P(None, "seq"),
            P(None, "seq"),
        ),
        out_specs=(
            P(),
            P(),
            P(),
            P(None, "seq", None),
            P(None, "seq", None),
            P(None, "seq", None),
            P(None, "seq"),
            P(None, "seq"),
            P(None, "seq"),
        ),
        check_vma=False,
    )
```

```python
import functools

import jax
import jax.numpy as jnp
from jax import lax
from jax.experimental import pallas as pl
from jax.experimental.pallas import tpu as pltpu
from jax.sharding import PartitionSpec as P

HEAD_DIM = 64
ROT = 16
STEP = 10


VOCAB_TILE = 1280
LANES = 128
NEGATIVE = -1e30
VMEM_BYTES = 60 * 1024 * 1024
norm_eps = 1e-05
clip_max = 0.001
beta_one = 0.9
beta_two = 0.999
learn_rate = 0.03
decay_rate = 0.01
adam_eps = 1e-08


def normalize(values, gain_row, offset_row):
    average = jnp.mean(values, axis=-1, keepdims=True)
    centered = values - average
    variance = jnp.mean(centered * centered, axis=-1, keepdims=True)
    return centered * lax.rsqrt(variance + norm_eps) * gain_row + offset_row


def norm_back(values, upstream, gain_row):
    average = jnp.mean(values, axis=-1, keepdims=True)
    centered = values - average
    variance = jnp.mean(centered * centered, axis=-1, keepdims=True)
    inverse = lax.rsqrt(variance + norm_eps)
    unit = centered * inverse
    scaled = upstream * gain_row
    return (
        scaled
        - jnp.mean(scaled, axis=-1, keepdims=True)
        - unit * jnp.mean(scaled * unit, axis=-1, keepdims=True)
    ) * inverse


def rotate(vectors, places):
    half_rot = ROT // 2
    frequency = 10000.0 ** (-2.0 * jnp.arange(half_rot, dtype=jnp.float32) / ROT)
    angles = places.astype(jnp.float32)[:, None] * frequency[None, :]
    cosine = jnp.cos(angles)[:, None, :]
    sine = jnp.sin(angles)[:, None, :]
    lower_part = vectors[..., :half_rot]
    upper_part = vectors[..., half_rot:ROT]
    return jnp.concatenate(
        [
            lower_part * cosine - upper_part * sine,
            upper_part * cosine + lower_part * sine,
            vectors[..., ROT:],
        ],
        axis=-1,
    )


def adam_update(weight, gradient, earlier, later):
    earlier = beta_one * earlier + (1.0 - beta_one) * gradient
    later = beta_two * later + (1.0 - beta_two) * gradient * gradient
    update = (
        earlier / (1.0 - beta_one**STEP) / (jnp.sqrt(later / (1.0 - beta_two**STEP)) + adam_eps)
    )
    return (earlier, later, weight * (1.0 - learn_rate * decay_rate) - learn_rate * update)


def forward_kernel(vocab, states_ref, table_ref, first_ref, second_ref, peaks_ref, sums_ref, cross_ref, turned, left, right, peak):
    step = pl.program_id(0)
    steps = pl.num_programs(0) - 1
    width = table_ref.shape[0]
    half = left.shape[1] // 3
    group = 16
    last = vocab - (pl.cdiv(vocab, width) - 1) * width
    row = lax.broadcasted_iota(jnp.int32, (group, LANES), 0)

    def reset(part):
        span = slice(part * half, (part + 1) * half)
        peak[:, span] = jnp.full((8, half), NEGATIVE, jnp.float32)
        sums_ref[:, :, span] = jnp.zeros((3, 8, half), jnp.float32)
        cross_ref[:, :, span] = jnp.zeros((2, 8, half), jnp.float32)

    @pl.when(step == 0)
    def _():
        reset(0)
        for state in range(3):
            for part in range(2):
                turned[part, :, state * half : (state + 1) * half] = jnp.transpose(
                    states_ref[state, part * half : (part + 1) * half, :]
                )

    @pl.when(step <= 1)
    def _():
        reset(1)

    def multiply(part, target, state):
        place = slice(state * half, (state + 1) * half)
        target[:, place] = jnp.dot(
            table_ref[...], turned[part, :, place], preferred_element_type=jnp.float32
        )

    def units(part, source, target, tile):
        limit = vocab - tile * width
        blocks = width // group
        result = []
        for lanes in range(half // LANES):
            span = slice(part * half + lanes * LANES, part * half + (lanes + 1) * LANES)
            local = slice(lanes * LANES, (lanes + 1) * LANES)
            held = {}

            def logits(state, block, lanes=lanes):
                begin = state * half + lanes * LANES
                value = source[block * group : (block + 1) * group, begin : begin + LANES]
                if (block + 1) * group > last:
                    value = jnp.where(row + block * group < limit, value, NEGATIVE)
                return value

            def tops(span=span, held=held, logits=logits):
                held["top"], held["sum"], held["cross"] = [], [], []
                for state in range(3):
                    top = logits(state, 0)
                    for block in range(1, blocks):
                        top = jnp.maximum(top, logits(state, block))
                    before = peak[state : state + 1, span]
                    now = jnp.maximum(before, jnp.max(top, axis=0, keepdims=True))
                    peak[state : state + 1, span] = now
                    peaks_ref[pl.ds(tile, 1), state, span] = now
                    fade = jnp.exp(before - now)
                    held["top"].append(jnp.broadcast_to(now, (group, LANES)))
                    held["sum"].append(sums_ref[state, :, span] * fade)
                    if state == 0:
                        held["cross"] = [cross_ref[other, :, span] * fade for other in range(2)]

            def fold(value):
                return value[:8] + value[8:]

            def powers(begin, end, held=held, logits=logits, local=local, fold=fold):
                for block in range(begin, end):
                    place = slice(block * group, (block + 1) * group)
                    base = logits(0, block)
                    base_exp = jnp.exp(base - held["top"][0])
                    held["sum"][0] += fold(base_exp)
                    target[0, 0, place, local] = base_exp.astype(jnp.bfloat16)
                    for state in range(1, 3):
                        value = logits(state, block)
                        value_exp = jnp.exp(value - held["top"][state])
                        held["sum"][state] += fold(value_exp)
                        target[0, state, place, local] = value_exp.astype(jnp.bfloat16)
                        held["cross"][state - 1] += fold(base_exp * (base - value))

            def finish(span=span, held=held):
                for state in range(3):
                    sums_ref[state, :, span] = held["sum"][state]
                for other in range(2):
                    cross_ref[other, :, span] = held["cross"][other]

            result.append(tops)
            cuts = 5
            for cut in range(cuts):
                result.append(
                    functools.partial(powers, cut * blocks // cuts, (cut + 1) * blocks // cuts)
                )
            result.append(finish)
        return result

    def stage(part, target, work):
        done = 0
        for state in range(3):
            multiply(part, target, state)
            upto = (state + 1) * len(work) // 3
            for unit in work[done:upto]:
                unit()
            done = upto

    before = jnp.maximum(step - 1, 0)

    @pl.when(step < steps)
    def _():
        stage(0, left, units(1, right, second_ref, before))
        stage(1, right, units(0, left, first_ref, step))

    @pl.when(step == steps)
    def _():
        for unit in units(1, right, second_ref, before):
            unit()


def vocab_forward(states, table):
    _, rows, depth = states.shape
    vocab = table.shape[0]
    tiles = pl.cdiv(vocab, VOCAB_TILE)
    half = rows // 2
    kept = jax.ShapeDtypeStruct((tiles, 3, VOCAB_TILE, half), jnp.bfloat16)
    block = (1, 3, VOCAB_TILE, half)
    whole = lambda *shape: pl.BlockSpec(shape, lambda i: (0,) * len(shape))
    return pl.pallas_call(
        functools.partial(forward_kernel, vocab),
        grid=(tiles + 1,),
        in_specs=[
            whole(3, rows, depth),
            pl.BlockSpec((VOCAB_TILE, depth), lambda i: (jnp.minimum(i, tiles - 1), 0)),
        ],
        out_specs=[
            pl.BlockSpec(block, lambda i: (jnp.minimum(i, tiles - 1), 0, 0, 0)),
            pl.BlockSpec(block, lambda i: (jnp.maximum(i - 1, 0), 0, 0, 0)),
            whole(tiles, 3, rows),
            whole(3, 8, rows),
            whole(2, 8, rows),
        ],
        out_shape=[
            kept,
            kept,
            jax.ShapeDtypeStruct((tiles, 3, rows), jnp.float32),
            jax.ShapeDtypeStruct((3, 8, rows), jnp.float32),
            jax.ShapeDtypeStruct((2, 8, rows), jnp.float32),
        ],
        scratch_shapes=[
            pltpu.VMEM((2, depth, 3 * half), jnp.bfloat16),
            pltpu.VMEM((VOCAB_TILE, 3 * half), jnp.float32),
            pltpu.VMEM((VOCAB_TILE, 3 * half), jnp.float32),
            pltpu.VMEM((8, rows), jnp.float32),
        ],
        compiler_params=pltpu.CompilerParams(vmem_limit_bytes=VMEM_BYTES),
        cost_estimate=pl.CostEstimate(
            flops=6 * rows * depth * vocab,
            bytes_accessed=2 * vocab * (depth + 3 * rows),
            transcendentals=3 * rows * vocab,
        ),
        name="vocab_forward",
    )(states, table)


def backward_kernel(vocab, first_ref, second_ref, scales_ref, table_ref, out_ref, left, right, tail):
    step = pl.program_id(0)
    tiles = pl.num_programs(0) - 1
    width, depth = table_ref.shape
    half = first_ref.shape[3]
    piece = 256
    last = vocab - (pl.cdiv(vocab, width) - 1) * width
    whole = last // piece * piece
    tile = jnp.maximum(step - 1, 0)
    limit = vocab - tile * width

    def units(part, source, target, index):
        result = []

        def turn(lanes, block):
            begin = part * half + lanes * LANES
            span = slice(begin, begin + LANES)
            place = slice(block * LANES, (block + 1) * LANES)
            local = slice(lanes * LANES, (lanes + 1) * LANES)
            factors = scales_ref[pl.ds(index, 1), :, span][0]
            base = source[0, 0, place, local].astype(jnp.float32) * factors[0:1]
            for state in range(1, 3):
                value = source[0, state, place, local].astype(jnp.float32) * factors[state : state + 1]
                first = (state - 1) * half + lanes * LANES
                target[first : first + LANES, place] = jnp.transpose(
                    (value - base).astype(jnp.bfloat16)
                )

        for lanes in range(half // LANES):
            for block in range(width // LANES):
                result.append(functools.partial(turn, lanes, block))
        return result

    def multiply(part, source, start):
        place = slice(start, start + piece)
        span = slice(part * half, (part + 1) * half)
        partial = jnp.dot(source[:, whole:], tail[:, place], preferred_element_type=jnp.float32)
        if whole > 0:
            partial += jnp.dot(
                source[:, :whole], table_ref[:whole, place], preferred_element_type=jnp.float32
            )
        for probe in range(2):
            out_ref[probe, span, place] += partial[probe * half : (probe + 1) * half]

    def stage(part, source, work):
        done = 0
        pieces = depth // piece
        for index in range(pieces):
            multiply(part, source, index * piece)
            upto = (index + 1) * len(work) // pieces
            for unit in work[done:upto]:
                unit()
            done = upto

    ahead = jnp.minimum(step, tiles - 1)

    @pl.when(step == 0)
    def _():
        out_ref[...] = jnp.zeros_like(out_ref)
        for unit in units(0, first_ref, left, ahead):
            unit()

    @pl.when(step > 0)
    def _():
        below = lax.broadcasted_iota(jnp.int32, (width - whole, depth), 0) + whole < limit
        tail[...] = jnp.where(below, table_ref[whole:, :], jnp.zeros((), tail.dtype))
        stage(0, left, units(1, second_ref, right, tile))
        stage(1, right, units(0, first_ref, left, ahead))


def vocab_backward(first, second, scales, table):
    tiles, _, _, half = first.shape
    vocab, depth = table.shape
    rows = 2 * half
    last = vocab - (tiles - 1) * VOCAB_TILE
    block = (1, 3, VOCAB_TILE, half)
    return pl.pallas_call(
        functools.partial(backward_kernel, vocab),
        grid=(tiles + 1,),
        in_specs=[
            pl.BlockSpec(block, lambda i: (jnp.minimum(i, tiles - 1), 0, 0, 0)),
            pl.BlockSpec(block, lambda i: (jnp.maximum(i - 1, 0), 0, 0, 0)),
            pl.BlockSpec((tiles, 3, rows), lambda i: (0, 0, 0)),
            pl.BlockSpec((VOCAB_TILE, depth), lambda i: (jnp.maximum(i - 1, 0), 0)),
        ],
        out_specs=pl.BlockSpec((2, rows, depth), lambda i: (0, 0, 0)),
        out_shape=jax.ShapeDtypeStruct((2, rows, depth), jnp.float32),
        scratch_shapes=[
            pltpu.VMEM((2 * half, VOCAB_TILE), jnp.bfloat16),
            pltpu.VMEM((2 * half, VOCAB_TILE), jnp.bfloat16),
            pltpu.VMEM((VOCAB_TILE - last // 256 * 256, depth), jnp.bfloat16),
        ],
        compiler_params=pltpu.CompilerParams(vmem_limit_bytes=VMEM_BYTES),
        cost_estimate=pl.CostEstimate(
            flops=4 * rows * depth * vocab,
            bytes_accessed=2 * vocab * (depth + 3 * rows),
            transcendentals=0,
        ),
        name="vocab_backward",
    )(first, second, scales, table)


def plane_place(place):
    core = lax.rem(place, 2)
    return core, lax.rem(place // 2, 2), place // 4


def plane_index(core, column, line):
    return (line * 2 + column) * 2 + core


def greet(partners):
    barrier = pltpu.get_barrier_semaphore()
    for partner in partners:
        pl.semaphore_signal(barrier, inc=1, device_id=partner, device_id_type=pl.DeviceIdType.MESH)
    pl.semaphore_wait(barrier, len(partners))


def push(source, target, send, receive, partner):
    copy = pltpu.make_async_remote_copy(
        src_ref=source,
        dst_ref=target,
        send_sem=send,
        recv_sem=receive,
        device_id=partner,
        device_id_type=pl.DeviceIdType.MESH,
    )
    copy.start()
    return copy


def arrived(target, receive, partner):
    pltpu.make_async_remote_copy(
        src_ref=target,
        dst_ref=target,
        send_sem=receive,
        recv_sem=receive,
        device_id=partner,
        device_id_type=pl.DeviceIdType.MESH,
    ).wait_recv()


def departed(source, send, partner):
    pltpu.make_async_remote_copy(
        src_ref=source,
        dst_ref=source,
        send_sem=send,
        recv_sem=send,
        device_id=partner,
        device_id_type=pl.DeviceIdType.MESH,
    ).wait_send()


class LineSum:
    def __init__(self, count, size, own, land, held, total, inner_sem, outer_sem, receive_sem):
        lines = lax.axis_size("batch")
        place = lax.axis_index("batch")
        near = place < lines // 2
        self.count, self.size = count, size
        self.own, self.land, self.held, self.total = own, land, held, total
        self.inner_sem, self.outer_sem, self.receive_sem = inner_sem, outer_sem, receive_sem
        self.middle = (place == lines // 2 - 1) | (place == lines // 2)
        self.end = (place == 0) | (place == lines - 1)
        self.inner = {"batch": jnp.where(near, place + 1, place - 1)}
        self.outer = {"batch": jnp.where(near, place - 1, place + 1)}
        self.slot = jnp.where(self.middle, 1, 0)

    def rows(self, index):
        return pl.ds(index * self.size, self.size)

    def send_in(self, index):
        rows = self.rows(index)
        push(
            self.held.at[rows],
            self.land.at[self.slot, rows],
            self.inner_sem.at[index],
            self.receive_sem.at[self.slot, index],
            self.inner,
        )

    def begin(self, indices):
        @pl.when(self.end)
        def _():
            for index in indices:
                rows = self.rows(index)
                self.held[rows, :] = self.own(rows).astype(jnp.bfloat16)
                self.send_in(index)

    def gather(self, index):
        rows = self.rows(index)

        @pl.when(jnp.logical_not(self.end))
        def _():
            arrived(self.land.at[0, rows], self.receive_sem.at[0, index], self.outer)
            own = self.own(rows).astype(jnp.float32)
            self.held[rows, :] = (own + self.land[0, rows, :].astype(jnp.float32)).astype(jnp.bfloat16)
            self.send_in(index)

    def spread(self, index):
        rows = self.rows(index)

        @pl.when(self.middle)
        def _():
            arrived(self.land.at[1, rows], self.receive_sem.at[1, index], self.inner)
            both = self.held[rows, :].astype(jnp.float32) + self.land[1, rows, :].astype(jnp.float32)
            self.total[rows, :] = both.astype(jnp.bfloat16)

        @pl.when(jnp.logical_not(self.middle))
        def _():
            arrived(self.total.at[rows], self.receive_sem.at[2, index], self.inner)

        @pl.when(jnp.logical_not(self.end))
        def _():
            push(
                self.total.at[rows],
                self.total.at[rows],
                self.outer_sem.at[index],
                self.receive_sem.at[2, index],
                self.outer,
            )

    def finish(self):
        for index in range(self.count):
            rows = self.rows(index)
            departed(self.held.at[rows], self.inner_sem.at[index], self.inner)

            @pl.when(jnp.logical_not(self.end))
            def _(rows=rows, index=index):
                departed(self.total.at[rows], self.outer_sem.at[index], self.outer)

    @staticmethod
    def scratch(count, rows, depth):
        return [
            pltpu.VMEM((2, rows, depth), jnp.bfloat16),
            pltpu.VMEM((rows, depth), jnp.bfloat16),
            pltpu.SemaphoreType.DMA((count,)),
            pltpu.SemaphoreType.DMA((count,)),
            pltpu.SemaphoreType.DMA((3, count)),
        ]


def others(axis):
    size = lax.axis_size(axis)
    place = lax.axis_index(axis)
    return [lax.rem(place + step, size) for step in range(1, size)]


def share_kernel(axis, tile_ref, out_ref, local_sem, send_sem, receive_sem):
    place = lax.axis_index(axis)
    peers = others(axis)
    local = pltpu.make_async_copy(tile_ref, out_ref.at[place], local_sem)
    local.start()
    greet([{axis: peer} for peer in peers])
    copies = [
        push(tile_ref, out_ref.at[place], send_sem.at[index], receive_sem.at[place], {axis: peer})
        for index, peer in enumerate(peers)
    ]
    for peer in peers:
        arrived(out_ref.at[peer], receive_sem.at[peer], {axis: peer})
    for copy in copies:
        copy.wait_send()
    local.wait()


def share(tile, axis, identity, name):
    size = lax.axis_size(axis)
    space = pl.BlockSpec(memory_space=pltpu.VMEM)
    return pl.pallas_call(
        functools.partial(share_kernel, axis),
        in_specs=[space],
        out_specs=space,
        out_shape=jax.ShapeDtypeStruct((size,) + tile.shape, tile.dtype),
        scratch_shapes=[
            pltpu.SemaphoreType.DMA,
            pltpu.SemaphoreType.DMA((size - 1,)),
            pltpu.SemaphoreType.DMA((size,)),
        ],
        compiler_params=pltpu.CompilerParams(collective_id=identity, has_side_effects=True),
        name=name,
    )(tile)


def swap_kernel(send_ref, out_ref, local_sem, send_sem, receive_sem):
    place = lax.axis_index("seq")
    peers = others("seq")
    local = pltpu.make_async_copy(send_ref.at[place], out_ref.at[place], local_sem)
    local.start()
    greet([{"seq": peer} for peer in peers])
    copies = [
        push(send_ref.at[peer], out_ref.at[place], send_sem.at[index], receive_sem.at[place], {"seq": peer})
        for index, peer in enumerate(peers)
    ]
    for peer in peers:
        arrived(out_ref.at[peer], receive_sem.at[peer], {"seq": peer})
    for copy in copies:
        copy.wait_send()
    local.wait()


def swap(blocks, identity, name):
    size = lax.axis_size("seq")
    space = pl.BlockSpec(memory_space=pltpu.VMEM)
    return pl.pallas_call(
        swap_kernel,
        in_specs=[space],
        out_specs=space,
        out_shape=jax.ShapeDtypeStruct(blocks.shape, blocks.dtype),
        scratch_shapes=[
            pltpu.SemaphoreType.DMA,
            pltpu.SemaphoreType.DMA((size - 1,)),
            pltpu.SemaphoreType.DMA((size,)),
        ],
        compiler_params=pltpu.CompilerParams(
            collective_id=identity, has_side_effects=True, vmem_limit_bytes=VMEM_BYTES
        ),
        name=name,
    )(blocks)


def lookup_kernel(ids_ref, table_ref, out_ref, window, rows_f32, sems):
    rows, depth = out_ref.shape
    vocab = table_ref.shape[0]
    ring = window.shape[0]
    group = window.shape[1]
    rows_f32[...] = jnp.zeros_like(rows_f32)
    line = lax.broadcasted_iota(jnp.int32, (group, depth), 0)

    def fetch(index, slot):
        base = pl.multiple_of(ids_ref[index] // group * group, group)
        return pltpu.make_async_copy(table_ref.at[pl.ds(base, group)], window.at[slot], sems.at[slot])

    def inside(index):
        value = ids_ref[index]
        return (value >= 0) & (value < vocab)

    def loop(index, carry):
        slot = lax.rem(index, ring)
        late = jnp.maximum(index - ring, 0)

        @pl.when((index >= ring) & inside(late))
        def _():
            fetch(late, slot).wait()
            place = lax.rem(ids_ref[late], group)
            block = window[slot].astype(jnp.float32)
            rows_f32[pl.ds(late, 1), :] = jnp.sum(jnp.where(line == place, block, 0.0), axis=0, keepdims=True)

        now = jnp.minimum(index, rows - 1)

        @pl.when((index < rows) & inside(now))
        def _():
            fetch(now, slot).start()

        return carry

    lax.fori_loop(0, rows + ring, loop, 0)
    out_ref[...] = rows_f32[...].astype(jnp.bfloat16)


def lookup(ids, table):
    rows = ids.shape[0]
    depth = table.shape[1]
    return pl.pallas_call(
        lookup_kernel,
        in_specs=[pl.BlockSpec(memory_space=pltpu.SMEM), pl.BlockSpec(memory_space=pl.ANY)],
        out_specs=pl.BlockSpec(memory_space=pltpu.VMEM),
        out_shape=jax.ShapeDtypeStruct((rows, depth), jnp.bfloat16),
        scratch_shapes=[
            pltpu.VMEM((64, 16, depth), jnp.bfloat16),
            pltpu.VMEM((rows, depth), jnp.float32),
            pltpu.SemaphoreType.DMA((64,)),
        ],
        compiler_params=pltpu.CompilerParams(vmem_limit_bytes=VMEM_BYTES),
        name="lookup",
    )(ids, table)


def front_kernel(
    count,
    picked_ref, joined_ref, fc_ref, proj_ref, bias_ref,
    stream_ref, joined_out, fc_out, proj_out, bias_out,
    land, held, inner_sem, outer_sem, receive_sem,
    local_sem, cross_send, cross_receive, plane_send, plane_receive, bias_send, bias_receive,
):
    lines = lax.axis_size("batch")
    place = lax.axis_index("batch")
    size = lax.axis_size("seq")
    spot = lax.axis_index("seq")
    core, column, line = plane_place(spot)
    rows = size // 4
    beside = plane_index(core, 1 - column, line)
    sibling = plane_index(1 - core, column, line)
    across = [plane_index(core, column, lax.rem(line + step, rows)) for step in range(1, rows)]
    corners = [plane_index(core, 1 - column, lax.rem(line + step, rows)) for step in range(1, rows)]
    planes = others("batch")
    peers = others("seq")
    outs = (joined_out, fc_out, proj_out)
    proj_rows = proj_ref.shape[0]

    def piece(array, half, slot):
        if array < 2:
            return outs[array].at[slot, pl.ds(half * (lines // 2), lines // 2)]
        return outs[array].at[slot, pl.ds(half * (proj_rows // 2), proj_rows // 2)]

    started = []

    def send(array, half, slot, way, index, target):
        view = piece(array, half, slot)
        started.append(
            push(view, view, plane_send.at[array, half, way, index], plane_receive.at[array, half, slot], {"seq": target})
        )

    def await_piece(array, half, slot):
        arrived(piece(array, half, slot), plane_receive.at[array, half, slot], {"seq": slot})

    def own(array):
        for half in range(2):
            send(array, half, spot, 0, 0, beside)
            for index, target in enumerate(across):
                send(array, half, spot, 1 + index, 0, target)
            send(array, half, spot, rows, 0, sibling)

    def relay_side(array):
        await_piece(array, 0, beside)
        for index, target in enumerate(across):
            send(array, 0, beside, 1 + index, 1, target)
        for index, source in enumerate(across):
            await_piece(array, 1, source)
            send(array, 1, source, 0, 1 + index, beside)

    def relay_core(array):
        send(array, 0, beside, rows, 1, sibling)
        await_piece(array, 1, beside)
        send(array, 1, beside, rows, 1, sibling)
        for index, source in enumerate(across):
            send(array, 1, source, rows, 2 + index, sibling)
            await_piece(array, 0, source)
            send(array, 0, source, rows, 2 + index, sibling)
        for index, source in enumerate(corners):
            for half in range(2):
                await_piece(array, half, source)
                send(array, half, source, rows, 1 + rows + index, sibling)

    def receive_core(array):
        for step in range(rows):
            for side in range(2):
                source = plane_index(1 - core, side, lax.rem(line + step, rows))
                for half in range(2):
                    await_piece(array, half, source)

    proj_copy = pltpu.make_async_copy(proj_ref, proj_out.at[spot], local_sem.at[0])
    proj_copy.start()
    locals_ = [
        pltpu.make_async_copy(source.at[place], out.at[spot, place], local_sem.at[1 + index])
        for index, (source, out) in enumerate(((joined_ref, joined_out), (fc_ref, fc_out)))
    ]
    for copy in locals_:
        copy.start()
    bias_copy = pltpu.make_async_copy(bias_ref, bias_out.at[spot], local_sem.at[3])
    bias_copy.start()
    greet([{"batch": plane} for plane in planes] + [{"seq": peer} for peer in peers])
    line_sum = LineSum(
        count, stream_ref.shape[0] // count, lambda at: picked_ref[at, :],
        land, held, stream_ref, inner_sem, outer_sem, receive_sem,
    )
    line_sum.begin(range(count))
    crossing = []
    for array, source, out in ((0, joined_ref, joined_out), (1, fc_ref, fc_out)):
        for index, plane in enumerate(planes):
            crossing.append(
                push(source.at[plane], out.at[spot, place], cross_send.at[array, index], cross_receive.at[array, place], {"batch": plane})
            )
    bias_copies = [
        push(bias_ref, bias_out.at[spot], bias_send.at[index], bias_receive.at[spot], {"seq": peer})
        for index, peer in enumerate(peers)
    ]
    proj_copy.wait()
    own(2)
    for copy in locals_:
        copy.wait()

    def receive_cross(array):
        for plane in planes:
            arrived(outs[array].at[spot, plane], cross_receive.at[array, plane], {"batch": plane})

    def turn(array):
        receive_cross(array)
        own(array)

    todo = [
        lambda: turn(0),
        lambda: relay_side(2),
        lambda: turn(1),
        lambda: relay_core(2),
        lambda: relay_side(0),
        lambda: relay_core(0),
        lambda: relay_side(1),
        lambda: relay_core(1),
        lambda: receive_core(2),
        lambda: receive_core(0),
        lambda: receive_core(1),
    ]
    for index in range(count + 1):
        if index < count:
            line_sum.gather(index)
        if index >= 1:
            line_sum.spread(index - 1)
        if todo:
            todo.pop(0)()
    for work in todo:
        work()
    for peer in peers:
        arrived(bias_out.at[peer], bias_receive.at[peer], {"seq": peer})
    bias_copy.wait()
    for copy in started + crossing + bias_copies:
        copy.wait_send()
    line_sum.finish()


def front(picked, joined, fc, proj, bias):
    size = lax.axis_size("seq")
    lines = lax.axis_size("batch")
    rows, depth = picked.shape
    count = 8
    vmem = pl.BlockSpec(memory_space=pltpu.VMEM)
    anywhere = pl.BlockSpec(memory_space=pl.ANY)
    dma = pltpu.SemaphoreType.DMA
    chips = size // 2
    return pl.pallas_call(
        functools.partial(front_kernel, count),
        in_specs=[vmem, anywhere, anywhere, anywhere, vmem],
        out_specs=[vmem, anywhere, anywhere, anywhere, vmem],
        out_shape=[
            jax.ShapeDtypeStruct((rows, depth), jnp.bfloat16),
            jax.ShapeDtypeStruct((size,) + joined.shape, jnp.bfloat16),
            jax.ShapeDtypeStruct((size,) + fc.shape, jnp.bfloat16),
            jax.ShapeDtypeStruct((size,) + proj.shape, jnp.bfloat16),
            jax.ShapeDtypeStruct((size,) + bias.shape, jnp.float32),
        ],
        scratch_shapes=LineSum.scratch(count, rows, depth) + [
            dma((4,)),
            dma((2, lines - 1)),
            dma((2, lines)),
            dma((3, 2, size // 4 + 1, chips + 1)),
            dma((3, 2, size)),
            dma((size - 1,)),
            dma((size,)),
        ],
        compiler_params=pltpu.CompilerParams(
            collective_id=1, has_side_effects=True, vmem_limit_bytes=VMEM_BYTES
        ),
        name="front",
    )(picked, joined, fc, proj, bias)


def layer_sum_kernel(count, part_ref, total_ref, land, held, inner_sem, outer_sem, receive_sem):
    line_sum = LineSum(
        count, part_ref.shape[0] // count, lambda at: part_ref[at, :],
        land, held, total_ref, inner_sem, outer_sem, receive_sem,
    )
    greet([{"batch": plane} for plane in others("batch")])
    line_sum.begin(range(count))
    for index in range(count + 1):
        if index < count:
            line_sum.gather(index)
        if index >= 1:
            line_sum.spread(index - 1)
    line_sum.finish()


def layer_sum(part):
    rows, depth = part.shape
    count = 8
    vmem = pl.BlockSpec(memory_space=pltpu.VMEM)
    return pl.pallas_call(
        functools.partial(layer_sum_kernel, count),
        in_specs=[vmem],
        out_specs=vmem,
        out_shape=jax.ShapeDtypeStruct((rows, depth), jnp.bfloat16),
        scratch_shapes=LineSum.scratch(count, rows, depth),
        compiler_params=pltpu.CompilerParams(
            collective_id=4, has_side_effects=True, vmem_limit_bytes=VMEM_BYTES
        ),
        name="layer_sum",
    )(part)


def attention_kernel(heads, in_ref, out_ref):
    sources, _, tokens, columns = in_ref.shape
    length = sources * tokens
    head_dim = columns // heads
    block = 2 * tokens
    lane = lax.broadcasted_iota(jnp.int32, (block, columns), 1) // head_dim
    keys = jnp.concatenate([in_ref[source, 1] for source in range(sources)], axis=0)
    values = jnp.concatenate([in_ref[source, 2] for source in range(sources)], axis=0)
    for first in range(0, length, block):
        end = first + block
        queries = jnp.concatenate([in_ref[source, 0] for source in range(first // tokens, end // tokens)], axis=0)
        allowed = lax.broadcasted_iota(jnp.int32, (block, end), 1) <= (
            lax.broadcasted_iota(jnp.int32, (block, end), 0) + first
        )
        mixed = None
        for head in range(heads):
            chosen = jnp.where(lane == head, queries, jnp.zeros((), queries.dtype))
            scores = lax.dot_general(
                chosen, keys[:end], (((1,), (1,)), ((), ())), preferred_element_type=jnp.float32
            ) * head_dim ** (-0.5)
            scores = jnp.where(allowed, scores, NEGATIVE)
            exponent = jnp.exp(scores - jnp.max(scores, axis=-1, keepdims=True))
            result = jnp.dot(
                exponent.astype(jnp.bfloat16), values[:end], preferred_element_type=jnp.float32
            ) / jnp.sum(exponent, axis=-1, keepdims=True)
            mixed = result if mixed is None else jnp.where(lane == head, result, mixed)
        mixed = mixed.astype(jnp.bfloat16)
        for index in range(block // tokens):
            out_ref[first // tokens + index] = mixed[index * tokens : (index + 1) * tokens]


def attention(blocks, heads):
    sources, _, tokens, columns = blocks.shape
    vmem = pl.BlockSpec(memory_space=pltpu.VMEM)
    return pl.pallas_call(
        functools.partial(attention_kernel, heads),
        in_specs=[vmem],
        out_specs=vmem,
        out_shape=jax.ShapeDtypeStruct((sources, tokens, columns), jnp.bfloat16),
        compiler_params=pltpu.CompilerParams(vmem_limit_bytes=VMEM_BYTES),
        name="attention",
    )(blocks)


def reduce_kernel(
    count,
    grad_ref, bias_ref, note_ref,
    total_ref, bias_out, note_out,
    mine, sibling_land, side_land, line_land, side_sum, line_sum_ref, last_land, own_sum,
    land, held, inner_sem, outer_sem, receive_sem,
    tile_land, tile_line, tile_out,
    local_sem, core_send, core_receive, side_send, side_receive, line_send, line_receive,
    last_send, last_receive, bias_send, bias_receive, plane_send, plane_receive, note_send, note_receive,
):
    size = lax.axis_size("seq")
    spot = lax.axis_index("seq")
    place = lax.axis_index("batch")
    core, column, line = plane_place(spot)
    rows = size // 4
    width = total_ref.shape[0] // 2
    beside = {"seq": plane_index(core, 1 - column, line)}
    sibling = {"seq": plane_index(1 - core, column, line)}
    across = [{"seq": plane_index(core, column, lax.rem(line + step, rows))} for step in range(1, rows)]
    peers = others("seq")
    planes = others("batch")
    f32 = jnp.float32
    order = [(lax.rem(line + step, rows), side) for step in range(rows) for side in (1 - column, column)]
    places = [(step, side) for step in range(rows) for side in range(2)]

    loads = [
        pltpu.make_async_copy(
            grad_ref.at[:, plane_index(core, side, at)], mine.at[step, index], local_sem.at[step, index]
        )
        for (step, index), (at, side) in zip(places, order)
    ]
    for copy in loads:
        copy.start()
    tile_land[spot] = bias_ref[spot]
    greet([{"batch": plane} for plane in planes] + [{"seq": peer} for peer in peers])
    sent = []
    for (step, index), (at, side) in zip(places, order):
        sent.append(
            push(
                grad_ref.at[:, plane_index(1 - core, side, at)], sibling_land.at[step, index],
                core_send.at[step, index], core_receive.at[step, index], sibling,
            )
        )
    for index, peer in enumerate(peers):
        sent.append(
            push(bias_ref.at[peer], tile_land.at[spot], bias_send.at[index], bias_receive.at[spot], {"seq": peer})
        )
    for (step, index), copy in zip(places, loads):
        copy.wait()
        arrived(sibling_land.at[step, index], core_receive.at[step, index], sibling)
        mine[step, index] = (
            mine[step, index].astype(f32) + sibling_land[step, index].astype(f32)
        ).astype(jnp.bfloat16)
        if index == 0:
            sent.append(
                push(mine.at[step, 0, 0], side_land.at[step], side_send.at[step], side_receive.at[step], beside)
            )
        if step > 0:
            sent.append(
                push(
                    mine.at[step, index, 1], line_land.at[step - 1, index],
                    line_send.at[step - 1, index], line_receive.at[step - 1, index], across[step - 1],
                )
            )
    for step in list(range(1, rows)) + [0]:
        arrived(side_land.at[step], side_receive.at[step], beside)
        both = mine[step, 1, 0].astype(f32) + side_land[step].astype(f32)
        if step > 0:
            side_sum[step - 1] = both.astype(jnp.bfloat16)
            sent.append(
                push(
                    side_sum.at[step - 1], last_land.at[step], last_send.at[step], last_receive.at[step],
                    across[step - 1],
                )
            )
        else:
            own_sum[0:width, :] = both
    for index in range(2):
        both = mine[0, index, 1].astype(f32)
        for step in range(1, rows):
            arrived(line_land.at[step - 1, index], line_receive.at[step - 1, index], across[-step])
            both += line_land[step - 1, index].astype(f32)
        if index == 0:
            line_sum_ref[...] = both.astype(jnp.bfloat16)
            sent.append(push(line_sum_ref, last_land.at[0], last_send.at[0], last_receive.at[0], beside))
        else:
            own_sum[width:, :] = both
    for step in range(1, rows):
        arrived(last_land.at[step], last_receive.at[step], across[-step])
        own_sum[0:width, :] += last_land[step].astype(f32)
    line_sum = LineSum(
        count, 2 * width // count, lambda at: own_sum[at, :],
        land, held, total_ref, inner_sem, outer_sem, receive_sem,
    )
    line_sum.begin(range(count // 2))
    for index in range(count // 2):
        line_sum.gather(index)
    arrived(last_land.at[0], last_receive.at[0], beside)
    own_sum[width:, :] += last_land[0].astype(f32)
    line_sum.begin(range(count // 2, count))
    for index in range(count // 2, count):
        line_sum.gather(index)
        line_sum.spread(index - count // 2)
    for peer in peers:
        arrived(tile_land.at[peer], bias_receive.at[peer], {"seq": peer})
    tile = tile_land[0]
    for source in range(1, size):
        tile += tile_land[source]
    tile_line[place] = tile
    for index, plane in enumerate(planes):
        sent.append(
            push(tile_line.at[place], tile_line.at[place], plane_send.at[index], plane_receive.at[place], {"batch": plane})
        )
    for plane in planes:
        arrived(tile_line.at[plane], plane_receive.at[plane], {"batch": plane})
    tile = tile_line[0]
    for source in range(1, lax.axis_size("batch")):
        tile += tile_line[source]
    bias_out[...] = tile
    squares = tile * tile
    for index in range(count // 2, count):
        line_sum.spread(index)
    for row in range(0, 2 * width, 16):
        value = total_ref[row : row + 16, :].astype(f32)
        value = value * value
        for begin in range(0, value.shape[1], LANES):
            squares += value[:8, begin : begin + LANES] + value[8:, begin : begin + LANES]
    head = jnp.sum(squares, axis=0, keepdims=True)
    line8 = lax.broadcasted_iota(jnp.int32, (8, LANES), 0)
    tile_out[...] = jnp.where(line8 == 0, head, note_ref[...])
    note_out[spot] = tile_out[...]
    for index, peer in enumerate(peers):
        sent.append(
            push(tile_out, note_out.at[spot], note_send.at[index], note_receive.at[spot], {"seq": peer})
        )
    for peer in peers:
        arrived(note_out.at[peer], note_receive.at[peer], {"seq": peer})
    for copy in sent:
        copy.wait_send()
    line_sum.finish()


def reduce_gradients(grad, bias, note):
    size = lax.axis_size("seq")
    lines = lax.axis_size("batch")
    _, _, width, depth = grad.shape
    rows = size // 4
    count = 4
    bf16 = jnp.bfloat16
    vmem = pl.BlockSpec(memory_space=pltpu.VMEM)
    dma = pltpu.SemaphoreType.DMA
    near = max(rows - 1, 1)
    return pl.pallas_call(
        functools.partial(reduce_kernel, count),
        in_specs=[pl.BlockSpec(memory_space=pl.ANY), vmem, vmem],
        out_specs=[vmem, vmem, vmem],
        out_shape=[
            jax.ShapeDtypeStruct((2 * width, depth), bf16),
            jax.ShapeDtypeStruct(bias.shape[1:], jnp.float32),
            jax.ShapeDtypeStruct((size,) + note.shape, jnp.float32),
        ],
        scratch_shapes=[
            pltpu.VMEM((rows, 2, 2, width, depth), bf16),
            pltpu.VMEM((rows, 2, 2, width, depth), bf16),
            pltpu.VMEM((rows, width, depth), bf16),
            pltpu.VMEM((near, 2, width, depth), bf16),
            pltpu.VMEM((near, width, depth), bf16),
            pltpu.VMEM((width, depth), bf16),
            pltpu.VMEM((rows, width, depth), bf16),
            pltpu.VMEM((2 * width, depth), jnp.float32),
        ] + LineSum.scratch(count, 2 * width, depth) + [
            pltpu.VMEM((size,) + bias.shape[1:], jnp.float32),
            pltpu.VMEM((lines,) + bias.shape[1:], jnp.float32),
            pltpu.VMEM(note.shape, jnp.float32),
            dma((rows, 2)),
            dma((rows, 2)),
            dma((rows, 2)),
            dma((rows,)),
            dma((rows,)),
            dma((near, 2)),
            dma((near, 2)),
            dma((rows,)),
            dma((rows,)),
            dma((size - 1,)),
            dma((size,)),
            dma((lines - 1,)),
            dma((lines,)),
            dma((size - 1,)),
            dma((size,)),
        ],
        compiler_params=pltpu.CompilerParams(
            collective_id=6, has_side_effects=True, vmem_limit_bytes=VMEM_BYTES
        ),
        name="reduce_gradients",
    )(grad, bias, note)


def body(
    token_ids,
    pos_weights,
    pad_lengths,
    embed_in,
    w_qkv,
    w_out,
    w_fc,
    w_proj,
    norm_gains,
    layer_biases,
    wide_bias,
    unembed,
    trans_weight,
    trans_bias,
    mom1_weight,
    mom2_weight,
    mom1_bias,
    mom2_bias,
):
    bf16 = jnp.bfloat16
    f32 = jnp.float32
    tok_rows = token_ids.shape[1]
    width = embed_in.shape[1]
    vocab_rows = unembed.shape[0]
    n_seq = lax.axis_size("seq")
    n_batch = lax.axis_size("batch")
    batch_index = lax.axis_index("batch")
    seq_index = lax.axis_index("seq")
    rows = n_batch * tok_rows
    head_count = width // HEAD_DIM
    plane_heads = head_count // n_batch
    plane_width = plane_heads * HEAD_DIM
    own_heads = head_count // n_seq
    hidden_rows = w_proj.shape[0]

    padding = jnp.broadcast_to(pad_lengths[:, None], (1, tok_rows))
    tile = jnp.concatenate([token_ids, pos_weights, padding, jnp.zeros((5, tok_rows), jnp.int32)], axis=0)
    tiles = share(tile, "batch", 0, "share_tokens")
    flat_ids = tiles[:, 0].reshape(-1)
    local_places = seq_index * tok_rows + jnp.arange(tok_rows, dtype=jnp.int32)
    living = local_places[None, :] < tok_rows * n_seq - tiles[:, 2]
    weights = jnp.where(living, tiles[:, 1], 0).astype(f32).reshape(-1)

    out_w = lax.all_gather(w_out, ("seq", "batch"), axis=0, tiled=True)
    out_w = lax.dynamic_slice_in_dim(out_w, batch_index * plane_width, plane_width, 0)
    trans_low = lax.all_gather(trans_weight.astype(bf16), "seq", axis=1, tiled=True)

    picked = lookup(flat_ids - batch_index * vocab_rows, embed_in)
    own_rows = w_qkv.shape[0]
    joined_cut = jnp.transpose(w_qkv.reshape(own_rows, 3, n_batch, plane_width), (2, 0, 1, 3))
    joined_cut = joined_cut.reshape(n_batch, own_rows, 3 * plane_width)
    fc_cut = jnp.transpose(w_fc.reshape(own_rows, n_seq, n_batch, hidden_rows), (2, 0, 1, 3))
    fc_cut = fc_cut.reshape(n_batch, own_rows, n_seq * hidden_rows)
    bias_tile = jnp.zeros((8, LANES), f32).at[:2, : trans_bias.shape[1]].set(trans_bias)
    stream_low, joined_w, fc_w, proj_w, bias_all = front(picked, joined_cut, fc_cut, w_proj, bias_tile)
    joined_w = joined_w.reshape(width, 3 * plane_width)
    fc_w = fc_w.reshape(width, n_seq * hidden_rows)
    proj_w = proj_w.reshape(n_seq * hidden_rows, width)
    bias_full = jnp.transpose(bias_all[:, :2, : trans_bias.shape[1]], (1, 0, 2)).reshape(2, width)
    stream0 = stream_low.astype(f32)

    def plane_part(vector, parts, size):
        return lax.dynamic_slice_in_dim(vector.reshape(parts, n_batch, size), batch_index, 1, 1).reshape(-1)

    x_attn = normalize(stream0, norm_gains[0], layer_biases[0]).astype(bf16)
    x_mlp = normalize(stream0, norm_gains[1], layer_biases[1]).astype(bf16)
    joined = jnp.dot(x_attn, joined_w, preferred_element_type=f32) + plane_part(
        wide_bias[: 3 * width], 3, plane_width
    )
    joined = joined.reshape(rows, 3, plane_heads, HEAD_DIM)
    all_places = jnp.tile(local_places, n_batch)
    heads = jnp.stack(
        [rotate(joined[:, 0], all_places), rotate(joined[:, 1], all_places), joined[:, 2]]
    ).astype(bf16)
    spread = heads.reshape(3, n_batch, tok_rows, plane_heads // own_heads, own_heads * HEAD_DIM)
    spread = jnp.transpose(spread, (1, 3, 0, 2, 4)).reshape(n_seq, 3, tok_rows, own_heads * HEAD_DIM)
    mixed = attention(swap(spread, 2, "swap_heads"), own_heads)
    attended = swap(mixed, 3, "swap_rows")
    attended = attended.reshape(n_batch, plane_heads // own_heads, tok_rows, own_heads * HEAD_DIM)
    attended = jnp.transpose(attended, (0, 2, 1, 3)).reshape(rows, plane_width)
    hidden = jax.nn.gelu(
        jnp.dot(x_mlp, fc_w, preferred_element_type=f32)
        + plane_part(wide_bias[3 * width :], n_seq, hidden_rows),
        approximate=False,
    ).astype(bf16)
    part = jnp.dot(attended, out_w, preferred_element_type=f32) + jnp.dot(
        hidden, proj_w, preferred_element_type=f32
    )
    stream1 = stream0 + layer_sum(part).astype(f32) + layer_biases[2] + layer_biases[3]
    gain_final = norm_gains[2]
    offset_final = layer_biases[4]
    probe_in = (stream0, stream1)
    probe_low = (stream_low, stream1.astype(bf16))
    translated = [
        probe_in[index]
        + jnp.dot(probe_low[index], trans_low[index], preferred_element_type=f32)
        + bias_full[index]
        for index in range(2)
    ]
    states = jnp.stack(
        [
            normalize(stream1, gain_final, offset_final),
            normalize(translated[0], gain_final, offset_final),
            normalize(translated[1], gain_final, offset_final),
        ]
    ).astype(bf16)
    first, second, peaks, sums_part, cross_part = vocab_forward(states, unembed)
    stats = jnp.concatenate([peaks[-1], jnp.sum(sums_part, axis=1), jnp.sum(cross_part, axis=1)], axis=0)
    gathered = share(stats, "batch", 5, "share_stats")
    peak_all = jnp.max(gathered[:, :3], axis=0)
    fades = jnp.exp(gathered[:, :3] - peak_all)
    sums_all = jnp.sum(gathered[:, 3:6] * fades, axis=0)
    cross_all = jnp.sum(gathered[:, 6:] * fades[:, :1], axis=0)
    log_totals = peak_all + jnp.log(sums_all)
    diverge = cross_all / sums_all[0] - log_totals[0] + log_totals[1:]
    loss_part = jnp.sum(weights * (diverge[0] + diverge[1]))
    scales = weights * jnp.exp(peaks - log_totals[None])
    dstates = vocab_backward(first, second, scales, unembed)
    grad_list = []
    bias_list = []
    for index in range(2):
        delta = norm_back(translated[index], dstates[index], gain_final)
        grad_list.append(
            jnp.einsum("td,te->de", probe_low[index], delta.astype(bf16), preferred_element_type=f32)
        )
        bias_list.append(jnp.sum(delta, axis=0))
    grad = jnp.stack(grad_list).astype(bf16).reshape(2, n_seq, width // n_seq, width)
    bias_grad = jnp.transpose(jnp.stack(bias_list).reshape(2, n_seq, width // n_seq), (1, 0, 2))
    bias_grad = jnp.pad(bias_grad, ((0, 0), (0, 6), (0, LANES - width // n_seq)))
    ones = jnp.ones((LANES,), f32) / LANES
    note = jnp.concatenate(
        [
            jnp.zeros((1, LANES), f32),
            (loss_part * ones)[None],
            (jnp.sum(weights) * ones)[None],
            jnp.zeros((5, LANES), f32),
        ]
    )
    grad_sum, bias_sum, notes = reduce_gradients(grad, bias_grad, note)
    sums = jnp.sum(notes, axis=(0, 2))
    loss_sum = sums[1]
    token_count = jnp.round(sums[2])
    grad_norm = jnp.sqrt(sums[0]) / token_count
    factor = jnp.minimum(1.0, clip_max / (grad_norm + 1e-06)) / token_count
    grad_w = grad_sum.astype(f32).reshape(trans_weight.shape) * factor
    grad_b = bias_sum[:2, : trans_bias.shape[1]] * factor
    first_w, second_w, new_w = adam_update(trans_weight, grad_w, mom1_weight, mom2_weight)
    first_b, second_b, new_b = adam_update(trans_bias, grad_b, mom1_bias, mom2_bias)
    return (loss_sum, token_count, grad_norm, first_w, second_w, new_w, first_b, second_b, new_b)


def solution(mesh):
    return jax.shard_map(
        body,
        mesh=mesh,
        in_specs=(
            P("batch", "seq"),
            P("batch", "seq"),
            P("batch"),
            P("batch", None),
            P(("seq", "batch"), None),
            P(("seq", "batch"), None),
            P(("seq", "batch"), None),
            P(("seq", "batch"), None),
            P(),
            P(),
            P(),
            P("batch", None),
            P(None, "seq", None),
            P(None, "seq"),
            P(None, "seq", None),
            P(None, "seq", None),
            P(None, "seq"),
            P(None, "seq"),
        ),
        out_specs=(
            P(),
            P(),
            P(),
            P(None, "seq", None),
            P(None, "seq", None),
            P(None, "seq", None),
            P(None, "seq"),
            P(None, "seq"),
            P(None, "seq"),
        ),
        check_vma=False,
    )
```

```python
import functools

import jax
import jax.numpy as jnp
from jax import lax
from jax.experimental import pallas as pl
from jax.experimental.pallas import tpu as pltpu
from jax.sharding import PartitionSpec as P

HEAD_DIM = 64
ROT = 16
STEP = 10


VOCAB_TILE = 1280
LANES = 128
NEGATIVE = -1e30
VMEM_BYTES = 60 * 1024 * 1024
norm_eps = 1e-05
clip_max = 0.001
beta_one = 0.9
beta_two = 0.999
learn_rate = 0.03
decay_rate = 0.01
adam_eps = 1e-08


def norm_back(values, upstream, gain_row):
    average = jnp.mean(values, axis=-1, keepdims=True)
    centered = values - average
    variance = jnp.mean(centered * centered, axis=-1, keepdims=True)
    inverse = lax.rsqrt(variance + norm_eps)
    unit = centered * inverse
    scaled = upstream * gain_row
    return (
        scaled
        - jnp.mean(scaled, axis=-1, keepdims=True)
        - unit * jnp.mean(scaled * unit, axis=-1, keepdims=True)
    ) * inverse


def adam_update(weight, gradient, earlier, later):
    earlier = beta_one * earlier + (1.0 - beta_one) * gradient
    later = beta_two * later + (1.0 - beta_two) * gradient * gradient
    update = (
        earlier / (1.0 - beta_one**STEP) / (jnp.sqrt(later / (1.0 - beta_two**STEP)) + adam_eps)
    )
    return (earlier, later, weight * (1.0 - learn_rate * decay_rate) - learn_rate * update)


def forward_kernel(vocab, states_ref, table_ref, first_ref, second_ref, peaks_ref, sums_ref, cross_ref, turned, left, right, peak):
    step = pl.program_id(0)
    steps = pl.num_programs(0) - 1
    width = table_ref.shape[0]
    half = left.shape[1] // 3
    group = 16
    last = vocab - (pl.cdiv(vocab, width) - 1) * width
    row = lax.broadcasted_iota(jnp.int32, (group, LANES), 0)

    def reset(part):
        span = slice(part * half, (part + 1) * half)
        peak[:, span] = jnp.full((8, half), NEGATIVE, jnp.float32)
        sums_ref[:, :, span] = jnp.zeros((3, 8, half), jnp.float32)
        cross_ref[:, :, span] = jnp.zeros((2, 8, half), jnp.float32)

    @pl.when(step == 0)
    def _():
        reset(0)
        for state in range(3):
            for part in range(2):
                turned[part, :, state * half : (state + 1) * half] = jnp.transpose(
                    states_ref[state, part * half : (part + 1) * half, :]
                )

    @pl.when(step <= 1)
    def _():
        reset(1)

    def multiply(part, target, state):
        place = slice(state * half, (state + 1) * half)
        target[:, place] = jnp.dot(
            table_ref[...], turned[part, :, place], preferred_element_type=jnp.float32
        )

    def units(part, source, target, tile):
        limit = vocab - tile * width
        blocks = width // group
        result = []
        for lanes in range(half // LANES):
            span = slice(part * half + lanes * LANES, part * half + (lanes + 1) * LANES)
            local = slice(lanes * LANES, (lanes + 1) * LANES)
            held = {}

            def logits(state, block, lanes=lanes):
                begin = state * half + lanes * LANES
                value = source[block * group : (block + 1) * group, begin : begin + LANES]
                if (block + 1) * group > last:
                    value = jnp.where(row + block * group < limit, value, NEGATIVE)
                return value

            def tops(span=span, held=held, logits=logits):
                held["top"], held["sum"], held["cross"] = [], [], []
                for state in range(3):
                    top = logits(state, 0)
                    for block in range(1, blocks):
                        top = jnp.maximum(top, logits(state, block))
                    before = peak[state : state + 1, span]
                    now = jnp.maximum(before, jnp.max(top, axis=0, keepdims=True))
                    peak[state : state + 1, span] = now
                    peaks_ref[pl.ds(tile, 1), state, span] = now
                    fade = jnp.exp(before - now)
                    held["top"].append(jnp.broadcast_to(now, (group, LANES)))
                    held["sum"].append(sums_ref[state, :, span] * fade)
                    if state == 0:
                        held["cross"] = [cross_ref[other, :, span] * fade for other in range(2)]

            def fold(value):
                return value[:8] + value[8:]

            def powers(begin, end, held=held, logits=logits, local=local, fold=fold):
                for block in range(begin, end):
                    place = slice(block * group, (block + 1) * group)
                    base = logits(0, block)
                    base_exp = jnp.exp(base - held["top"][0])
                    held["sum"][0] += fold(base_exp)
                    target[0, 0, place, local] = base_exp.astype(jnp.bfloat16)
                    for state in range(1, 3):
                        value = logits(state, block)
                        value_exp = jnp.exp(value - held["top"][state])
                        held["sum"][state] += fold(value_exp)
                        target[0, state, place, local] = value_exp.astype(jnp.bfloat16)
                        held["cross"][state - 1] += fold(base_exp * (base - value))

            def finish(span=span, held=held):
                for state in range(3):
                    sums_ref[state, :, span] = held["sum"][state]
                for other in range(2):
                    cross_ref[other, :, span] = held["cross"][other]

            result.append(tops)
            cuts = 5
            for cut in range(cuts):
                result.append(
                    functools.partial(powers, cut * blocks // cuts, (cut + 1) * blocks // cuts)
                )
            result.append(finish)
        return result

    def stage(part, target, work):
        done = 0
        for state in range(3):
            multiply(part, target, state)
            upto = (state + 1) * len(work) // 3
            for unit in work[done:upto]:
                unit()
            done = upto

    before = jnp.maximum(step - 1, 0)

    @pl.when(step < steps)
    def _():
        stage(0, left, units(1, right, second_ref, before))
        stage(1, right, units(0, left, first_ref, step))

    @pl.when(step == steps)
    def _():
        for unit in units(1, right, second_ref, before):
            unit()


def vocab_forward(states, table):
    _, rows, depth = states.shape
    vocab = table.shape[0]
    tiles = pl.cdiv(vocab, VOCAB_TILE)
    half = rows // 2
    kept = jax.ShapeDtypeStruct((tiles, 3, VOCAB_TILE, half), jnp.bfloat16)
    block = (1, 3, VOCAB_TILE, half)
    whole = lambda *shape: pl.BlockSpec(shape, lambda i: (0,) * len(shape))
    return pl.pallas_call(
        functools.partial(forward_kernel, vocab),
        grid=(tiles + 1,),
        in_specs=[
            whole(3, rows, depth),
            pl.BlockSpec((VOCAB_TILE, depth), lambda i: (jnp.minimum(i, tiles - 1), 0)),
        ],
        out_specs=[
            pl.BlockSpec(block, lambda i: (jnp.minimum(i, tiles - 1), 0, 0, 0)),
            pl.BlockSpec(block, lambda i: (jnp.maximum(i - 1, 0), 0, 0, 0)),
            whole(tiles, 3, rows),
            whole(3, 8, rows),
            whole(2, 8, rows),
        ],
        out_shape=[
            kept,
            kept,
            jax.ShapeDtypeStruct((tiles, 3, rows), jnp.float32),
            jax.ShapeDtypeStruct((3, 8, rows), jnp.float32),
            jax.ShapeDtypeStruct((2, 8, rows), jnp.float32),
        ],
        scratch_shapes=[
            pltpu.VMEM((2, depth, 3 * half), jnp.bfloat16),
            pltpu.VMEM((VOCAB_TILE, 3 * half), jnp.float32),
            pltpu.VMEM((VOCAB_TILE, 3 * half), jnp.float32),
            pltpu.VMEM((8, rows), jnp.float32),
        ],
        compiler_params=pltpu.CompilerParams(vmem_limit_bytes=VMEM_BYTES),
        cost_estimate=pl.CostEstimate(
            flops=6 * rows * depth * vocab,
            bytes_accessed=2 * vocab * (depth + 3 * rows),
            transcendentals=3 * rows * vocab,
        ),
        name="vocab_forward",
    )(states, table)


def backward_kernel(vocab, first_ref, second_ref, scales_ref, table_ref, out_ref, left, right, tail):
    step = pl.program_id(0)
    tiles = pl.num_programs(0) - 1
    width, depth = table_ref.shape
    half = first_ref.shape[3]
    piece = 256
    last = vocab - (pl.cdiv(vocab, width) - 1) * width
    whole = last // piece * piece
    tile = jnp.maximum(step - 1, 0)
    limit = vocab - tile * width

    def units(part, source, target, index):
        result = []

        def turn(lanes, block):
            begin = part * half + lanes * LANES
            span = slice(begin, begin + LANES)
            place = slice(block * LANES, (block + 1) * LANES)
            local = slice(lanes * LANES, (lanes + 1) * LANES)
            factors = scales_ref[pl.ds(index, 1), :, span][0]
            base = source[0, 0, place, local].astype(jnp.float32) * factors[0:1]
            for state in range(1, 3):
                value = source[0, state, place, local].astype(jnp.float32) * factors[state : state + 1]
                first = (state - 1) * half + lanes * LANES
                target[first : first + LANES, place] = jnp.transpose(
                    (value - base).astype(jnp.bfloat16)
                )

        for lanes in range(half // LANES):
            for block in range(width // LANES):
                result.append(functools.partial(turn, lanes, block))
        return result

    def multiply(part, source, start):
        place = slice(start, start + piece)
        span = slice(part * half, (part + 1) * half)
        partial = jnp.dot(source[:, whole:], tail[:, place], preferred_element_type=jnp.float32)
        if whole > 0:
            partial += jnp.dot(
                source[:, :whole], table_ref[:whole, place], preferred_element_type=jnp.float32
            )
        for probe in range(2):
            out_ref[probe, span, place] += partial[probe * half : (probe + 1) * half]

    def stage(part, source, work):
        done = 0
        pieces = depth // piece
        for index in range(pieces):
            multiply(part, source, index * piece)
            upto = (index + 1) * len(work) // pieces
            for unit in work[done:upto]:
                unit()
            done = upto

    ahead = jnp.minimum(step, tiles - 1)

    @pl.when(step == 0)
    def _():
        out_ref[...] = jnp.zeros_like(out_ref)
        for unit in units(0, first_ref, left, ahead):
            unit()

    @pl.when(step > 0)
    def _():
        below = lax.broadcasted_iota(jnp.int32, (width - whole, depth), 0) + whole < limit
        tail[...] = jnp.where(below, table_ref[whole:, :], jnp.zeros((), tail.dtype))
        stage(0, left, units(1, second_ref, right, tile))
        stage(1, right, units(0, first_ref, left, ahead))


def vocab_backward(first, second, scales, table):
    tiles, _, _, half = first.shape
    vocab, depth = table.shape
    rows = 2 * half
    last = vocab - (tiles - 1) * VOCAB_TILE
    block = (1, 3, VOCAB_TILE, half)
    return pl.pallas_call(
        functools.partial(backward_kernel, vocab),
        grid=(tiles + 1,),
        in_specs=[
            pl.BlockSpec(block, lambda i: (jnp.minimum(i, tiles - 1), 0, 0, 0)),
            pl.BlockSpec(block, lambda i: (jnp.maximum(i - 1, 0), 0, 0, 0)),
            pl.BlockSpec((tiles, 3, rows), lambda i: (0, 0, 0)),
            pl.BlockSpec((VOCAB_TILE, depth), lambda i: (jnp.maximum(i - 1, 0), 0)),
        ],
        out_specs=pl.BlockSpec((2, rows, depth), lambda i: (0, 0, 0)),
        out_shape=jax.ShapeDtypeStruct((2, rows, depth), jnp.float32),
        scratch_shapes=[
            pltpu.VMEM((2 * half, VOCAB_TILE), jnp.bfloat16),
            pltpu.VMEM((2 * half, VOCAB_TILE), jnp.bfloat16),
            pltpu.VMEM((VOCAB_TILE - last // 256 * 256, depth), jnp.bfloat16),
        ],
        compiler_params=pltpu.CompilerParams(vmem_limit_bytes=VMEM_BYTES),
        cost_estimate=pl.CostEstimate(
            flops=4 * rows * depth * vocab,
            bytes_accessed=2 * vocab * (depth + 3 * rows),
            transcendentals=0,
        ),
        name="vocab_backward",
    )(first, second, scales, table)


def plane_place(place):
    core = lax.rem(place, 2)
    return core, lax.rem(place // 2, 2), place // 4


def plane_index(core, column, line):
    return (line * 2 + column) * 2 + core


def greet(partners):
    barrier = pltpu.get_barrier_semaphore()
    for partner in partners:
        pl.semaphore_signal(barrier, inc=1, device_id=partner, device_id_type=pl.DeviceIdType.MESH)
    pl.semaphore_wait(barrier, len(partners))


def push(source, target, send, receive, partner):
    copy = pltpu.make_async_remote_copy(
        src_ref=source,
        dst_ref=target,
        send_sem=send,
        recv_sem=receive,
        device_id=partner,
        device_id_type=pl.DeviceIdType.MESH,
    )
    copy.start()
    return copy


def arrived(target, receive, partner):
    pltpu.make_async_remote_copy(
        src_ref=target,
        dst_ref=target,
        send_sem=receive,
        recv_sem=receive,
        device_id=partner,
        device_id_type=pl.DeviceIdType.MESH,
    ).wait_recv()


def departed(source, send, partner):
    pltpu.make_async_remote_copy(
        src_ref=source,
        dst_ref=source,
        send_sem=send,
        recv_sem=send,
        device_id=partner,
        device_id_type=pl.DeviceIdType.MESH,
    ).wait_send()


class LineSum:
    def __init__(self, count, size, own, land, held, total, inner_sem, outer_sem, receive_sem):
        lines = lax.axis_size("batch")
        place = lax.axis_index("batch")
        near = place < lines // 2
        self.count, self.size = count, size
        self.own, self.land, self.held, self.total = own, land, held, total
        self.inner_sem, self.outer_sem, self.receive_sem = inner_sem, outer_sem, receive_sem
        self.middle = (place == lines // 2 - 1) | (place == lines // 2)
        self.end = (place == 0) | (place == lines - 1)
        self.inner = {"batch": jnp.where(near, place + 1, place - 1)}
        self.outer = {"batch": jnp.where(near, place - 1, place + 1)}
        self.slot = jnp.where(self.middle, 1, 0)

    def rows(self, index):
        return pl.ds(index * self.size, self.size)

    def send_in(self, index):
        rows = self.rows(index)
        push(
            self.held.at[rows],
            self.land.at[self.slot, rows],
            self.inner_sem.at[index],
            self.receive_sem.at[self.slot, index],
            self.inner,
        )

    def begin(self, indices):
        @pl.when(self.end)
        def _():
            for index in indices:
                rows = self.rows(index)
                self.held[rows, :] = self.own(rows).astype(jnp.bfloat16)
                self.send_in(index)

    def gather(self, index):
        rows = self.rows(index)

        @pl.when(jnp.logical_not(self.end))
        def _():
            arrived(self.land.at[0, rows], self.receive_sem.at[0, index], self.outer)
            own = self.own(rows).astype(jnp.float32)
            self.held[rows, :] = (own + self.land[0, rows, :].astype(jnp.float32)).astype(jnp.bfloat16)
            self.send_in(index)

    def spread(self, index):
        rows = self.rows(index)

        @pl.when(self.middle)
        def _():
            arrived(self.land.at[1, rows], self.receive_sem.at[1, index], self.inner)
            both = self.held[rows, :].astype(jnp.float32) + self.land[1, rows, :].astype(jnp.float32)
            self.total[rows, :] = both.astype(jnp.bfloat16)

        @pl.when(jnp.logical_not(self.middle))
        def _():
            arrived(self.total.at[rows], self.receive_sem.at[2, index], self.inner)

        @pl.when(jnp.logical_not(self.end))
        def _():
            push(
                self.total.at[rows],
                self.total.at[rows],
                self.outer_sem.at[index],
                self.receive_sem.at[2, index],
                self.outer,
            )

    def finish(self):
        for index in range(self.count):
            rows = self.rows(index)
            departed(self.held.at[rows], self.inner_sem.at[index], self.inner)

            @pl.when(jnp.logical_not(self.end))
            def _(rows=rows, index=index):
                departed(self.total.at[rows], self.outer_sem.at[index], self.outer)

    @staticmethod
    def scratch(count, rows, depth):
        return [
            pltpu.VMEM((2, rows, depth), jnp.bfloat16),
            pltpu.VMEM((rows, depth), jnp.bfloat16),
            pltpu.SemaphoreType.DMA((count,)),
            pltpu.SemaphoreType.DMA((count,)),
            pltpu.SemaphoreType.DMA((3, count)),
        ]


def others(axis):
    size = lax.axis_size(axis)
    place = lax.axis_index(axis)
    return [lax.rem(place + step, size) for step in range(1, size)]


def share_kernel(axis, tile_ref, out_ref, local_sem, send_sem, receive_sem):
    place = lax.axis_index(axis)
    peers = others(axis)
    local = pltpu.make_async_copy(tile_ref, out_ref.at[place], local_sem)
    local.start()
    greet([{axis: peer} for peer in peers])
    copies = [
        push(tile_ref, out_ref.at[place], send_sem.at[index], receive_sem.at[place], {axis: peer})
        for index, peer in enumerate(peers)
    ]
    for peer in peers:
        arrived(out_ref.at[peer], receive_sem.at[peer], {axis: peer})
    for copy in copies:
        copy.wait_send()
    local.wait()


def share(tile, axis, identity, name):
    size = lax.axis_size(axis)
    space = pl.BlockSpec(memory_space=pltpu.VMEM)
    return pl.pallas_call(
        functools.partial(share_kernel, axis),
        in_specs=[space],
        out_specs=space,
        out_shape=jax.ShapeDtypeStruct((size,) + tile.shape, tile.dtype),
        scratch_shapes=[
            pltpu.SemaphoreType.DMA,
            pltpu.SemaphoreType.DMA((size - 1,)),
            pltpu.SemaphoreType.DMA((size,)),
        ],
        compiler_params=pltpu.CompilerParams(collective_id=identity, has_side_effects=True),
        name=name,
    )(tile)


def front_kernel(
    count,
    tile_ref, table_ref, joined_ref, fc_ref, proj_ref, out_ref, trans_ref, bias_ref,
    tiles_out, stream_ref, joined_out, fc_out, proj_out, out_out, trans_out, bias_out,
    table, column_ids, chosen, picked, trans_low,
    land, held, inner_sem, outer_sem, receive_sem,
    local_sem, table_sem, tile_send, tile_receive, cross_send, cross_receive, plane_send, plane_receive, bias_send, bias_receive,
):
    lines = lax.axis_size("batch")
    place = lax.axis_index("batch")
    size = lax.axis_size("seq")
    spot = lax.axis_index("seq")
    core, column, line = plane_place(spot)
    rows = size // 4
    beside = plane_index(core, 1 - column, line)
    sibling = plane_index(1 - core, column, line)
    across = [plane_index(core, column, lax.rem(line + step, rows)) for step in range(1, rows)]
    corners = [plane_index(core, 1 - column, lax.rem(line + step, rows)) for step in range(1, rows)]
    planes = others("batch")
    peers = others("seq")
    outs = (joined_out, fc_out, proj_out, out_out, trans_out)
    total_rows, depth = stream_ref.shape
    chunk = total_rows // count
    tokens = tile_ref.shape[1]
    vocab = table_ref.shape[0]
    number = spot * lines + place
    goal = {"seq": lax.rem(number, size), "batch": number // size}
    wanted = place * size + spot
    origin = {"seq": wanted // lines, "batch": lax.rem(wanted, lines)}
    stays = number == wanted

    def piece(array, half, slot):
        out = outs[array]
        if array < 2:
            return out.at[slot, pl.ds(half * (lines // 2), lines // 2)]
        return out.at[slot, :, pl.ds(half * (depth // 2), depth // 2)]

    started = []

    def send(array, half, slot, way, index, target):
        view = piece(array, half, slot)
        started.append(
            push(view, view, plane_send.at[array, half, way, index], plane_receive.at[array, half, slot], {"seq": target})
        )

    def await_piece(array, half, slot):
        arrived(piece(array, half, slot), plane_receive.at[array, half, slot], {"seq": slot})

    def own(array):
        for half in range(2):
            send(array, half, spot, 0, 0, beside)
            for index, target in enumerate(across):
                send(array, half, spot, 1 + index, 0, target)
            send(array, half, spot, rows, 0, sibling)

    def relay_side(array):
        await_piece(array, 0, beside)
        for index, target in enumerate(across):
            send(array, 0, beside, 1 + index, 1, target)
        for index, source in enumerate(across):
            await_piece(array, 1, source)
            send(array, 1, source, 0, 1 + index, beside)

    def relay_core(array):
        send(array, 0, beside, rows, 1, sibling)
        await_piece(array, 1, beside)
        send(array, 1, beside, rows, 1, sibling)
        for index, source in enumerate(across):
            send(array, 1, source, rows, 2 + index, sibling)
            await_piece(array, 0, source)
            send(array, 0, source, rows, 2 + index, sibling)
        for index, source in enumerate(corners):
            for half in range(2):
                await_piece(array, half, source)
                send(array, half, source, rows, 1 + rows + index, sibling)

    def receive_core(array):
        for step in range(rows):
            for side in range(2):
                source = plane_index(1 - core, side, lax.rem(line + step, rows))
                for half in range(2):
                    await_piece(array, half, source)

    width = chosen.shape[1]
    cuts = table.shape[0] // width
    table_copies = [
        pltpu.make_async_copy(
            table_ref.at[pl.ds(cut * width, min(width, vocab - cut * width))],
            table.at[pl.ds(cut * width, min(width, vocab - cut * width))],
            table_sem.at[cut],
        )
        for cut in range(cuts)
    ]
    for copy in table_copies:
        copy.start()
    if table.shape[0] > vocab:
        table[vocab:, :] = jnp.zeros((table.shape[0] - vocab, depth), table.dtype)
    trans_low[...] = trans_ref[...].astype(jnp.bfloat16)
    locals_ = [
        pltpu.make_async_copy(source, target, local_sem.at[index])
        for index, (source, target) in enumerate(
            (
                (proj_ref, proj_out.at[spot]),
                (trans_low, trans_out.at[spot]),
                (joined_ref.at[place], joined_out.at[spot, place]),
                (fc_ref.at[place], fc_out.at[spot, place]),
                (tile_ref, tiles_out.at[place]),
                (bias_ref, bias_out.at[spot]),
            )
        )
    ]
    for copy in locals_:
        copy.start()
    out_copy = pltpu.make_async_copy(out_ref, out_out.at[spot], local_sem.at[6])

    @pl.when(stays)
    def _():
        out_copy.start()

    barrier = pltpu.get_barrier_semaphore()
    for partner in [{"batch": plane} for plane in planes] + [{"seq": peer} for peer in peers]:
        pl.semaphore_signal(barrier, inc=1, device_id=partner, device_id_type=pl.DeviceIdType.MESH)

    @pl.when(jnp.logical_not(stays))
    def _():
        pl.semaphore_signal(barrier, inc=1, device_id=origin, device_id_type=pl.DeviceIdType.MESH)

    pl.semaphore_wait(barrier, jnp.where(stays, 0, 1) + len(planes) + len(peers))

    tile_copies = [
        push(tile_ref, tiles_out.at[place], tile_send.at[index], tile_receive.at[place], {"batch": plane})
        for index, plane in enumerate(planes)
    ]
    for copy in locals_[:2]:
        copy.wait()
    own(2)
    crossing = []
    for array, source, out in ((0, joined_ref, joined_out), (1, fc_ref, fc_out)):
        for index, plane in enumerate(planes):
            crossing.append(
                push(source.at[plane], out.at[spot, place], cross_send.at[array, index], cross_receive.at[array, place], {"batch": plane})
            )
    out_push = pltpu.make_async_remote_copy(
        src_ref=out_ref, dst_ref=out_out.at[goal["seq"]], send_sem=cross_send.at[2, 0],
        recv_sem=cross_receive.at[2, 0], device_id=goal, device_id_type=pl.DeviceIdType.MESH,
    )

    @pl.when(jnp.logical_not(stays))
    def _():
        out_push.start()

    own(4)
    bias_copies = [
        push(bias_ref, bias_out.at[spot], bias_send.at[index], bias_receive.at[spot], {"seq": peer})
        for index, peer in enumerate(peers)
    ]
    for copy in locals_[2:]:
        copy.wait()
    for plane in planes:
        arrived(tiles_out.at[plane], tile_receive.at[plane], {"batch": plane})
    for sequence in range(lines):
        turned = jnp.transpose(tiles_out[sequence].astype(jnp.float32))
        column_ids[sequence * tokens : (sequence + 1) * tokens, :] = jnp.broadcast_to(
            turned[:, 0:1] - (place * vocab).astype(jnp.float32), (tokens, LANES)
        )
    half = total_rows // 2
    lane = lax.broadcasted_iota(jnp.int32, (half, LANES), 1)

    def look(part):
        at = slice(part * half, (part + 1) * half)
        for cut in range(cuts):
            if part == 0:
                table_copies[cut].wait()
            for block in range(width // LANES):
                number_ = (lane + (cut * width + block * LANES)).astype(jnp.float32)
                chosen[:, block * LANES : (block + 1) * LANES] = jnp.where(
                    column_ids[at, :] == number_, 1.0, 0.0
                ).astype(jnp.bfloat16)
            found = jnp.dot(
                chosen[...], table[cut * width : (cut + 1) * width, :], preferred_element_type=jnp.float32
            )
            if cut == 0:
                picked[at, :] = found
            else:
                picked[at, :] += found

    line_sum = LineSum(
        count, chunk, lambda at: picked[at, :],
        land, held, stream_ref, inner_sem, outer_sem, receive_sem,
    )

    def turn(array):
        for plane in planes:
            arrived(outs[array].at[spot, plane], cross_receive.at[array, plane], {"batch": plane})
        own(array)

    def turn_out():
        @pl.when(stays)
        def _():
            out_copy.wait()

        @pl.when(jnp.logical_not(stays))
        def _():
            arrived(out_out.at[spot], cross_receive.at[2, 0], origin)

        own(3)

    todo = [
        lambda: relay_side(2),
        lambda: turn(0),
        turn_out,
        lambda: relay_side(4),
        lambda: turn(1),
        lambda: relay_core(2),
        lambda: relay_side(0),
        lambda: relay_side(3),
        lambda: relay_core(4),
        lambda: relay_core(0),
        lambda: relay_side(1),
        lambda: relay_core(3),
        lambda: relay_core(1),
        lambda: receive_core(2),
        lambda: receive_core(4),
        lambda: receive_core(0),
        lambda: receive_core(3),
        lambda: receive_core(1),
    ]
    for part in range(2):
        look(part)
        line_sum.begin(range(part * count // 2, (part + 1) * count // 2))
        todo.pop(0)()
    for index in range(count + 1):
        if index < count:
            line_sum.gather(index)
        if index >= 1:
            line_sum.spread(index - 1)
        if todo and index % 2:
            todo.pop(0)()
    for work in todo:
        work()
    for peer in peers:
        arrived(bias_out.at[peer], bias_receive.at[peer], {"seq": peer})
    for copy in started + crossing + bias_copies + tile_copies:
        copy.wait_send()

    @pl.when(jnp.logical_not(stays))
    def _():
        out_push.wait_send()

    line_sum.finish()


def front(tile, table, joined, fc, proj, out, trans, bias):
    size = lax.axis_size("seq")
    lines = lax.axis_size("batch")
    vocab, depth = table.shape
    rows = lines * tile.shape[1]
    count = 16
    vmem = pl.BlockSpec(memory_space=pltpu.VMEM)
    anywhere = pl.BlockSpec(memory_space=pl.ANY)
    dma = pltpu.SemaphoreType.DMA
    chips = size // 2
    bf16 = jnp.bfloat16
    spread = lambda part, kind: jax.ShapeDtypeStruct((size,) + part.shape, kind)
    return pl.pallas_call(
        functools.partial(front_kernel, count),
        in_specs=[vmem, anywhere, anywhere, anywhere, anywhere, anywhere, vmem, vmem],
        out_specs=[vmem, vmem, anywhere, anywhere, anywhere, anywhere, anywhere, vmem],
        out_shape=[
            jax.ShapeDtypeStruct((lines,) + tile.shape, tile.dtype),
            jax.ShapeDtypeStruct((rows, depth), bf16),
            spread(joined, bf16),
            spread(fc, bf16),
            spread(proj, bf16),
            spread(out, bf16),
            spread(trans, bf16),
            spread(bias, jnp.float32),
        ],
        scratch_shapes=[
            pltpu.VMEM((pl.cdiv(vocab, VOCAB_TILE) * VOCAB_TILE, depth), bf16),
            pltpu.VMEM((rows, LANES), jnp.float32),
            pltpu.VMEM((rows // 2, VOCAB_TILE), bf16),
            pltpu.VMEM((rows, depth), jnp.float32),
            pltpu.VMEM(trans.shape, bf16),
        ] + LineSum.scratch(count, rows, depth) + [
            dma((7,)),
            dma((pl.cdiv(vocab, VOCAB_TILE),)),
            dma((lines - 1,)),
            dma((lines,)),
            dma((3, lines - 1)),
            dma((3, lines)),
            dma((5, 2, size // 4 + 1, chips + 1)),
            dma((5, 2, size)),
            dma((size - 1,)),
            dma((size,)),
        ],
        compiler_params=pltpu.CompilerParams(
            collective_id=1, has_side_effects=True, vmem_limit_bytes=VMEM_BYTES
        ),
        name="front",
    )(tile, table, joined, fc, proj, out, trans, bias)


def row_norm(values):
    average = jnp.mean(values, axis=-1, keepdims=True)
    centered = values - average
    variance = jnp.mean(centered * centered, axis=-1, keepdims=True)
    return centered * lax.rsqrt(variance + norm_eps)


def layer_kernel(
    count, heads,
    stream_ref, joined_ref, fc_ref, proj_ref, out_ref, trans_ref, next_ref,
    gains_ref, offsets_ref, joined_bias, fc_bias, trans_bias, turns_ref,
    states_ref, moved_ref, low_ref,
    own_next, next_all, x_attn, x_mlp, spread, gathered, mixed, returned, part,
    land, held, total, inner_sem, outer_sem, receive_sem,
    local_sem, heads_send, heads_receive, rows_send, rows_receive, next_send, next_receive,
):
    f32 = jnp.float32
    bf16 = jnp.bfloat16
    lines = lax.axis_size("batch")
    place = lax.axis_index("batch")
    size = lax.axis_size("seq")
    spot = lax.axis_index("seq")
    planes = others("batch")
    peers = others("seq")
    rows, depth = stream_ref.shape
    tokens = rows // lines
    plane_width = joined_ref.shape[1] // 3
    columns = spread.shape[3]
    groups = plane_width // columns
    head_dim = columns // heads
    step_rows = 32

    own_next[...] = next_ref[...].astype(bf16)
    greet([{"batch": plane} for plane in planes] + [{"seq": peer} for peer in peers])
    sent = [
        push(own_next, next_all.at[spot], next_send.at[index], next_receive.at[spot], {"seq": peer})
        for index, peer in enumerate(peers)
    ]
    next_copy = pltpu.make_async_copy(own_next, next_all.at[spot], local_sem.at[0])
    next_copy.start()

    def norms(index, carry):
        at = pl.ds(pl.multiple_of(index * step_rows, step_rows), step_rows)
        unit = row_norm(stream_ref[at, :].astype(f32))
        x_attn[at, :] = (unit * gains_ref[0:1, :] + offsets_ref[0:1, :]).astype(bf16)
        x_mlp[at, :] = (unit * gains_ref[1:2, :] + offsets_ref[1:2, :]).astype(bf16)
        return carry

    lax.fori_loop(0, rows // step_rows, norms, 0)
    half_rot = ROT // 2
    for sequence in range(lines):
        at = slice(sequence * tokens, (sequence + 1) * tokens)
        for kind in range(3):
            place_ = slice(kind * plane_width, (kind + 1) * plane_width)
            value = jnp.dot(x_attn[at, :], joined_ref[:, place_], preferred_element_type=f32)
            value = value + joined_bias[0:1, place_]
            if kind < 2:
                value = (
                    value * turns_ref[0]
                    + pltpu.roll(value, plane_width - half_rot, 1) * turns_ref[1]
                    + pltpu.roll(value, half_rot, 1) * turns_ref[2]
                )
            value = value.astype(bf16)
            for group in range(groups):
                spread[sequence * groups + group, kind] = value[:, group * columns : (group + 1) * columns]
    for index, peer in enumerate(peers):
        sent.append(
            push(spread.at[peer], gathered.at[spot], heads_send.at[index], heads_receive.at[spot], {"seq": peer})
        )
    heads_copy = pltpu.make_async_copy(spread.at[spot], gathered.at[spot], local_sem.at[1])
    heads_copy.start()

    def hidden_part(index, carry):
        at = pl.ds(pl.multiple_of(index * tokens, tokens), tokens)
        value = jnp.dot(x_mlp[at, :], fc_ref[...], preferred_element_type=f32) + fc_bias[...]
        value = 0.5 * value * (1.0 + lax.erf(value * (0.5 ** 0.5)))
        part[at, :] = jnp.dot(value.astype(bf16), proj_ref[...], preferred_element_type=f32)
        return carry

    lax.fori_loop(0, lines, hidden_part, 0)

    def translate(probe, stream, low, weights, at):
        moved = stream + jnp.dot(low, weights, preferred_element_type=f32) + trans_bias[probe : probe + 1, :]
        moved_ref[probe, at, :] = moved
        states_ref[1 + probe, at, :] = (
            row_norm(moved) * gains_ref[2:3, :] + offsets_ref[4:5, :]
        ).astype(bf16)

    def first_probe(index, carry):
        at = pl.ds(pl.multiple_of(index * tokens, tokens), tokens)
        low = stream_ref[at, :]
        translate(0, low.astype(f32), low, trans_ref[...], at)
        return carry

    lax.fori_loop(0, lines, first_probe, 0)
    heads_copy.wait()
    for peer in peers:
        arrived(gathered.at[peer], heads_receive.at[peer], {"seq": peer})
    length = size * tokens
    block = 2 * tokens
    lane = lax.broadcasted_iota(jnp.int32, (block, columns), 1) // head_dim
    keys = jnp.concatenate([gathered[source, 1] for source in range(size)], axis=0)
    values = jnp.concatenate([gathered[source, 2] for source in range(size)], axis=0)
    for first in range(0, length, block):
        end = first + block
        queries = jnp.concatenate([gathered[first // tokens, 0], gathered[first // tokens + 1, 0]], axis=0)
        allowed = lax.broadcasted_iota(jnp.int32, (block, end), 1) <= (
            lax.broadcasted_iota(jnp.int32, (block, end), 0) + first
        )
        result = None
        for head in range(heads):
            chosen = jnp.where(lane == head, queries, jnp.zeros((), bf16))
            scores = lax.dot_general(
                chosen, keys[:end], (((1,), (1,)), ((), ())), preferred_element_type=f32
            ) * head_dim ** (-0.5)
            scores = jnp.where(allowed, scores, NEGATIVE)
            exponent = jnp.exp(scores - jnp.max(scores, axis=-1, keepdims=True))
            value = jnp.dot(
                exponent.astype(bf16), values[:end], preferred_element_type=f32
            ) / jnp.sum(exponent, axis=-1, keepdims=True)
            result = value if result is None else jnp.where(lane == head, value, result)
        result = result.astype(bf16)
        for index in range(2):
            mixed[first // tokens + index] = result[index * tokens : (index + 1) * tokens]
    for index, peer in enumerate(peers):
        sent.append(
            push(mixed.at[peer], returned.at[spot], rows_send.at[index], rows_receive.at[spot], {"seq": peer})
        )
    rows_copy = pltpu.make_async_copy(mixed.at[spot], returned.at[spot], local_sem.at[2])
    rows_copy.start()
    rows_copy.wait()
    for peer in peers:
        arrived(returned.at[peer], rows_receive.at[peer], {"seq": peer})
    for sequence in range(lines):
        at = slice(sequence * tokens, (sequence + 1) * tokens)
        attended = jnp.concatenate(
            [returned[sequence * groups + group] for group in range(groups)], axis=1
        )
        part[at, :] += jnp.dot(attended, out_ref[...], preferred_element_type=f32)
    line_sum = LineSum(
        count, rows // count, lambda at: part[at, :],
        land, held, total, inner_sem, outer_sem, receive_sem,
    )
    line_sum.begin(range(count))
    for index in range(count + 1):
        if index < count:
            line_sum.gather(index)
        if index >= 1:
            line_sum.spread(index - 1)
    next_copy.wait()
    for peer in peers:
        arrived(next_all.at[peer], next_receive.at[peer], {"seq": peer})
    weights = next_all[...].reshape(depth, depth)

    def second_probe(index, carry):
        at = pl.ds(pl.multiple_of(index * tokens, tokens), tokens)
        stream = (
            stream_ref[at, :].astype(f32) + total[at, :].astype(f32) + offsets_ref[2:3, :] + offsets_ref[3:4, :]
        )
        states_ref[0, at, :] = (row_norm(stream) * gains_ref[2:3, :] + offsets_ref[4:5, :]).astype(bf16)
        low = stream.astype(bf16)
        low_ref[at, :] = low
        translate(1, stream, low, next_all[...].reshape(depth, depth), at)
        return carry

    lax.fori_loop(0, lines, second_probe, 0)
    for copy in sent:
        copy.wait_send()
    line_sum.finish()


def layer(stream, joined, fc, proj, out, trans, next_trans, gains, offsets, joined_bias, fc_bias, trans_bias, turns):
    size = lax.axis_size("seq")
    lines = lax.axis_size("batch")
    rows, depth = stream.shape
    tokens = rows // lines
    own_heads = depth // HEAD_DIM // size
    columns = own_heads * HEAD_DIM
    count = 32
    bf16 = jnp.bfloat16
    f32 = jnp.float32
    vmem = pl.BlockSpec(memory_space=pltpu.VMEM)
    dma = pltpu.SemaphoreType.DMA
    return pl.pallas_call(
        functools.partial(layer_kernel, count, own_heads),
        in_specs=[vmem] * 13,
        out_specs=[vmem] * 3,
        out_shape=[
            jax.ShapeDtypeStruct((3, rows, depth), bf16),
            jax.ShapeDtypeStruct((2, rows, depth), f32),
            jax.ShapeDtypeStruct((rows, depth), bf16),
        ],
        scratch_shapes=[
            pltpu.VMEM(next_trans.shape, bf16),
            pltpu.VMEM((size,) + next_trans.shape, bf16),
            pltpu.VMEM((rows, depth), bf16),
            pltpu.VMEM((rows, depth), bf16),
            pltpu.VMEM((size, 3, tokens, columns), bf16),
            pltpu.VMEM((size, 3, tokens, columns), bf16),
            pltpu.VMEM((size, tokens, columns), bf16),
            pltpu.VMEM((size, tokens, columns), bf16),
            pltpu.VMEM((rows, depth), f32),
        ] + LineSum.scratch(count, rows, depth)[:2] + [
            pltpu.VMEM((rows, depth), bf16),
        ] + LineSum.scratch(count, rows, depth)[2:] + [
            dma((3,)),
            dma((size - 1,)),
            dma((size,)),
            dma((size - 1,)),
            dma((size,)),
            dma((size - 1,)),
            dma((size,)),
        ],
        compiler_params=pltpu.CompilerParams(
            collective_id=2, has_side_effects=True, vmem_limit_bytes=VMEM_BYTES
        ),
        name="layer",
    )(stream, joined, fc, proj, out, trans, next_trans, gains, offsets, joined_bias, fc_bias, trans_bias, turns)


def reduce_kernel(
    count,
    grad_ref, bias_ref, note_ref,
    total_ref, bias_out, note_out,
    mine, sibling_land, side_land, line_land, side_sum, line_sum_ref, last_land, own_sum,
    land, held, inner_sem, outer_sem, receive_sem,
    tile_land, tile_line, tile_out,
    local_sem, core_send, core_receive, side_send, side_receive, line_send, line_receive,
    last_send, last_receive, bias_send, bias_receive, plane_send, plane_receive, note_send, note_receive,
):
    size = lax.axis_size("seq")
    spot = lax.axis_index("seq")
    place = lax.axis_index("batch")
    core, column, line = plane_place(spot)
    rows = size // 4
    width = total_ref.shape[0] // 2
    beside = {"seq": plane_index(core, 1 - column, line)}
    sibling = {"seq": plane_index(1 - core, column, line)}
    across = [{"seq": plane_index(core, column, lax.rem(line + step, rows))} for step in range(1, rows)]
    peers = others("seq")
    planes = others("batch")
    f32 = jnp.float32
    order = [(lax.rem(line + step, rows), side) for step in range(rows) for side in (1 - column, column)]
    places = [(step, side) for step in range(rows) for side in range(2)]

    loads = [
        pltpu.make_async_copy(
            grad_ref.at[:, plane_index(core, side, at)], mine.at[step, index], local_sem.at[step, index]
        )
        for (step, index), (at, side) in zip(places, order)
    ]
    for copy in loads:
        copy.start()
    tile_land[spot] = bias_ref[spot]
    greet([{"batch": plane} for plane in planes] + [{"seq": peer} for peer in peers])
    sent = []
    for (step, index), (at, side) in zip(places, order):
        sent.append(
            push(
                grad_ref.at[:, plane_index(1 - core, side, at)], sibling_land.at[step, index],
                core_send.at[step, index], core_receive.at[step, index], sibling,
            )
        )
    for index, peer in enumerate(peers):
        sent.append(
            push(bias_ref.at[peer], tile_land.at[spot], bias_send.at[index], bias_receive.at[spot], {"seq": peer})
        )
    for (step, index), copy in zip(places, loads):
        copy.wait()
        arrived(sibling_land.at[step, index], core_receive.at[step, index], sibling)
        mine[step, index] = (
            mine[step, index].astype(f32) + sibling_land[step, index].astype(f32)
        ).astype(jnp.bfloat16)
        if index == 0:
            sent.append(
                push(mine.at[step, 0, 0], side_land.at[step], side_send.at[step], side_receive.at[step], beside)
            )
        if step > 0:
            sent.append(
                push(
                    mine.at[step, index, 1], line_land.at[step - 1, index],
                    line_send.at[step - 1, index], line_receive.at[step - 1, index], across[step - 1],
                )
            )
    for step in list(range(1, rows)) + [0]:
        arrived(side_land.at[step], side_receive.at[step], beside)
        both = mine[step, 1, 0].astype(f32) + side_land[step].astype(f32)
        if step > 0:
            side_sum[step - 1] = both.astype(jnp.bfloat16)
            sent.append(
                push(
                    side_sum.at[step - 1], last_land.at[step], last_send.at[step], last_receive.at[step],
                    across[step - 1],
                )
            )
        else:
            own_sum[0:width, :] = both
    for index in range(2):
        both = mine[0, index, 1].astype(f32)
        for step in range(1, rows):
            arrived(line_land.at[step - 1, index], line_receive.at[step - 1, index], across[-step])
            both += line_land[step - 1, index].astype(f32)
        if index == 0:
            line_sum_ref[...] = both.astype(jnp.bfloat16)
            sent.append(push(line_sum_ref, last_land.at[0], last_send.at[0], last_receive.at[0], beside))
        else:
            own_sum[width:, :] = both
    for step in range(1, rows):
        arrived(last_land.at[step], last_receive.at[step], across[-step])
        own_sum[0:width, :] += last_land[step].astype(f32)
    line_sum = LineSum(
        count, 2 * width // count, lambda at: own_sum[at, :],
        land, held, total_ref, inner_sem, outer_sem, receive_sem,
    )
    line_sum.begin(range(count // 2))
    for index in range(count // 2):
        line_sum.gather(index)
    arrived(last_land.at[0], last_receive.at[0], beside)
    own_sum[width:, :] += last_land[0].astype(f32)
    line_sum.begin(range(count // 2, count))
    for index in range(count // 2, count):
        line_sum.gather(index)
        line_sum.spread(index - count // 2)
    for peer in peers:
        arrived(tile_land.at[peer], bias_receive.at[peer], {"seq": peer})
    tile = tile_land[0]
    for source in range(1, size):
        tile += tile_land[source]
    tile_line[place] = tile
    for index, plane in enumerate(planes):
        sent.append(
            push(tile_line.at[place], tile_line.at[place], plane_send.at[index], plane_receive.at[place], {"batch": plane})
        )
    for plane in planes:
        arrived(tile_line.at[plane], plane_receive.at[plane], {"batch": plane})
    tile = tile_line[0]
    for source in range(1, lax.axis_size("batch")):
        tile += tile_line[source]
    bias_out[...] = tile
    squares = tile * tile
    for index in range(count // 2, count):
        line_sum.spread(index)
    for row in range(0, 2 * width, 16):
        value = total_ref[row : row + 16, :].astype(f32)
        value = value * value
        for begin in range(0, value.shape[1], LANES):
            squares += value[:8, begin : begin + LANES] + value[8:, begin : begin + LANES]
    head = jnp.sum(squares, axis=0, keepdims=True)
    line8 = lax.broadcasted_iota(jnp.int32, (8, LANES), 0)
    tile_out[...] = jnp.where(line8 == 0, head, note_ref[...])
    note_out[spot] = tile_out[...]
    for index, peer in enumerate(peers):
        sent.append(
            push(tile_out, note_out.at[spot], note_send.at[index], note_receive.at[spot], {"seq": peer})
        )
    for peer in peers:
        arrived(note_out.at[peer], note_receive.at[peer], {"seq": peer})
    for copy in sent:
        copy.wait_send()
    line_sum.finish()


def reduce_gradients(grad, bias, note):
    size = lax.axis_size("seq")
    lines = lax.axis_size("batch")
    _, _, width, depth = grad.shape
    rows = size // 4
    count = 4
    bf16 = jnp.bfloat16
    vmem = pl.BlockSpec(memory_space=pltpu.VMEM)
    dma = pltpu.SemaphoreType.DMA
    near = max(rows - 1, 1)
    return pl.pallas_call(
        functools.partial(reduce_kernel, count),
        in_specs=[pl.BlockSpec(memory_space=pl.ANY), vmem, vmem],
        out_specs=[vmem, vmem, vmem],
        out_shape=[
            jax.ShapeDtypeStruct((2 * width, depth), bf16),
            jax.ShapeDtypeStruct(bias.shape[1:], jnp.float32),
            jax.ShapeDtypeStruct((size,) + note.shape, jnp.float32),
        ],
        scratch_shapes=[
            pltpu.VMEM((rows, 2, 2, width, depth), bf16),
            pltpu.VMEM((rows, 2, 2, width, depth), bf16),
            pltpu.VMEM((rows, width, depth), bf16),
            pltpu.VMEM((near, 2, width, depth), bf16),
            pltpu.VMEM((near, width, depth), bf16),
            pltpu.VMEM((width, depth), bf16),
            pltpu.VMEM((rows, width, depth), bf16),
            pltpu.VMEM((2 * width, depth), jnp.float32),
        ] + LineSum.scratch(count, 2 * width, depth) + [
            pltpu.VMEM((size,) + bias.shape[1:], jnp.float32),
            pltpu.VMEM((lines,) + bias.shape[1:], jnp.float32),
            pltpu.VMEM(note.shape, jnp.float32),
            dma((rows, 2)),
            dma((rows, 2)),
            dma((rows, 2)),
            dma((rows,)),
            dma((rows,)),
            dma((near, 2)),
            dma((near, 2)),
            dma((rows,)),
            dma((rows,)),
            dma((size - 1,)),
            dma((size,)),
            dma((lines - 1,)),
            dma((lines,)),
            dma((size - 1,)),
            dma((size,)),
        ],
        compiler_params=pltpu.CompilerParams(
            collective_id=6, has_side_effects=True, vmem_limit_bytes=VMEM_BYTES
        ),
        name="reduce_gradients",
    )(grad, bias, note)


def body(
    token_ids,
    pos_weights,
    pad_lengths,
    embed_in,
    w_qkv,
    w_out,
    w_fc,
    w_proj,
    norm_gains,
    layer_biases,
    wide_bias,
    unembed,
    trans_weight,
    trans_bias,
    mom1_weight,
    mom2_weight,
    mom1_bias,
    mom2_bias,
):
    bf16 = jnp.bfloat16
    f32 = jnp.float32
    tok_rows = token_ids.shape[1]
    width = embed_in.shape[1]
    vocab_rows = unembed.shape[0]
    n_seq = lax.axis_size("seq")
    n_batch = lax.axis_size("batch")
    batch_index = lax.axis_index("batch")
    seq_index = lax.axis_index("seq")
    head_count = width // HEAD_DIM
    plane_heads = head_count // n_batch
    plane_width = plane_heads * HEAD_DIM
    hidden_rows = w_proj.shape[0]

    half_rot = ROT // 2
    local_places = seq_index * tok_rows + jnp.arange(tok_rows, dtype=jnp.int32)
    frequency = 10000.0 ** (-2.0 * jnp.arange(half_rot, dtype=f32) / ROT)
    angles = local_places.astype(f32)[:, None] * frequency[None, :]
    cosine = jnp.cos(angles)
    sine = jnp.sin(angles)
    still = jnp.zeros((tok_rows, HEAD_DIM - ROT), f32)
    blank = jnp.zeros((tok_rows, half_rot), f32)
    turns = jnp.stack(
        [
            jnp.concatenate([cosine, cosine, still + 1.0], axis=1),
            jnp.concatenate([-sine, blank, still], axis=1),
            jnp.concatenate([blank, sine, still], axis=1),
        ]
    )
    turns = jnp.tile(turns, (1, 1, plane_heads))

    def plane_part(vector, parts, size):
        return lax.dynamic_slice_in_dim(vector.reshape(parts, n_batch, size), batch_index, 1, 1).reshape(1, -1)

    joined_bias = plane_part(wide_bias[: 3 * width], 3, plane_width)
    fc_bias = plane_part(wide_bias[3 * width :], n_seq, hidden_rows)
    padding = jnp.broadcast_to(pad_lengths[:, None], (1, tok_rows))
    tile = jnp.concatenate([token_ids, pos_weights, padding, jnp.zeros((5, tok_rows), jnp.int32)], axis=0)
    own_rows = w_qkv.shape[0]
    joined_cut = jnp.transpose(w_qkv.reshape(own_rows, 3, n_batch, plane_width), (2, 0, 1, 3))
    joined_cut = joined_cut.reshape(n_batch, own_rows, 3 * plane_width)
    fc_cut = jnp.transpose(w_fc.reshape(own_rows, n_seq, n_batch, hidden_rows), (2, 0, 1, 3))
    fc_cut = fc_cut.reshape(n_batch, own_rows, n_seq * hidden_rows)
    own_width = trans_bias.shape[1]
    bias_tile = jnp.zeros((8, LANES), f32).at[:2, :own_width].set(trans_bias)
    tiles, stream_low, joined_w, fc_w, proj_w, out_w, trans_low, bias_all = front(
        tile, embed_in, joined_cut, fc_cut, w_proj, w_out, trans_weight[0], bias_tile
    )
    living = local_places[None, :] < tok_rows * n_seq - tiles[:, 2]
    weights = jnp.where(living, tiles[:, 1], 0).astype(f32).reshape(-1)
    bias_full = jnp.transpose(bias_all[:, :2, :own_width], (1, 0, 2)).reshape(2, width)
    states, translated, low1 = layer(
        stream_low,
        joined_w.reshape(width, 3 * plane_width),
        fc_w.reshape(width, n_seq * hidden_rows),
        proj_w.reshape(n_seq * hidden_rows, width),
        out_w.reshape(plane_width, width),
        trans_low.reshape(width, width),
        trans_weight[1],
        norm_gains,
        layer_biases,
        joined_bias,
        fc_bias,
        bias_full,
        turns,
    )
    probe_low = (stream_low, low1)
    gain_final = norm_gains[2]
    first, second, peaks, sums_part, cross_part = vocab_forward(states, unembed)
    stats = jnp.concatenate([peaks[-1], jnp.sum(sums_part, axis=1), jnp.sum(cross_part, axis=1)], axis=0)
    gathered = share(stats, "batch", 5, "share_stats")
    peak_all = jnp.max(gathered[:, :3], axis=0)
    fades = jnp.exp(gathered[:, :3] - peak_all)
    sums_all = jnp.sum(gathered[:, 3:6] * fades, axis=0)
    cross_all = jnp.sum(gathered[:, 6:] * fades[:, :1], axis=0)
    log_totals = peak_all + jnp.log(sums_all)
    diverge = cross_all / sums_all[0] - log_totals[0] + log_totals[1:]
    loss_part = jnp.sum(weights * (diverge[0] + diverge[1]))
    scales = weights * jnp.exp(peaks - log_totals[None])
    dstates = vocab_backward(first, second, scales, unembed)
    grad_list = []
    bias_list = []
    for index in range(2):
        delta = norm_back(translated[index], dstates[index], gain_final)
        grad_list.append(
            jnp.einsum("td,te->de", probe_low[index], delta.astype(bf16), preferred_element_type=f32)
        )
        bias_list.append(jnp.sum(delta, axis=0))
    grad = jnp.stack(grad_list).astype(bf16).reshape(2, n_seq, width // n_seq, width)
    bias_grad = jnp.transpose(jnp.stack(bias_list).reshape(2, n_seq, width // n_seq), (1, 0, 2))
    bias_grad = jnp.pad(bias_grad, ((0, 0), (0, 6), (0, LANES - width // n_seq)))
    ones = jnp.ones((LANES,), f32) / LANES
    note = jnp.concatenate(
        [
            jnp.zeros((1, LANES), f32),
            (loss_part * ones)[None],
            (jnp.sum(weights) * ones)[None],
            jnp.zeros((5, LANES), f32),
        ]
    )
    grad_sum, bias_sum, notes = reduce_gradients(grad, bias_grad, note)
    sums = jnp.sum(notes, axis=(0, 2))
    loss_sum = sums[1]
    token_count = jnp.round(sums[2])
    grad_norm = jnp.sqrt(sums[0]) / token_count
    factor = jnp.minimum(1.0, clip_max / (grad_norm + 1e-06)) / token_count
    grad_w = grad_sum.astype(f32).reshape(trans_weight.shape) * factor
    grad_b = bias_sum[:2, : trans_bias.shape[1]] * factor
    first_w, second_w, new_w = adam_update(trans_weight, grad_w, mom1_weight, mom2_weight)
    first_b, second_b, new_b = adam_update(trans_bias, grad_b, mom1_bias, mom2_bias)
    return (loss_sum, token_count, grad_norm, first_w, second_w, new_w, first_b, second_b, new_b)


def solution(mesh):
    return jax.shard_map(
        body,
        mesh=mesh,
        in_specs=(
            P("batch", "seq"),
            P("batch", "seq"),
            P("batch"),
            P("batch", None),
            P(("seq", "batch"), None),
            P(("seq", "batch"), None),
            P(("seq", "batch"), None),
            P(("seq", "batch"), None),
            P(),
            P(),
            P(),
            P("batch", None),
            P(None, "seq", None),
            P(None, "seq"),
            P(None, "seq", None),
            P(None, "seq", None),
            P(None, "seq"),
            P(None, "seq"),
        ),
        out_specs=(
            P(),
            P(),
            P(),
            P(None, "seq", None),
            P(None, "seq", None),
            P(None, "seq", None),
            P(None, "seq"),
            P(None, "seq"),
            P(None, "seq"),
        ),
        check_vma=False,
    )
```

```python
import functools

import jax
import jax.numpy as jnp
from jax import lax
from jax.experimental import pallas as pl
from jax.experimental.pallas import tpu as pltpu
from jax.sharding import PartitionSpec as P

HEAD_DIM = 64
ROT = 16
STEP = 10


VOCAB_TILE = 1280
LANES = 128
NEGATIVE = -1e30
VMEM_BYTES = 60 * 1024 * 1024
norm_eps = 1e-05
clip_max = 0.001
beta_one = 0.9
beta_two = 0.999
learn_rate = 0.03
decay_rate = 0.01
adam_eps = 1e-08


def norm_back(values, upstream, gain_row):
    average = jnp.mean(values, axis=-1, keepdims=True)
    centered = values - average
    variance = jnp.mean(centered * centered, axis=-1, keepdims=True)
    inverse = lax.rsqrt(variance + norm_eps)
    unit = centered * inverse
    scaled = upstream * gain_row
    return (
        scaled
        - jnp.mean(scaled, axis=-1, keepdims=True)
        - unit * jnp.mean(scaled * unit, axis=-1, keepdims=True)
    ) * inverse


def adam_update(weight, gradient, earlier, later):
    earlier = beta_one * earlier + (1.0 - beta_one) * gradient
    later = beta_two * later + (1.0 - beta_two) * gradient * gradient
    update = (
        earlier / (1.0 - beta_one**STEP) / (jnp.sqrt(later / (1.0 - beta_two**STEP)) + adam_eps)
    )
    return (earlier, later, weight * (1.0 - learn_rate * decay_rate) - learn_rate * update)


def forward_kernel(vocab, states_ref, table_ref, first_ref, second_ref, peaks_ref, sums_ref, cross_ref, turned, left, right, peak):
    step = pl.program_id(0)
    steps = pl.num_programs(0) - 1
    width = table_ref.shape[0]
    half = left.shape[1] // 3
    group = 16
    last = vocab - (pl.cdiv(vocab, width) - 1) * width
    row = lax.broadcasted_iota(jnp.int32, (group, LANES), 0)

    def reset(part):
        span = slice(part * half, (part + 1) * half)
        peak[:, span] = jnp.full((8, half), NEGATIVE, jnp.float32)
        sums_ref[:, :, span] = jnp.zeros((3, 8, half), jnp.float32)
        cross_ref[:, :, span] = jnp.zeros((2, 8, half), jnp.float32)

    @pl.when(step == 0)
    def _():
        reset(0)
        for state in range(3):
            for part in range(2):
                turned[part, :, state * half : (state + 1) * half] = jnp.transpose(
                    states_ref[state, part * half : (part + 1) * half, :]
                )

    @pl.when(step <= 1)
    def _():
        reset(1)

    def multiply(part, target, state):
        place = slice(state * half, (state + 1) * half)
        target[:, place] = jnp.dot(
            table_ref[...], turned[part, :, place], preferred_element_type=jnp.float32
        )

    def units(part, source, target, tile):
        limit = vocab - tile * width
        blocks = width // group
        result = []
        for lanes in range(half // LANES):
            span = slice(part * half + lanes * LANES, part * half + (lanes + 1) * LANES)
            local = slice(lanes * LANES, (lanes + 1) * LANES)
            held = {}

            def logits(state, block, lanes=lanes):
                begin = state * half + lanes * LANES
                value = source[block * group : (block + 1) * group, begin : begin + LANES]
                if (block + 1) * group > last:
                    value = jnp.where(row + block * group < limit, value, NEGATIVE)
                return value

            def tops(span=span, held=held, logits=logits):
                held["top"], held["sum"], held["cross"] = [], [], []
                for state in range(3):
                    top = logits(state, 0)
                    for block in range(1, blocks):
                        top = jnp.maximum(top, logits(state, block))
                    before = peak[state : state + 1, span]
                    now = jnp.maximum(before, jnp.max(top, axis=0, keepdims=True))
                    peak[state : state + 1, span] = now
                    peaks_ref[pl.ds(tile, 1), state, span] = now
                    fade = jnp.exp(before - now)
                    held["top"].append(jnp.broadcast_to(now, (group, LANES)))
                    held["sum"].append(sums_ref[state, :, span] * fade)
                    if state == 0:
                        held["cross"] = [cross_ref[other, :, span] * fade for other in range(2)]

            def fold(value):
                return value[:8] + value[8:]

            def powers(begin, end, held=held, logits=logits, local=local, fold=fold):
                for block in range(begin, end):
                    place = slice(block * group, (block + 1) * group)
                    base = logits(0, block)
                    base_exp = jnp.exp(base - held["top"][0])
                    held["sum"][0] += fold(base_exp)
                    target[0, 0, place, local] = base_exp.astype(jnp.bfloat16)
                    for state in range(1, 3):
                        value = logits(state, block)
                        value_exp = jnp.exp(value - held["top"][state])
                        held["sum"][state] += fold(value_exp)
                        target[0, state, place, local] = value_exp.astype(jnp.bfloat16)
                        held["cross"][state - 1] += fold(base_exp * (base - value))

            def finish(span=span, held=held):
                for state in range(3):
                    sums_ref[state, :, span] = held["sum"][state]
                for other in range(2):
                    cross_ref[other, :, span] = held["cross"][other]

            result.append(tops)
            cuts = 5
            for cut in range(cuts):
                result.append(
                    functools.partial(powers, cut * blocks // cuts, (cut + 1) * blocks // cuts)
                )
            result.append(finish)
        return result

    def stage(part, target, work):
        done = 0
        for state in range(3):
            multiply(part, target, state)
            upto = (state + 1) * len(work) // 3
            for unit in work[done:upto]:
                unit()
            done = upto

    before = jnp.maximum(step - 1, 0)

    @pl.when(step < steps)
    def _():
        stage(0, left, units(1, right, second_ref, before))
        stage(1, right, units(0, left, first_ref, step))

    @pl.when(step == steps)
    def _():
        for unit in units(1, right, second_ref, before):
            unit()


def vocab_forward(states, table):
    _, rows, depth = states.shape
    vocab = table.shape[0]
    tiles = pl.cdiv(vocab, VOCAB_TILE)
    half = rows // 2
    kept = jax.ShapeDtypeStruct((tiles, 3, VOCAB_TILE, half), jnp.bfloat16)
    block = (1, 3, VOCAB_TILE, half)
    whole = lambda *shape: pl.BlockSpec(shape, lambda i: (0,) * len(shape))
    return pl.pallas_call(
        functools.partial(forward_kernel, vocab),
        grid=(tiles + 1,),
        in_specs=[
            whole(3, rows, depth),
            pl.BlockSpec((VOCAB_TILE, depth), lambda i: (jnp.minimum(i, tiles - 1), 0)),
        ],
        out_specs=[
            pl.BlockSpec(block, lambda i: (jnp.minimum(i, tiles - 1), 0, 0, 0)),
            pl.BlockSpec(block, lambda i: (jnp.maximum(i - 1, 0), 0, 0, 0)),
            whole(tiles, 3, rows),
            whole(3, 8, rows),
            whole(2, 8, rows),
        ],
        out_shape=[
            kept,
            kept,
            jax.ShapeDtypeStruct((tiles, 3, rows), jnp.float32),
            jax.ShapeDtypeStruct((3, 8, rows), jnp.float32),
            jax.ShapeDtypeStruct((2, 8, rows), jnp.float32),
        ],
        scratch_shapes=[
            pltpu.VMEM((2, depth, 3 * half), jnp.bfloat16),
            pltpu.VMEM((VOCAB_TILE, 3 * half), jnp.float32),
            pltpu.VMEM((VOCAB_TILE, 3 * half), jnp.float32),
            pltpu.VMEM((8, rows), jnp.float32),
        ],
        compiler_params=pltpu.CompilerParams(vmem_limit_bytes=VMEM_BYTES),
        cost_estimate=pl.CostEstimate(
            flops=6 * rows * depth * vocab,
            bytes_accessed=2 * vocab * (depth + 3 * rows),
            transcendentals=3 * rows * vocab,
        ),
        name="vocab_forward",
    )(states, table)


def backward_kernel(
    vocab, first_ref, second_ref, scales_ref, table_ref, moved_ref, low0_ref, low1_ref, gain_ref,
    grad_ref, bias_ref, out_ref, left, right, tail, delta, turned,
):
    step = pl.program_id(0)
    tiles = pl.num_programs(0) - 1
    width, depth = table_ref.shape
    half = first_ref.shape[3]
    piece = 256
    last = vocab - (pl.cdiv(vocab, width) - 1) * width
    whole = last // piece * piece
    tile = jnp.maximum(step - 1, 0)
    limit = vocab - tile * width

    def units(part, source, target, index):
        result = []

        def turn(lanes, block):
            begin = part * half + lanes * LANES
            span = slice(begin, begin + LANES)
            place = slice(block * LANES, (block + 1) * LANES)
            local = slice(lanes * LANES, (lanes + 1) * LANES)
            factors = scales_ref[pl.ds(index, 1), :, span][0]
            base = source[0, 0, place, local].astype(jnp.float32) * factors[0:1]
            for state in range(1, 3):
                value = source[0, state, place, local].astype(jnp.float32) * factors[state : state + 1]
                first = (state - 1) * half + lanes * LANES
                target[first : first + LANES, place] = jnp.transpose(
                    (value - base).astype(jnp.bfloat16)
                )

        for lanes in range(half // LANES):
            for block in range(width // LANES):
                result.append(functools.partial(turn, lanes, block))
        return result

    def multiply(part, source, start):
        place = slice(start, start + piece)
        span = slice(part * half, (part + 1) * half)
        partial = jnp.dot(source[:, whole:], tail[:, place], preferred_element_type=jnp.float32)
        if whole > 0:
            partial += jnp.dot(
                source[:, :whole], table_ref[:whole, place], preferred_element_type=jnp.float32
            )
        for probe in range(2):
            out_ref[probe, span, place] += partial[probe * half : (probe + 1) * half]

    def stage(part, source, work):
        done = 0
        pieces = depth // piece
        for index in range(pieces):
            multiply(part, source, index * piece)
            upto = (index + 1) * len(work) // pieces
            for unit in work[done:upto]:
                unit()
            done = upto

    ahead = jnp.minimum(step, tiles - 1)

    @pl.when(step == 0)
    def _():
        out_ref[...] = jnp.zeros_like(out_ref)
        for unit in units(0, first_ref, left, ahead):
            unit()

    @pl.when(step > 0)
    def _():
        below = lax.broadcasted_iota(jnp.int32, (width - whole, depth), 0) + whole < limit
        tail[...] = jnp.where(below, table_ref[whole:, :], jnp.zeros((), tail.dtype))
        stage(0, left, units(1, second_ref, right, tile))
        stage(1, right, units(0, first_ref, left, ahead))

    @pl.when(step == tiles)
    def _():
        rows = out_ref.shape[1]
        chunk = 32
        block = 256
        for probe in range(2):
            low_ref = (low0_ref, low1_ref)[probe]

            def back(index, total, probe=probe):
                at = pl.ds(pl.multiple_of(index * chunk, chunk), chunk)
                value = norm_back(moved_ref[probe, at, :], out_ref[probe, at, :], gain_ref[2:3, :])
                delta[at, :] = value.astype(jnp.bfloat16)
                return total + jnp.sum(value, axis=0, keepdims=True)

            bias_ref[probe : probe + 1, :] = lax.fori_loop(
                0, rows // chunk, back, jnp.zeros((1, depth), jnp.float32)
            )
            turned[...] = jnp.transpose(low_ref[...])
            for begin in range(0, depth, block):
                grad_ref[probe, begin : begin + block, :] = jnp.dot(
                    turned[begin : begin + block, :], delta[...], preferred_element_type=jnp.float32
                ).astype(jnp.bfloat16)


def vocab_backward(first, second, scales, table, moved, low0, low1, gains):
    tiles, _, _, half = first.shape
    vocab, depth = table.shape
    rows = 2 * half
    last = vocab - (tiles - 1) * VOCAB_TILE
    block = (1, 3, VOCAB_TILE, half)
    whole = lambda *shape: pl.BlockSpec(shape, lambda i: (0,) * len(shape))
    return pl.pallas_call(
        functools.partial(backward_kernel, vocab),
        grid=(tiles + 1,),
        in_specs=[
            pl.BlockSpec(block, lambda i: (jnp.minimum(i, tiles - 1), 0, 0, 0)),
            pl.BlockSpec(block, lambda i: (jnp.maximum(i - 1, 0), 0, 0, 0)),
            whole(tiles, 3, rows),
            pl.BlockSpec((VOCAB_TILE, depth), lambda i: (jnp.maximum(i - 1, 0), 0)),
            whole(2, rows, depth),
            whole(rows, depth),
            whole(rows, depth),
            whole(*gains.shape),
        ],
        out_specs=[whole(2, depth, depth), whole(2, depth)],
        out_shape=[
            jax.ShapeDtypeStruct((2, depth, depth), jnp.bfloat16),
            jax.ShapeDtypeStruct((2, depth), jnp.float32),
        ],
        scratch_shapes=[
            pltpu.VMEM((2, rows, depth), jnp.float32),
            pltpu.VMEM((2 * half, VOCAB_TILE), jnp.bfloat16),
            pltpu.VMEM((2 * half, VOCAB_TILE), jnp.bfloat16),
            pltpu.VMEM((VOCAB_TILE - last // 256 * 256, depth), jnp.bfloat16),
            pltpu.VMEM((rows, depth), jnp.bfloat16),
            pltpu.VMEM((depth, rows), jnp.bfloat16),
        ],
        compiler_params=pltpu.CompilerParams(vmem_limit_bytes=VMEM_BYTES),
        cost_estimate=pl.CostEstimate(
            flops=4 * rows * depth * (vocab + depth),
            bytes_accessed=2 * vocab * (depth + 3 * rows),
            transcendentals=0,
        ),
        name="vocab_backward",
    )(first, second, scales, table, moved, low0, low1, gains)


def plane_place(place):
    core = lax.rem(place, 2)
    return core, lax.rem(place // 2, 2), place // 4


def plane_index(core, column, line):
    return (line * 2 + column) * 2 + core


def greet(partners):
    barrier = pltpu.get_barrier_semaphore()
    for partner in partners:
        pl.semaphore_signal(barrier, inc=1, device_id=partner, device_id_type=pl.DeviceIdType.MESH)
    pl.semaphore_wait(barrier, len(partners))


def push(source, target, send, receive, partner):
    copy = pltpu.make_async_remote_copy(
        src_ref=source,
        dst_ref=target,
        send_sem=send,
        recv_sem=receive,
        device_id=partner,
        device_id_type=pl.DeviceIdType.MESH,
    )
    copy.start()
    return copy


def arrived(target, receive, partner):
    pltpu.make_async_remote_copy(
        src_ref=target,
        dst_ref=target,
        send_sem=receive,
        recv_sem=receive,
        device_id=partner,
        device_id_type=pl.DeviceIdType.MESH,
    ).wait_recv()


def departed(source, send, partner):
    pltpu.make_async_remote_copy(
        src_ref=source,
        dst_ref=source,
        send_sem=send,
        recv_sem=send,
        device_id=partner,
        device_id_type=pl.DeviceIdType.MESH,
    ).wait_send()


class LineSum:
    def __init__(self, count, size, own, land, held, total, inner_sem, outer_sem, receive_sem):
        lines = lax.axis_size("batch")
        place = lax.axis_index("batch")
        near = place < lines // 2
        self.count, self.size = count, size
        self.own, self.land, self.held, self.total = own, land, held, total
        self.inner_sem, self.outer_sem, self.receive_sem = inner_sem, outer_sem, receive_sem
        self.middle = (place == lines // 2 - 1) | (place == lines // 2)
        self.end = (place == 0) | (place == lines - 1)
        self.inner = {"batch": jnp.where(near, place + 1, place - 1)}
        self.outer = {"batch": jnp.where(near, place - 1, place + 1)}
        self.slot = jnp.where(self.middle, 1, 0)

    def rows(self, index):
        return pl.ds(index * self.size, self.size)

    def send_in(self, index):
        rows = self.rows(index)
        push(
            self.held.at[rows],
            self.land.at[self.slot, rows],
            self.inner_sem.at[index],
            self.receive_sem.at[self.slot, index],
            self.inner,
        )

    def begin(self, indices):
        @pl.when(self.end)
        def _():
            for index in indices:
                rows = self.rows(index)
                self.held[rows, :] = self.own(rows).astype(jnp.bfloat16)
                self.send_in(index)

    def gather(self, index):
        rows = self.rows(index)

        @pl.when(jnp.logical_not(self.end))
        def _():
            arrived(self.land.at[0, rows], self.receive_sem.at[0, index], self.outer)
            own = self.own(rows).astype(jnp.float32)
            self.held[rows, :] = (own + self.land[0, rows, :].astype(jnp.float32)).astype(jnp.bfloat16)
            self.send_in(index)

    def spread(self, index):
        rows = self.rows(index)

        @pl.when(self.middle)
        def _():
            arrived(self.land.at[1, rows], self.receive_sem.at[1, index], self.inner)
            both = self.held[rows, :].astype(jnp.float32) + self.land[1, rows, :].astype(jnp.float32)
            self.total[rows, :] = both.astype(jnp.bfloat16)

        @pl.when(jnp.logical_not(self.middle))
        def _():
            arrived(self.total.at[rows], self.receive_sem.at[2, index], self.inner)

        @pl.when(jnp.logical_not(self.end))
        def _():
            push(
                self.total.at[rows],
                self.total.at[rows],
                self.outer_sem.at[index],
                self.receive_sem.at[2, index],
                self.outer,
            )

    def run(self, lag, todo=()):
        todo = list(todo)
        for index in range(self.count + lag):
            if index < self.count:
                self.gather(index)
            if index >= lag:
                self.spread(index - lag)
            if todo:
                todo.pop(0)()
        for work in todo:
            work()

    def finish(self):
        for index in range(self.count):
            rows = self.rows(index)
            departed(self.held.at[rows], self.inner_sem.at[index], self.inner)

            @pl.when(jnp.logical_not(self.end))
            def _(rows=rows, index=index):
                departed(self.total.at[rows], self.outer_sem.at[index], self.outer)

    @staticmethod
    def scratch(count, rows, depth):
        return [
            pltpu.VMEM((2, rows, depth), jnp.bfloat16),
            pltpu.VMEM((rows, depth), jnp.bfloat16),
            pltpu.SemaphoreType.DMA((count,)),
            pltpu.SemaphoreType.DMA((count,)),
            pltpu.SemaphoreType.DMA((3, count)),
        ]


class PlaneGather:
    def __init__(self, views, send_sem, receive_sem):
        self.views, self.send_sem, self.receive_sem = views, send_sem, receive_sem
        self.size = lax.axis_size("seq")
        self.spot = lax.axis_index("seq")
        core, column, line = self.where = plane_place(self.spot)
        self.rows = self.size // 4
        self.beside = plane_index(core, 1 - column, line)
        self.sibling = plane_index(1 - core, column, line)
        lines = [lax.rem(line + step, self.rows) for step in range(1, self.rows)]
        self.across = [plane_index(core, column, at) for at in lines]
        self.corners = [plane_index(core, 1 - column, at) for at in lines]
        self.started = []

    def send(self, array, half, slot, way, index, target):
        view = self.views[array](half, slot)
        self.started.append(
            push(
                view, view, self.send_sem.at[array, half, way, index], self.receive_sem.at[array, half, slot],
                {"seq": target},
            )
        )

    def wait(self, array, half, slot):
        arrived(self.views[array](half, slot), self.receive_sem.at[array, half, slot], {"seq": slot})

    def own(self, array):
        for half in range(2):
            self.send(array, half, self.spot, 0, 0, self.beside)
            for index, target in enumerate(self.across):
                self.send(array, half, self.spot, 1 + index, 0, target)
            self.send(array, half, self.spot, self.rows, 0, self.sibling)

    def relay_side(self, array):
        self.wait(array, 0, self.beside)
        for index, target in enumerate(self.across):
            self.send(array, 0, self.beside, 1 + index, 1, target)
        for index, source in enumerate(self.across):
            self.wait(array, 1, source)
            self.send(array, 1, source, 0, 1 + index, self.beside)

    def relay_core(self, array):
        self.send(array, 0, self.beside, self.rows, 1, self.sibling)
        self.wait(array, 1, self.beside)
        self.send(array, 1, self.beside, self.rows, 1, self.sibling)
        for index, source in enumerate(self.across):
            self.send(array, 1, source, self.rows, 2 + index, self.sibling)
            self.wait(array, 0, source)
            self.send(array, 0, source, self.rows, 2 + index, self.sibling)
        for index, source in enumerate(self.corners):
            for half in range(2):
                self.wait(array, half, source)
                self.send(array, half, source, self.rows, 1 + self.rows + index, self.sibling)

    def receive_core(self, array):
        core, _, line = self.where
        for step in range(self.rows):
            for side in range(2):
                source = plane_index(1 - core, side, lax.rem(line + step, self.rows))
                for half in range(2):
                    self.wait(array, half, source)

    def finish(self):
        for copy in self.started:
            copy.wait_send()

    @staticmethod
    def scratch(arrays):
        size = lax.axis_size("seq")
        dma = pltpu.SemaphoreType.DMA
        return [dma((arrays, 2, size // 4 + 1, size // 2 + 1)), dma((arrays, 2, size))]


def others(axis):
    size = lax.axis_size(axis)
    place = lax.axis_index(axis)
    return [lax.rem(place + step, size) for step in range(1, size)]


def front_kernel(
    count,
    tile_ref, table_ref, joined_ref, fc_ref, proj_ref, out_ref, bias_ref,
    tiles_out, stream_ref, joined_out, fc_out, proj_out, out_out, bias_out,
    table, column_ids, chosen, picked,
    land, held, inner_sem, outer_sem, receive_sem,
    local_sem, table_sem, tile_send, tile_receive, cross_send, cross_receive, plane_send, plane_receive, bias_send, bias_receive,
):
    lines = lax.axis_size("batch")
    place = lax.axis_index("batch")
    size = lax.axis_size("seq")
    spot = lax.axis_index("seq")
    planes = others("batch")
    peers = others("seq")
    outs = (joined_out, fc_out, proj_out, out_out)
    total_rows, depth = stream_ref.shape
    chunk = total_rows // count
    tokens = tile_ref.shape[1]
    vocab = table_ref.shape[0]
    number = spot * lines + place
    goal = {"seq": lax.rem(number, size), "batch": number // size}
    wanted = place * size + spot
    origin = {"seq": wanted // lines, "batch": lax.rem(wanted, lines)}
    stays = number == wanted

    def view(array):
        out = outs[array]
        if array < 2:
            return lambda half, slot: out.at[slot, pl.ds(half * (lines // 2), lines // 2)]
        return lambda half, slot: out.at[slot, :, pl.ds(half * (depth // 2), depth // 2)]

    plane = PlaneGather([view(array) for array in range(4)], plane_send, plane_receive)
    width = chosen.shape[1]
    cuts = table.shape[0] // width
    table_copies = [
        pltpu.make_async_copy(
            table_ref.at[pl.ds(cut * width, min(width, vocab - cut * width))],
            table.at[pl.ds(cut * width, min(width, vocab - cut * width))],
            table_sem.at[cut],
        )
        for cut in range(cuts)
    ]
    for copy in table_copies:
        copy.start()
    if table.shape[0] > vocab:
        table[vocab:, :] = jnp.zeros((table.shape[0] - vocab, depth), table.dtype)
    locals_ = [
        pltpu.make_async_copy(source, target, local_sem.at[index])
        for index, (source, target) in enumerate(
            (
                (proj_ref, proj_out.at[spot]),
                (joined_ref.at[place], joined_out.at[spot, place]),
                (fc_ref.at[place], fc_out.at[spot, place]),
                (tile_ref, tiles_out.at[place]),
                (bias_ref, bias_out.at[spot]),
            )
        )
    ]
    for copy in locals_:
        copy.start()
    out_copy = pltpu.make_async_copy(out_ref, out_out.at[spot], local_sem.at[5])

    @pl.when(stays)
    def _():
        out_copy.start()

    barrier = pltpu.get_barrier_semaphore()
    for partner in [{"batch": other} for other in planes] + [{"seq": peer} for peer in peers]:
        pl.semaphore_signal(barrier, inc=1, device_id=partner, device_id_type=pl.DeviceIdType.MESH)

    @pl.when(jnp.logical_not(stays))
    def _():
        pl.semaphore_signal(barrier, inc=1, device_id=origin, device_id_type=pl.DeviceIdType.MESH)

    pl.semaphore_wait(barrier, jnp.where(stays, 0, 1) + len(planes) + len(peers))

    tile_copies = [
        push(tile_ref, tiles_out.at[place], tile_send.at[index], tile_receive.at[place], {"batch": other})
        for index, other in enumerate(planes)
    ]
    locals_[0].wait()
    plane.own(2)
    crossing = []
    for array, source, out in ((0, joined_ref, joined_out), (1, fc_ref, fc_out)):
        for index, other in enumerate(planes):
            crossing.append(
                push(source.at[other], out.at[spot, place], cross_send.at[array, index], cross_receive.at[array, place], {"batch": other})
            )
    out_push = pltpu.make_async_remote_copy(
        src_ref=out_ref, dst_ref=out_out.at[goal["seq"]], send_sem=cross_send.at[2, 0],
        recv_sem=cross_receive.at[2, 0], device_id=goal, device_id_type=pl.DeviceIdType.MESH,
    )

    @pl.when(jnp.logical_not(stays))
    def _():
        out_push.start()

    bias_copies = [
        push(bias_ref, bias_out.at[spot], bias_send.at[index], bias_receive.at[spot], {"seq": peer})
        for index, peer in enumerate(peers)
    ]
    for copy in locals_[1:]:
        copy.wait()
    for other in planes:
        arrived(tiles_out.at[other], tile_receive.at[other], {"batch": other})
    for sequence in range(lines):
        turned = jnp.transpose(tiles_out[sequence].astype(jnp.float32))
        column_ids[sequence * tokens : (sequence + 1) * tokens, :] = jnp.broadcast_to(
            turned[:, 0:1] - (place * vocab).astype(jnp.float32), (tokens, LANES)
        )
    half = total_rows // 2
    lane = lax.broadcasted_iota(jnp.int32, (half, LANES), 1)

    def look(part):
        at = slice(part * half, (part + 1) * half)
        for cut in range(cuts):
            if part == 0:
                table_copies[cut].wait()
            for block in range(width // LANES):
                number_ = (lane + (cut * width + block * LANES)).astype(jnp.float32)
                chosen[:, block * LANES : (block + 1) * LANES] = jnp.where(
                    column_ids[at, :] == number_, 1.0, 0.0
                ).astype(jnp.bfloat16)
            found = jnp.dot(
                chosen[...], table[cut * width : (cut + 1) * width, :], preferred_element_type=jnp.float32
            )
            if cut == 0:
                picked[at, :] = found
            else:
                picked[at, :] += found

    line_sum = LineSum(
        count, chunk, lambda at: picked[at, :],
        land, held, stream_ref, inner_sem, outer_sem, receive_sem,
    )

    def turn(array):
        for other in planes:
            arrived(outs[array].at[spot, other], cross_receive.at[array, other], {"batch": other})
        plane.own(array)

    def turn_out():
        @pl.when(stays)
        def _():
            out_copy.wait()

        @pl.when(jnp.logical_not(stays))
        def _():
            arrived(out_out.at[spot], cross_receive.at[2, 0], origin)

        plane.own(3)

    todo = [
        lambda: turn(0),
        lambda: (plane.relay_side(2), turn(1)),
        lambda: (turn_out(), plane.relay_core(2)),
        lambda: plane.relay_side(0),
        lambda: None,
        lambda: plane.relay_core(0),
        lambda: None,
        lambda: plane.relay_side(1),
        lambda: plane.relay_side(3),
        lambda: None,
        lambda: plane.relay_core(1),
        lambda: None,
        lambda: plane.relay_core(3),
        lambda: plane.receive_core(2),
        lambda: plane.receive_core(0),
        lambda: plane.receive_core(1),
        lambda: plane.receive_core(3),
    ]
    for part in range(2):
        look(part)
        line_sum.begin(range(part * count // 2, (part + 1) * count // 2))
        todo.pop(0)()
    line_sum.run(3, todo)
    for peer in peers:
        arrived(bias_out.at[peer], bias_receive.at[peer], {"seq": peer})
    for copy in crossing + bias_copies + tile_copies:
        copy.wait_send()

    @pl.when(jnp.logical_not(stays))
    def _():
        out_push.wait_send()

    plane.finish()
    line_sum.finish()


def front(tile, table, joined, fc, proj, out, bias):
    size = lax.axis_size("seq")
    lines = lax.axis_size("batch")
    vocab, depth = table.shape
    rows = lines * tile.shape[1]
    count = 16
    vmem = pl.BlockSpec(memory_space=pltpu.VMEM)
    anywhere = pl.BlockSpec(memory_space=pl.ANY)
    dma = pltpu.SemaphoreType.DMA
    bf16 = jnp.bfloat16
    spread = lambda part, kind: jax.ShapeDtypeStruct((size,) + part.shape, kind)
    return pl.pallas_call(
        functools.partial(front_kernel, count),
        in_specs=[vmem, anywhere, anywhere, anywhere, anywhere, anywhere, vmem],
        out_specs=[vmem, vmem, anywhere, anywhere, anywhere, anywhere, vmem],
        out_shape=[
            jax.ShapeDtypeStruct((lines,) + tile.shape, tile.dtype),
            jax.ShapeDtypeStruct((rows, depth), bf16),
            spread(joined, bf16),
            spread(fc, bf16),
            spread(proj, bf16),
            spread(out, bf16),
            spread(bias, jnp.float32),
        ],
        scratch_shapes=[
            pltpu.VMEM((pl.cdiv(vocab, VOCAB_TILE) * VOCAB_TILE, depth), bf16),
            pltpu.VMEM((rows, LANES), jnp.float32),
            pltpu.VMEM((rows // 2, VOCAB_TILE), bf16),
            pltpu.VMEM((rows, depth), jnp.float32),
        ] + LineSum.scratch(count, rows, depth) + [
            dma((6,)),
            dma((pl.cdiv(vocab, VOCAB_TILE),)),
            dma((lines - 1,)),
            dma((lines,)),
            dma((3, lines - 1)),
            dma((3, lines)),
        ] + PlaneGather.scratch(4) + [
            dma((size - 1,)),
            dma((size,)),
        ],
        compiler_params=pltpu.CompilerParams(
            collective_id=1, has_side_effects=True, vmem_limit_bytes=VMEM_BYTES
        ),
        name="front",
    )(tile, table, joined, fc, proj, out, bias)


def row_norm(values):
    average = jnp.mean(values, axis=-1, keepdims=True)
    centered = values - average
    variance = jnp.mean(centered * centered, axis=-1, keepdims=True)
    return centered * lax.rsqrt(variance + norm_eps)


def layer_kernel(
    count, heads,
    stream_ref, joined_ref, fc_ref, proj_ref, out_ref, trans_ref,
    gains_ref, offsets_ref, joined_bias, fc_bias, trans_bias, turns_ref,
    states_ref, moved_ref, low_ref,
    first_trans, second_trans, x_attn, x_mlp, spread, gathered, mixed, returned, part,
    land, held, total, inner_sem, outer_sem, receive_sem,
    local_sem, heads_send, heads_receive, rows_send, rows_receive, plane_send, plane_receive,
):
    f32 = jnp.float32
    bf16 = jnp.bfloat16
    lines = lax.axis_size("batch")
    place = lax.axis_index("batch")
    size = lax.axis_size("seq")
    spot = lax.axis_index("seq")
    planes = others("batch")
    peers = others("seq")
    rows, depth = stream_ref.shape
    tokens = rows // lines
    plane_width = joined_ref.shape[1] // 3
    columns = spread.shape[3]
    groups = plane_width // columns
    head_dim = columns // heads
    step_rows = 32

    spans = (first_trans, second_trans)
    for probe in range(2):
        spans[probe][spot] = trans_ref[probe].astype(bf16)
    greet([{"batch": plane} for plane in planes] + [{"seq": peer} for peer in peers])
    sent = []

    def view(array):
        return lambda half, slot: spans[array].at[slot, :, pl.ds(half * (depth // 2), depth // 2)]

    plane = PlaneGather([view(0), view(1)], plane_send, plane_receive)

    def norms(index, carry):
        at = pl.ds(pl.multiple_of(index * step_rows, step_rows), step_rows)
        unit = row_norm(stream_ref[at, :].astype(f32))
        x_attn[at, :] = (unit * gains_ref[0:1, :] + offsets_ref[0:1, :]).astype(bf16)
        x_mlp[at, :] = (unit * gains_ref[1:2, :] + offsets_ref[1:2, :]).astype(bf16)
        return carry

    lax.fori_loop(0, rows // step_rows, norms, 0)
    half_rot = ROT // 2
    for sequence in range(lines):
        at = slice(sequence * tokens, (sequence + 1) * tokens)
        for kind in range(3):
            place_ = slice(kind * plane_width, (kind + 1) * plane_width)
            value = jnp.dot(x_attn[at, :], joined_ref[:, place_], preferred_element_type=f32)
            value = value + joined_bias[0:1, place_]
            if kind < 2:
                value = (
                    value * turns_ref[0]
                    + pltpu.roll(value, plane_width - half_rot, 1) * turns_ref[1]
                    + pltpu.roll(value, half_rot, 1) * turns_ref[2]
                )
            value = value.astype(bf16)
            for group in range(groups):
                spread[sequence * groups + group, kind] = value[:, group * columns : (group + 1) * columns]
    for index, peer in enumerate(peers):
        sent.append(
            push(spread.at[peer], gathered.at[spot], heads_send.at[index], heads_receive.at[spot], {"seq": peer})
        )
    heads_copy = pltpu.make_async_copy(spread.at[spot], gathered.at[spot], local_sem.at[0])
    heads_copy.start()
    plane.own(0)
    plane.own(1)

    def hidden_part(index, carry):
        at = pl.ds(pl.multiple_of(index * tokens, tokens), tokens)
        value = jnp.dot(x_mlp[at, :], fc_ref[...], preferred_element_type=f32) + fc_bias[...]
        value = 0.5 * value * (1.0 + lax.erf(value * (0.5 ** 0.5)))
        part[at, :] = jnp.dot(value.astype(bf16), proj_ref[...], preferred_element_type=f32)
        return carry

    lax.fori_loop(0, lines, hidden_part, 0)

    def translate(probe, stream, low, weights, at):
        moved = stream + jnp.dot(low, weights, preferred_element_type=f32) + trans_bias[probe : probe + 1, :]
        moved_ref[probe, at, :] = moved
        states_ref[1 + probe, at, :] = (
            row_norm(moved) * gains_ref[2:3, :] + offsets_ref[4:5, :]
        ).astype(bf16)

    def first_probe(sequence):
        at = slice(sequence * tokens, (sequence + 1) * tokens)
        low = stream_ref[at, :]
        translate(0, low.astype(f32), low, first_trans[...].reshape(depth, depth), at)

    plane.relay_side(0)
    heads_copy.wait()
    for peer in peers:
        arrived(gathered.at[peer], heads_receive.at[peer], {"seq": peer})
    length = size * tokens
    block = 2 * tokens
    lane = lax.broadcasted_iota(jnp.int32, (block, columns), 1) // head_dim
    keys = jnp.concatenate([gathered[source, 1] for source in range(size)], axis=0)
    values = jnp.concatenate([gathered[source, 2] for source in range(size)], axis=0)
    for first in range(0, length, block):
        end = first + block
        queries = jnp.concatenate([gathered[first // tokens, 0], gathered[first // tokens + 1, 0]], axis=0)
        allowed = lax.broadcasted_iota(jnp.int32, (block, end), 1) <= (
            lax.broadcasted_iota(jnp.int32, (block, end), 0) + first
        )
        result = None
        for head in range(heads):
            chosen = jnp.where(lane == head, queries, jnp.zeros((), bf16))
            scores = lax.dot_general(
                chosen, keys[:end], (((1,), (1,)), ((), ())), preferred_element_type=f32
            ) * head_dim ** (-0.5)
            scores = jnp.where(allowed, scores, NEGATIVE)
            exponent = jnp.exp(scores - jnp.max(scores, axis=-1, keepdims=True))
            value = jnp.dot(
                exponent.astype(bf16), values[:end], preferred_element_type=f32
            ) / jnp.sum(exponent, axis=-1, keepdims=True)
            result = value if result is None else jnp.where(lane == head, value, result)
        result = result.astype(bf16)
        for index in range(2):
            mixed[first // tokens + index] = result[index * tokens : (index + 1) * tokens]
    for index, peer in enumerate(peers):
        sent.append(
            push(mixed.at[peer], returned.at[spot], rows_send.at[index], rows_receive.at[spot], {"seq": peer})
        )
    rows_copy = pltpu.make_async_copy(mixed.at[spot], returned.at[spot], local_sem.at[1])
    rows_copy.start()
    plane.relay_core(0)
    plane.relay_side(1)
    rows_copy.wait()
    for peer in peers:
        arrived(returned.at[peer], rows_receive.at[peer], {"seq": peer})
    for sequence in range(lines):
        at = slice(sequence * tokens, (sequence + 1) * tokens)
        attended = jnp.concatenate(
            [returned[sequence * groups + group] for group in range(groups)], axis=1
        )
        part[at, :] += jnp.dot(attended, out_ref[...], preferred_element_type=f32)
    line_sum = LineSum(
        count, rows // count, lambda at: part[at, :],
        land, held, total, inner_sem, outer_sem, receive_sem,
    )
    line_sum.begin(range(count))
    todo = [lambda: None, lambda: plane.relay_core(1), lambda: plane.receive_core(0)]
    todo += [functools.partial(first_probe, sequence) for sequence in range(lines)]
    todo += [lambda: plane.receive_core(1)]
    line_sum.run(3, todo)

    def second_probe(index, carry):
        at = pl.ds(pl.multiple_of(index * tokens, tokens), tokens)
        stream = (
            stream_ref[at, :].astype(f32) + total[at, :].astype(f32) + offsets_ref[2:3, :] + offsets_ref[3:4, :]
        )
        states_ref[0, at, :] = (row_norm(stream) * gains_ref[2:3, :] + offsets_ref[4:5, :]).astype(bf16)
        low = stream.astype(bf16)
        low_ref[at, :] = low
        translate(1, stream, low, second_trans[...].reshape(depth, depth), at)
        return carry

    lax.fori_loop(0, lines, second_probe, 0)
    for copy in sent:
        copy.wait_send()
    plane.finish()
    line_sum.finish()


def layer(stream, joined, fc, proj, out, trans, gains, offsets, joined_bias, fc_bias, trans_bias, turns):
    size = lax.axis_size("seq")
    lines = lax.axis_size("batch")
    rows, depth = stream.shape
    tokens = rows // lines
    own_heads = depth // HEAD_DIM // size
    columns = own_heads * HEAD_DIM
    count = 16
    bf16 = jnp.bfloat16
    f32 = jnp.float32
    vmem = pl.BlockSpec(memory_space=pltpu.VMEM)
    dma = pltpu.SemaphoreType.DMA
    return pl.pallas_call(
        functools.partial(layer_kernel, count, own_heads),
        in_specs=[vmem] * 12,
        out_specs=[vmem] * 3,
        out_shape=[
            jax.ShapeDtypeStruct((3, rows, depth), bf16),
            jax.ShapeDtypeStruct((2, rows, depth), f32),
            jax.ShapeDtypeStruct((rows, depth), bf16),
        ],
        scratch_shapes=[
            pltpu.VMEM((size,) + trans.shape[1:], bf16),
            pltpu.VMEM((size,) + trans.shape[1:], bf16),
            pltpu.VMEM((rows, depth), bf16),
            pltpu.VMEM((rows, depth), bf16),
            pltpu.VMEM((size, 3, tokens, columns), bf16),
            pltpu.VMEM((size, 3, tokens, columns), bf16),
            pltpu.VMEM((size, tokens, columns), bf16),
            pltpu.VMEM((size, tokens, columns), bf16),
            pltpu.VMEM((rows, depth), f32),
        ] + LineSum.scratch(count, rows, depth)[:2] + [
            pltpu.VMEM((rows, depth), bf16),
        ] + LineSum.scratch(count, rows, depth)[2:] + [
            dma((2,)),
            dma((size - 1,)),
            dma((size,)),
            dma((size - 1,)),
            dma((size,)),
        ] + PlaneGather.scratch(2),
        compiler_params=pltpu.CompilerParams(
            collective_id=2, has_side_effects=True, vmem_limit_bytes=VMEM_BYTES
        ),
        name="layer",
    )(stream, joined, fc, proj, out, trans, gains, offsets, joined_bias, fc_bias, trans_bias, turns)


def stats_kernel(
    tiles_ref, peaks_ref, sums_ref, cross_ref, scales_ref, note_ref,
    gathered, send_sem, receive_sem,
):
    place = lax.axis_index("batch")
    spot = lax.axis_index("seq")
    size = lax.axis_size("seq")
    planes = others("batch")
    tiles = peaks_ref.shape[0]
    rows = peaks_ref.shape[2]
    lines = gathered.shape[0]
    tokens = rows // lines
    gathered[place, 0:3, :] = peaks_ref[tiles - 1]
    for state in range(3):
        gathered[place, 3 + state : 4 + state, :] = jnp.sum(sums_ref[state], axis=0, keepdims=True)
    for other in range(2):
        gathered[place, 6 + other : 7 + other, :] = jnp.sum(cross_ref[other], axis=0, keepdims=True)
    greet([{"batch": plane} for plane in planes])
    copies = [
        push(gathered.at[place], gathered.at[place], send_sem.at[index], receive_sem.at[place], {"batch": plane})
        for index, plane in enumerate(planes)
    ]
    position = spot * tokens + lax.broadcasted_iota(jnp.int32, (1, tokens), 1)
    weights = jnp.concatenate(
        [
            jnp.where(position < size * tokens - tiles_ref[line, 2:3, :], tiles_ref[line, 1:2, :], 0).astype(jnp.float32)
            for line in range(lines)
        ],
        axis=1,
    )
    for plane in planes:
        arrived(gathered.at[plane], receive_sem.at[plane], {"batch": plane})
    tops = gathered[0, 0:3, :]
    for line in range(1, lines):
        tops = jnp.maximum(tops, gathered[line, 0:3, :])
    sums = jnp.zeros((3, rows), jnp.float32)
    cross = jnp.zeros((2, rows), jnp.float32)
    for line in range(lines):
        fade = jnp.exp(gathered[line, 0:3, :] - tops)
        sums += gathered[line, 3:6, :] * fade
        cross += gathered[line, 6:8, :] * fade[0:1]
    totals = tops + jnp.log(sums)
    diverge = cross / sums[0:1] - totals[0:1] + totals[1:3]
    loss = weights * (diverge[0:1] + diverge[1:2])
    for tile in range(tiles):
        scales_ref[tile] = weights * jnp.exp(peaks_ref[tile] - totals)
    note_ref[...] = jnp.zeros_like(note_ref)
    for line in range(rows // LANES):
        at = slice(line * LANES, (line + 1) * LANES)
        note_ref[1:2, :] += loss[:, at]
        note_ref[2:3, :] += weights[:, at]
    for copy in copies:
        copy.wait_send()


def statistics(tiles, peaks, sums, cross):
    lines = lax.axis_size("batch")
    rows = peaks.shape[2]
    vmem = pl.BlockSpec(memory_space=pltpu.VMEM)
    return pl.pallas_call(
        stats_kernel,
        in_specs=[vmem] * 4,
        out_specs=[vmem] * 2,
        out_shape=[
            jax.ShapeDtypeStruct(peaks.shape, jnp.float32),
            jax.ShapeDtypeStruct((8, LANES), jnp.float32),
        ],
        scratch_shapes=[
            pltpu.VMEM((lines, 8, rows), jnp.float32),
            pltpu.SemaphoreType.DMA((lines - 1,)),
            pltpu.SemaphoreType.DMA((lines,)),
        ],
        compiler_params=pltpu.CompilerParams(collective_id=5, has_side_effects=True),
        name="statistics",
    )(tiles, peaks, sums, cross)


def reduce_kernel(
    count,
    grad_ref, bias_ref, note_ref,
    total_ref, bias_out, note_out,
    mine, sibling_land, side_land, line_land, side_sum, line_part, last_land, own_sum,
    land, held, inner_sem, outer_sem, receive_sem,
    tile_land, tile_line, tile_out,
    local_sem, core_send, core_receive, side_send, side_receive, line_send, line_receive,
    last_send, last_receive, bias_send, bias_receive, plane_send, plane_receive, note_send, note_receive,
):
    size = lax.axis_size("seq")
    spot = lax.axis_index("seq")
    place = lax.axis_index("batch")
    core, column, line = plane_place(spot)
    rows = size // 4
    step_rows = total_ref.shape[0] // count // 2
    beside = {"seq": plane_index(core, 1 - column, line)}
    sibling = {"seq": plane_index(1 - core, column, line)}
    across = [{"seq": plane_index(core, column, lax.rem(line + step, rows))} for step in range(1, rows)]
    peers = others("seq")
    planes = others("batch")
    f32 = jnp.float32
    bf16 = jnp.bfloat16
    chips = [
        (step, index, lax.rem(line + step, rows), side)
        for step in range(rows)
        for index, side in enumerate((1 - column, column))
    ]
    sent = []

    def cut(chunk):
        return pl.ds(chunk * step_rows, step_rows)

    loads = {}
    for chunk in range(count):
        for step, index, at, side in chips:
            copy = pltpu.make_async_copy(
                grad_ref.at[:, plane_index(core, side, at), cut(chunk)], mine.at[chunk, step, index],
                local_sem.at[chunk, step, index],
            )
            copy.start()
            loads[chunk, step, index] = copy
    tile_land[spot] = bias_ref[spot]
    greet([{"batch": plane} for plane in planes] + [{"seq": peer} for peer in peers])
    for chunk in range(count):
        for step, index, at, side in chips:
            sent.append(
                push(
                    grad_ref.at[:, plane_index(1 - core, side, at), cut(chunk)], sibling_land.at[chunk, step, index],
                    core_send.at[chunk, step, index], core_receive.at[chunk, step, index], sibling,
                )
            )
    for index, peer in enumerate(peers):
        sent.append(
            push(bias_ref.at[peer], tile_land.at[spot], bias_send.at[index], bias_receive.at[spot], {"seq": peer})
        )
    line_sum = LineSum(
        count, 2 * step_rows, lambda at: own_sum[at, :],
        land, held, total_ref, inner_sem, outer_sem, receive_sem,
    )

    def pair(chunk):
        for step, index, _, _ in chips:
            loads[chunk, step, index].wait()
            arrived(sibling_land.at[chunk, step, index], core_receive.at[chunk, step, index], sibling)
            mine[chunk, step, index] = (
                mine[chunk, step, index].astype(f32) + sibling_land[chunk, step, index].astype(f32)
            ).astype(bf16)
            if index == 0:
                sent.append(
                    push(
                        mine.at[chunk, step, 0, 0], side_land.at[chunk, step],
                        side_send.at[chunk, step], side_receive.at[chunk, step], beside,
                    )
                )
            if step > 0:
                sent.append(
                    push(
                        mine.at[chunk, step, index, 1], line_land.at[chunk, step - 1, index],
                        line_send.at[chunk, step - 1, index], line_receive.at[chunk, step - 1, index],
                        across[step - 1],
                    )
                )

    def second(chunk):
        begin = chunk * 2 * step_rows
        for step in list(range(1, rows)) + [0]:
            arrived(side_land.at[chunk, step], side_receive.at[chunk, step], beside)
            both = mine[chunk, step, 1, 0].astype(f32) + side_land[chunk, step].astype(f32)
            if step > 0:
                side_sum[chunk, step - 1] = both.astype(bf16)
                sent.append(
                    push(
                        side_sum.at[chunk, step - 1], last_land.at[chunk, step],
                        last_send.at[chunk, step], last_receive.at[chunk, step], across[step - 1],
                    )
                )
            else:
                own_sum[begin : begin + step_rows, :] = both
        for index in range(2):
            both = mine[chunk, 0, index, 1].astype(f32)
            for step in range(1, rows):
                arrived(
                    line_land.at[chunk, step - 1, index], line_receive.at[chunk, step - 1, index], across[-step]
                )
                both += line_land[chunk, step - 1, index].astype(f32)
            if index == 0:
                line_part[chunk] = both.astype(bf16)
                sent.append(
                    push(
                        line_part.at[chunk], last_land.at[chunk, 0],
                        last_send.at[chunk, 0], last_receive.at[chunk, 0], beside,
                    )
                )
            else:
                own_sum[begin + step_rows : begin + 2 * step_rows, :] = both

    def third(chunk):
        begin = chunk * 2 * step_rows
        for step in range(1, rows):
            arrived(last_land.at[chunk, step], last_receive.at[chunk, step], across[-step])
            own_sum[begin : begin + step_rows, :] += last_land[chunk, step].astype(f32)
        arrived(last_land.at[chunk, 0], last_receive.at[chunk, 0], beside)
        own_sum[begin + step_rows : begin + 2 * step_rows, :] += last_land[chunk, 0].astype(f32)
        line_sum.begin([chunk])
        line_sum.gather(chunk)

    def tiles_in_plane():
        for peer in peers:
            arrived(tile_land.at[peer], bias_receive.at[peer], {"seq": peer})
        tile = tile_land[0]
        for source in range(1, size):
            tile += tile_land[source]
        tile_line[place] = tile
        for index, plane in enumerate(planes):
            sent.append(
                push(
                    tile_line.at[place], tile_line.at[place], plane_send.at[index], plane_receive.at[place],
                    {"batch": plane},
                )
            )

    squares = []

    def square(chunk):
        line_sum.spread(chunk)
        for row in range(chunk * 2 * step_rows, (chunk + 1) * 2 * step_rows, 16):
            value = total_ref[row : row + 16, :].astype(f32)
            value = value * value
            for begin in range(0, value.shape[1], LANES):
                block = value[:8, begin : begin + LANES] + value[8:, begin : begin + LANES]
                squares[:] = [block + squares[0]] if squares else [block]

    for time in range(count + 5):
        if time < count:
            pair(time)
        if 0 <= time - 2 < count:
            second(time - 2)
        if 0 <= time - 3 < count:
            third(time - 3)
        if time == count:
            tiles_in_plane()
        if 0 <= time - 5 < count:
            square(time - 5)
    for plane in planes:
        arrived(tile_line.at[plane], plane_receive.at[plane], {"batch": plane})
    tile = tile_line[0]
    for source in range(1, lax.axis_size("batch")):
        tile += tile_line[source]
    bias_out[...] = tile
    head = jnp.sum(squares[0] + tile * tile, axis=0, keepdims=True)
    row8 = lax.broadcasted_iota(jnp.int32, (8, LANES), 0)
    tile_out[...] = jnp.where(row8 == 0, head, note_ref[...])
    note_out[spot] = tile_out[...]
    for index, peer in enumerate(peers):
        sent.append(
            push(tile_out, note_out.at[spot], note_send.at[index], note_receive.at[spot], {"seq": peer})
        )
    for peer in peers:
        arrived(note_out.at[peer], note_receive.at[peer], {"seq": peer})
    for copy in sent:
        copy.wait_send()
    line_sum.finish()


def reduce_gradients(grad, bias, note):
    size = lax.axis_size("seq")
    lines = lax.axis_size("batch")
    _, _, width, depth = grad.shape
    rows = size // 4
    count = 4
    cut = width // count
    bf16 = jnp.bfloat16
    vmem = pl.BlockSpec(memory_space=pltpu.VMEM)
    dma = pltpu.SemaphoreType.DMA
    near = max(rows - 1, 1)
    total, bias_sum, notes = pl.pallas_call(
        functools.partial(reduce_kernel, count),
        in_specs=[pl.BlockSpec(memory_space=pl.ANY), vmem, vmem],
        out_specs=[vmem, vmem, vmem],
        out_shape=[
            jax.ShapeDtypeStruct((2 * width, depth), bf16),
            jax.ShapeDtypeStruct(bias.shape[1:], jnp.float32),
            jax.ShapeDtypeStruct((size,) + note.shape, jnp.float32),
        ],
        scratch_shapes=[
            pltpu.VMEM((count, rows, 2, 2, cut, depth), bf16),
            pltpu.VMEM((count, rows, 2, 2, cut, depth), bf16),
            pltpu.VMEM((count, rows, cut, depth), bf16),
            pltpu.VMEM((count, near, 2, cut, depth), bf16),
            pltpu.VMEM((count, near, cut, depth), bf16),
            pltpu.VMEM((count, cut, depth), bf16),
            pltpu.VMEM((count, rows, cut, depth), bf16),
            pltpu.VMEM((2 * width, depth), jnp.float32),
        ] + LineSum.scratch(count, 2 * width, depth) + [
            pltpu.VMEM((size,) + bias.shape[1:], jnp.float32),
            pltpu.VMEM((lines,) + bias.shape[1:], jnp.float32),
            pltpu.VMEM(note.shape, jnp.float32),
            dma((count, rows, 2)),
            dma((count, rows, 2)),
            dma((count, rows, 2)),
            dma((count, rows)),
            dma((count, rows)),
            dma((count, near, 2)),
            dma((count, near, 2)),
            dma((count, rows)),
            dma((count, rows)),
            dma((size - 1,)),
            dma((size,)),
            dma((lines - 1,)),
            dma((lines,)),
            dma((size - 1,)),
            dma((size,)),
        ],
        compiler_params=pltpu.CompilerParams(
            collective_id=6, has_side_effects=True, vmem_limit_bytes=VMEM_BYTES
        ),
        name="reduce_gradients",
    )(grad, bias, note)
    total = jnp.transpose(total.reshape(count, 2, cut, depth), (1, 0, 2, 3)).reshape(2, width, depth)
    return total, bias_sum, notes


def body(
    token_ids,
    pos_weights,
    pad_lengths,
    embed_in,
    w_qkv,
    w_out,
    w_fc,
    w_proj,
    norm_gains,
    layer_biases,
    wide_bias,
    unembed,
    trans_weight,
    trans_bias,
    mom1_weight,
    mom2_weight,
    mom1_bias,
    mom2_bias,
):
    bf16 = jnp.bfloat16
    f32 = jnp.float32
    tok_rows = token_ids.shape[1]
    width = embed_in.shape[1]
    vocab_rows = unembed.shape[0]
    n_seq = lax.axis_size("seq")
    n_batch = lax.axis_size("batch")
    batch_index = lax.axis_index("batch")
    seq_index = lax.axis_index("seq")
    head_count = width // HEAD_DIM
    plane_heads = head_count // n_batch
    plane_width = plane_heads * HEAD_DIM
    hidden_rows = w_proj.shape[0]

    half_rot = ROT // 2
    local_places = seq_index * tok_rows + jnp.arange(tok_rows, dtype=jnp.int32)
    frequency = 10000.0 ** (-2.0 * jnp.arange(half_rot, dtype=f32) / ROT)
    angles = local_places.astype(f32)[:, None] * frequency[None, :]
    cosine = jnp.cos(angles)
    sine = jnp.sin(angles)
    still = jnp.zeros((tok_rows, HEAD_DIM - ROT), f32)
    blank = jnp.zeros((tok_rows, half_rot), f32)
    turns = jnp.stack(
        [
            jnp.concatenate([cosine, cosine, still + 1.0], axis=1),
            jnp.concatenate([-sine, blank, still], axis=1),
            jnp.concatenate([blank, sine, still], axis=1),
        ]
    )
    turns = jnp.tile(turns, (1, 1, plane_heads))

    def plane_part(vector, parts, size):
        return lax.dynamic_slice_in_dim(vector.reshape(parts, n_batch, size), batch_index, 1, 1).reshape(1, -1)

    joined_bias = plane_part(wide_bias[: 3 * width], 3, plane_width)
    fc_bias = plane_part(wide_bias[3 * width :], n_seq, hidden_rows)
    padding = jnp.broadcast_to(pad_lengths[:, None], (1, tok_rows))
    tile = jnp.concatenate([token_ids, pos_weights, padding, jnp.zeros((5, tok_rows), jnp.int32)], axis=0)
    own_rows = w_qkv.shape[0]
    joined_cut = jnp.transpose(w_qkv.reshape(own_rows, 3, n_batch, plane_width), (2, 0, 1, 3))
    joined_cut = joined_cut.reshape(n_batch, own_rows, 3 * plane_width)
    fc_cut = jnp.transpose(w_fc.reshape(own_rows, n_seq, n_batch, hidden_rows), (2, 0, 1, 3))
    fc_cut = fc_cut.reshape(n_batch, own_rows, n_seq * hidden_rows)
    own_width = trans_bias.shape[1]
    bias_tile = jnp.zeros((8, LANES), f32).at[:2, :own_width].set(trans_bias)
    tiles, stream_low, joined_w, fc_w, proj_w, out_w, bias_all = front(
        tile, embed_in, joined_cut, fc_cut, w_proj, w_out, bias_tile
    )
    bias_full = jnp.transpose(bias_all[:, :2, :own_width], (1, 0, 2)).reshape(2, width)
    states, translated, low1 = layer(
        stream_low,
        joined_w.reshape(width, 3 * plane_width),
        fc_w.reshape(width, n_seq * hidden_rows),
        proj_w.reshape(n_seq * hidden_rows, width),
        out_w.reshape(plane_width, width),
        trans_weight,
        norm_gains,
        layer_biases,
        joined_bias,
        fc_bias,
        bias_full,
        turns,
    )
    first, second, peaks, sums_part, cross_part = vocab_forward(states, unembed)
    scales, note = statistics(tiles, peaks, sums_part, cross_part)
    grad, bias_grad = vocab_backward(
        first, second, scales, unembed, translated, stream_low, low1, norm_gains
    )
    bias_grad = jnp.transpose(bias_grad.reshape(2, n_seq, own_width), (1, 0, 2))
    bias_grad = jnp.pad(bias_grad, ((0, 0), (0, 6), (0, LANES - own_width)))
    grad = grad.reshape(2, n_seq, own_width, width)
    grad_sum, bias_sum, notes = reduce_gradients(grad, bias_grad, note)
    sums = jnp.sum(notes, axis=(0, 2))
    loss_sum = sums[1]
    token_count = jnp.round(sums[2])
    grad_norm = jnp.sqrt(sums[0]) / token_count
    factor = jnp.minimum(1.0, clip_max / (grad_norm + 1e-06)) / token_count
    grad_w = grad_sum.astype(f32) * factor
    grad_b = bias_sum[:2, : trans_bias.shape[1]] * factor
    first_w, second_w, new_w = adam_update(trans_weight, grad_w, mom1_weight, mom2_weight)
    first_b, second_b, new_b = adam_update(trans_bias, grad_b, mom1_bias, mom2_bias)
    return (loss_sum, token_count, grad_norm, first_w, second_w, new_w, first_b, second_b, new_b)


def solution(mesh):
    return jax.shard_map(
        body,
        mesh=mesh,
        in_specs=(
            P("batch", "seq"),
            P("batch", "seq"),
            P("batch"),
            P("batch", None),
            P(("seq", "batch"), None),
            P(("seq", "batch"), None),
            P(("seq", "batch"), None),
            P(("seq", "batch"), None),
            P(),
            P(),
            P(),
            P("batch", None),
            P(None, "seq", None),
            P(None, "seq"),
            P(None, "seq", None),
            P(None, "seq", None),
            P(None, "seq"),
            P(None, "seq"),
        ),
        out_specs=(
            P(),
            P(),
            P(),
            P(None, "seq", None),
            P(None, "seq", None),
            P(None, "seq", None),
            P(None, "seq"),
            P(None, "seq"),
            P(None, "seq"),
        ),
        check_vma=False,
    )
```

```python
import functools

import jax
import jax.numpy as jnp
from jax import lax
from jax.experimental import pallas as pl
from jax.experimental.pallas import tpu as pltpu
from jax.sharding import PartitionSpec as P

HEAD_DIM = 64
ROT = 16
STEP = 10


VOCAB_TILE = 1280
LANES = 128
NEGATIVE = -1e30
VMEM_BYTES = 60 * 1024 * 1024
norm_eps = 1e-05
clip_max = 0.001
beta_one = 0.9
beta_two = 0.999
learn_rate = 0.03
decay_rate = 0.01
adam_eps = 1e-08


def norm_back(values, upstream, gain_row):
    average = jnp.mean(values, axis=-1, keepdims=True)
    centered = values - average
    variance = jnp.mean(centered * centered, axis=-1, keepdims=True)
    inverse = lax.rsqrt(variance + norm_eps)
    unit = centered * inverse
    scaled = upstream * gain_row
    return (
        scaled
        - jnp.mean(scaled, axis=-1, keepdims=True)
        - unit * jnp.mean(scaled * unit, axis=-1, keepdims=True)
    ) * inverse


def adam_update(weight, gradient, earlier, later):
    earlier = beta_one * earlier + (1.0 - beta_one) * gradient
    later = beta_two * later + (1.0 - beta_two) * gradient * gradient
    update = (
        earlier / (1.0 - beta_one**STEP) / (jnp.sqrt(later / (1.0 - beta_two**STEP)) + adam_eps)
    )
    return (earlier, later, weight * (1.0 - learn_rate * decay_rate) - learn_rate * update)


def forward_kernel(vocab, states_ref, table_ref, probe0_ref, probe1_ref, first_ref, second_ref, peaks_ref, sums_ref, cross_ref, turned, left, right, peak):
    step = pl.program_id(0)
    steps = pl.num_programs(0) - 1
    width = table_ref.shape[0]
    half = left.shape[1] // 2
    group = 16
    given = (probe0_ref, probe1_ref)
    last = vocab - (pl.cdiv(vocab, width) - 1) * width
    row = lax.broadcasted_iota(jnp.int32, (group, LANES), 0)

    def reset(part):
        span = slice(part * half, (part + 1) * half)
        peak[:, span] = jnp.full((8, half), NEGATIVE, jnp.float32)
        sums_ref[:, :, span] = jnp.zeros((3, 8, half), jnp.float32)
        cross_ref[:, :, span] = jnp.zeros((2, 8, half), jnp.float32)

    @pl.when(step == 0)
    def _():
        reset(0)
        for state in range(2):
            for part in range(2):
                turned[part, :, state * half : (state + 1) * half] = jnp.transpose(
                    states_ref[2 * state, part * half : (part + 1) * half, :]
                )

    @pl.when(step <= 1)
    def _():
        reset(1)

    def multiply(part, target, state, cut):
        place = slice(state * half, (state + 1) * half)
        at = slice(cut * width // 2, (cut + 1) * width // 2)
        target[at, place] = jnp.dot(
            table_ref[at, :], turned[part, :, place], preferred_element_type=jnp.float32
        )

    def units(part, source, target, tile):
        limit = vocab - tile * width
        blocks = width // group
        result = []
        for lanes in range(half // LANES):
            span = slice(part * half + lanes * LANES, part * half + (lanes + 1) * LANES)
            local = slice(lanes * LANES, (lanes + 1) * LANES)
            held = {}

            def logits(state, block, lanes=lanes):
                at = slice(block * group, (block + 1) * group)
                if state == 1:
                    value = given[part][0, at, lanes * LANES : (lanes + 1) * LANES]
                else:
                    begin = state // 2 * half + lanes * LANES
                    value = source[at, begin : begin + LANES]
                if (block + 1) * group > last:
                    value = jnp.where(row + block * group < limit, value, NEGATIVE)
                return value

            def tops(span=span, held=held, logits=logits):
                held["top"], held["sum"], held["cross"] = [], [], []
                for state in range(3):
                    top = logits(state, 0)
                    for block in range(1, blocks):
                        top = jnp.maximum(top, logits(state, block))
                    before = peak[state : state + 1, span]
                    now = jnp.maximum(before, jnp.max(top, axis=0, keepdims=True))
                    peak[state : state + 1, span] = now
                    peaks_ref[pl.ds(tile, 1), state, span] = now
                    fade = jnp.exp(before - now)
                    held["top"].append(jnp.broadcast_to(now, (group, LANES)))
                    held["sum"].append(sums_ref[state, :, span] * fade)
                    if state == 0:
                        held["cross"] = [cross_ref[other, :, span] * fade for other in range(2)]

            def fold(value):
                return value[:8] + value[8:]

            def powers(begin, end, held=held, logits=logits, local=local, fold=fold):
                for block in range(begin, end):
                    place = slice(block * group, (block + 1) * group)
                    base = logits(0, block)
                    base_exp = jnp.exp(base - held["top"][0])
                    held["sum"][0] += fold(base_exp)
                    target[0, 0, place, local] = base_exp.astype(jnp.bfloat16)
                    for state in range(1, 3):
                        value = logits(state, block)
                        value_exp = jnp.exp(value - held["top"][state])
                        held["sum"][state] += fold(value_exp)
                        target[0, state, place, local] = value_exp.astype(jnp.bfloat16)
                        held["cross"][state - 1] += fold(base_exp * (base - value))

            def finish(span=span, held=held):
                for state in range(3):
                    sums_ref[state, :, span] = held["sum"][state]
                for other in range(2):
                    cross_ref[other, :, span] = held["cross"][other]

            result.append(tops)
            cuts = 5
            for cut in range(cuts):
                result.append(
                    functools.partial(powers, cut * blocks // cuts, (cut + 1) * blocks // cuts)
                )
            result.append(finish)
        return result

    def stage(part, target, work):
        done = 0
        for piece in range(4):
            multiply(part, target, piece // 2, piece % 2)
            upto = (piece + 1) * len(work) // 4
            for unit in work[done:upto]:
                unit()
            done = upto

    before = jnp.maximum(step - 1, 0)

    @pl.when(step < steps)
    def _():
        stage(0, left, units(1, right, second_ref, before))
        stage(1, right, units(0, left, first_ref, step))

    @pl.when(step == steps)
    def _():
        for unit in units(1, right, second_ref, before):
            unit()


def vocab_forward(states, table, given):
    _, rows, depth = states.shape
    vocab = table.shape[0]
    tiles = pl.cdiv(vocab, VOCAB_TILE)
    half = rows // 2
    kept = jax.ShapeDtypeStruct((tiles, 3, VOCAB_TILE, half), jnp.bfloat16)
    block = (1, 3, VOCAB_TILE, half)
    whole = lambda *shape: pl.BlockSpec(shape, lambda i: (0,) * len(shape))
    return pl.pallas_call(
        functools.partial(forward_kernel, vocab),
        grid=(tiles + 1,),
        in_specs=[
            whole(3, rows, depth),
            pl.BlockSpec((VOCAB_TILE, depth), lambda i: (jnp.minimum(i, tiles - 1), 0)),
            pl.BlockSpec((1, VOCAB_TILE, half), lambda i: (jnp.minimum(i, tiles - 1), 0, 0)),
            pl.BlockSpec((1, VOCAB_TILE, half), lambda i: (jnp.maximum(i - 1, 0), 0, 1)),
        ],
        out_specs=[
            pl.BlockSpec(block, lambda i: (jnp.minimum(i, tiles - 1), 0, 0, 0)),
            pl.BlockSpec(block, lambda i: (jnp.maximum(i - 1, 0), 0, 0, 0)),
            whole(tiles, 3, rows),
            whole(3, 8, rows),
            whole(2, 8, rows),
        ],
        out_shape=[
            kept,
            kept,
            jax.ShapeDtypeStruct((tiles, 3, rows), jnp.float32),
            jax.ShapeDtypeStruct((3, 8, rows), jnp.float32),
            jax.ShapeDtypeStruct((2, 8, rows), jnp.float32),
        ],
        scratch_shapes=[
            pltpu.VMEM((2, depth, 2 * half), jnp.bfloat16),
            pltpu.VMEM((VOCAB_TILE, 2 * half), jnp.float32),
            pltpu.VMEM((VOCAB_TILE, 2 * half), jnp.float32),
            pltpu.VMEM((8, rows), jnp.float32),
        ],
        compiler_params=pltpu.CompilerParams(vmem_limit_bytes=VMEM_BYTES),
        cost_estimate=pl.CostEstimate(
            flops=4 * rows * depth * vocab,
            bytes_accessed=2 * vocab * (depth + 5 * rows),
            transcendentals=3 * rows * vocab,
        ),
        name="vocab_forward",
    )(states, table, given, given)


def backward_kernel(
    vocab, first_ref, second_ref, scales_ref, table_ref, moved_ref, low0_ref, low1_ref, gain_ref,
    grad_ref, bias_ref, out_ref, left, right, tail, delta, turned,
):
    step = pl.program_id(0)
    tiles = pl.num_programs(0) - 1
    width, depth = table_ref.shape
    half = first_ref.shape[3]
    piece = 256
    last = vocab - (pl.cdiv(vocab, width) - 1) * width
    whole = last // piece * piece
    tile = jnp.maximum(step - 1, 0)
    limit = vocab - tile * width

    def units(part, source, target, index):
        result = []

        def turn(lanes, block):
            begin = part * half + lanes * LANES
            span = slice(begin, begin + LANES)
            place = slice(block * LANES, (block + 1) * LANES)
            local = slice(lanes * LANES, (lanes + 1) * LANES)
            factors = scales_ref[pl.ds(index, 1), :, span][0]
            base = source[0, 0, place, local].astype(jnp.float32) * factors[0:1]
            for state in range(1, 3):
                value = source[0, state, place, local].astype(jnp.float32) * factors[state : state + 1]
                first = (state - 1) * half + lanes * LANES
                target[first : first + LANES, place] = jnp.transpose(
                    (value - base).astype(jnp.bfloat16)
                )

        for lanes in range(half // LANES):
            for block in range(width // LANES):
                result.append(functools.partial(turn, lanes, block))
        return result

    def multiply(part, source, start):
        place = slice(start, start + piece)
        span = slice(part * half, (part + 1) * half)
        partial = jnp.dot(source[:, whole:], tail[:, place], preferred_element_type=jnp.float32)
        if whole > 0:
            partial += jnp.dot(
                source[:, :whole], table_ref[:whole, place], preferred_element_type=jnp.float32
            )
        for probe in range(2):
            out_ref[probe, span, place] += partial[probe * half : (probe + 1) * half]

    def stage(part, source, work):
        done = 0
        pieces = depth // piece
        for index in range(pieces):
            multiply(part, source, index * piece)
            upto = (index + 1) * len(work) // pieces
            for unit in work[done:upto]:
                unit()
            done = upto

    ahead = jnp.minimum(step, tiles - 1)

    @pl.when(step == 0)
    def _():
        out_ref[...] = jnp.zeros_like(out_ref)
        for unit in units(0, first_ref, left, ahead):
            unit()

    @pl.when(step > 0)
    def _():
        below = lax.broadcasted_iota(jnp.int32, (width - whole, depth), 0) + whole < limit
        tail[...] = jnp.where(below, table_ref[whole:, :], jnp.zeros((), tail.dtype))
        stage(0, left, units(1, second_ref, right, tile))
        stage(1, right, units(0, first_ref, left, ahead))

    @pl.when(step == tiles)
    def _():
        rows = out_ref.shape[1]
        chunk = 32
        block = 256
        for probe in range(2):
            low_ref = (low0_ref, low1_ref)[probe]

            def back(index, total, probe=probe):
                at = pl.ds(pl.multiple_of(index * chunk, chunk), chunk)
                value = norm_back(moved_ref[probe, at, :], out_ref[probe, at, :], gain_ref[2:3, :])
                delta[at, :] = value.astype(jnp.bfloat16)
                return total + jnp.sum(value, axis=0, keepdims=True)

            bias_ref[probe : probe + 1, :] = lax.fori_loop(
                0, rows // chunk, back, jnp.zeros((1, depth), jnp.float32), unroll=4
            )
            turned[...] = jnp.transpose(low_ref[...])
            for begin in range(0, depth, block):
                grad_ref[probe, begin : begin + block, :] = jnp.dot(
                    turned[begin : begin + block, :], delta[...], preferred_element_type=jnp.float32
                ).astype(jnp.bfloat16)


def vocab_backward(first, second, scales, table, moved, low0, low1, gains):
    tiles, _, _, half = first.shape
    vocab, depth = table.shape
    rows = 2 * half
    last = vocab - (tiles - 1) * VOCAB_TILE
    block = (1, 3, VOCAB_TILE, half)
    whole = lambda *shape: pl.BlockSpec(shape, lambda i: (0,) * len(shape))
    return pl.pallas_call(
        functools.partial(backward_kernel, vocab),
        grid=(tiles + 1,),
        in_specs=[
            pl.BlockSpec(block, lambda i: (jnp.minimum(i, tiles - 1), 0, 0, 0)),
            pl.BlockSpec(block, lambda i: (jnp.maximum(i - 1, 0), 0, 0, 0)),
            whole(tiles, 3, rows),
            pl.BlockSpec((VOCAB_TILE, depth), lambda i: (jnp.maximum(i - 1, 0), 0)),
            whole(2, rows, depth),
            whole(rows, depth),
            whole(rows, depth),
            whole(*gains.shape),
        ],
        out_specs=[whole(2, depth, depth), whole(2, depth)],
        out_shape=[
            jax.ShapeDtypeStruct((2, depth, depth), jnp.bfloat16),
            jax.ShapeDtypeStruct((2, depth), jnp.float32),
        ],
        scratch_shapes=[
            pltpu.VMEM((2, rows, depth), jnp.float32),
            pltpu.VMEM((2 * half, VOCAB_TILE), jnp.bfloat16),
            pltpu.VMEM((2 * half, VOCAB_TILE), jnp.bfloat16),
            pltpu.VMEM((VOCAB_TILE - last // 256 * 256, depth), jnp.bfloat16),
            pltpu.VMEM((rows, depth), jnp.bfloat16),
            pltpu.VMEM((depth, rows), jnp.bfloat16),
        ],
        compiler_params=pltpu.CompilerParams(vmem_limit_bytes=VMEM_BYTES),
        cost_estimate=pl.CostEstimate(
            flops=4 * rows * depth * (vocab + depth),
            bytes_accessed=2 * vocab * (depth + 3 * rows),
            transcendentals=0,
        ),
        name="vocab_backward",
    )(first, second, scales, table, moved, low0, low1, gains)


def plane_place(place):
    core = lax.rem(place, 2)
    return core, lax.rem(place // 2, 2), place // 4


def plane_index(core, column, line):
    return (line * 2 + column) * 2 + core


def greet(partners):
    barrier = pltpu.get_barrier_semaphore()
    for partner in partners:
        pl.semaphore_signal(barrier, inc=1, device_id=partner, device_id_type=pl.DeviceIdType.MESH)
    pl.semaphore_wait(barrier, len(partners))


def push(source, target, send, receive, partner):
    copy = pltpu.make_async_remote_copy(
        src_ref=source,
        dst_ref=target,
        send_sem=send,
        recv_sem=receive,
        device_id=partner,
        device_id_type=pl.DeviceIdType.MESH,
    )
    copy.start()
    return copy


def arrived(target, receive, partner):
    pltpu.make_async_remote_copy(
        src_ref=target,
        dst_ref=target,
        send_sem=receive,
        recv_sem=receive,
        device_id=partner,
        device_id_type=pl.DeviceIdType.MESH,
    ).wait_recv()


def departed(source, send, partner):
    pltpu.make_async_remote_copy(
        src_ref=source,
        dst_ref=source,
        send_sem=send,
        recv_sem=send,
        device_id=partner,
        device_id_type=pl.DeviceIdType.MESH,
    ).wait_send()


class LineSum:
    def __init__(self, count, size, own, land, held, total, inner_sem, outer_sem, receive_sem):
        lines = lax.axis_size("batch")
        place = lax.axis_index("batch")
        near = place < lines // 2
        self.count, self.size = count, size
        self.own, self.land, self.held, self.total = own, land, held, total
        self.inner_sem, self.outer_sem, self.receive_sem = inner_sem, outer_sem, receive_sem
        self.middle = (place == lines // 2 - 1) | (place == lines // 2)
        self.end = (place == 0) | (place == lines - 1)
        self.inner = {"batch": jnp.where(near, place + 1, place - 1)}
        self.outer = {"batch": jnp.where(near, place - 1, place + 1)}
        self.slot = jnp.where(self.middle, 1, 0)

    def rows(self, index):
        return pl.ds(index * self.size, self.size)

    def send_in(self, index):
        rows = self.rows(index)
        push(
            self.held.at[rows],
            self.land.at[self.slot, rows],
            self.inner_sem.at[index],
            self.receive_sem.at[self.slot, index],
            self.inner,
        )

    def begin(self, indices):
        @pl.when(self.end)
        def _():
            for index in indices:
                rows = self.rows(index)
                self.held[rows, :] = self.own(rows).astype(jnp.bfloat16)
                self.send_in(index)

    def gather(self, index):
        rows = self.rows(index)

        @pl.when(jnp.logical_not(self.end))
        def _():
            arrived(self.land.at[0, rows], self.receive_sem.at[0, index], self.outer)
            own = self.own(rows).astype(jnp.float32)
            self.held[rows, :] = (own + self.land[0, rows, :].astype(jnp.float32)).astype(jnp.bfloat16)
            self.send_in(index)

    def spread(self, index):
        rows = self.rows(index)

        @pl.when(self.middle)
        def _():
            arrived(self.land.at[1, rows], self.receive_sem.at[1, index], self.inner)
            both = self.held[rows, :].astype(jnp.float32) + self.land[1, rows, :].astype(jnp.float32)
            self.total[rows, :] = both.astype(jnp.bfloat16)

        @pl.when(jnp.logical_not(self.middle))
        def _():
            arrived(self.total.at[rows], self.receive_sem.at[2, index], self.inner)

        @pl.when(jnp.logical_not(self.end))
        def _():
            push(
                self.total.at[rows],
                self.total.at[rows],
                self.outer_sem.at[index],
                self.receive_sem.at[2, index],
                self.outer,
            )

    def run(self, lag, todo=()):
        todo = list(todo)
        for index in range(self.count + lag):
            if index < self.count:
                self.gather(index)
            if index >= lag:
                self.spread(index - lag)
            if todo:
                todo.pop(0)()
        for work in todo:
            work()

    def finish(self):
        for index in range(self.count):
            rows = self.rows(index)
            departed(self.held.at[rows], self.inner_sem.at[index], self.inner)

            @pl.when(jnp.logical_not(self.end))
            def _(rows=rows, index=index):
                departed(self.total.at[rows], self.outer_sem.at[index], self.outer)

    @staticmethod
    def scratch(count, rows, depth):
        return [
            pltpu.VMEM((2, rows, depth), jnp.bfloat16),
            pltpu.VMEM((rows, depth), jnp.bfloat16),
            pltpu.SemaphoreType.DMA((count,)),
            pltpu.SemaphoreType.DMA((count,)),
            pltpu.SemaphoreType.DMA((3, count)),
        ]


class PlaneGather:
    def __init__(self, views, send_sem, receive_sem):
        self.views, self.send_sem, self.receive_sem = views, send_sem, receive_sem
        self.size = lax.axis_size("seq")
        self.spot = lax.axis_index("seq")
        core, column, line = self.where = plane_place(self.spot)
        self.rows = self.size // 4
        self.beside = plane_index(core, 1 - column, line)
        self.sibling = plane_index(1 - core, column, line)
        lines = [lax.rem(line + step, self.rows) for step in range(1, self.rows)]
        self.across = [plane_index(core, column, at) for at in lines]
        self.corners = [plane_index(core, 1 - column, at) for at in lines]
        self.started = []

    def send(self, array, half, slot, way, index, target):
        view = self.views[array](half, slot)
        self.started.append(
            push(
                view, view, self.send_sem.at[array, half, way, index], self.receive_sem.at[array, half, slot],
                {"seq": target},
            )
        )

    def wait(self, array, half, slot):
        arrived(self.views[array](half, slot), self.receive_sem.at[array, half, slot], {"seq": slot})

    def own(self, array):
        for half in range(2):
            self.send(array, half, self.spot, 0, 0, self.beside)
            for index, target in enumerate(self.across):
                self.send(array, half, self.spot, 1 + index, 0, target)
            self.send(array, half, self.spot, self.rows, 0, self.sibling)

    def relay_side(self, array):
        self.wait(array, 0, self.beside)
        for index, target in enumerate(self.across):
            self.send(array, 0, self.beside, 1 + index, 1, target)
        for index, source in enumerate(self.across):
            self.wait(array, 1, source)
            self.send(array, 1, source, 0, 1 + index, self.beside)

    def relay_core(self, array):
        self.send(array, 0, self.beside, self.rows, 1, self.sibling)
        self.wait(array, 1, self.beside)
        self.send(array, 1, self.beside, self.rows, 1, self.sibling)
        for index, source in enumerate(self.across):
            self.send(array, 1, source, self.rows, 2 + index, self.sibling)
            self.wait(array, 0, source)
            self.send(array, 0, source, self.rows, 2 + index, self.sibling)
        for index, source in enumerate(self.corners):
            for half in range(2):
                self.wait(array, half, source)
                self.send(array, half, source, self.rows, 1 + self.rows + index, self.sibling)

    def receive_core(self, array):
        core, _, line = self.where
        for step in range(self.rows):
            for side in range(2):
                source = plane_index(1 - core, side, lax.rem(line + step, self.rows))
                for half in range(2):
                    self.wait(array, half, source)

    def finish(self):
        for copy in self.started:
            copy.wait_send()

    @staticmethod
    def scratch(arrays):
        size = lax.axis_size("seq")
        dma = pltpu.SemaphoreType.DMA
        return [dma((arrays, 2, size // 4 + 1, size // 2 + 1)), dma((arrays, 2, size))]


def others(axis):
    size = lax.axis_size(axis)
    place = lax.axis_index(axis)
    return [lax.rem(place + step, size) for step in range(1, size)]


def front_kernel(
    count,
    tile_ref, table_ref, joined_ref, fc_ref, proj_ref, out_ref, bias_ref,
    tiles_out, stream_ref, joined_out, fc_out, proj_out, out_out, bias_out,
    table, column_ids, chosen, picked,
    land, held, inner_sem, outer_sem, receive_sem,
    local_sem, table_sem, tile_send, tile_receive, cross_send, cross_receive, plane_send, plane_receive, bias_send, bias_receive,
):
    lines = lax.axis_size("batch")
    place = lax.axis_index("batch")
    size = lax.axis_size("seq")
    spot = lax.axis_index("seq")
    planes = others("batch")
    peers = others("seq")
    outs = (joined_out, fc_out, proj_out, out_out)
    total_rows, depth = stream_ref.shape
    chunk = total_rows // count
    tokens = tile_ref.shape[1]
    vocab = table_ref.shape[0]
    number = spot * lines + place
    goal = {"seq": lax.rem(number, size), "batch": number // size}
    wanted = place * size + spot
    origin = {"seq": wanted // lines, "batch": lax.rem(wanted, lines)}
    stays = number == wanted

    def view(array):
        out = outs[array]
        if array < 2:
            return lambda half, slot: out.at[slot, pl.ds(half * (lines // 2), lines // 2)]
        return lambda half, slot: out.at[slot, :, pl.ds(half * (depth // 2), depth // 2)]

    plane = PlaneGather([view(array) for array in range(4)], plane_send, plane_receive)
    width = chosen.shape[1]
    cuts = table.shape[0] // width
    table_copies = [
        pltpu.make_async_copy(
            table_ref.at[pl.ds(cut * width, min(width, vocab - cut * width))],
            table.at[pl.ds(cut * width, min(width, vocab - cut * width))],
            table_sem.at[cut],
        )
        for cut in range(cuts)
    ]
    for copy in table_copies:
        copy.start()
    if table.shape[0] > vocab:
        table[vocab:, :] = jnp.zeros((table.shape[0] - vocab, depth), table.dtype)
    locals_ = [
        pltpu.make_async_copy(source, target, local_sem.at[index])
        for index, (source, target) in enumerate(
            (
                (proj_ref, proj_out.at[spot]),
                (joined_ref.at[place], joined_out.at[spot, place]),
                (fc_ref.at[place], fc_out.at[spot, place]),
                (tile_ref, tiles_out.at[place]),
                (bias_ref, bias_out.at[spot]),
            )
        )
    ]
    for copy in locals_:
        copy.start()
    out_copy = pltpu.make_async_copy(out_ref, out_out.at[spot], local_sem.at[5])

    @pl.when(stays)
    def _():
        out_copy.start()

    barrier = pltpu.get_barrier_semaphore()
    for partner in [{"batch": other} for other in planes] + [{"seq": peer} for peer in peers]:
        pl.semaphore_signal(barrier, inc=1, device_id=partner, device_id_type=pl.DeviceIdType.MESH)

    @pl.when(jnp.logical_not(stays))
    def _():
        pl.semaphore_signal(barrier, inc=1, device_id=origin, device_id_type=pl.DeviceIdType.MESH)

    pl.semaphore_wait(barrier, jnp.where(stays, 0, 1) + len(planes) + len(peers))

    tile_copies = [
        push(tile_ref, tiles_out.at[place], tile_send.at[index], tile_receive.at[place], {"batch": other})
        for index, other in enumerate(planes)
    ]
    locals_[0].wait()
    plane.own(2)
    crossing = []
    for array, source, out in ((0, joined_ref, joined_out), (1, fc_ref, fc_out)):
        for index, other in enumerate(planes):
            crossing.append(
                push(source.at[other], out.at[spot, place], cross_send.at[array, index], cross_receive.at[array, place], {"batch": other})
            )
    out_push = pltpu.make_async_remote_copy(
        src_ref=out_ref, dst_ref=out_out.at[goal["seq"]], send_sem=cross_send.at[2, 0],
        recv_sem=cross_receive.at[2, 0], device_id=goal, device_id_type=pl.DeviceIdType.MESH,
    )

    @pl.when(jnp.logical_not(stays))
    def _():
        out_push.start()

    bias_copies = [
        push(bias_ref, bias_out.at[spot], bias_send.at[index], bias_receive.at[spot], {"seq": peer})
        for index, peer in enumerate(peers)
    ]
    for copy in locals_[1:]:
        copy.wait()
    for other in planes:
        arrived(tiles_out.at[other], tile_receive.at[other], {"batch": other})
    for sequence in range(lines):
        turned = jnp.transpose(tiles_out[sequence].astype(jnp.float32))
        column_ids[sequence * tokens : (sequence + 1) * tokens, :] = jnp.broadcast_to(
            turned[:, 0:1] - (place * vocab).astype(jnp.float32), (tokens, LANES)
        )
    half = total_rows // 2
    lane = lax.broadcasted_iota(jnp.int32, (half, LANES), 1)

    def look(part, cut):
        at = slice(part * half, (part + 1) * half)
        if part == 0:
            table_copies[cut].wait()
        for block in range(width // LANES):
            number_ = (lane + (cut * width + block * LANES)).astype(jnp.float32)
            chosen[:, block * LANES : (block + 1) * LANES] = jnp.where(
                column_ids[at, :] == number_, 1.0, 0.0
            ).astype(jnp.bfloat16)
        found = jnp.dot(chosen[...], table[cut * width : (cut + 1) * width, :], preferred_element_type=jnp.float32)
        if cut == 0:
            picked[at, :] = found
        else:
            picked[at, :] += found

    line_sum = LineSum(
        count, chunk, lambda at: picked[at, :],
        land, held, stream_ref, inner_sem, outer_sem, receive_sem,
    )

    def turn(array):
        for other in planes:
            arrived(outs[array].at[spot, other], cross_receive.at[array, other], {"batch": other})
        plane.own(array)

    def turn_out():
        @pl.when(stays)
        def _():
            out_copy.wait()

        @pl.when(jnp.logical_not(stays))
        def _():
            arrived(out_out.at[spot], cross_receive.at[2, 0], origin)

        plane.own(3)

    between = {
        (0, 0): lambda: turn(0),
        (0, 1): lambda: plane.relay_side(2),
        (0, 3): lambda: turn(1),
        (0, 4): lambda: turn_out(),
        (0, 5): lambda: plane.relay_core(2),
        (0, 7): lambda: plane.relay_side(0),
    }
    for part in range(2):
        for cut in range(cuts):
            if (part, cut) in between:
                between.pop((part, cut))()
            look(part, cut)
        for work in [between.pop(key) for key in list(between) if key[0] == part]:
            work()
        line_sum.begin(range(part * count // 2, (part + 1) * count // 2))
    todo = [
        lambda: plane.relay_core(0),
        lambda: None,
        lambda: plane.relay_side(1),
        lambda: plane.relay_side(3),
        lambda: None,
        lambda: None,
        lambda: plane.relay_core(1),
        lambda: plane.relay_core(3),
        lambda: None,
        lambda: plane.receive_core(2),
        lambda: plane.receive_core(0),
        lambda: plane.receive_core(1),
        lambda: plane.receive_core(3),
    ]
    line_sum.run(3, todo)
    for peer in peers:
        arrived(bias_out.at[peer], bias_receive.at[peer], {"seq": peer})
    for copy in crossing + bias_copies + tile_copies:
        copy.wait_send()

    @pl.when(jnp.logical_not(stays))
    def _():
        out_push.wait_send()

    plane.finish()
    line_sum.finish()


def front(tile, table, joined, fc, proj, out, bias):
    size = lax.axis_size("seq")
    lines = lax.axis_size("batch")
    vocab, depth = table.shape
    rows = lines * tile.shape[1]
    count = 16
    vmem = pl.BlockSpec(memory_space=pltpu.VMEM)
    anywhere = pl.BlockSpec(memory_space=pl.ANY)
    dma = pltpu.SemaphoreType.DMA
    bf16 = jnp.bfloat16
    spread = lambda part, kind: jax.ShapeDtypeStruct((size,) + part.shape, kind)
    return pl.pallas_call(
        functools.partial(front_kernel, count),
        in_specs=[vmem, anywhere, anywhere, anywhere, anywhere, anywhere, vmem],
        out_specs=[vmem, vmem, anywhere, anywhere, anywhere, anywhere, vmem],
        out_shape=[
            jax.ShapeDtypeStruct((lines,) + tile.shape, tile.dtype),
            jax.ShapeDtypeStruct((rows, depth), bf16),
            spread(joined, bf16),
            spread(fc, bf16),
            spread(proj, bf16),
            spread(out, bf16),
            spread(bias, jnp.float32),
        ],
        scratch_shapes=[
            pltpu.VMEM((pl.cdiv(vocab, VOCAB_TILE) * VOCAB_TILE, depth), bf16),
            pltpu.VMEM((rows, LANES), jnp.float32),
            pltpu.VMEM((rows // 2, VOCAB_TILE), bf16),
            pltpu.VMEM((rows, depth), jnp.float32),
        ] + LineSum.scratch(count, rows, depth) + [
            dma((6,)),
            dma((pl.cdiv(vocab, VOCAB_TILE),)),
            dma((lines - 1,)),
            dma((lines,)),
            dma((3, lines - 1)),
            dma((3, lines)),
        ] + PlaneGather.scratch(4) + [
            dma((size - 1,)),
            dma((size,)),
        ],
        compiler_params=pltpu.CompilerParams(
            collective_id=1, has_side_effects=True, vmem_limit_bytes=VMEM_BYTES
        ),
        name="front",
    )(tile, table, joined, fc, proj, out, bias)


def row_norm(values):
    average = jnp.mean(values, axis=-1, keepdims=True)
    centered = values - average
    variance = jnp.mean(centered * centered, axis=-1, keepdims=True)
    return centered * lax.rsqrt(variance + norm_eps)


def layer_kernel(
    count, heads,
    stream_ref, joined_ref, fc_ref, proj_ref, out_ref, trans_ref,
    gains_ref, offsets_ref, joined_bias, fc_bias, trans_bias, turns_ref, table_ref,
    states_ref, moved_ref, low_ref, logits_ref,
    first_trans, second_trans, x_attn, x_mlp, spread, gathered, mixed, returned, part,
    land, inner_sem, outer_sem, receive_sem,
    tables, turned, logits, table_sem, logits_sem,
    local_sem, heads_send, heads_receive, rows_send, rows_receive, plane_send, plane_receive,
):
    f32 = jnp.float32
    bf16 = jnp.bfloat16
    lines = lax.axis_size("batch")
    place = lax.axis_index("batch")
    size = lax.axis_size("seq")
    spot = lax.axis_index("seq")
    planes = others("batch")
    peers = others("seq")
    rows, depth = stream_ref.shape
    tokens = rows // lines
    plane_width = joined_ref.shape[1] // 3
    columns = spread.shape[3]
    groups = plane_width // columns
    head_dim = columns // heads
    step_rows = 32

    vocab = table_ref.shape[0]
    cut_rows = tables.shape[1]
    cuts = pl.cdiv(vocab, cut_rows)
    sizes = [min(cut_rows, vocab - cut * cut_rows) for cut in range(cuts)]
    loads = [
        pltpu.make_async_copy(
            table_ref.at[pl.ds(cut * cut_rows, sizes[cut])],
            tables.at[cut % 2, pl.ds(0, sizes[cut])],
            table_sem.at[cut % 2],
        )
        for cut in range(cuts)
    ]
    stores = [
        pltpu.make_async_copy(
            logits.at[cut % 2],
            logits_ref.at[cut * cut_rows // VOCAB_TILE, pl.ds(cut * cut_rows % VOCAB_TILE, cut_rows)],
            logits_sem.at[cut % 2],
        )
        for cut in range(cuts)
    ]
    loads[0].start()
    loads[1].start()

    def probe_logits(cut):
        loads[cut].wait()
        if cut >= 2:
            stores[cut - 2].wait()
        logits[cut % 2] = jnp.dot(tables[cut % 2], turned[...], preferred_element_type=f32)
        stores[cut].start()
        if cut + 2 < cuts:
            loads[cut + 2].start()

    spans = (first_trans, second_trans)
    for probe in range(2):
        spans[probe][spot] = trans_ref[probe].astype(bf16)
    greet([{"batch": plane} for plane in planes] + [{"seq": peer} for peer in peers])
    sent = []

    def view(array):
        return lambda half, slot: spans[array].at[slot, :, pl.ds(half * (depth // 2), depth // 2)]

    plane = PlaneGather([view(0), view(1)], plane_send, plane_receive)

    def norms(index, carry):
        at = pl.ds(pl.multiple_of(index * step_rows, step_rows), step_rows)
        unit = row_norm(stream_ref[at, :].astype(f32))
        x_attn[at, :] = (unit * gains_ref[0:1, :] + offsets_ref[0:1, :]).astype(bf16)
        x_mlp[at, :] = (unit * gains_ref[1:2, :] + offsets_ref[1:2, :]).astype(bf16)
        return carry

    lax.fori_loop(0, rows // step_rows, norms, 0, unroll=4)
    half_rot = ROT // 2
    for sequence in range(lines):
        at = slice(sequence * tokens, (sequence + 1) * tokens)
        for kind in range(3):
            place_ = slice(kind * plane_width, (kind + 1) * plane_width)
            value = jnp.dot(x_attn[at, :], joined_ref[:, place_], preferred_element_type=f32)
            value = value + joined_bias[0:1, place_]
            if kind < 2:
                value = (
                    value * turns_ref[0]
                    + pltpu.roll(value, plane_width - half_rot, 1) * turns_ref[1]
                    + pltpu.roll(value, half_rot, 1) * turns_ref[2]
                )
            value = value.astype(bf16)
            for group in range(groups):
                spread[sequence * groups + group, kind] = value[:, group * columns : (group + 1) * columns]
    for index, peer in enumerate(peers):
        sent.append(
            push(spread.at[peer], gathered.at[spot], heads_send.at[index], heads_receive.at[spot], {"seq": peer})
        )
    heads_copy = pltpu.make_async_copy(spread.at[spot], gathered.at[spot], local_sem.at[0])
    heads_copy.start()
    plane.own(0)
    plane.own(1)

    def hidden_part(index, carry):
        at = pl.ds(pl.multiple_of(index * tokens, tokens), tokens)
        value = jnp.dot(x_mlp[at, :], fc_ref[...], preferred_element_type=f32) + fc_bias[...]
        value = 0.5 * value * (1.0 + lax.erf(value * (0.5 ** 0.5)))
        part[at, :] = jnp.dot(value.astype(bf16), proj_ref[...], preferred_element_type=f32)
        return carry

    lax.fori_loop(0, lines, hidden_part, 0)

    def translate(probe, stream, low, weights, at):
        moved = stream + jnp.dot(low, weights, preferred_element_type=f32) + trans_bias[probe : probe + 1, :]
        moved_ref[probe, at, :] = moved
        states_ref[1 + probe, at, :] = (
            row_norm(moved) * gains_ref[2:3, :] + offsets_ref[4:5, :]
        ).astype(bf16)

    def first_probe(sequence):
        at = slice(sequence * tokens, (sequence + 1) * tokens)
        low = stream_ref[at, :]
        translate(0, low.astype(f32), low, first_trans[...].reshape(depth, depth), at)

    plane.relay_side(0)
    plane.relay_core(0)
    heads_copy.wait()
    for peer in peers:
        arrived(gathered.at[peer], heads_receive.at[peer], {"seq": peer})
    length = size * tokens
    block = 2 * tokens
    lane = lax.broadcasted_iota(jnp.int32, (block, columns), 1) // head_dim
    keys = jnp.concatenate([gathered[source, 1] for source in range(size)], axis=0)
    values = jnp.concatenate([gathered[source, 2] for source in range(size)], axis=0)
    for first in range(0, length, block):
        end = first + block
        queries = jnp.concatenate([gathered[first // tokens, 0], gathered[first // tokens + 1, 0]], axis=0)
        allowed = lax.broadcasted_iota(jnp.int32, (block, end), 1) <= (
            lax.broadcasted_iota(jnp.int32, (block, end), 0) + first
        )
        result = None
        for head in range(heads):
            chosen = jnp.where(lane == head, queries, jnp.zeros((), bf16))
            scores = lax.dot_general(
                chosen, keys[:end], (((1,), (1,)), ((), ())), preferred_element_type=f32
            ) * head_dim ** (-0.5)
            scores = jnp.where(allowed, scores, NEGATIVE)
            exponent = jnp.exp(scores - jnp.max(scores, axis=-1, keepdims=True))
            value = jnp.dot(
                exponent.astype(bf16), values[:end], preferred_element_type=f32
            ) / jnp.sum(exponent, axis=-1, keepdims=True)
            result = value if result is None else jnp.where(lane == head, value, result)
        result = result.astype(bf16)
        for index in range(2):
            mixed[first // tokens + index] = result[index * tokens : (index + 1) * tokens]
    for index, peer in enumerate(peers):
        sent.append(
            push(mixed.at[peer], returned.at[spot], rows_send.at[index], rows_receive.at[spot], {"seq": peer})
        )
    rows_copy = pltpu.make_async_copy(mixed.at[spot], returned.at[spot], local_sem.at[1])
    rows_copy.start()
    plane.relay_side(1)
    plane.receive_core(0)
    for sequence in range(lines):
        first_probe(sequence)
    turned[...] = jnp.transpose(states_ref[1])
    rows_copy.wait()
    for peer in peers:
        arrived(returned.at[peer], rows_receive.at[peer], {"seq": peer})
    for sequence in range(lines):
        at = slice(sequence * tokens, (sequence + 1) * tokens)
        attended = jnp.concatenate(
            [returned[sequence * groups + group] for group in range(groups)], axis=1
        )
        part[at, :] += jnp.dot(attended, out_ref[...], preferred_element_type=f32)
    line_sum = LineSum(
        count, rows // count, lambda at: part[at, :],
        land, x_attn, x_mlp, inner_sem, outer_sem, receive_sem,
    )
    line_sum.begin(range(count))
    todo = [functools.partial(probe_logits, cut) for cut in range(cuts)]
    todo[3:3] = [lambda: plane.relay_core(1)]
    todo[7:7] = [lambda: plane.receive_core(1)]
    line_sum.run(3, todo)

    def second_probe(index, carry):
        at = pl.ds(pl.multiple_of(index * tokens, tokens), tokens)
        stream = (
            stream_ref[at, :].astype(f32) + x_mlp[at, :].astype(f32) + offsets_ref[2:3, :] + offsets_ref[3:4, :]
        )
        states_ref[0, at, :] = (row_norm(stream) * gains_ref[2:3, :] + offsets_ref[4:5, :]).astype(bf16)
        low = stream.astype(bf16)
        low_ref[at, :] = low
        translate(1, stream, low, second_trans[...].reshape(depth, depth), at)
        return carry

    lax.fori_loop(0, lines, second_probe, 0)
    for copy in sent:
        copy.wait_send()
    for copy in stores[-2:]:
        copy.wait()
    plane.finish()
    line_sum.finish()


def layer(stream, joined, fc, proj, out, trans, gains, offsets, joined_bias, fc_bias, trans_bias, turns, table):
    size = lax.axis_size("seq")
    lines = lax.axis_size("batch")
    rows, depth = stream.shape
    tokens = rows // lines
    own_heads = depth // HEAD_DIM // size
    columns = own_heads * HEAD_DIM
    count = 16
    tiles = pl.cdiv(table.shape[0], VOCAB_TILE)
    bf16 = jnp.bfloat16
    f32 = jnp.float32
    vmem = pl.BlockSpec(memory_space=pltpu.VMEM)
    anywhere = pl.BlockSpec(memory_space=pl.ANY)
    dma = pltpu.SemaphoreType.DMA
    return pl.pallas_call(
        functools.partial(layer_kernel, count, own_heads),
        in_specs=[vmem] * 12 + [anywhere],
        out_specs=[vmem] * 3 + [anywhere],
        out_shape=[
            jax.ShapeDtypeStruct((3, rows, depth), bf16),
            jax.ShapeDtypeStruct((2, rows, depth), f32),
            jax.ShapeDtypeStruct((rows, depth), bf16),
            jax.ShapeDtypeStruct((tiles, VOCAB_TILE, rows), f32),
        ],
        scratch_shapes=[
            pltpu.VMEM((size,) + trans.shape[1:], bf16),
            pltpu.VMEM((size,) + trans.shape[1:], bf16),
            pltpu.VMEM((rows, depth), bf16),
            pltpu.VMEM((rows, depth), bf16),
            pltpu.VMEM((size, 3, tokens, columns), bf16),
            pltpu.VMEM((size, 3, tokens, columns), bf16),
            pltpu.VMEM((size, tokens, columns), bf16),
            pltpu.VMEM((size, tokens, columns), bf16),
            pltpu.VMEM((rows, depth), f32),
        ] + LineSum.scratch(count, rows, depth)[:1] + LineSum.scratch(count, rows, depth)[2:] + [
            pltpu.VMEM((2, VOCAB_TILE // 2, depth), bf16),
            pltpu.VMEM((depth, rows), bf16),
            pltpu.VMEM((2, VOCAB_TILE // 2, rows), f32),
            dma((2,)),
            dma((2,)),
            dma((2,)),
            dma((size - 1,)),
            dma((size,)),
            dma((size - 1,)),
            dma((size,)),
        ] + PlaneGather.scratch(2),
        compiler_params=pltpu.CompilerParams(
            collective_id=2, has_side_effects=True, vmem_limit_bytes=VMEM_BYTES
        ),
        name="layer",
    )(stream, joined, fc, proj, out, trans, gains, offsets, joined_bias, fc_bias, trans_bias, turns, table)


def stats_kernel(
    tiles_ref, peaks_ref, sums_ref, cross_ref, scales_ref, note_ref,
    gathered, send_sem, receive_sem,
):
    place = lax.axis_index("batch")
    spot = lax.axis_index("seq")
    size = lax.axis_size("seq")
    planes = others("batch")
    tiles = peaks_ref.shape[0]
    rows = peaks_ref.shape[2]
    lines = gathered.shape[0]
    tokens = rows // lines
    gathered[place, 0:3, :] = peaks_ref[tiles - 1]
    for state in range(3):
        gathered[place, 3 + state : 4 + state, :] = jnp.sum(sums_ref[state], axis=0, keepdims=True)
    for other in range(2):
        gathered[place, 6 + other : 7 + other, :] = jnp.sum(cross_ref[other], axis=0, keepdims=True)
    greet([{"batch": plane} for plane in planes])
    copies = [
        push(gathered.at[place], gathered.at[place], send_sem.at[index], receive_sem.at[place], {"batch": plane})
        for index, plane in enumerate(planes)
    ]
    position = spot * tokens + lax.broadcasted_iota(jnp.int32, (1, tokens), 1)
    weights = jnp.concatenate(
        [
            jnp.where(position < size * tokens - tiles_ref[line, 2:3, :], tiles_ref[line, 1:2, :], 0).astype(jnp.float32)
            for line in range(lines)
        ],
        axis=1,
    )
    for plane in planes:
        arrived(gathered.at[plane], receive_sem.at[plane], {"batch": plane})
    tops = gathered[0, 0:3, :]
    for line in range(1, lines):
        tops = jnp.maximum(tops, gathered[line, 0:3, :])
    sums = jnp.zeros((3, rows), jnp.float32)
    cross = jnp.zeros((2, rows), jnp.float32)
    for line in range(lines):
        fade = jnp.exp(gathered[line, 0:3, :] - tops)
        sums += gathered[line, 3:6, :] * fade
        cross += gathered[line, 6:8, :] * fade[0:1]
    totals = tops + jnp.log(sums)
    diverge = cross / sums[0:1] - totals[0:1] + totals[1:3]
    loss = weights * (diverge[0:1] + diverge[1:2])
    for tile in range(tiles):
        scales_ref[tile] = weights * jnp.exp(peaks_ref[tile] - totals)
    note_ref[...] = jnp.zeros_like(note_ref)
    for line in range(rows // LANES):
        at = slice(line * LANES, (line + 1) * LANES)
        note_ref[1:2, :] += loss[:, at]
        note_ref[2:3, :] += weights[:, at]
    for copy in copies:
        copy.wait_send()


def statistics(tiles, peaks, sums, cross):
    lines = lax.axis_size("batch")
    rows = peaks.shape[2]
    vmem = pl.BlockSpec(memory_space=pltpu.VMEM)
    return pl.pallas_call(
        stats_kernel,
        in_specs=[vmem] * 4,
        out_specs=[vmem] * 2,
        out_shape=[
            jax.ShapeDtypeStruct(peaks.shape, jnp.float32),
            jax.ShapeDtypeStruct((8, LANES), jnp.float32),
        ],
        scratch_shapes=[
            pltpu.VMEM((lines, 8, rows), jnp.float32),
            pltpu.SemaphoreType.DMA((lines - 1,)),
            pltpu.SemaphoreType.DMA((lines,)),
        ],
        compiler_params=pltpu.CompilerParams(collective_id=5, has_side_effects=True),
        name="statistics",
    )(tiles, peaks, sums, cross)


def reduce_kernel(
    count,
    grad_ref, bias_ref, note_ref,
    total_ref, bias_out, note_out,
    mine, sibling_land, side_land, line_land, side_sum, line_part, last_land, own_sum,
    land, held, inner_sem, outer_sem, receive_sem,
    tile_land, tile_line, tile_out,
    local_sem, core_send, core_receive, side_send, side_receive, line_send, line_receive,
    last_send, last_receive, bias_send, bias_receive, plane_send, plane_receive, note_send, note_receive,
):
    size = lax.axis_size("seq")
    spot = lax.axis_index("seq")
    place = lax.axis_index("batch")
    core, column, line = plane_place(spot)
    rows = size // 4
    step_rows = total_ref.shape[0] // count // 2
    beside = {"seq": plane_index(core, 1 - column, line)}
    sibling = {"seq": plane_index(1 - core, column, line)}
    across = [{"seq": plane_index(core, column, lax.rem(line + step, rows))} for step in range(1, rows)]
    peers = others("seq")
    planes = others("batch")
    f32 = jnp.float32
    bf16 = jnp.bfloat16
    chips = [
        (step, index, lax.rem(line + step, rows), side)
        for step in range(rows)
        for index, side in enumerate((1 - column, column))
    ]
    sent = []

    def cut(chunk):
        return pl.ds(chunk * step_rows, step_rows)

    loads = {}
    for chunk in range(count):
        for step, index, at, side in chips:
            copy = pltpu.make_async_copy(
                grad_ref.at[:, plane_index(core, side, at), cut(chunk)], mine.at[chunk, step, index],
                local_sem.at[chunk, step, index],
            )
            copy.start()
            loads[chunk, step, index] = copy
    tile_land[spot] = bias_ref[spot]
    greet([{"batch": plane} for plane in planes] + [{"seq": peer} for peer in peers])
    for chunk in range(count):
        for step, index, at, side in chips:
            sent.append(
                push(
                    grad_ref.at[:, plane_index(1 - core, side, at), cut(chunk)], sibling_land.at[chunk, step, index],
                    core_send.at[chunk, step, index], core_receive.at[chunk, step, index], sibling,
                )
            )
    for index, peer in enumerate(peers):
        sent.append(
            push(bias_ref.at[peer], tile_land.at[spot], bias_send.at[index], bias_receive.at[spot], {"seq": peer})
        )
    line_sum = LineSum(
        count, 2 * step_rows, lambda at: own_sum[at, :],
        land, held, total_ref, inner_sem, outer_sem, receive_sem,
    )

    def pair(chunk):
        for step, index, _, _ in chips:
            loads[chunk, step, index].wait()
            arrived(sibling_land.at[chunk, step, index], core_receive.at[chunk, step, index], sibling)
            mine[chunk, step, index] = (
                mine[chunk, step, index].astype(f32) + sibling_land[chunk, step, index].astype(f32)
            ).astype(bf16)
            if index == 0:
                sent.append(
                    push(
                        mine.at[chunk, step, 0, 0], side_land.at[chunk, step],
                        side_send.at[chunk, step], side_receive.at[chunk, step], beside,
                    )
                )
            if step > 0:
                sent.append(
                    push(
                        mine.at[chunk, step, index, 1], line_land.at[chunk, step - 1, index],
                        line_send.at[chunk, step - 1, index], line_receive.at[chunk, step - 1, index],
                        across[step - 1],
                    )
                )

    def second(chunk):
        begin = chunk * 2 * step_rows
        for step in list(range(1, rows)) + [0]:
            arrived(side_land.at[chunk, step], side_receive.at[chunk, step], beside)
            both = mine[chunk, step, 1, 0].astype(f32) + side_land[chunk, step].astype(f32)
            if step > 0:
                side_sum[chunk, step - 1] = both.astype(bf16)
                sent.append(
                    push(
                        side_sum.at[chunk, step - 1], last_land.at[chunk, step],
                        last_send.at[chunk, step], last_receive.at[chunk, step], across[step - 1],
                    )
                )
            else:
                own_sum[begin : begin + step_rows, :] = both
        for index in range(2):
            both = mine[chunk, 0, index, 1].astype(f32)
            for step in range(1, rows):
                arrived(
                    line_land.at[chunk, step - 1, index], line_receive.at[chunk, step - 1, index], across[-step]
                )
                both += line_land[chunk, step - 1, index].astype(f32)
            if index == 0:
                line_part[chunk] = both.astype(bf16)
                sent.append(
                    push(
                        line_part.at[chunk], last_land.at[chunk, 0],
                        last_send.at[chunk, 0], last_receive.at[chunk, 0], beside,
                    )
                )
            else:
                own_sum[begin + step_rows : begin + 2 * step_rows, :] = both

    def third(chunk):
        begin = chunk * 2 * step_rows
        for step in range(1, rows):
            arrived(last_land.at[chunk, step], last_receive.at[chunk, step], across[-step])
            own_sum[begin : begin + step_rows, :] += last_land[chunk, step].astype(f32)
        arrived(last_land.at[chunk, 0], last_receive.at[chunk, 0], beside)
        own_sum[begin + step_rows : begin + 2 * step_rows, :] += last_land[chunk, 0].astype(f32)
        line_sum.begin([chunk])
        line_sum.gather(chunk)

    def tiles_in_plane():
        for peer in peers:
            arrived(tile_land.at[peer], bias_receive.at[peer], {"seq": peer})
        tile = tile_land[0]
        for source in range(1, size):
            tile += tile_land[source]
        tile_line[place] = tile
        for index, plane in enumerate(planes):
            sent.append(
                push(
                    tile_line.at[place], tile_line.at[place], plane_send.at[index], plane_receive.at[place],
                    {"batch": plane},
                )
            )

    squares = []

    def square(chunk):
        line_sum.spread(chunk)
        for row in range(chunk * 2 * step_rows, (chunk + 1) * 2 * step_rows, 16):
            value = total_ref[row : row + 16, :].astype(f32)
            value = value * value
            for begin in range(0, value.shape[1], LANES):
                block = value[:8, begin : begin + LANES] + value[8:, begin : begin + LANES]
                squares[:] = [block + squares[0]] if squares else [block]

    for time in range(count + 5):
        if time < count:
            pair(time)
        if 0 <= time - 2 < count:
            second(time - 2)
        if 0 <= time - 3 < count:
            third(time - 3)
        if time == count:
            tiles_in_plane()
        if 0 <= time - 5 < count:
            square(time - 5)
    for plane in planes:
        arrived(tile_line.at[plane], plane_receive.at[plane], {"batch": plane})
    tile = tile_line[0]
    for source in range(1, lax.axis_size("batch")):
        tile += tile_line[source]
    bias_out[...] = tile
    head = jnp.sum(squares[0] + tile * tile, axis=0, keepdims=True)
    row8 = lax.broadcasted_iota(jnp.int32, (8, LANES), 0)
    tile_out[...] = jnp.where(row8 == 0, head, note_ref[...])
    note_out[spot] = tile_out[...]
    for index, peer in enumerate(peers):
        sent.append(
            push(tile_out, note_out.at[spot], note_send.at[index], note_receive.at[spot], {"seq": peer})
        )
    for peer in peers:
        arrived(note_out.at[peer], note_receive.at[peer], {"seq": peer})
    for copy in sent:
        copy.wait_send()
    line_sum.finish()


def reduce_gradients(grad, bias, note):
    size = lax.axis_size("seq")
    lines = lax.axis_size("batch")
    _, _, width, depth = grad.shape
    rows = size // 4
    count = 4
    cut = width // count
    bf16 = jnp.bfloat16
    vmem = pl.BlockSpec(memory_space=pltpu.VMEM)
    dma = pltpu.SemaphoreType.DMA
    near = max(rows - 1, 1)
    total, bias_sum, notes = pl.pallas_call(
        functools.partial(reduce_kernel, count),
        in_specs=[pl.BlockSpec(memory_space=pl.ANY), vmem, vmem],
        out_specs=[vmem, vmem, vmem],
        out_shape=[
            jax.ShapeDtypeStruct((2 * width, depth), bf16),
            jax.ShapeDtypeStruct(bias.shape[1:], jnp.float32),
            jax.ShapeDtypeStruct((size,) + note.shape, jnp.float32),
        ],
        scratch_shapes=[
            pltpu.VMEM((count, rows, 2, 2, cut, depth), bf16),
            pltpu.VMEM((count, rows, 2, 2, cut, depth), bf16),
            pltpu.VMEM((count, rows, cut, depth), bf16),
            pltpu.VMEM((count, near, 2, cut, depth), bf16),
            pltpu.VMEM((count, near, cut, depth), bf16),
            pltpu.VMEM((count, cut, depth), bf16),
            pltpu.VMEM((count, rows, cut, depth), bf16),
            pltpu.VMEM((2 * width, depth), jnp.float32),
        ] + LineSum.scratch(count, 2 * width, depth) + [
            pltpu.VMEM((size,) + bias.shape[1:], jnp.float32),
            pltpu.VMEM((lines,) + bias.shape[1:], jnp.float32),
            pltpu.VMEM(note.shape, jnp.float32),
            dma((count, rows, 2)),
            dma((count, rows, 2)),
            dma((count, rows, 2)),
            dma((count, rows)),
            dma((count, rows)),
            dma((count, near, 2)),
            dma((count, near, 2)),
            dma((count, rows)),
            dma((count, rows)),
            dma((size - 1,)),
            dma((size,)),
            dma((lines - 1,)),
            dma((lines,)),
            dma((size - 1,)),
            dma((size,)),
        ],
        compiler_params=pltpu.CompilerParams(
            collective_id=6, has_side_effects=True, vmem_limit_bytes=VMEM_BYTES
        ),
        name="reduce_gradients",
    )(grad, bias, note)
    total = jnp.transpose(total.reshape(count, 2, cut, depth), (1, 0, 2, 3)).reshape(2, width, depth)
    return total, bias_sum, notes


def body(
    token_ids,
    pos_weights,
    pad_lengths,
    embed_in,
    w_qkv,
    w_out,
    w_fc,
    w_proj,
    norm_gains,
    layer_biases,
    wide_bias,
    unembed,
    trans_weight,
    trans_bias,
    mom1_weight,
    mom2_weight,
    mom1_bias,
    mom2_bias,
):
    bf16 = jnp.bfloat16
    f32 = jnp.float32
    tok_rows = token_ids.shape[1]
    width = embed_in.shape[1]
    vocab_rows = unembed.shape[0]
    n_seq = lax.axis_size("seq")
    n_batch = lax.axis_size("batch")
    batch_index = lax.axis_index("batch")
    seq_index = lax.axis_index("seq")
    head_count = width // HEAD_DIM
    plane_heads = head_count // n_batch
    plane_width = plane_heads * HEAD_DIM
    hidden_rows = w_proj.shape[0]

    half_rot = ROT // 2
    local_places = seq_index * tok_rows + jnp.arange(tok_rows, dtype=jnp.int32)
    frequency = 10000.0 ** (-2.0 * jnp.arange(half_rot, dtype=f32) / ROT)
    angles = local_places.astype(f32)[:, None] * frequency[None, :]
    cosine = jnp.cos(angles)
    sine = jnp.sin(angles)
    still = jnp.zeros((tok_rows, HEAD_DIM - ROT), f32)
    blank = jnp.zeros((tok_rows, half_rot), f32)
    turns = jnp.stack(
        [
            jnp.concatenate([cosine, cosine, still + 1.0], axis=1),
            jnp.concatenate([-sine, blank, still], axis=1),
            jnp.concatenate([blank, sine, still], axis=1),
        ]
    )
    turns = jnp.tile(turns, (1, 1, plane_heads))

    def plane_part(vector, parts, size):
        return lax.dynamic_slice_in_dim(vector.reshape(parts, n_batch, size), batch_index, 1, 1).reshape(1, -1)

    joined_bias = plane_part(wide_bias[: 3 * width], 3, plane_width)
    fc_bias = plane_part(wide_bias[3 * width :], n_seq, hidden_rows)
    padding = jnp.broadcast_to(pad_lengths[:, None], (1, tok_rows))
    tile = jnp.concatenate([token_ids, pos_weights, padding, jnp.zeros((5, tok_rows), jnp.int32)], axis=0)
    own_rows = w_qkv.shape[0]
    joined_cut = jnp.transpose(w_qkv.reshape(own_rows, 3, n_batch, plane_width), (2, 0, 1, 3))
    joined_cut = joined_cut.reshape(n_batch, own_rows, 3 * plane_width)
    fc_cut = jnp.transpose(w_fc.reshape(own_rows, n_seq, n_batch, hidden_rows), (2, 0, 1, 3))
    fc_cut = fc_cut.reshape(n_batch, own_rows, n_seq * hidden_rows)
    own_width = trans_bias.shape[1]
    bias_tile = jnp.zeros((8, LANES), f32).at[:2, :own_width].set(trans_bias)
    tiles, stream_low, joined_w, fc_w, proj_w, out_w, bias_all = front(
        tile, embed_in, joined_cut, fc_cut, w_proj, w_out, bias_tile
    )
    bias_full = jnp.transpose(bias_all[:, :2, :own_width], (1, 0, 2)).reshape(2, width)
    states, translated, low1, probe_logits = layer(
        stream_low,
        joined_w.reshape(width, 3 * plane_width),
        fc_w.reshape(width, n_seq * hidden_rows),
        proj_w.reshape(n_seq * hidden_rows, width),
        out_w.reshape(plane_width, width),
        trans_weight,
        norm_gains,
        layer_biases,
        joined_bias,
        fc_bias,
        bias_full,
        turns,
        unembed,
    )
    first, second, peaks, sums_part, cross_part = vocab_forward(states, unembed, probe_logits)
    scales, note = statistics(tiles, peaks, sums_part, cross_part)
    grad, bias_grad = vocab_backward(
        first, second, scales, unembed, translated, stream_low, low1, norm_gains
    )
    bias_grad = jnp.transpose(bias_grad.reshape(2, n_seq, own_width), (1, 0, 2))
    bias_grad = jnp.pad(bias_grad, ((0, 0), (0, 6), (0, LANES - own_width)))
    grad = grad.reshape(2, n_seq, own_width, width)
    grad_sum, bias_sum, notes = reduce_gradients(grad, bias_grad, note)
    sums = jnp.sum(notes, axis=(0, 2))
    loss_sum = sums[1]
    token_count = jnp.round(sums[2])
    grad_norm = jnp.sqrt(sums[0]) / token_count
    factor = jnp.minimum(1.0, clip_max / (grad_norm + 1e-06)) / token_count
    grad_w = grad_sum.astype(f32) * factor
    grad_b = bias_sum[:2, : trans_bias.shape[1]] * factor
    first_w, second_w, new_w = adam_update(trans_weight, grad_w, mom1_weight, mom2_weight)
    first_b, second_b, new_b = adam_update(trans_bias, grad_b, mom1_bias, mom2_bias)
    return (loss_sum, token_count, grad_norm, first_w, second_w, new_w, first_b, second_b, new_b)


def solution(mesh):
    return jax.shard_map(
        body,
        mesh=mesh,
        in_specs=(
            P("batch", "seq"),
            P("batch", "seq"),
            P("batch"),
            P("batch", None),
            P(("seq", "batch"), None),
            P(("seq", "batch"), None),
            P(("seq", "batch"), None),
            P(("seq", "batch"), None),
            P(),
            P(),
            P(),
            P("batch", None),
            P(None, "seq", None),
            P(None, "seq"),
            P(None, "seq", None),
            P(None, "seq", None),
            P(None, "seq"),
            P(None, "seq"),
        ),
        out_specs=(
            P(),
            P(),
            P(),
            P(None, "seq", None),
            P(None, "seq", None),
            P(None, "seq", None),
            P(None, "seq"),
            P(None, "seq"),
            P(None, "seq"),
        ),
        check_vma=False,
    )
```

```python
import functools
import math

import jax
import jax.numpy as jnp
from jax import lax
from jax.experimental import pallas as pl
from jax.experimental.pallas import tpu as pltpu
from jax.sharding import PartitionSpec as P

HEAD_DIM = 64
ROT = 16
STEP = 10


VOCAB_TILE = 1280
LANES = 128
NEGATIVE = -1e30
VMEM_BYTES = 62 * 1024 * 1024
norm_eps = 1e-05
clip_max = 0.001
beta_one = 0.9
beta_two = 0.999
learn_rate = 0.03
decay_rate = 0.01
adam_eps = 1e-08


def norm_back(values, upstream, gain_row):
    average = jnp.mean(values, axis=-1, keepdims=True)
    centered = values - average
    variance = jnp.mean(centered * centered, axis=-1, keepdims=True)
    inverse = lax.rsqrt(variance + norm_eps)
    unit = centered * inverse
    scaled = upstream * gain_row
    return (
        scaled
        - jnp.mean(scaled, axis=-1, keepdims=True)
        - unit * jnp.mean(scaled * unit, axis=-1, keepdims=True)
    ) * inverse


def adam_update(weight, gradient, earlier, later):
    earlier = beta_one * earlier + (1.0 - beta_one) * gradient
    later = beta_two * later + (1.0 - beta_two) * gradient * gradient
    update = (
        earlier / (1.0 - beta_one**STEP) / (jnp.sqrt(later / (1.0 - beta_two**STEP)) + adam_eps)
    )
    return (earlier, later, weight * (1.0 - learn_rate * decay_rate) - learn_rate * update)


def forward_kernel(vocab, states_ref, table_ref, probe0_ref, probe1_ref, first_ref, second_ref, peaks_ref, sums_ref, cross_ref, turned, left, right, peak):
    step = pl.program_id(0)
    steps = pl.num_programs(0) - 1
    width = table_ref.shape[0]
    half = left.shape[1] // 2
    group = 16
    given = (probe0_ref, probe1_ref)
    last = vocab - (pl.cdiv(vocab, width) - 1) * width
    row = lax.broadcasted_iota(jnp.int32, (group, LANES), 0)

    def reset(part):
        span = slice(part * half, (part + 1) * half)
        peak[:, span] = jnp.full((8, half), NEGATIVE, jnp.float32)
        sums_ref[:, :, span] = jnp.zeros((3, 8, half), jnp.float32)
        cross_ref[:, :, span] = jnp.zeros((2, 8, half), jnp.float32)

    @pl.when(step == 0)
    def _():
        reset(0)
        for state in range(2):
            for part in range(2):
                turned[part, :, state * half : (state + 1) * half] = jnp.transpose(
                    states_ref[2 * state, part * half : (part + 1) * half, :]
                )

    @pl.when(step <= 1)
    def _():
        reset(1)

    def multiply(part, target, state, cut):
        place = slice(state * half, (state + 1) * half)
        at = slice(cut * width // 5, (cut + 1) * width // 5)
        target[at, place] = jnp.dot(
            table_ref[at, :], turned[part, :, place], preferred_element_type=jnp.float32
        )

    def units(part, source, target, tile):
        limit = vocab - tile * width
        blocks = width // group
        result = []
        for lanes in range(half // LANES):
            span = slice(part * half + lanes * LANES, part * half + (lanes + 1) * LANES)
            local = slice(lanes * LANES, (lanes + 1) * LANES)
            held = {}

            def logits(state, block, lanes=lanes):
                at = slice(block * group, (block + 1) * group)
                if state == 1:
                    value = given[part][0, at, lanes * LANES : (lanes + 1) * LANES]
                else:
                    begin = state // 2 * half + lanes * LANES
                    value = source[at, begin : begin + LANES]
                if (block + 1) * group > last:
                    value = jnp.where(row + block * group < limit, value, NEGATIVE)
                return value

            def tops(span=span, held=held, logits=logits):
                held["top"], held["sum"], held["cross"] = [], [], []
                for state in range(3):
                    top = logits(state, 0)
                    for block in range(1, blocks):
                        top = jnp.maximum(top, logits(state, block))
                    before = peak[state : state + 1, span]
                    now = jnp.maximum(before, jnp.max(top, axis=0, keepdims=True))
                    peak[state : state + 1, span] = now
                    peaks_ref[pl.ds(tile, 1), state, span] = now
                    fade = jnp.exp(before - now)
                    held["top"].append(jnp.broadcast_to(now, (group, LANES)))
                    held["sum"].append(sums_ref[state, :, span] * fade)
                    if state == 0:
                        held["cross"] = [cross_ref[other, :, span] * fade for other in range(2)]

            def fold(value):
                return value[:8] + value[8:]

            def powers(begin, end, held=held, logits=logits, local=local, fold=fold):
                for block in range(begin, end):
                    place = slice(block * group, (block + 1) * group)
                    base = logits(0, block)
                    base_exp = jnp.exp(base - held["top"][0])
                    held["sum"][0] += fold(base_exp)
                    target[0, 0, place, local] = base_exp.astype(jnp.bfloat16)
                    for state in range(1, 3):
                        value = logits(state, block)
                        value_exp = jnp.exp(value - held["top"][state])
                        held["sum"][state] += fold(value_exp)
                        target[0, state, place, local] = value_exp.astype(jnp.bfloat16)
                        held["cross"][state - 1] += fold(base_exp * (base - value))

            def finish(span=span, held=held):
                for state in range(3):
                    sums_ref[state, :, span] = held["sum"][state]
                for other in range(2):
                    cross_ref[other, :, span] = held["cross"][other]

            result.append(tops)
            cuts = 10
            for cut in range(cuts):
                result.append(
                    functools.partial(powers, cut * blocks // cuts, (cut + 1) * blocks // cuts)
                )
            result.append(finish)
        return result

    def stage(part, target, work):
        done = 0
        for piece in range(10):
            multiply(part, target, piece // 5, piece % 5)
            upto = (piece + 1) * len(work) // 10
            for unit in work[done:upto]:
                unit()
            done = upto

    before = jnp.maximum(step - 1, 0)

    @pl.when(step < steps)
    def _():
        stage(0, left, units(1, right, second_ref, before))
        stage(1, right, units(0, left, first_ref, step))

    @pl.when(step == steps)
    def _():
        for unit in units(1, right, second_ref, before):
            unit()


def vocab_forward(states, table, given):
    _, rows, depth = states.shape
    vocab = table.shape[0]
    tiles = pl.cdiv(vocab, VOCAB_TILE)
    half = rows // 2
    kept = jax.ShapeDtypeStruct((tiles, 3, VOCAB_TILE, half), jnp.bfloat16)
    block = (1, 3, VOCAB_TILE, half)
    whole = lambda *shape: pl.BlockSpec(shape, lambda i: (0,) * len(shape))
    return pl.pallas_call(
        functools.partial(forward_kernel, vocab),
        grid=(tiles + 1,),
        in_specs=[
            whole(3, rows, depth),
            pl.BlockSpec((VOCAB_TILE, depth), lambda i: (jnp.minimum(i, tiles - 1), 0)),
            pl.BlockSpec((1, VOCAB_TILE, half), lambda i: (jnp.minimum(i, tiles - 1), 0, 0)),
            pl.BlockSpec((1, VOCAB_TILE, half), lambda i: (jnp.maximum(i - 1, 0), 0, 1)),
        ],
        out_specs=[
            pl.BlockSpec(block, lambda i: (jnp.minimum(i, tiles - 1), 0, 0, 0)),
            pl.BlockSpec(block, lambda i: (jnp.maximum(i - 1, 0), 0, 0, 0)),
            whole(tiles, 3, rows),
            whole(3, 8, rows),
            whole(2, 8, rows),
        ],
        out_shape=[
            kept,
            kept,
            jax.ShapeDtypeStruct((tiles, 3, rows), jnp.float32),
            jax.ShapeDtypeStruct((3, 8, rows), jnp.float32),
            jax.ShapeDtypeStruct((2, 8, rows), jnp.float32),
        ],
        scratch_shapes=[
            pltpu.VMEM((2, depth, 2 * half), jnp.bfloat16),
            pltpu.VMEM((VOCAB_TILE, 2 * half), jnp.float32),
            pltpu.VMEM((VOCAB_TILE, 2 * half), jnp.float32),
            pltpu.VMEM((8, rows), jnp.float32),
        ],
        compiler_params=pltpu.CompilerParams(vmem_limit_bytes=VMEM_BYTES),
        cost_estimate=pl.CostEstimate(
            flops=4 * rows * depth * vocab,
            bytes_accessed=2 * vocab * (depth + 5 * rows),
            transcendentals=3 * rows * vocab,
        ),
        name="vocab_forward",
    )(states, table, given, given)


def backward_kernel(
    vocab, first_ref, second_ref, scales_ref, table_ref, moved_ref, low0_ref, low1_ref, gain_ref,
    grad_ref, bias_ref, out_ref, left, right, tail, delta, turned,
):
    step = pl.program_id(0)
    tiles = pl.num_programs(0) - 1
    width, depth = table_ref.shape
    half = first_ref.shape[3]
    piece = 256
    last = vocab - (pl.cdiv(vocab, width) - 1) * width
    whole = last // piece * piece
    tile = jnp.maximum(step - 1, 0)
    limit = vocab - tile * width

    def units(part, source, target, index):
        result = []

        def turn(lanes, block):
            begin = part * half + lanes * LANES
            span = slice(begin, begin + LANES)
            place = slice(block * LANES, (block + 1) * LANES)
            local = slice(lanes * LANES, (lanes + 1) * LANES)
            factors = scales_ref[pl.ds(index, 1), :, span][0]
            base = source[0, 0, place, local].astype(jnp.float32) * factors[0:1]
            for state in range(1, 3):
                value = source[0, state, place, local].astype(jnp.float32) * factors[state : state + 1]
                first = (state - 1) * half + lanes * LANES
                target[first : first + LANES, place] = jnp.transpose(
                    (value - base).astype(jnp.bfloat16)
                )

        for lanes in range(half // LANES):
            for block in range(width // LANES):
                result.append(functools.partial(turn, lanes, block))
        return result

    def multiply(part, source, start):
        place = slice(start, start + piece)
        span = slice(part * half, (part + 1) * half)
        partial = jnp.dot(source[:, whole:], tail[:, place], preferred_element_type=jnp.float32)
        if whole > 0:
            partial += jnp.dot(
                source[:, :whole], table_ref[:whole, place], preferred_element_type=jnp.float32
            )
        for probe in range(2):
            out_ref[probe, span, place] += partial[probe * half : (probe + 1) * half]

    def stage(part, source, work):
        done = 0
        pieces = depth // piece
        for index in range(pieces):
            multiply(part, source, index * piece)
            upto = (index + 1) * len(work) // pieces
            for unit in work[done:upto]:
                unit()
            done = upto

    ahead = jnp.minimum(step, tiles - 1)

    @pl.when(step == 0)
    def _():
        out_ref[...] = jnp.zeros_like(out_ref)
        for unit in units(0, first_ref, left, ahead):
            unit()

    @pl.when(step > 0)
    def _():
        below = lax.broadcasted_iota(jnp.int32, (width - whole, depth), 0) + whole < limit
        tail[...] = jnp.where(below, table_ref[whole:, :], jnp.zeros((), tail.dtype))
        stage(0, left, units(1, second_ref, right, tile))
        stage(1, right, units(0, first_ref, left, ahead))

    @pl.when(step == tiles)
    def _():
        rows = out_ref.shape[1]
        chunk = 32
        block = 256
        for probe in range(2):
            low_ref = (low0_ref, low1_ref)[probe]

            def back(index, total, probe=probe):
                at = pl.ds(pl.multiple_of(index * chunk, chunk), chunk)
                value = norm_back(moved_ref[probe, at, :], out_ref[probe, at, :], gain_ref[2:3, :])
                delta[at, :] = value.astype(jnp.bfloat16)
                return total + jnp.sum(value, axis=0, keepdims=True)

            bias_ref[probe : probe + 1, :] = lax.fori_loop(
                0, rows // chunk, back, jnp.zeros((1, depth), jnp.float32), unroll=4
            )
            turned[...] = jnp.transpose(low_ref[...])
            for begin in range(0, depth, block):
                grad_ref[probe, begin : begin + block, :] = jnp.dot(
                    turned[begin : begin + block, :], delta[...], preferred_element_type=jnp.float32
                ).astype(jnp.bfloat16)


def vocab_backward(first, second, scales, table, moved, low0, low1, gains):
    tiles, _, _, half = first.shape
    vocab, depth = table.shape
    rows = 2 * half
    last = vocab - (tiles - 1) * VOCAB_TILE
    block = (1, 3, VOCAB_TILE, half)
    whole = lambda *shape: pl.BlockSpec(shape, lambda i: (0,) * len(shape))
    return pl.pallas_call(
        functools.partial(backward_kernel, vocab),
        grid=(tiles + 1,),
        in_specs=[
            pl.BlockSpec(block, lambda i: (jnp.minimum(i, tiles - 1), 0, 0, 0)),
            pl.BlockSpec(block, lambda i: (jnp.maximum(i - 1, 0), 0, 0, 0)),
            whole(tiles, 3, rows),
            pl.BlockSpec((VOCAB_TILE, depth), lambda i: (jnp.maximum(i - 1, 0), 0)),
            whole(2, rows, depth),
            whole(rows, depth),
            whole(rows, depth),
            whole(*gains.shape),
        ],
        out_specs=[whole(2, depth, depth), whole(2, depth)],
        out_shape=[
            jax.ShapeDtypeStruct((2, depth, depth), jnp.bfloat16),
            jax.ShapeDtypeStruct((2, depth), jnp.float32),
        ],
        scratch_shapes=[
            pltpu.VMEM((2, rows, depth), jnp.float32),
            pltpu.VMEM((2 * half, VOCAB_TILE), jnp.bfloat16),
            pltpu.VMEM((2 * half, VOCAB_TILE), jnp.bfloat16),
            pltpu.VMEM((VOCAB_TILE - last // 256 * 256, depth), jnp.bfloat16),
            pltpu.VMEM((rows, depth), jnp.bfloat16),
            pltpu.VMEM((depth, rows), jnp.bfloat16),
        ],
        compiler_params=pltpu.CompilerParams(vmem_limit_bytes=VMEM_BYTES),
        cost_estimate=pl.CostEstimate(
            flops=4 * rows * depth * (vocab + depth),
            bytes_accessed=2 * vocab * (depth + 3 * rows),
            transcendentals=0,
        ),
        name="vocab_backward",
    )(first, second, scales, table, moved, low0, low1, gains)


def plane_place(place):
    core = lax.rem(place, 2)
    return core, lax.rem(place // 2, 2), place // 4


def plane_index(core, column, line):
    return (line * 2 + column) * 2 + core


def greet(partners):
    barrier = pltpu.get_barrier_semaphore()
    for partner in partners:
        pl.semaphore_signal(barrier, inc=1, device_id=partner, device_id_type=pl.DeviceIdType.MESH)
    pl.semaphore_wait(barrier, len(partners))


def push(source, target, send, receive, partner):
    copy = pltpu.make_async_remote_copy(
        src_ref=source,
        dst_ref=target,
        send_sem=send,
        recv_sem=receive,
        device_id=partner,
        device_id_type=pl.DeviceIdType.MESH,
    )
    copy.start()
    return copy


def arrived(target, receive, partner):
    pltpu.make_async_remote_copy(
        src_ref=target,
        dst_ref=target,
        send_sem=receive,
        recv_sem=receive,
        device_id=partner,
        device_id_type=pl.DeviceIdType.MESH,
    ).wait_recv()


def departed(source, send, partner):
    pltpu.make_async_remote_copy(
        src_ref=source,
        dst_ref=source,
        send_sem=send,
        recv_sem=send,
        device_id=partner,
        device_id_type=pl.DeviceIdType.MESH,
    ).wait_send()


class LineSum:
    def __init__(self, count, halves, own, land, held, total, inner_sem, outer_sem, receive_sem):
        lines = lax.axis_size("batch")
        rows, depth = held.shape
        self.blocks = count // halves
        place = lax.axis_index("batch")
        near = place < lines // 2
        self.count, self.size, self.columns = count, rows // self.blocks, depth // halves
        self.own, self.land, self.held, self.total = own, land, held, total
        self.inner_sem, self.outer_sem, self.receive_sem = inner_sem, outer_sem, receive_sem
        self.middle = (place == lines // 2 - 1) | (place == lines // 2)
        self.end = (place == 0) | (place == lines - 1)
        self.inner = {"batch": jnp.where(near, place + 1, place - 1)}
        self.outer = {"batch": jnp.where(near, place - 1, place + 1)}
        self.slot = jnp.where(self.middle, 1, 0)

    def rows(self, index):
        return (
            pl.ds(index % self.blocks * self.size, self.size),
            pl.ds(index // self.blocks * self.columns, self.columns),
        )

    def send_in(self, index):
        rows = self.rows(index)
        push(
            self.held.at[*rows],
            self.land.at[self.slot, *rows],
            self.inner_sem.at[index],
            self.receive_sem.at[self.slot, index],
            self.inner,
        )

    def begin(self, indices):
        @pl.when(self.end)
        def _():
            for index in indices:
                rows = self.rows(index)
                self.held[rows] = self.own(rows).astype(jnp.bfloat16)
                self.send_in(index)

    def gather(self, index):
        rows = self.rows(index)

        @pl.when(jnp.logical_not(self.end))
        def _():
            arrived(self.land.at[0, *rows], self.receive_sem.at[0, index], self.outer)
            own = self.own(rows).astype(jnp.float32)
            self.held[rows] = (own + self.land[(0, *rows)].astype(jnp.float32)).astype(jnp.bfloat16)
            self.send_in(index)

    def spread(self, index):
        rows = self.rows(index)

        @pl.when(self.middle)
        def _():
            arrived(self.land.at[1, *rows], self.receive_sem.at[1, index], self.inner)
            both = self.held[rows].astype(jnp.float32) + self.land[(1, *rows)].astype(jnp.float32)
            self.total[rows] = both.astype(jnp.bfloat16)

        @pl.when(jnp.logical_not(self.middle))
        def _():
            arrived(self.total.at[*rows], self.receive_sem.at[2, index], self.inner)

        @pl.when(jnp.logical_not(self.end))
        def _():
            push(
                self.total.at[*rows],
                self.total.at[*rows],
                self.outer_sem.at[index],
                self.receive_sem.at[2, index],
                self.outer,
            )

    def run(self, lag, todo=()):
        todo = list(todo)
        for index in range(self.count + lag):
            if index < self.count:
                self.gather(index)
            if index >= lag:
                self.spread(index - lag)
            if todo:
                todo.pop(0)()
        for work in todo:
            work()

    def finish(self):
        for index in range(self.count):
            rows = self.rows(index)
            departed(self.held.at[*rows], self.inner_sem.at[index], self.inner)

            @pl.when(jnp.logical_not(self.end))
            def _(rows=rows, index=index):
                departed(self.total.at[*rows], self.outer_sem.at[index], self.outer)

    @staticmethod
    def scratch(count, rows, depth):
        return [
            pltpu.VMEM((2, rows, depth), jnp.bfloat16),
            pltpu.VMEM((rows, depth), jnp.bfloat16),
            pltpu.SemaphoreType.DMA((count,)),
            pltpu.SemaphoreType.DMA((count,)),
            pltpu.SemaphoreType.DMA((3, count)),
        ]


class PlaneGather:
    def __init__(self, views, send_sem, receive_sem):
        self.views, self.send_sem, self.receive_sem = views, send_sem, receive_sem
        self.size = lax.axis_size("seq")
        self.spot = lax.axis_index("seq")
        core, column, line = self.where = plane_place(self.spot)
        self.rows = self.size // 4
        self.beside = plane_index(core, 1 - column, line)
        self.sibling = plane_index(1 - core, column, line)
        lines = [lax.rem(line + step, self.rows) for step in range(1, self.rows)]
        self.across = [plane_index(core, column, at) for at in lines]
        self.corners = [plane_index(core, 1 - column, at) for at in lines]
        self.started = []

    def send(self, array, half, slot, way, index, target):
        view = self.views[array](half, slot)
        self.started.append(
            push(
                view, view, self.send_sem.at[array, half, way, index], self.receive_sem.at[array, half, slot],
                {"seq": target},
            )
        )

    def wait(self, array, half, slot):
        arrived(self.views[array](half, slot), self.receive_sem.at[array, half, slot], {"seq": slot})

    def own(self, array):
        for half in range(2):
            self.send(array, half, self.spot, 0, 0, self.beside)
            for index, target in enumerate(self.across):
                self.send(array, half, self.spot, 1 + index, 0, target)
            self.send(array, half, self.spot, self.rows, 0, self.sibling)

    def relay_side(self, array):
        self.wait(array, 0, self.beside)
        for index, target in enumerate(self.across):
            self.send(array, 0, self.beside, 1 + index, 1, target)
        for index, source in enumerate(self.across):
            self.wait(array, 1, source)
            self.send(array, 1, source, 0, 1 + index, self.beside)

    def relay_core(self, array):
        self.send(array, 0, self.beside, self.rows, 1, self.sibling)
        self.wait(array, 1, self.beside)
        self.send(array, 1, self.beside, self.rows, 1, self.sibling)
        for index, source in enumerate(self.across):
            self.send(array, 1, source, self.rows, 2 + index, self.sibling)
            self.wait(array, 0, source)
            self.send(array, 0, source, self.rows, 2 + index, self.sibling)
        for index, source in enumerate(self.corners):
            for half in range(2):
                self.wait(array, half, source)
                self.send(array, half, source, self.rows, 1 + self.rows + index, self.sibling)

    def receive_core(self, array):
        core, _, line = self.where
        for step in range(self.rows):
            for side in range(2):
                source = plane_index(1 - core, side, lax.rem(line + step, self.rows))
                for half in range(2):
                    self.wait(array, half, source)

    def finish(self):
        for copy in self.started:
            copy.wait_send()

    @staticmethod
    def scratch(arrays):
        size = lax.axis_size("seq")
        dma = pltpu.SemaphoreType.DMA
        return [dma((arrays, 2, size // 4 + 1, size // 2 + 1)), dma((arrays, 2, size))]


def others(axis):
    size = lax.axis_size(axis)
    place = lax.axis_index(axis)
    return [lax.rem(place + step, size) for step in range(1, size)]


def front_kernel(
    count,
    ids_ref, weights_ref, padding_ref, table_ref, joined_ref, fc_ref, trans_ref, out_ref, trans_bias_ref,
    tiles_out, stream_ref, joined_out, fc_out, trans_out, out_out, bias_out,
    table, column_ids, chosen, picked, tile_ref, bias_ref, trans_low,
    land, held, inner_sem, outer_sem, receive_sem,
    local_sem, table_sem, tile_send, tile_receive, cross_send, cross_receive, plane_send, plane_receive, bias_send, bias_receive,
):
    lines = lax.axis_size("batch")
    place = lax.axis_index("batch")
    size = lax.axis_size("seq")
    spot = lax.axis_index("seq")
    planes = others("batch")
    peers = others("seq")
    outs = (joined_out, fc_out, trans_out, out_out)
    total_rows, depth = stream_ref.shape
    tokens = tile_ref.shape[1]
    plane_width = joined_out.shape[3] // 3
    hidden_rows = fc_out.shape[3] // size
    vocab = table_ref.shape[0]
    number = spot * lines + place
    goal = {"seq": lax.rem(number, size), "batch": number // size}
    wanted = place * size + spot
    origin = {"seq": wanted // lines, "batch": lax.rem(wanted, lines)}
    stays = number == wanted

    def view(array):
        out = outs[array]
        if array < 2:
            return lambda half, slot: out.at[slot, pl.ds(half * (lines // 2), lines // 2)]
        return lambda half, slot: out.at[slot, :, pl.ds(half * (depth // 2), depth // 2)]

    plane = PlaneGather([view(array) for array in range(4)], plane_send, plane_receive)
    width = VOCAB_TILE
    cuts = table.shape[0] // width
    table_copies = [
        pltpu.make_async_copy(
            table_ref.at[pl.ds(cut * width, min(width, vocab - cut * width))],
            table.at[pl.ds(cut * width, min(width, vocab - cut * width))],
            table_sem.at[cut],
        )
        for cut in range(cuts)
    ]
    for copy in table_copies:
        copy.start()
    if table.shape[0] > vocab:
        table[vocab:, :] = jnp.zeros((table.shape[0] - vocab, depth), table.dtype)

    def joined_cuts(goal):
        return [
            (
                joined_ref.at[:, pl.ds(pl.multiple_of(part * depth + goal * plane_width, LANES), plane_width)],
                joined_out.at[spot, place, :, pl.ds(part * plane_width, plane_width)],
            )
            for part in range(3)
        ]

    def fc_cuts(goal):
        if len(fc_ref.shape) == 3:
            return [(fc_ref.at[goal], fc_out.at[spot, place])]
        return [
            (
                fc_ref.at[:, pl.ds(pl.multiple_of((part * lines + goal) * hidden_rows, LANES), hidden_rows)],
                fc_out.at[spot, place, :, pl.ds(part * hidden_rows, hidden_rows)],
            )
            for part in range(size)
        ]

    trans_low[...] = trans_ref[0].astype(jnp.bfloat16)
    tile_ref[...] = jnp.zeros_like(tile_ref)
    tile_ref[0:1, :] = ids_ref[...]
    tile_ref[1:2, :] = weights_ref[...]
    tile_ref[2:3, :] = jnp.full((1, tokens), padding_ref[0], jnp.int32)
    bias_ref[...] = jnp.zeros_like(bias_ref)
    bias_ref[0:2, 0 : trans_bias_ref.shape[1]] = trans_bias_ref[...]
    locals_ = [
        pltpu.make_async_copy(source, target, local_sem.at[index])
        for index, (source, target) in enumerate(
            [
                (trans_low, trans_out.at[spot]),
                (tile_ref, tiles_out.at[place]),
                (bias_ref, bias_out.at[spot]),
            ]
            + joined_cuts(place)
            + fc_cuts(place)
        )
    ]
    for copy in locals_:
        copy.start()
    out_copy = pltpu.make_async_copy(out_ref, out_out.at[spot], local_sem.at[6 + size])

    @pl.when(stays)
    def _():
        out_copy.start()

    barrier = pltpu.get_barrier_semaphore()
    for partner in [{"batch": other} for other in planes] + [{"seq": peer} for peer in peers]:
        pl.semaphore_signal(barrier, inc=1, device_id=partner, device_id_type=pl.DeviceIdType.MESH)

    @pl.when(jnp.logical_not(stays))
    def _():
        pl.semaphore_signal(barrier, inc=1, device_id=origin, device_id_type=pl.DeviceIdType.MESH)

    pl.semaphore_wait(barrier, jnp.where(stays, 0, 1) + len(planes) + len(peers))

    tile_copies = [
        push(tile_ref, tiles_out.at[place], tile_send.at[index], tile_receive.at[place], {"batch": other})
        for index, other in enumerate(planes)
    ]
    locals_[0].wait()
    plane.own(2)
    for array, cuts_of in ((0, joined_cuts), (1, fc_cuts)):
        for index, other in enumerate(planes):
            for source, target in cuts_of(other):
                push(source, target, cross_send.at[array, index], cross_receive.at[array, place], {"batch": other})
    out_push = pltpu.make_async_remote_copy(
        src_ref=out_ref, dst_ref=out_out.at[goal["seq"]], send_sem=cross_send.at[2, 0],
        recv_sem=cross_receive.at[2, 0], device_id=goal, device_id_type=pl.DeviceIdType.MESH,
    )

    @pl.when(jnp.logical_not(stays))
    def _():
        out_push.start()

    bias_copies = [
        push(bias_ref, bias_out.at[spot], bias_send.at[index], bias_receive.at[spot], {"seq": peer})
        for index, peer in enumerate(peers)
    ]
    for copy in locals_[1:]:
        copy.wait()
    for other in planes:
        arrived(tiles_out.at[other], tile_receive.at[other], {"batch": other})
    for sequence in range(lines):
        turned = jnp.transpose(tiles_out[sequence].astype(jnp.float32))
        column_ids[sequence * tokens : (sequence + 1) * tokens, :] = jnp.broadcast_to(
            turned[:, 0:1] - (place * vocab).astype(jnp.float32), (tokens, LANES)
        )
    lane = lax.broadcasted_iota(jnp.int32, (total_rows, LANES), 1)

    def choose(cut):
        for block in range(width // LANES):
            begin = cut * width + block * LANES
            chosen[:, begin : begin + LANES] = jnp.where(
                column_ids[...] == (lane + begin).astype(jnp.float32), 1.0, 0.0
            ).astype(jnp.bfloat16)

    def look(part, cut):
        at = slice(part * (depth // 2), (part + 1) * (depth // 2))
        span = slice(cut * width, (cut + 1) * width)
        if part == 0:
            table_copies[cut].wait()
        found = jnp.dot(chosen[:, span], table[span, at], preferred_element_type=jnp.float32)
        if cut == 0:
            picked[:, at] = found
        else:
            picked[:, at] += found
        if part == 0 and cut + 1 < cuts:
            choose(cut + 1)

    line_sum = LineSum(
        count, 2, lambda at: picked[at],
        land, held, stream_ref, inner_sem, outer_sem, receive_sem,
    )

    def turn(array):
        for other in planes:
            arrived(outs[array].at[spot, other], cross_receive.at[array, other], {"batch": other})
        plane.own(array)

    def turn_out():
        @pl.when(stays)
        def _():
            out_copy.wait()

        @pl.when(jnp.logical_not(stays))
        def _():
            arrived(out_out.at[spot], cross_receive.at[2, 0], origin)

        plane.own(3)

    between = {
        (0, 0): lambda: choose(0),
        (0, 3): lambda: turn(0),
        (0, 4): lambda: turn_out(),
        (0, 5): lambda: plane.relay_side(2),
        (0, 7): lambda: turn(1),
        (0, 9): lambda: plane.relay_core(2),
        (1, 4): lambda: plane.relay_side(0),
        (1, 8): lambda: plane.relay_core(0),
    }
    for part in range(2):
        for cut in range(cuts):
            if (part, cut) in between:
                between.pop((part, cut))()
            look(part, cut)
        for work in [between.pop(key) for key in list(between) if key[0] == part]:
            work()
        line_sum.begin(range(part * count // 2, (part + 1) * count // 2))
    todo = [
        lambda: plane.relay_side(1),
        lambda: plane.relay_side(3),
        lambda: None,
        lambda: None,
        lambda: plane.relay_core(1),
        lambda: plane.relay_core(3),
        lambda: None,
        lambda: plane.receive_core(2),
        lambda: plane.receive_core(0),
        lambda: plane.receive_core(1),
        lambda: plane.receive_core(3),
    ]
    line_sum.run(3, todo)
    for peer in peers:
        arrived(bias_out.at[peer], bias_receive.at[peer], {"seq": peer})
    for copy in bias_copies + tile_copies:
        copy.wait_send()
    for array in range(2):
        for index, other in enumerate(planes):
            departed(outs[array].at[spot, place], cross_send.at[array, index], {"batch": other})

    @pl.when(jnp.logical_not(stays))
    def _():
        out_push.wait_send()

    plane.finish()
    line_sum.finish()


def front(ids, weights, padding, table, joined, fc, trans, out, bias):
    size = lax.axis_size("seq")
    lines = lax.axis_size("batch")
    vocab, depth = table.shape
    tokens = ids.shape[1]
    rows = lines * tokens
    own_rows = joined.shape[0]
    count = 16
    vmem = pl.BlockSpec(memory_space=pltpu.VMEM)
    smem = pl.BlockSpec(memory_space=pltpu.SMEM)
    anywhere = pl.BlockSpec(memory_space=pl.ANY)
    dma = pltpu.SemaphoreType.DMA
    bf16 = jnp.bfloat16
    padded = pl.cdiv(vocab, VOCAB_TILE) * VOCAB_TILE
    hidden = math.prod(fc.shape) // own_rows // lines
    return pl.pallas_call(
        functools.partial(front_kernel, count),
        in_specs=[vmem, vmem, smem, anywhere, anywhere, anywhere, vmem, anywhere, vmem],
        out_specs=[vmem, vmem, anywhere, anywhere, anywhere, anywhere, vmem],
        out_shape=[
            jax.ShapeDtypeStruct((lines, 8, tokens), jnp.int32),
            jax.ShapeDtypeStruct((rows, depth), bf16),
            jax.ShapeDtypeStruct((size, lines, own_rows, 3 * depth // lines), bf16),
            jax.ShapeDtypeStruct((size, lines, own_rows, hidden), bf16),
            jax.ShapeDtypeStruct((size,) + trans.shape[1:], bf16),
            jax.ShapeDtypeStruct((size,) + out.shape, bf16),
            jax.ShapeDtypeStruct((size, 8, LANES), jnp.float32),
        ],
        scratch_shapes=[
            pltpu.VMEM((padded, depth), bf16),
            pltpu.VMEM((rows, LANES), jnp.float32),
            pltpu.VMEM((rows, padded), bf16),
            pltpu.VMEM((rows, depth), jnp.float32),
            pltpu.VMEM((8, tokens), jnp.int32),
            pltpu.VMEM((8, LANES), jnp.float32),
            pltpu.VMEM(trans.shape[1:], bf16),
        ] + LineSum.scratch(count, rows, depth) + [
            dma((7 + size,)),
            dma((padded // VOCAB_TILE,)),
            dma((lines - 1,)),
            dma((lines,)),
            dma((3, lines - 1)),
            dma((3, lines)),
        ] + PlaneGather.scratch(4) + [
            dma((size - 1,)),
            dma((size,)),
        ],
        compiler_params=pltpu.CompilerParams(
            collective_id=1, has_side_effects=True, vmem_limit_bytes=VMEM_BYTES
        ),
        name="front",
    )(ids, weights, padding, table, joined, fc, trans, out, bias)


def row_norm(values):
    average = jnp.mean(values, axis=-1, keepdims=True)
    centered = values - average
    variance = jnp.mean(centered * centered, axis=-1, keepdims=True)
    return centered * lax.rsqrt(variance + norm_eps)


def layer_kernel(
    count, heads,
    stream_ref, joined_ref, fc_ref, proj_ref, out_ref, trans_ref, next_ref,
    gains_ref, offsets_ref, wide_ref, bias_ref, turns_ref, table_ref,
    states_ref, moved_ref, low_ref, logits_ref,
    proj_all, second_trans, trans_bias, fc_bias, hidden, x_attn, x_mlp, spread, gathered, mixed, returned, part,
    land, inner_sem, outer_sem, receive_sem,
    tables, turned, logits, table_sem, logits_sem,
    local_sem, heads_send, heads_receive, rows_send, rows_receive, plane_send, plane_receive,
):
    f32 = jnp.float32
    bf16 = jnp.bfloat16
    lines = lax.axis_size("batch")
    place = lax.axis_index("batch")
    size = lax.axis_size("seq")
    spot = lax.axis_index("seq")
    planes = others("batch")
    peers = others("seq")
    rows, depth = stream_ref.shape
    tokens = rows // lines
    plane_width = joined_ref.shape[1] // 3
    columns = spread.shape[3]
    groups = plane_width // columns
    head_dim = columns // heads
    hidden_rows = proj_ref.shape[0]
    own_width = next_ref.shape[1]
    step_rows = 32
    wide_rows = 2 * tokens
    vocab = table_ref.shape[0]
    cut_rows = tables.shape[1]
    cuts = pl.cdiv(vocab, cut_rows)
    sizes = [min(cut_rows, vocab - cut * cut_rows) for cut in range(cuts)]
    loads = [
        pltpu.make_async_copy(
            table_ref.at[pl.ds(cut * cut_rows, sizes[cut])],
            tables.at[cut % 2, pl.ds(0, sizes[cut])],
            table_sem.at[cut % 2],
        )
        for cut in range(cuts)
    ]
    stores = [
        pltpu.make_async_copy(
            logits.at[cut % 2],
            logits_ref.at[cut * cut_rows // VOCAB_TILE, pl.ds(cut * cut_rows % VOCAB_TILE, cut_rows)],
            logits_sem.at[cut % 2],
        )
        for cut in range(cuts)
    ]
    loads[0].start()
    loads[1].start()

    def probe_logits(cut):
        loads[cut].wait()
        if cut >= 2:
            stores[cut - 2].wait()
        logits[cut % 2] = jnp.dot(tables[cut % 2], turned[...], preferred_element_type=f32)
        stores[cut].start()
        if cut + 2 < cuts:
            loads[cut + 2].start()

    spans = (proj_all, second_trans)
    proj_all[spot] = proj_ref[...]
    second_trans[spot] = next_ref[1].astype(bf16)
    greet([{"batch": plane} for plane in planes] + [{"seq": peer} for peer in peers])
    sent = []

    def view(array):
        return lambda half, slot: spans[array].at[slot, :, pl.ds(half * (depth // 2), depth // 2)]

    plane = PlaneGather([view(0), view(1)], plane_send, plane_receive)

    def norms(index, carry):
        at = pl.ds(pl.multiple_of(index * step_rows, step_rows), step_rows)
        unit = row_norm(stream_ref[at, :].astype(f32))
        x_attn[at, :] = (unit * gains_ref[0:1, :] + offsets_ref[0:1, :]).astype(bf16)
        x_mlp[at, :] = (unit * gains_ref[1:2, :] + offsets_ref[1:2, :]).astype(bf16)
        return carry

    lax.fori_loop(0, rows // step_rows, norms, 0, unroll=4)
    half_rot = ROT // 2
    for kind in range(3):
        bias = wide_ref[0:1, pl.ds(pl.multiple_of(kind * depth + place * plane_width, LANES), plane_width)]
        whole = jnp.dot(
            x_attn[...], joined_ref[:, kind * plane_width : (kind + 1) * plane_width], preferred_element_type=f32
        )
        for sequence in range(lines):
            value = whole[sequence * tokens : (sequence + 1) * tokens] + bias
            if kind < 2:
                value = (
                    value * turns_ref[0]
                    + pltpu.roll(value, plane_width - half_rot, 1) * turns_ref[1]
                    + pltpu.roll(value, half_rot, 1) * turns_ref[2]
                )
            value = value.astype(bf16)
            for group in range(groups):
                spread[sequence * groups + group, kind] = value[:, group * columns : (group + 1) * columns]
    for index, peer in enumerate(peers):
        sent.append(
            push(spread.at[peer], gathered.at[spot], heads_send.at[index], heads_receive.at[spot], {"seq": peer})
        )
    heads_copy = pltpu.make_async_copy(spread.at[spot], gathered.at[spot], local_sem.at[0])
    heads_copy.start()
    plane.own(0)
    plane.own(1)
    for source in range(size):
        at = slice(source * own_width, (source + 1) * own_width)
        trans_bias[:, at] = bias_ref[source, 0:2, 0:own_width]
        at = slice(source * hidden_rows, (source + 1) * hidden_rows)
        if hidden_rows % LANES:
            begin = wide_ref.shape[1] - fc_ref.shape[1]
            fc_bias[:, at] = wide_ref[0:1, begin + source * hidden_rows : begin + (source + 1) * hidden_rows]
        else:
            begin = pl.multiple_of(3 * depth + (source * lines + place) * hidden_rows, LANES)
            fc_bias[:, at] = wide_ref[0:1, pl.ds(begin, hidden_rows)]

    def translate(probe, stream, low, weights, at):
        moved = stream + jnp.dot(low, weights, preferred_element_type=f32) + trans_bias[probe : probe + 1, :]
        moved_ref[probe, at, :] = moved
        states_ref[1 + probe, at, :] = (
            row_norm(moved) * gains_ref[2:3, :] + offsets_ref[4:5, :]
        ).astype(bf16)

    for begin in range(0, rows, wide_rows):
        at = slice(begin, begin + wide_rows)
        low = stream_ref[at, :]
        translate(0, low.astype(f32), low, trans_ref[...], at)
    turned[...] = jnp.transpose(states_ref[1])
    for begin in range(0, fc_ref.shape[1], 256):
        at = slice(begin, begin + 256)
        for row in range(0, rows, 512):
            span = slice(row, row + 512)
            value = jnp.dot(x_mlp[span, :], fc_ref[:, at], preferred_element_type=f32) + fc_bias[:, at]
            hidden[span, at] = (0.5 * value * (1.0 + lax.erf(value * (0.5 ** 0.5)))).astype(bf16)
    heads_copy.wait()
    for peer in peers:
        arrived(gathered.at[peer], heads_receive.at[peer], {"seq": peer})
    length = size * tokens
    block = 2 * tokens
    lane = lax.broadcasted_iota(jnp.int32, (block, columns), 1) // head_dim
    keys = jnp.concatenate([gathered[source, 1] for source in range(size)], axis=0)
    values = jnp.concatenate([gathered[source, 2] for source in range(size)], axis=0)
    for first in range(0, length, block):
        end = first + block
        queries = jnp.concatenate([gathered[first // tokens, 0], gathered[first // tokens + 1, 0]], axis=0)
        allowed = lax.broadcasted_iota(jnp.int32, (block, end), 1) <= (
            lax.broadcasted_iota(jnp.int32, (block, end), 0) + first
        )
        result = None
        for head in range(heads):
            chosen = jnp.where(lane == head, queries, jnp.zeros((), bf16))
            scores = lax.dot_general(
                chosen, keys[:end], (((1,), (1,)), ((), ())), preferred_element_type=f32
            ) * head_dim ** (-0.5)
            scores = jnp.where(allowed, scores, NEGATIVE)
            exponent = jnp.exp(scores - jnp.max(scores, axis=-1, keepdims=True))
            value = jnp.dot(
                exponent.astype(bf16), values[:end], preferred_element_type=f32
            ) / jnp.sum(exponent, axis=-1, keepdims=True)
            result = value if result is None else jnp.where(lane == head, value, result)
        result = result.astype(bf16)
        for index in range(2):
            mixed[first // tokens + index] = result[index * tokens : (index + 1) * tokens]
    for index, peer in enumerate(peers):
        sent.append(
            push(mixed.at[peer], returned.at[spot], rows_send.at[index], rows_receive.at[spot], {"seq": peer})
        )
    rows_copy = pltpu.make_async_copy(mixed.at[spot], returned.at[spot], local_sem.at[1])
    rows_copy.start()
    plane.relay_side(0)
    plane.relay_side(1)
    probe_logits(0)
    probe_logits(1)
    plane.relay_core(0)
    probe_logits(2)
    plane.receive_core(0)
    for begin in range(0, depth, 256):
        at = slice(begin, begin + 256)
        part[:, at] = jnp.dot(
            hidden[...], proj_all[:, :, at].reshape(size * hidden_rows, 256), preferred_element_type=f32
        )
    rows_copy.wait()
    for peer in peers:
        arrived(returned.at[peer], rows_receive.at[peer], {"seq": peer})
    for sequence in range(lines):
        at = slice(sequence * tokens, (sequence + 1) * tokens)
        attended = jnp.concatenate(
            [returned[sequence * groups + group] for group in range(groups)], axis=1
        )
        part[at, :] += jnp.dot(attended, out_ref[...], preferred_element_type=f32)
    line_sum = LineSum(
        count, 1, lambda at: part[at],
        land, x_attn, x_mlp, inner_sem, outer_sem, receive_sem,
    )
    line_sum.begin(range(count))
    todo = [functools.partial(probe_logits, cut) for cut in range(3, cuts)]
    todo[2:2] = [lambda: plane.relay_core(1)]
    todo[7:7] = [lambda: plane.receive_core(1)]
    line_sum.run(3, todo)

    for begin in range(0, rows, wide_rows):
        at = slice(begin, begin + wide_rows)
        stream = stream_ref[at, :].astype(f32) + x_mlp[at, :].astype(f32) + offsets_ref[2:3, :] + offsets_ref[3:4, :]
        states_ref[0, at, :] = (row_norm(stream) * gains_ref[2:3, :] + offsets_ref[4:5, :]).astype(bf16)
        low = stream.astype(bf16)
        low_ref[at, :] = low
        translate(1, stream, low, second_trans[...].reshape(depth, depth), at)
    for copy in sent:
        copy.wait_send()
    for copy in stores[-2:]:
        copy.wait()
    plane.finish()
    line_sum.finish()


def layer(stream, joined, fc, proj, out, trans, next_trans, gains, offsets, wide, bias, turns, table):
    size = lax.axis_size("seq")
    lines = lax.axis_size("batch")
    rows, depth = stream.shape
    tokens = rows // lines
    own_heads = depth // HEAD_DIM // size
    columns = own_heads * HEAD_DIM
    count = 16
    tiles = pl.cdiv(table.shape[0], VOCAB_TILE)
    bf16 = jnp.bfloat16
    f32 = jnp.float32
    vmem = pl.BlockSpec(memory_space=pltpu.VMEM)
    anywhere = pl.BlockSpec(memory_space=pl.ANY)
    dma = pltpu.SemaphoreType.DMA
    sums = LineSum.scratch(count, rows, depth)
    return pl.pallas_call(
        functools.partial(layer_kernel, count, own_heads),
        in_specs=[vmem] * 12 + [anywhere],
        out_specs=[vmem] * 3 + [anywhere],
        out_shape=[
            jax.ShapeDtypeStruct((3, rows, depth), bf16),
            jax.ShapeDtypeStruct((2, rows, depth), f32),
            jax.ShapeDtypeStruct((rows, depth), bf16),
            jax.ShapeDtypeStruct((tiles, VOCAB_TILE, rows), f32),
        ],
        scratch_shapes=[
            pltpu.VMEM((size,) + proj.shape, bf16),
            pltpu.VMEM((size,) + next_trans.shape[1:], bf16),
            pltpu.VMEM((2, depth), f32),
            pltpu.VMEM((1, fc.shape[1]), f32),
            pltpu.VMEM((rows, fc.shape[1]), bf16),
            pltpu.VMEM((rows, depth), bf16),
            pltpu.VMEM((rows, depth), bf16),
            pltpu.VMEM((size, 3, tokens, columns), bf16),
            pltpu.VMEM((size, 3, tokens, columns), bf16),
            pltpu.VMEM((size, tokens, columns), bf16),
            pltpu.VMEM((size, tokens, columns), bf16),
            pltpu.VMEM((rows, depth), f32),
        ] + sums[:1] + sums[2:] + [
            pltpu.VMEM((2, VOCAB_TILE // 2, depth), bf16),
            pltpu.VMEM((depth, rows), bf16),
            pltpu.VMEM((2, VOCAB_TILE // 2, rows), f32),
            dma((2,)),
            dma((2,)),
            dma((2,)),
            dma((size - 1,)),
            dma((size,)),
            dma((size - 1,)),
            dma((size,)),
        ] + PlaneGather.scratch(2),
        compiler_params=pltpu.CompilerParams(
            collective_id=2, has_side_effects=True, vmem_limit_bytes=VMEM_BYTES
        ),
        name="layer",
    )(stream, joined, fc, proj, out, trans, next_trans, gains, offsets, wide, bias, turns, table)


def stats_kernel(
    tiles_ref, peaks_ref, sums_ref, cross_ref, scales_ref, note_ref,
    gathered, send_sem, receive_sem,
):
    place = lax.axis_index("batch")
    spot = lax.axis_index("seq")
    size = lax.axis_size("seq")
    planes = others("batch")
    tiles = peaks_ref.shape[0]
    rows = peaks_ref.shape[2]
    lines = gathered.shape[0]
    tokens = rows // lines
    gathered[place, 0:3, :] = peaks_ref[tiles - 1]
    for state in range(3):
        gathered[place, 3 + state : 4 + state, :] = jnp.sum(sums_ref[state], axis=0, keepdims=True)
    for other in range(2):
        gathered[place, 6 + other : 7 + other, :] = jnp.sum(cross_ref[other], axis=0, keepdims=True)
    greet([{"batch": plane} for plane in planes])
    copies = [
        push(gathered.at[place], gathered.at[place], send_sem.at[index], receive_sem.at[place], {"batch": plane})
        for index, plane in enumerate(planes)
    ]
    position = spot * tokens + lax.broadcasted_iota(jnp.int32, (1, tokens), 1)
    weights = jnp.concatenate(
        [
            jnp.where(position < size * tokens - tiles_ref[line, 2:3, :], tiles_ref[line, 1:2, :], 0).astype(jnp.float32)
            for line in range(lines)
        ],
        axis=1,
    )
    for plane in planes:
        arrived(gathered.at[plane], receive_sem.at[plane], {"batch": plane})
    tops = gathered[0, 0:3, :]
    for line in range(1, lines):
        tops = jnp.maximum(tops, gathered[line, 0:3, :])
    sums = jnp.zeros((3, rows), jnp.float32)
    cross = jnp.zeros((2, rows), jnp.float32)
    for line in range(lines):
        fade = jnp.exp(gathered[line, 0:3, :] - tops)
        sums += gathered[line, 3:6, :] * fade
        cross += gathered[line, 6:8, :] * fade[0:1]
    totals = tops + jnp.log(sums)
    diverge = cross / sums[0:1] - totals[0:1] + totals[1:3]
    loss = weights * (diverge[0:1] + diverge[1:2])
    for tile in range(tiles):
        scales_ref[tile] = weights * jnp.exp(peaks_ref[tile] - totals)
    note_ref[...] = jnp.zeros_like(note_ref)
    for line in range(rows // LANES):
        at = slice(line * LANES, (line + 1) * LANES)
        note_ref[1:2, :] += loss[:, at]
        note_ref[2:3, :] += weights[:, at]
    for copy in copies:
        copy.wait_send()


def statistics(tiles, peaks, sums, cross):
    lines = lax.axis_size("batch")
    rows = peaks.shape[2]
    vmem = pl.BlockSpec(memory_space=pltpu.VMEM)
    return pl.pallas_call(
        stats_kernel,
        in_specs=[vmem] * 4,
        out_specs=[vmem] * 2,
        out_shape=[
            jax.ShapeDtypeStruct(peaks.shape, jnp.float32),
            jax.ShapeDtypeStruct((8, LANES), jnp.float32),
        ],
        scratch_shapes=[
            pltpu.VMEM((lines, 8, rows), jnp.float32),
            pltpu.SemaphoreType.DMA((lines - 1,)),
            pltpu.SemaphoreType.DMA((lines,)),
        ],
        compiler_params=pltpu.CompilerParams(collective_id=5, has_side_effects=True),
        name="statistics",
    )(tiles, peaks, sums, cross)


def reduce_kernel(
    count,
    grad_ref, bias_ref, note_ref, trans_ref, mom1_ref, mom2_ref, trans_bias, mom1_bias, mom2_bias,
    first_out, second_out, weight_out, first_bias, second_bias, weight_bias, result_out,
    total_ref, note_out, weights, firsts, seconds, adam_sem,
    mine, sibling_land, side_land, line_land, side_sum, line_part, last_land, own_sum,
    land, held, inner_sem, outer_sem, receive_sem,
    tile_land, tile_line, tile_out,
    local_sem, core_send, core_receive, side_send, side_receive, line_send, line_receive,
    last_send, last_receive, bias_send, bias_receive, plane_send, plane_receive, note_send, note_receive,
):
    size = lax.axis_size("seq")
    spot = lax.axis_index("seq")
    place = lax.axis_index("batch")
    core, column, line = plane_place(spot)
    rows = size // 4
    step_rows = total_ref.shape[0] // count // 2
    beside = {"seq": plane_index(core, 1 - column, line)}
    sibling = {"seq": plane_index(1 - core, column, line)}
    across = [{"seq": plane_index(core, column, lax.rem(line + step, rows))} for step in range(1, rows)]
    peers = others("seq")
    planes = others("batch")
    f32 = jnp.float32
    bf16 = jnp.bfloat16
    chips = [
        (step, index, lax.rem(line + step, rows), side)
        for step in range(rows)
        for index, side in enumerate((1 - column, column))
    ]
    sent = []

    def cut(chunk):
        return pl.ds(chunk * step_rows, step_rows)

    loads = {}
    for chunk in range(count):
        for step, index, at, side in chips:
            copy = pltpu.make_async_copy(
                grad_ref.at[:, plane_index(core, side, at), cut(chunk)], mine.at[chunk, step, index],
                local_sem.at[chunk, step, index],
            )
            copy.start()
            loads[chunk, step, index] = copy
    fetches = [
        pltpu.make_async_copy(source, target, adam_sem.at[index])
        for index, (source, target) in enumerate(((trans_ref, weights), (mom1_ref, firsts), (mom2_ref, seconds)))
    ]
    for copy in fetches:
        copy.start()
    tile_land[spot] = bias_ref[spot]
    greet([{"batch": plane} for plane in planes] + [{"seq": peer} for peer in peers])
    for chunk in range(count):
        for step, index, at, side in chips:
            sent.append(
                push(
                    grad_ref.at[:, plane_index(1 - core, side, at), cut(chunk)], sibling_land.at[chunk, step, index],
                    core_send.at[chunk, step, index], core_receive.at[chunk, step, index], sibling,
                )
            )
    for index, peer in enumerate(peers):
        sent.append(
            push(bias_ref.at[peer], tile_land.at[spot], bias_send.at[index], bias_receive.at[spot], {"seq": peer})
        )
    line_sum = LineSum(
        count, 1, lambda at: own_sum[at],
        land, held, total_ref, inner_sem, outer_sem, receive_sem,
    )

    def pair(chunk):
        for step, index, _, _ in chips:
            loads[chunk, step, index].wait()
            arrived(sibling_land.at[chunk, step, index], core_receive.at[chunk, step, index], sibling)
            mine[chunk, step, index] = (
                mine[chunk, step, index].astype(f32) + sibling_land[chunk, step, index].astype(f32)
            ).astype(bf16)
            if index == 0:
                sent.append(
                    push(
                        mine.at[chunk, step, 0, 0], side_land.at[chunk, step],
                        side_send.at[chunk, step], side_receive.at[chunk, step], beside,
                    )
                )
            if step > 0:
                sent.append(
                    push(
                        mine.at[chunk, step, index, 1], line_land.at[chunk, step - 1, index],
                        line_send.at[chunk, step - 1, index], line_receive.at[chunk, step - 1, index],
                        across[step - 1],
                    )
                )

    def second(chunk):
        begin = chunk * 2 * step_rows
        for step in list(range(1, rows)) + [0]:
            arrived(side_land.at[chunk, step], side_receive.at[chunk, step], beside)
            both = mine[chunk, step, 1, 0].astype(f32) + side_land[chunk, step].astype(f32)
            if step > 0:
                side_sum[chunk, step - 1] = both.astype(bf16)
                sent.append(
                    push(
                        side_sum.at[chunk, step - 1], last_land.at[chunk, step],
                        last_send.at[chunk, step], last_receive.at[chunk, step], across[step - 1],
                    )
                )
            else:
                own_sum[begin : begin + step_rows, :] = both
        for index in range(2):
            both = mine[chunk, 0, index, 1].astype(f32)
            for step in range(1, rows):
                arrived(
                    line_land.at[chunk, step - 1, index], line_receive.at[chunk, step - 1, index], across[-step]
                )
                both += line_land[chunk, step - 1, index].astype(f32)
            if index == 0:
                line_part[chunk] = both.astype(bf16)
                sent.append(
                    push(
                        line_part.at[chunk], last_land.at[chunk, 0],
                        last_send.at[chunk, 0], last_receive.at[chunk, 0], beside,
                    )
                )
            else:
                own_sum[begin + step_rows : begin + 2 * step_rows, :] = both

    def third(chunk):
        begin = chunk * 2 * step_rows
        for step in range(1, rows):
            arrived(last_land.at[chunk, step], last_receive.at[chunk, step], across[-step])
            own_sum[begin : begin + step_rows, :] += last_land[chunk, step].astype(f32)
        arrived(last_land.at[chunk, 0], last_receive.at[chunk, 0], beside)
        own_sum[begin + step_rows : begin + 2 * step_rows, :] += last_land[chunk, 0].astype(f32)
        line_sum.begin([chunk])
        line_sum.gather(chunk)

    def tiles_in_plane():
        for peer in peers:
            arrived(tile_land.at[peer], bias_receive.at[peer], {"seq": peer})
        tile = tile_land[0]
        for source in range(1, size):
            tile += tile_land[source]
        tile_line[place] = tile
        for index, plane in enumerate(planes):
            sent.append(
                push(
                    tile_line.at[place], tile_line.at[place], plane_send.at[index], plane_receive.at[place],
                    {"batch": plane},
                )
            )

    squares = []

    def square(chunk):
        line_sum.spread(chunk)
        for row in range(chunk * 2 * step_rows, (chunk + 1) * 2 * step_rows, 16):
            value = total_ref[row : row + 16, :].astype(f32)
            value = value * value
            for begin in range(0, value.shape[1], LANES):
                block = value[:8, begin : begin + LANES] + value[8:, begin : begin + LANES]
                squares[:] = [block + squares[0]] if squares else [block]

    for time in range(count + 5):
        if time < count:
            pair(time)
        if 0 <= time - 2 < count:
            second(time - 2)
        if 0 <= time - 3 < count:
            third(time - 3)
        if time == count:
            tiles_in_plane()
        if 0 <= time - 5 < count:
            square(time - 5)
    for plane in planes:
        arrived(tile_line.at[plane], plane_receive.at[plane], {"batch": plane})
    tile = tile_line[0]
    for source in range(1, lax.axis_size("batch")):
        tile += tile_line[source]
    head = jnp.sum(squares[0] + tile * tile, axis=0, keepdims=True)
    row8 = lax.broadcasted_iota(jnp.int32, (8, LANES), 0)
    tile_out[...] = jnp.where(row8 == 0, head, note_ref[...])
    note_out[spot] = tile_out[...]
    for index, peer in enumerate(peers):
        sent.append(
            push(tile_out, note_out.at[spot], note_send.at[index], note_receive.at[spot], {"seq": peer})
        )
    for peer in peers:
        arrived(note_out.at[peer], note_receive.at[peer], {"seq": peer})
    notes = note_out[0]
    for source in range(1, size):
        notes += note_out[source]
    sums = jnp.sum(notes, axis=-1, keepdims=True)
    norm = jnp.sqrt(sums[0:1]) / sums[2:3]
    result_out[...] = jnp.broadcast_to(jnp.where(row8[:, 0:1] == 0, norm, sums), (8, LANES))
    factor = jnp.minimum(1.0, clip_max / (norm + 1e-06)) / sums[2:3]
    for copy in fetches:
        copy.wait()
    for chunk in range(count):
        for probe in range(2):
            begin = (2 * chunk + probe) * step_rows
            at = slice(chunk * step_rows, (chunk + 1) * step_rows)
            gradient = total_ref[begin : begin + step_rows, :].astype(f32) * factor
            first_out[probe, at, :], second_out[probe, at, :], weight_out[probe, at, :] = adam_update(
                weights[probe, at, :], gradient, firsts[probe, at, :], seconds[probe, at, :]
            )
    gradient = tile[0:2, 0 : trans_bias.shape[1]] * factor
    first_bias[...], second_bias[...], weight_bias[...] = adam_update(
        trans_bias[...], gradient, mom1_bias[...], mom2_bias[...]
    )
    for copy in sent:
        copy.wait_send()
    line_sum.finish()


def reduce_gradients(grad, bias, note, *optimizer):
    size = lax.axis_size("seq")
    lines = lax.axis_size("batch")
    _, _, width, depth = grad.shape
    rows = size // 4
    count = 4
    cut = width // count
    bf16 = jnp.bfloat16
    vmem = pl.BlockSpec(memory_space=pltpu.VMEM)
    dma = pltpu.SemaphoreType.DMA
    near = max(rows - 1, 1)
    anywhere = pl.BlockSpec(memory_space=pl.ANY)
    f32 = jnp.float32
    return pl.pallas_call(
        functools.partial(reduce_kernel, count),
        in_specs=[anywhere, vmem, vmem, anywhere, anywhere, anywhere, vmem, vmem, vmem],
        out_specs=[vmem] * 7,
        out_shape=[jax.ShapeDtypeStruct((2, width, depth), f32)] * 3
        + [jax.ShapeDtypeStruct((2, width), f32)] * 3
        + [jax.ShapeDtypeStruct(note.shape, f32)],
        scratch_shapes=[
            pltpu.VMEM((2 * width, depth), bf16),
            pltpu.VMEM((size,) + note.shape, f32),
            pltpu.VMEM((2, width, depth), f32),
            pltpu.VMEM((2, width, depth), f32),
            pltpu.VMEM((2, width, depth), f32),
            dma((3,)),
            pltpu.VMEM((count, rows, 2, 2, cut, depth), bf16),
            pltpu.VMEM((count, rows, 2, 2, cut, depth), bf16),
            pltpu.VMEM((count, rows, cut, depth), bf16),
            pltpu.VMEM((count, near, 2, cut, depth), bf16),
            pltpu.VMEM((count, near, cut, depth), bf16),
            pltpu.VMEM((count, cut, depth), bf16),
            pltpu.VMEM((count, rows, cut, depth), bf16),
            pltpu.VMEM((2 * width, depth), jnp.float32),
        ] + LineSum.scratch(count, 2 * width, depth) + [
            pltpu.VMEM((size,) + bias.shape[1:], jnp.float32),
            pltpu.VMEM((lines,) + bias.shape[1:], jnp.float32),
            pltpu.VMEM(note.shape, jnp.float32),
            dma((count, rows, 2)),
            dma((count, rows, 2)),
            dma((count, rows, 2)),
            dma((count, rows)),
            dma((count, rows)),
            dma((count, near, 2)),
            dma((count, near, 2)),
            dma((count, rows)),
            dma((count, rows)),
            dma((size - 1,)),
            dma((size,)),
            dma((lines - 1,)),
            dma((lines,)),
            dma((size - 1,)),
            dma((size,)),
        ],
        compiler_params=pltpu.CompilerParams(
            collective_id=6, has_side_effects=True, vmem_limit_bytes=VMEM_BYTES
        ),
        name="reduce_gradients",
    )(grad, bias, note, *optimizer)


def body(
    token_ids,
    pos_weights,
    pad_lengths,
    embed_in,
    w_qkv,
    w_out,
    w_fc,
    w_proj,
    norm_gains,
    layer_biases,
    wide_bias,
    unembed,
    trans_weight,
    trans_bias,
    mom1_weight,
    mom2_weight,
    mom1_bias,
    mom2_bias,
):
    bf16 = jnp.bfloat16
    f32 = jnp.float32
    tok_rows = token_ids.shape[1]
    width = embed_in.shape[1]
    vocab_rows = unembed.shape[0]
    n_seq = lax.axis_size("seq")
    n_batch = lax.axis_size("batch")
    batch_index = lax.axis_index("batch")
    seq_index = lax.axis_index("seq")
    head_count = width // HEAD_DIM
    plane_heads = head_count // n_batch
    plane_width = plane_heads * HEAD_DIM
    hidden_rows = w_proj.shape[0]

    half_rot = ROT // 2
    local_places = seq_index * tok_rows + jnp.arange(tok_rows, dtype=jnp.int32)
    frequency = 10000.0 ** (-2.0 * jnp.arange(half_rot, dtype=f32) / ROT)
    angles = local_places.astype(f32)[:, None] * frequency[None, :]
    cosine = jnp.cos(angles)
    sine = jnp.sin(angles)
    still = jnp.zeros((tok_rows, HEAD_DIM - ROT), f32)
    blank = jnp.zeros((tok_rows, half_rot), f32)
    turns = jnp.stack(
        [
            jnp.concatenate([cosine, cosine, still + 1.0], axis=1),
            jnp.concatenate([-sine, blank, still], axis=1),
            jnp.concatenate([blank, sine, still], axis=1),
        ]
    )
    turns = jnp.tile(turns, (1, 1, plane_heads))

    wide = wide_bias[None, :]
    fc = w_fc
    if hidden_rows % LANES:
        fc = jnp.transpose(w_fc.reshape(-1, n_seq, n_batch, hidden_rows), (2, 0, 1, 3))
        fc = fc.reshape(n_batch, -1, n_seq * hidden_rows)
        fc_bias = lax.dynamic_slice_in_dim(
            wide_bias[3 * width :].reshape(n_seq, n_batch, hidden_rows), batch_index, 1, 1
        ).reshape(1, -1)
        wide = jnp.concatenate([wide, fc_bias], axis=1)
    own_width = trans_bias.shape[1]
    tiles, stream_low, joined_w, fc_w, trans_low, out_w, bias_all = front(
        token_ids, pos_weights, pad_lengths, embed_in, w_qkv, fc, trans_weight, w_out, trans_bias
    )
    states, translated, low1, probe_logits = layer(
        stream_low,
        joined_w.reshape(width, 3 * plane_width),
        fc_w.reshape(width, n_seq * hidden_rows),
        w_proj,
        out_w.reshape(plane_width, width),
        trans_low.reshape(width, width),
        trans_weight,
        norm_gains,
        layer_biases,
        wide,
        bias_all,
        turns,
        unembed,
    )
    first, second, peaks, sums_part, cross_part = vocab_forward(states, unembed, probe_logits)
    scales, note = statistics(tiles, peaks, sums_part, cross_part)
    grad, bias_grad = vocab_backward(
        first, second, scales, unembed, translated, stream_low, low1, norm_gains
    )
    bias_grad = jnp.transpose(bias_grad.reshape(2, n_seq, own_width), (1, 0, 2))
    bias_grad = jnp.pad(bias_grad, ((0, 0), (0, 6), (0, LANES - own_width)))
    grad = grad.reshape(2, n_seq, own_width, width)
    first_w, second_w, new_w, first_b, second_b, new_b, result = reduce_gradients(
        grad, bias_grad, note, trans_weight, mom1_weight, mom2_weight, trans_bias, mom1_bias, mom2_bias
    )
    return (result[1, 0], result[2, 0], result[0, 0], first_w, second_w, new_w, first_b, second_b, new_b)


def solution(mesh):
    return jax.shard_map(
        body,
        mesh=mesh,
        in_specs=(
            P("batch", "seq"),
            P("batch", "seq"),
            P("batch"),
            P("batch", None),
            P(("seq", "batch"), None),
            P(("seq", "batch"), None),
            P(("seq", "batch"), None),
            P(("seq", "batch"), None),
            P(),
            P(),
            P(),
            P("batch", None),
            P(None, "seq", None),
            P(None, "seq"),
            P(None, "seq", None),
            P(None, "seq", None),
            P(None, "seq"),
            P(None, "seq"),
        ),
        out_specs=(
            P(),
            P(),
            P(),
            P(None, "seq", None),
            P(None, "seq", None),
            P(None, "seq", None),
            P(None, "seq"),
            P(None, "seq"),
            P(None, "seq"),
        ),
        check_vma=False,
    )
```

```python
import functools
import math

import jax
import jax.numpy as jnp
from jax import lax
from jax.experimental import pallas as pl
from jax.experimental.pallas import tpu as pltpu
from jax.sharding import PartitionSpec as P

HEAD_DIM = 64
ROT = 16
STEP = 10


VOCAB_TILE = 1280
LANES = 128
NEGATIVE = -1e30
VMEM_BYTES = 62 * 1024 * 1024
norm_eps = 1e-05
clip_max = 0.001
beta_one = 0.9
beta_two = 0.999
learn_rate = 0.03
decay_rate = 0.01
adam_eps = 1e-08


def norm_back(values, upstream, gain_row):
    average = jnp.mean(values, axis=-1, keepdims=True)
    centered = values - average
    variance = jnp.mean(centered * centered, axis=-1, keepdims=True)
    inverse = lax.rsqrt(variance + norm_eps)
    unit = centered * inverse
    scaled = upstream * gain_row
    return (
        scaled
        - jnp.mean(scaled, axis=-1, keepdims=True)
        - unit * jnp.mean(scaled * unit, axis=-1, keepdims=True)
    ) * inverse


def adam_update(weight, gradient, earlier, later):
    earlier = beta_one * earlier + (1.0 - beta_one) * gradient
    later = beta_two * later + (1.0 - beta_two) * gradient * gradient
    update = (
        earlier / (1.0 - beta_one**STEP) / (jnp.sqrt(later / (1.0 - beta_two**STEP)) + adam_eps)
    )
    return (earlier, later, weight * (1.0 - learn_rate * decay_rate) - learn_rate * update)


def forward_kernel(vocab, states_ref, table_ref, probe0_ref, probe1_ref, first_ref, second_ref, peaks_ref, sums_ref, cross_ref, turned, left, right, peak):
    step = pl.program_id(0)
    steps = pl.num_programs(0) - 1
    width = table_ref.shape[0]
    half = left.shape[1] // 2
    group = 16
    given = (probe0_ref, probe1_ref)
    last = vocab - (pl.cdiv(vocab, width) - 1) * width
    row = lax.broadcasted_iota(jnp.int32, (group, LANES), 0)

    def reset(part):
        span = slice(part * half, (part + 1) * half)
        peak[:, span] = jnp.full((8, half), NEGATIVE, jnp.float32)
        sums_ref[:, :, span] = jnp.zeros((3, 8, half), jnp.float32)
        cross_ref[:, :, span] = jnp.zeros((2, 8, half), jnp.float32)

    @pl.when(step == 0)
    def _():
        reset(0)
        for state in range(2):
            for part in range(2):
                turned[part, :, state * half : (state + 1) * half] = jnp.transpose(
                    states_ref[2 * state, part * half : (part + 1) * half, :]
                )

    @pl.when(step <= 1)
    def _():
        reset(1)

    def multiply(part, target, state, cut):
        place = slice(state * half, (state + 1) * half)
        at = slice(cut * width // 5, (cut + 1) * width // 5)
        target[at, place] = jnp.dot(
            table_ref[at, :], turned[part, :, place], preferred_element_type=jnp.float32
        )

    def units(part, source, target, tile):
        limit = vocab - tile * width
        blocks = width // group
        result = []
        for lanes in range(half // LANES):
            span = slice(part * half + lanes * LANES, part * half + (lanes + 1) * LANES)
            local = slice(lanes * LANES, (lanes + 1) * LANES)
            held = {}

            def logits(state, block, lanes=lanes):
                at = slice(block * group, (block + 1) * group)
                if state == 1:
                    value = given[part][0, at, lanes * LANES : (lanes + 1) * LANES]
                else:
                    begin = state // 2 * half + lanes * LANES
                    value = source[at, begin : begin + LANES]
                if (block + 1) * group > last:
                    value = jnp.where(row + block * group < limit, value, NEGATIVE)
                return value

            def tops(span=span, held=held, logits=logits):
                held["top"], held["sum"], held["cross"] = [], [], []
                for state in range(3):
                    top = logits(state, 0)
                    for block in range(1, blocks):
                        top = jnp.maximum(top, logits(state, block))
                    before = peak[state : state + 1, span]
                    now = jnp.maximum(before, jnp.max(top, axis=0, keepdims=True))
                    peak[state : state + 1, span] = now
                    peaks_ref[pl.ds(tile, 1), state, span] = now
                    fade = jnp.exp(before - now)
                    held["top"].append(jnp.broadcast_to(now, (group, LANES)))
                    held["sum"].append(sums_ref[state, :, span] * fade)
                    if state == 0:
                        held["cross"] = [cross_ref[other, :, span] * fade for other in range(2)]

            def fold(value):
                return value[:8] + value[8:]

            def powers(begin, end, held=held, logits=logits, local=local, fold=fold):
                for block in range(begin, end):
                    place = slice(block * group, (block + 1) * group)
                    base = logits(0, block)
                    base_exp = jnp.exp(base - held["top"][0])
                    held["sum"][0] += fold(base_exp)
                    target[0, 0, place, local] = base_exp.astype(jnp.bfloat16)
                    for state in range(1, 3):
                        value = logits(state, block)
                        value_exp = jnp.exp(value - held["top"][state])
                        held["sum"][state] += fold(value_exp)
                        target[0, state, place, local] = value_exp.astype(jnp.bfloat16)
                        held["cross"][state - 1] += fold(base_exp * (base - value))

            def finish(span=span, held=held):
                for state in range(3):
                    sums_ref[state, :, span] = held["sum"][state]
                for other in range(2):
                    cross_ref[other, :, span] = held["cross"][other]

            result.append(tops)
            cuts = 10
            for cut in range(cuts):
                result.append(
                    functools.partial(powers, cut * blocks // cuts, (cut + 1) * blocks // cuts)
                )
            result.append(finish)
        return result

    def stage(part, target, work):
        done = 0
        for piece in range(10):
            multiply(part, target, piece // 5, piece % 5)
            upto = (piece + 1) * len(work) // 10
            for unit in work[done:upto]:
                unit()
            done = upto

    before = jnp.maximum(step - 1, 0)

    @pl.when(step < steps)
    def _():
        stage(0, left, units(1, right, second_ref, before))
        stage(1, right, units(0, left, first_ref, step))

    @pl.when(step == steps)
    def _():
        for unit in units(1, right, second_ref, before):
            unit()


def vocab_forward(states, table, given):
    _, rows, depth = states.shape
    vocab = table.shape[0]
    tiles = pl.cdiv(vocab, VOCAB_TILE)
    half = rows // 2
    kept = jax.ShapeDtypeStruct((tiles, 3, VOCAB_TILE, half), jnp.bfloat16)
    block = (1, 3, VOCAB_TILE, half)
    whole = lambda *shape: pl.BlockSpec(shape, lambda i: (0,) * len(shape))
    return pl.pallas_call(
        functools.partial(forward_kernel, vocab),
        grid=(tiles + 1,),
        in_specs=[
            whole(3, rows, depth),
            pl.BlockSpec((VOCAB_TILE, depth), lambda i: (jnp.minimum(i, tiles - 1), 0)),
            pl.BlockSpec((1, VOCAB_TILE, half), lambda i: (jnp.minimum(i, tiles - 1), 0, 0)),
            pl.BlockSpec((1, VOCAB_TILE, half), lambda i: (jnp.maximum(i - 1, 0), 0, 1)),
        ],
        out_specs=[
            pl.BlockSpec(block, lambda i: (jnp.minimum(i, tiles - 1), 0, 0, 0)),
            pl.BlockSpec(block, lambda i: (jnp.maximum(i - 1, 0), 0, 0, 0)),
            whole(tiles, 3, rows),
            whole(3, 8, rows),
            whole(2, 8, rows),
        ],
        out_shape=[
            kept,
            kept,
            jax.ShapeDtypeStruct((tiles, 3, rows), jnp.float32),
            jax.ShapeDtypeStruct((3, 8, rows), jnp.float32),
            jax.ShapeDtypeStruct((2, 8, rows), jnp.float32),
        ],
        scratch_shapes=[
            pltpu.VMEM((2, depth, 2 * half), jnp.bfloat16),
            pltpu.VMEM((VOCAB_TILE, 2 * half), jnp.float32),
            pltpu.VMEM((VOCAB_TILE, 2 * half), jnp.float32),
            pltpu.VMEM((8, rows), jnp.float32),
        ],
        compiler_params=pltpu.CompilerParams(vmem_limit_bytes=VMEM_BYTES),
        cost_estimate=pl.CostEstimate(
            flops=4 * rows * depth * vocab,
            bytes_accessed=2 * vocab * (depth + 5 * rows),
            transcendentals=3 * rows * vocab,
        ),
        name="vocab_forward",
    )(states, table, given, given)


def backward_kernel(
    vocab, first_ref, second_ref, scales_ref, table_ref, moved_ref, low0_ref, low1_ref, gain_ref,
    grad_ref, bias_ref, out_ref, left, right, tail, delta, turned,
):
    step = pl.program_id(0)
    tiles = pl.num_programs(0) - 1
    width, depth = table_ref.shape
    half = first_ref.shape[3]
    piece = 256
    last = vocab - (pl.cdiv(vocab, width) - 1) * width
    whole = last // piece * piece
    tile = jnp.maximum(step - 1, 0)
    limit = vocab - tile * width

    def units(part, source, target, index):
        result = []

        def turn(lanes, block):
            begin = part * half + lanes * LANES
            span = slice(begin, begin + LANES)
            place = slice(block * LANES, (block + 1) * LANES)
            local = slice(lanes * LANES, (lanes + 1) * LANES)
            factors = scales_ref[pl.ds(index, 1), :, span][0]
            base = source[0, 0, place, local].astype(jnp.float32) * factors[0:1]
            for state in range(1, 3):
                value = source[0, state, place, local].astype(jnp.float32) * factors[state : state + 1]
                first = (state - 1) * half + lanes * LANES
                target[first : first + LANES, place] = jnp.transpose(
                    (value - base).astype(jnp.bfloat16)
                )

        for lanes in range(half // LANES):
            for block in range(width // LANES):
                result.append(functools.partial(turn, lanes, block))
        return result

    def multiply(part, source, start):
        place = slice(start, start + piece)
        span = slice(part * half, (part + 1) * half)
        partial = jnp.dot(source[:, whole:], tail[:, place], preferred_element_type=jnp.float32)
        if whole > 0:
            partial += jnp.dot(
                source[:, :whole], table_ref[:whole, place], preferred_element_type=jnp.float32
            )
        for probe in range(2):
            out_ref[probe, span, place] += partial[probe * half : (probe + 1) * half]

    def stage(part, source, work):
        done = 0
        pieces = depth // piece
        for index in range(pieces):
            multiply(part, source, index * piece)
            upto = (index + 1) * len(work) // pieces
            for unit in work[done:upto]:
                unit()
            done = upto

    ahead = jnp.minimum(step, tiles - 1)

    @pl.when(step == 0)
    def _():
        out_ref[...] = jnp.zeros_like(out_ref)
        for unit in units(0, first_ref, left, ahead):
            unit()

    @pl.when(step > 0)
    def _():
        below = lax.broadcasted_iota(jnp.int32, (width - whole, depth), 0) + whole < limit
        tail[...] = jnp.where(below, table_ref[whole:, :], jnp.zeros((), tail.dtype))
        stage(0, left, units(1, second_ref, right, tile))
        stage(1, right, units(0, first_ref, left, ahead))

    @pl.when(step == tiles)
    def _():
        rows = out_ref.shape[1]
        chunk = 32
        block = 256
        for probe in range(2):
            low_ref = (low0_ref, low1_ref)[probe]

            def back(index, total, probe=probe):
                at = pl.ds(pl.multiple_of(index * chunk, chunk), chunk)
                value = norm_back(moved_ref[probe, at, :], out_ref[probe, at, :], gain_ref[2:3, :])
                delta[at, :] = value.astype(jnp.bfloat16)
                return total + jnp.sum(value, axis=0, keepdims=True)

            bias_ref[probe : probe + 1, :] = lax.fori_loop(
                0, rows // chunk, back, jnp.zeros((1, depth), jnp.float32), unroll=4
            )
            turned[...] = jnp.transpose(low_ref[...])
            for begin in range(0, depth, block):
                grad_ref[probe, begin : begin + block, :] = jnp.dot(
                    turned[begin : begin + block, :], delta[...], preferred_element_type=jnp.float32
                ).astype(jnp.bfloat16)


def vocab_backward(first, second, scales, table, moved, low0, low1, gains):
    tiles, _, _, half = first.shape
    vocab, depth = table.shape
    rows = 2 * half
    last = vocab - (tiles - 1) * VOCAB_TILE
    block = (1, 3, VOCAB_TILE, half)
    whole = lambda *shape: pl.BlockSpec(shape, lambda i: (0,) * len(shape))
    return pl.pallas_call(
        functools.partial(backward_kernel, vocab),
        grid=(tiles + 1,),
        in_specs=[
            pl.BlockSpec(block, lambda i: (jnp.minimum(i, tiles - 1), 0, 0, 0)),
            pl.BlockSpec(block, lambda i: (jnp.maximum(i - 1, 0), 0, 0, 0)),
            whole(tiles, 3, rows),
            pl.BlockSpec((VOCAB_TILE, depth), lambda i: (jnp.maximum(i - 1, 0), 0)),
            whole(2, rows, depth),
            whole(rows, depth),
            whole(rows, depth),
            whole(*gains.shape),
        ],
        out_specs=[whole(2, depth, depth), whole(2, depth)],
        out_shape=[
            jax.ShapeDtypeStruct((2, depth, depth), jnp.bfloat16),
            jax.ShapeDtypeStruct((2, depth), jnp.float32),
        ],
        scratch_shapes=[
            pltpu.VMEM((2, rows, depth), jnp.float32),
            pltpu.VMEM((2 * half, VOCAB_TILE), jnp.bfloat16),
            pltpu.VMEM((2 * half, VOCAB_TILE), jnp.bfloat16),
            pltpu.VMEM((VOCAB_TILE - last // 256 * 256, depth), jnp.bfloat16),
            pltpu.VMEM((rows, depth), jnp.bfloat16),
            pltpu.VMEM((depth, rows), jnp.bfloat16),
        ],
        compiler_params=pltpu.CompilerParams(vmem_limit_bytes=VMEM_BYTES),
        cost_estimate=pl.CostEstimate(
            flops=4 * rows * depth * (vocab + depth),
            bytes_accessed=2 * vocab * (depth + 3 * rows),
            transcendentals=0,
        ),
        name="vocab_backward",
    )(first, second, scales, table, moved, low0, low1, gains)


def plane_place(place):
    core = lax.rem(place, 2)
    return core, lax.rem(place // 2, 2), place // 4


def plane_index(core, column, line):
    return (line * 2 + column) * 2 + core


def greet(partners):
    barrier = pltpu.get_barrier_semaphore()
    for partner in partners:
        pl.semaphore_signal(barrier, inc=1, device_id=partner, device_id_type=pl.DeviceIdType.MESH)
    pl.semaphore_wait(barrier, len(partners))


def push(source, target, send, receive, partner):
    copy = pltpu.make_async_remote_copy(
        src_ref=source,
        dst_ref=target,
        send_sem=send,
        recv_sem=receive,
        device_id=partner,
        device_id_type=pl.DeviceIdType.MESH,
    )
    copy.start()
    return copy


def arrived(target, receive, partner):
    pltpu.make_async_remote_copy(
        src_ref=target,
        dst_ref=target,
        send_sem=receive,
        recv_sem=receive,
        device_id=partner,
        device_id_type=pl.DeviceIdType.MESH,
    ).wait_recv()


def departed(source, send, partner):
    pltpu.make_async_remote_copy(
        src_ref=source,
        dst_ref=source,
        send_sem=send,
        recv_sem=send,
        device_id=partner,
        device_id_type=pl.DeviceIdType.MESH,
    ).wait_send()


class LineSum:
    def __init__(self, count, halves, own, land, held, total, inner_sem, outer_sem, receive_sem):
        lines = lax.axis_size("batch")
        rows, depth = held.shape
        self.blocks = count // halves
        place = lax.axis_index("batch")
        near = place < lines // 2
        self.count, self.size, self.columns = count, rows // self.blocks, depth // halves
        self.own, self.land, self.held, self.total = own, land, held, total
        self.inner_sem, self.outer_sem, self.receive_sem = inner_sem, outer_sem, receive_sem
        self.middle = (place == lines // 2 - 1) | (place == lines // 2)
        self.end = (place == 0) | (place == lines - 1)
        self.inner = {"batch": jnp.where(near, place + 1, place - 1)}
        self.outer = {"batch": jnp.where(near, place - 1, place + 1)}
        self.slot = jnp.where(self.middle, 1, 0)

    def rows(self, index):
        return (
            pl.ds(index % self.blocks * self.size, self.size),
            pl.ds(index // self.blocks * self.columns, self.columns),
        )

    def send_in(self, index):
        rows = self.rows(index)
        push(
            self.held.at[*rows],
            self.land.at[self.slot, *rows],
            self.inner_sem.at[index],
            self.receive_sem.at[self.slot, index],
            self.inner,
        )

    def begin(self, indices):
        @pl.when(self.end)
        def _():
            for index in indices:
                rows = self.rows(index)
                self.held[rows] = self.own(rows).astype(jnp.bfloat16)
                self.send_in(index)

    def gather(self, index):
        rows = self.rows(index)

        @pl.when(jnp.logical_not(self.end))
        def _():
            arrived(self.land.at[0, *rows], self.receive_sem.at[0, index], self.outer)
            own = self.own(rows).astype(jnp.float32)
            self.held[rows] = (own + self.land[(0, *rows)].astype(jnp.float32)).astype(jnp.bfloat16)
            self.send_in(index)

    def spread(self, index):
        rows = self.rows(index)

        @pl.when(self.middle)
        def _():
            arrived(self.land.at[1, *rows], self.receive_sem.at[1, index], self.inner)
            both = self.held[rows].astype(jnp.float32) + self.land[(1, *rows)].astype(jnp.float32)
            self.total[rows] = both.astype(jnp.bfloat16)

        @pl.when(jnp.logical_not(self.middle))
        def _():
            arrived(self.total.at[*rows], self.receive_sem.at[2, index], self.inner)

        @pl.when(jnp.logical_not(self.end))
        def _():
            push(
                self.total.at[*rows],
                self.total.at[*rows],
                self.outer_sem.at[index],
                self.receive_sem.at[2, index],
                self.outer,
            )

    def run(self, lag, todo=(), done=0):
        todo = list(todo)
        for index in range(self.count + lag):
            if done <= index < self.count:
                self.gather(index)
            if index >= lag:
                self.spread(index - lag)
            if todo:
                todo.pop(0)()
        for work in todo:
            work()

    def finish(self):
        for index in range(self.count):
            rows = self.rows(index)
            departed(self.held.at[*rows], self.inner_sem.at[index], self.inner)

            @pl.when(jnp.logical_not(self.end))
            def _(rows=rows, index=index):
                departed(self.total.at[*rows], self.outer_sem.at[index], self.outer)

    @staticmethod
    def scratch(count, rows, depth):
        return [
            pltpu.VMEM((2, rows, depth), jnp.bfloat16),
            pltpu.VMEM((rows, depth), jnp.bfloat16),
            pltpu.SemaphoreType.DMA((count,)),
            pltpu.SemaphoreType.DMA((count,)),
            pltpu.SemaphoreType.DMA((3, count)),
        ]


class PlaneGather:
    def __init__(self, views, send_sem, receive_sem):
        self.views, self.send_sem, self.receive_sem = views, send_sem, receive_sem
        self.size = lax.axis_size("seq")
        self.spot = lax.axis_index("seq")
        core, column, line = self.where = plane_place(self.spot)
        self.rows = self.size // 4
        self.beside = plane_index(core, 1 - column, line)
        self.sibling = plane_index(1 - core, column, line)
        lines = [lax.rem(line + step, self.rows) for step in range(1, self.rows)]
        self.across = [plane_index(core, column, at) for at in lines]
        self.corners = [plane_index(core, 1 - column, at) for at in lines]
        self.started = []

    def send(self, array, half, slot, way, index, target):
        view = self.views[array](half, slot)
        self.started.append(
            push(
                view, view, self.send_sem.at[array, half, way, index], self.receive_sem.at[array, half, slot],
                {"seq": target},
            )
        )

    def wait(self, array, half, slot):
        arrived(self.views[array](half, slot), self.receive_sem.at[array, half, slot], {"seq": slot})

    def own(self, array):
        for half in range(2):
            self.send(array, half, self.spot, 0, 0, self.beside)
            for index, target in enumerate(self.across):
                self.send(array, half, self.spot, 1 + index, 0, target)
            self.send(array, half, self.spot, self.rows, 0, self.sibling)

    def relay_side(self, array):
        self.wait(array, 0, self.beside)
        for index, target in enumerate(self.across):
            self.send(array, 0, self.beside, 1 + index, 1, target)
        for index, source in enumerate(self.across):
            self.wait(array, 1, source)
            self.send(array, 1, source, 0, 1 + index, self.beside)

    def relay_core(self, array):
        self.send(array, 0, self.beside, self.rows, 1, self.sibling)
        self.wait(array, 1, self.beside)
        self.send(array, 1, self.beside, self.rows, 1, self.sibling)
        for index, source in enumerate(self.across):
            self.send(array, 1, source, self.rows, 2 + index, self.sibling)
            self.wait(array, 0, source)
            self.send(array, 0, source, self.rows, 2 + index, self.sibling)
        for index, source in enumerate(self.corners):
            for half in range(2):
                self.wait(array, half, source)
                self.send(array, half, source, self.rows, 1 + self.rows + index, self.sibling)

    def receive_core(self, array):
        core, _, line = self.where
        for step in range(self.rows):
            for side in range(2):
                source = plane_index(1 - core, side, lax.rem(line + step, self.rows))
                for half in range(2):
                    self.wait(array, half, source)

    def finish(self):
        for copy in self.started:
            copy.wait_send()

    @staticmethod
    def scratch(arrays):
        size = lax.axis_size("seq")
        dma = pltpu.SemaphoreType.DMA
        return [dma((arrays, 2, size // 4 + 1, size // 2 + 1)), dma((arrays, 2, size))]


def others(axis):
    size = lax.axis_size(axis)
    place = lax.axis_index(axis)
    return [lax.rem(place + step, size) for step in range(1, size)]


def front_kernel(
    count,
    ids_ref, weights_ref, padding_ref, table_ref, joined_ref, fc_ref, trans_ref, out_ref, trans_bias_ref,
    tiles_out, stream_ref, joined_out, fc_out, trans_out, out_out, bias_out,
    table, column_ids, chosen, picked, tile_ref, bias_ref, trans_low,
    land, held, inner_sem, outer_sem, receive_sem,
    local_sem, table_sem, tile_send, tile_receive, cross_send, cross_receive, plane_send, plane_receive, bias_send, bias_receive,
):
    lines = lax.axis_size("batch")
    place = lax.axis_index("batch")
    size = lax.axis_size("seq")
    spot = lax.axis_index("seq")
    planes = others("batch")
    peers = others("seq")
    outs = (joined_out, fc_out, trans_out, out_out)
    total_rows, depth = stream_ref.shape
    tokens = tile_ref.shape[1]
    plane_width = joined_out.shape[3] // 3
    hidden_rows = fc_out.shape[3] // size
    vocab = table_ref.shape[0]
    number = spot * lines + place
    goal = {"seq": lax.rem(number, size), "batch": number // size}
    wanted = place * size + spot
    origin = {"seq": wanted // lines, "batch": lax.rem(wanted, lines)}
    stays = number == wanted

    def view(array):
        out = outs[array]
        if array < 2:
            return lambda half, slot: out.at[slot, pl.ds(half * (lines // 2), lines // 2)]
        return lambda half, slot: out.at[slot, :, pl.ds(half * (depth // 2), depth // 2)]

    plane = PlaneGather([view(array) for array in range(4)], plane_send, plane_receive)
    width = VOCAB_TILE
    parts = 4
    cuts = table.shape[0] // width
    table_copies = [
        pltpu.make_async_copy(
            table_ref.at[pl.ds(cut * width, min(width, vocab - cut * width))],
            table.at[pl.ds(cut * width, min(width, vocab - cut * width))],
            table_sem.at[cut],
        )
        for cut in range(cuts)
    ]
    for copy in table_copies:
        copy.start()
    if table.shape[0] > vocab:
        table[vocab:, :] = jnp.zeros((table.shape[0] - vocab, depth), table.dtype)

    def joined_cuts(goal):
        return [
            (
                joined_ref.at[:, pl.ds(pl.multiple_of(part * depth + goal * plane_width, LANES), plane_width)],
                joined_out.at[spot, place, :, pl.ds(part * plane_width, plane_width)],
            )
            for part in range(3)
        ]

    def fc_cuts(goal):
        if len(fc_ref.shape) == 3:
            return [(fc_ref.at[goal], fc_out.at[spot, place])]
        return [
            (
                fc_ref.at[:, pl.ds(pl.multiple_of((part * lines + goal) * hidden_rows, LANES), hidden_rows)],
                fc_out.at[spot, place, :, pl.ds(part * hidden_rows, hidden_rows)],
            )
            for part in range(size)
        ]

    trans_low[...] = trans_ref[0].astype(jnp.bfloat16)
    tile_ref[...] = jnp.zeros_like(tile_ref)
    tile_ref[0:1, :] = ids_ref[...]
    tile_ref[1:2, :] = weights_ref[...]
    tile_ref[2:3, :] = jnp.full((1, tokens), padding_ref[0], jnp.int32)
    bias_ref[...] = jnp.zeros_like(bias_ref)
    bias_ref[0:2, 0 : trans_bias_ref.shape[1]] = trans_bias_ref[...]
    locals_ = [
        pltpu.make_async_copy(source, target, local_sem.at[index])
        for index, (source, target) in enumerate(
            [
                (trans_low, trans_out.at[spot]),
                (tile_ref, tiles_out.at[place]),
                (bias_ref, bias_out.at[spot]),
            ]
            + joined_cuts(place)
            + fc_cuts(place)
        )
    ]
    for copy in locals_:
        copy.start()
    out_copy = pltpu.make_async_copy(out_ref, out_out.at[spot], local_sem.at[6 + size])

    @pl.when(stays)
    def _():
        out_copy.start()

    barrier = pltpu.get_barrier_semaphore()
    for partner in [{"batch": other} for other in planes] + [{"seq": peer} for peer in peers]:
        pl.semaphore_signal(barrier, inc=1, device_id=partner, device_id_type=pl.DeviceIdType.MESH)

    @pl.when(jnp.logical_not(stays))
    def _():
        pl.semaphore_signal(barrier, inc=1, device_id=origin, device_id_type=pl.DeviceIdType.MESH)

    pl.semaphore_wait(barrier, jnp.where(stays, 0, 1) + len(planes) + len(peers))

    tile_copies = [
        push(tile_ref, tiles_out.at[place], tile_send.at[index], tile_receive.at[place], {"batch": other})
        for index, other in enumerate(planes)
    ]
    locals_[0].wait()
    plane.own(2)
    for array, cuts_of in ((0, joined_cuts), (1, fc_cuts)):
        for index, other in enumerate(planes):
            for source, target in cuts_of(other):
                push(source, target, cross_send.at[array, index], cross_receive.at[array, place], {"batch": other})
    out_push = pltpu.make_async_remote_copy(
        src_ref=out_ref, dst_ref=out_out.at[goal["seq"]], send_sem=cross_send.at[2, 0],
        recv_sem=cross_receive.at[2, 0], device_id=goal, device_id_type=pl.DeviceIdType.MESH,
    )

    @pl.when(jnp.logical_not(stays))
    def _():
        out_push.start()

    bias_copies = [
        push(bias_ref, bias_out.at[spot], bias_send.at[index], bias_receive.at[spot], {"seq": peer})
        for index, peer in enumerate(peers)
    ]
    for copy in locals_[1:]:
        copy.wait()
    for other in planes:
        arrived(tiles_out.at[other], tile_receive.at[other], {"batch": other})
    for sequence in range(lines):
        turned = jnp.transpose(tiles_out[sequence].astype(jnp.float32))
        column_ids[sequence * tokens : (sequence + 1) * tokens, :] = jnp.broadcast_to(
            turned[:, 0:1] - (place * vocab).astype(jnp.float32), (tokens, LANES)
        )
    lane = lax.broadcasted_iota(jnp.int32, (total_rows, LANES), 1)

    def choose(cut):
        for block in range(width // LANES):
            begin = cut * width + block * LANES
            chosen[:, begin : begin + LANES] = jnp.where(
                column_ids[...] == (lane + begin).astype(jnp.float32), 1.0, 0.0
            ).astype(jnp.bfloat16)

    def look(part, cut):
        at = slice(part * (depth // parts), (part + 1) * (depth // parts))
        span = slice(cut * width, (cut + 1) * width)
        if part == 0:
            table_copies[cut].wait()
        found = jnp.dot(chosen[:, span], table[span, at], preferred_element_type=jnp.float32)
        if cut == 0:
            picked[:, at] = found
        else:
            picked[:, at] += found
        if part == 0 and cut + 1 < cuts:
            choose(cut + 1)

    line_sum = LineSum(
        count, parts, lambda at: picked[at],
        land, held, stream_ref, inner_sem, outer_sem, receive_sem,
    )

    def turn(array):
        for other in planes:
            arrived(outs[array].at[spot, other], cross_receive.at[array, other], {"batch": other})
        plane.own(array)

    def turn_out():
        @pl.when(stays)
        def _():
            out_copy.wait()

        @pl.when(jnp.logical_not(stays))
        def _():
            arrived(out_out.at[spot], cross_receive.at[2, 0], origin)

        plane.own(3)

    between = {
        (0, 0): lambda: choose(0),
        (0, 4): lambda: turn(0),
        (0, 6): lambda: turn_out(),
        (0, 8): lambda: plane.relay_side(2),
        (1, 1): lambda: turn(1),
        (1, 5): lambda: plane.relay_core(2),
        (2, 2): lambda: plane.relay_side(0),
        (3, 2): lambda: plane.relay_core(0),
    }
    for part in range(parts):
        for cut in range(cuts):
            if (part, cut) in between:
                between.pop((part, cut))()
            look(part, cut)
        for work in [between.pop(key) for key in list(between) if key[0] == part]:
            work()
        line_sum.begin(range(part * count // parts, (part + 1) * count // parts))
        if part == parts - 2:
            for index in range(count // parts):
                line_sum.gather(index)
    todo = [
        lambda: None,
        lambda: plane.relay_side(1),
        lambda: plane.relay_side(3),
        lambda: None,
        lambda: None,
        lambda: None,
        lambda: plane.relay_core(1),
        lambda: plane.relay_core(3),
        lambda: None,
        lambda: None,
        lambda: plane.receive_core(2),
        lambda: plane.receive_core(0),
        lambda: None,
        lambda: plane.receive_core(1),
        lambda: plane.receive_core(3),
    ]
    line_sum.run(5, todo, count // parts)
    for peer in peers:
        arrived(bias_out.at[peer], bias_receive.at[peer], {"seq": peer})
    for copy in bias_copies + tile_copies:
        copy.wait_send()
    for array in range(2):
        for index, other in enumerate(planes):
            departed(outs[array].at[spot, place], cross_send.at[array, index], {"batch": other})

    @pl.when(jnp.logical_not(stays))
    def _():
        out_push.wait_send()

    plane.finish()
    line_sum.finish()


def front(ids, weights, padding, table, joined, fc, trans, out, bias):
    size = lax.axis_size("seq")
    lines = lax.axis_size("batch")
    vocab, depth = table.shape
    tokens = ids.shape[1]
    rows = lines * tokens
    own_rows = joined.shape[0]
    count = 32
    vmem = pl.BlockSpec(memory_space=pltpu.VMEM)
    smem = pl.BlockSpec(memory_space=pltpu.SMEM)
    anywhere = pl.BlockSpec(memory_space=pl.ANY)
    dma = pltpu.SemaphoreType.DMA
    bf16 = jnp.bfloat16
    padded = pl.cdiv(vocab, VOCAB_TILE) * VOCAB_TILE
    hidden = math.prod(fc.shape) // own_rows // lines
    return pl.pallas_call(
        functools.partial(front_kernel, count),
        in_specs=[vmem, vmem, smem, anywhere, anywhere, anywhere, vmem, anywhere, vmem],
        out_specs=[vmem, vmem, anywhere, anywhere, anywhere, anywhere, vmem],
        out_shape=[
            jax.ShapeDtypeStruct((lines, 8, tokens), jnp.int32),
            jax.ShapeDtypeStruct((rows, depth), bf16),
            jax.ShapeDtypeStruct((size, lines, own_rows, 3 * depth // lines), bf16),
            jax.ShapeDtypeStruct((size, lines, own_rows, hidden), bf16),
            jax.ShapeDtypeStruct((size,) + trans.shape[1:], bf16),
            jax.ShapeDtypeStruct((size,) + out.shape, bf16),
            jax.ShapeDtypeStruct((size, 8, LANES), jnp.float32),
        ],
        scratch_shapes=[
            pltpu.VMEM((padded, depth), bf16),
            pltpu.VMEM((rows, LANES), jnp.float32),
            pltpu.VMEM((rows, padded), bf16),
            pltpu.VMEM((rows, depth), jnp.float32),
            pltpu.VMEM((8, tokens), jnp.int32),
            pltpu.VMEM((8, LANES), jnp.float32),
            pltpu.VMEM(trans.shape[1:], bf16),
        ] + LineSum.scratch(count, rows, depth) + [
            dma((7 + size,)),
            dma((padded // VOCAB_TILE,)),
            dma((lines - 1,)),
            dma((lines,)),
            dma((3, lines - 1)),
            dma((3, lines)),
        ] + PlaneGather.scratch(4) + [
            dma((size - 1,)),
            dma((size,)),
        ],
        compiler_params=pltpu.CompilerParams(
            collective_id=1, has_side_effects=True, vmem_limit_bytes=VMEM_BYTES
        ),
        name="front",
    )(ids, weights, padding, table, joined, fc, trans, out, bias)


def row_norm(values):
    average = jnp.mean(values, axis=-1, keepdims=True)
    centered = values - average
    variance = jnp.mean(centered * centered, axis=-1, keepdims=True)
    return centered * lax.rsqrt(variance + norm_eps)


def layer_kernel(
    count, heads,
    stream_ref, joined_ref, fc_ref, proj_ref, out_ref, trans_ref, next_ref,
    gains_ref, offsets_ref, wide_ref, bias_ref, turns_ref, table_ref,
    states_ref, moved_ref, low_ref, logits_ref,
    proj_all, second_trans, trans_bias, fc_bias, hidden, x_attn, x_mlp, spread, gathered, mixed, returned, part,
    land, inner_sem, outer_sem, receive_sem,
    tables, turned, logits, table_sem, logits_sem,
    local_sem, heads_send, heads_receive, rows_send, rows_receive, plane_send, plane_receive,
):
    f32 = jnp.float32
    bf16 = jnp.bfloat16
    lines = lax.axis_size("batch")
    place = lax.axis_index("batch")
    size = lax.axis_size("seq")
    spot = lax.axis_index("seq")
    planes = others("batch")
    peers = others("seq")
    rows, depth = stream_ref.shape
    tokens = rows // lines
    plane_width = joined_ref.shape[1] // 3
    columns = spread.shape[3]
    groups = plane_width // columns
    head_dim = columns // heads
    hidden_rows = proj_ref.shape[0]
    own_width = next_ref.shape[1]
    step_rows = 32
    wide_rows = 2 * tokens
    vocab = table_ref.shape[0]
    cut_rows = tables.shape[1]
    cuts = pl.cdiv(vocab, cut_rows)
    sizes = [min(cut_rows, vocab - cut * cut_rows) for cut in range(cuts)]
    loads = [
        pltpu.make_async_copy(
            table_ref.at[pl.ds(cut * cut_rows, sizes[cut])],
            tables.at[cut % 2, pl.ds(0, sizes[cut])],
            table_sem.at[cut % 2],
        )
        for cut in range(cuts)
    ]
    stores = [
        pltpu.make_async_copy(
            logits.at[cut % 2],
            logits_ref.at[cut * cut_rows // VOCAB_TILE, pl.ds(cut * cut_rows % VOCAB_TILE, cut_rows)],
            logits_sem.at[cut % 2],
        )
        for cut in range(cuts)
    ]
    loads[0].start()
    loads[1].start()

    def probe_logits(cut):
        loads[cut].wait()
        if cut >= 2:
            stores[cut - 2].wait()
        logits[cut % 2] = jnp.dot(tables[cut % 2], turned[...], preferred_element_type=f32)
        stores[cut].start()
        if cut + 2 < cuts:
            loads[cut + 2].start()

    spans = (proj_all, second_trans)
    proj_all[spot] = proj_ref[...]
    second_trans[spot] = next_ref[1].astype(bf16)
    greet([{"batch": plane} for plane in planes] + [{"seq": peer} for peer in peers])
    sent = []

    def view(array):
        return lambda half, slot: spans[array].at[slot, :, pl.ds(half * (depth // 2), depth // 2)]

    plane = PlaneGather([view(0), view(1)], plane_send, plane_receive)

    def norms(index, carry):
        at = pl.ds(pl.multiple_of(index * step_rows, step_rows), step_rows)
        unit = row_norm(stream_ref[at, :].astype(f32))
        x_attn[at, :] = (unit * gains_ref[0:1, :] + offsets_ref[0:1, :]).astype(bf16)
        x_mlp[at, :] = (unit * gains_ref[1:2, :] + offsets_ref[1:2, :]).astype(bf16)
        return carry

    lax.fori_loop(0, rows // step_rows, norms, 0, unroll=4)
    half_rot = ROT // 2
    for kind in range(3):
        bias = wide_ref[0:1, pl.ds(pl.multiple_of(kind * depth + place * plane_width, LANES), plane_width)]
        whole = jnp.dot(
            x_attn[...], joined_ref[:, kind * plane_width : (kind + 1) * plane_width], preferred_element_type=f32
        )
        for sequence in range(lines):
            value = whole[sequence * tokens : (sequence + 1) * tokens] + bias
            if kind < 2:
                value = (
                    value * turns_ref[0]
                    + pltpu.roll(value, plane_width - half_rot, 1) * turns_ref[1]
                    + pltpu.roll(value, half_rot, 1) * turns_ref[2]
                )
            value = value.astype(bf16)
            for group in range(groups):
                spread[sequence * groups + group, kind] = value[:, group * columns : (group + 1) * columns]
    for index, peer in enumerate(peers):
        sent.append(
            push(spread.at[peer], gathered.at[spot], heads_send.at[index], heads_receive.at[spot], {"seq": peer})
        )
    heads_copy = pltpu.make_async_copy(spread.at[spot], gathered.at[spot], local_sem.at[0])
    heads_copy.start()
    plane.own(0)
    for source in range(size):
        at = slice(source * own_width, (source + 1) * own_width)
        trans_bias[:, at] = bias_ref[source, 0:2, 0:own_width]
        at = slice(source * hidden_rows, (source + 1) * hidden_rows)
        if hidden_rows % LANES:
            begin = wide_ref.shape[1] - fc_ref.shape[1]
            fc_bias[:, at] = wide_ref[0:1, begin + source * hidden_rows : begin + (source + 1) * hidden_rows]
        else:
            begin = pl.multiple_of(3 * depth + (source * lines + place) * hidden_rows, LANES)
            fc_bias[:, at] = wide_ref[0:1, pl.ds(begin, hidden_rows)]

    def translate(probe, stream, low, weights, at):
        moved = stream + jnp.dot(low, weights, preferred_element_type=f32) + trans_bias[probe : probe + 1, :]
        moved_ref[probe, at, :] = moved
        states_ref[1 + probe, at, :] = (
            row_norm(moved) * gains_ref[2:3, :] + offsets_ref[4:5, :]
        ).astype(bf16)

    for begin in range(0, rows, wide_rows):
        at = slice(begin, begin + wide_rows)
        low = stream_ref[at, :]
        translate(0, low.astype(f32), low, trans_ref[...], at)
    turned[...] = jnp.transpose(states_ref[1])
    for begin in range(0, fc_ref.shape[1], 256):
        at = slice(begin, begin + 256)
        for row in range(0, rows, 512):
            span = slice(row, row + 512)
            value = jnp.dot(x_mlp[span, :], fc_ref[:, at], preferred_element_type=f32) + fc_bias[:, at]
            hidden[span, at] = (0.5 * value * (1.0 + lax.erf(value * (0.5 ** 0.5)))).astype(bf16)
    plane.relay_side(0)
    heads_copy.wait()
    for peer in peers:
        arrived(gathered.at[peer], heads_receive.at[peer], {"seq": peer})
    length = size * tokens
    block = 2 * tokens
    lane = lax.broadcasted_iota(jnp.int32, (block, columns), 1) // head_dim
    keys = jnp.concatenate([gathered[source, 1] for source in range(size)], axis=0)
    values = jnp.concatenate([gathered[source, 2] for source in range(size)], axis=0)
    for first in range(0, length, block):
        end = first + block
        queries = jnp.concatenate([gathered[first // tokens, 0], gathered[first // tokens + 1, 0]], axis=0)
        allowed = lax.broadcasted_iota(jnp.int32, (block, end), 1) <= (
            lax.broadcasted_iota(jnp.int32, (block, end), 0) + first
        )
        result = None
        for head in range(heads):
            chosen = jnp.where(lane == head, queries, jnp.zeros((), bf16))
            scores = lax.dot_general(
                chosen, keys[:end], (((1,), (1,)), ((), ())), preferred_element_type=f32
            ) * head_dim ** (-0.5)
            scores = jnp.where(allowed, scores, NEGATIVE)
            exponent = jnp.exp(scores - jnp.max(scores, axis=-1, keepdims=True))
            value = jnp.dot(
                exponent.astype(bf16), values[:end], preferred_element_type=f32
            ) / jnp.sum(exponent, axis=-1, keepdims=True)
            result = value if result is None else jnp.where(lane == head, value, result)
        result = result.astype(bf16)
        for index in range(2):
            mixed[first // tokens + index] = result[index * tokens : (index + 1) * tokens]
    for index, peer in enumerate(peers):
        sent.append(
            push(mixed.at[peer], returned.at[spot], rows_send.at[index], rows_receive.at[spot], {"seq": peer})
        )
    rows_copy = pltpu.make_async_copy(mixed.at[spot], returned.at[spot], local_sem.at[1])
    rows_copy.start()
    plane.own(1)
    plane.relay_core(0)
    probe_logits(0)
    probe_logits(1)
    plane.receive_core(0)
    for begin in range(0, depth, 256):
        at = slice(begin, begin + 256)
        part[:, at] = jnp.dot(
            hidden[...], proj_all[:, :, at].reshape(size * hidden_rows, 256), preferred_element_type=f32
        )
    rows_copy.wait()
    for peer in peers:
        arrived(returned.at[peer], rows_receive.at[peer], {"seq": peer})
    for sequence in range(lines):
        at = slice(sequence * tokens, (sequence + 1) * tokens)
        attended = jnp.concatenate(
            [returned[sequence * groups + group] for group in range(groups)], axis=1
        )
        part[at, :] += jnp.dot(attended, out_ref[...], preferred_element_type=f32)
    line_sum = LineSum(
        count, 1, lambda at: part[at],
        land, x_attn, x_mlp, inner_sem, outer_sem, receive_sem,
    )
    line_sum.begin(range(count))
    todo = []
    for cut in range(2, cuts):
        todo += [functools.partial(probe_logits, cut), lambda: None]
    todo[9:9] = [lambda: plane.relay_side(1)]
    todo[17:17] = [lambda: plane.relay_core(1)]
    todo[25:25] = [lambda: plane.receive_core(1)]
    line_sum.run(5, todo)

    for begin in range(0, rows, wide_rows):
        at = slice(begin, begin + wide_rows)
        stream = stream_ref[at, :].astype(f32) + x_mlp[at, :].astype(f32) + offsets_ref[2:3, :] + offsets_ref[3:4, :]
        states_ref[0, at, :] = (row_norm(stream) * gains_ref[2:3, :] + offsets_ref[4:5, :]).astype(bf16)
        low = stream.astype(bf16)
        low_ref[at, :] = low
        translate(1, stream, low, second_trans[...].reshape(depth, depth), at)
    for copy in sent:
        copy.wait_send()
    for copy in stores[-2:]:
        copy.wait()
    plane.finish()
    line_sum.finish()


def layer(stream, joined, fc, proj, out, trans, next_trans, gains, offsets, wide, bias, turns, table):
    size = lax.axis_size("seq")
    lines = lax.axis_size("batch")
    rows, depth = stream.shape
    tokens = rows // lines
    own_heads = depth // HEAD_DIM // size
    columns = own_heads * HEAD_DIM
    count = 32
    tiles = pl.cdiv(table.shape[0], VOCAB_TILE)
    bf16 = jnp.bfloat16
    f32 = jnp.float32
    vmem = pl.BlockSpec(memory_space=pltpu.VMEM)
    anywhere = pl.BlockSpec(memory_space=pl.ANY)
    dma = pltpu.SemaphoreType.DMA
    sums = LineSum.scratch(count, rows, depth)
    return pl.pallas_call(
        functools.partial(layer_kernel, count, own_heads),
        in_specs=[vmem] * 12 + [anywhere],
        out_specs=[vmem] * 3 + [anywhere],
        out_shape=[
            jax.ShapeDtypeStruct((3, rows, depth), bf16),
            jax.ShapeDtypeStruct((2, rows, depth), f32),
            jax.ShapeDtypeStruct((rows, depth), bf16),
            jax.ShapeDtypeStruct((tiles, VOCAB_TILE, rows), f32),
        ],
        scratch_shapes=[
            pltpu.VMEM((size,) + proj.shape, bf16),
            pltpu.VMEM((size,) + next_trans.shape[1:], bf16),
            pltpu.VMEM((2, depth), f32),
            pltpu.VMEM((1, fc.shape[1]), f32),
            pltpu.VMEM((rows, fc.shape[1]), bf16),
            pltpu.VMEM((rows, depth), bf16),
            pltpu.VMEM((rows, depth), bf16),
            pltpu.VMEM((size, 3, tokens, columns), bf16),
            pltpu.VMEM((size, 3, tokens, columns), bf16),
            pltpu.VMEM((size, tokens, columns), bf16),
            pltpu.VMEM((size, tokens, columns), bf16),
            pltpu.VMEM((rows, depth), f32),
        ] + sums[:1] + sums[2:] + [
            pltpu.VMEM((2, VOCAB_TILE // 2, depth), bf16),
            pltpu.VMEM((depth, rows), bf16),
            pltpu.VMEM((2, VOCAB_TILE // 2, rows), f32),
            dma((2,)),
            dma((2,)),
            dma((2,)),
            dma((size - 1,)),
            dma((size,)),
            dma((size - 1,)),
            dma((size,)),
        ] + PlaneGather.scratch(2),
        compiler_params=pltpu.CompilerParams(
            collective_id=2, has_side_effects=True, vmem_limit_bytes=VMEM_BYTES
        ),
        name="layer",
    )(stream, joined, fc, proj, out, trans, next_trans, gains, offsets, wide, bias, turns, table)


def stats_kernel(
    tiles_ref, peaks_ref, sums_ref, cross_ref, scales_ref, note_ref,
    gathered, send_sem, receive_sem,
):
    place = lax.axis_index("batch")
    spot = lax.axis_index("seq")
    size = lax.axis_size("seq")
    planes = others("batch")
    tiles = peaks_ref.shape[0]
    rows = peaks_ref.shape[2]
    lines = gathered.shape[0]
    tokens = rows // lines
    gathered[place, 0:3, :] = peaks_ref[tiles - 1]
    for state in range(3):
        gathered[place, 3 + state : 4 + state, :] = jnp.sum(sums_ref[state], axis=0, keepdims=True)
    for other in range(2):
        gathered[place, 6 + other : 7 + other, :] = jnp.sum(cross_ref[other], axis=0, keepdims=True)
    greet([{"batch": plane} for plane in planes])
    copies = [
        push(gathered.at[place], gathered.at[place], send_sem.at[index], receive_sem.at[place], {"batch": plane})
        for index, plane in enumerate(planes)
    ]
    position = spot * tokens + lax.broadcasted_iota(jnp.int32, (1, tokens), 1)
    weights = jnp.concatenate(
        [
            jnp.where(position < size * tokens - tiles_ref[line, 2:3, :], tiles_ref[line, 1:2, :], 0).astype(jnp.float32)
            for line in range(lines)
        ],
        axis=1,
    )
    for plane in planes:
        arrived(gathered.at[plane], receive_sem.at[plane], {"batch": plane})
    tops = gathered[0, 0:3, :]
    for line in range(1, lines):
        tops = jnp.maximum(tops, gathered[line, 0:3, :])
    sums = jnp.zeros((3, rows), jnp.float32)
    cross = jnp.zeros((2, rows), jnp.float32)
    for line in range(lines):
        fade = jnp.exp(gathered[line, 0:3, :] - tops)
        sums += gathered[line, 3:6, :] * fade
        cross += gathered[line, 6:8, :] * fade[0:1]
    totals = tops + jnp.log(sums)
    diverge = cross / sums[0:1] - totals[0:1] + totals[1:3]
    loss = weights * (diverge[0:1] + diverge[1:2])
    for tile in range(tiles):
        scales_ref[tile] = weights * jnp.exp(peaks_ref[tile] - totals)
    note_ref[...] = jnp.zeros_like(note_ref)
    for line in range(rows // LANES):
        at = slice(line * LANES, (line + 1) * LANES)
        note_ref[1:2, :] += loss[:, at]
        note_ref[2:3, :] += weights[:, at]
    for copy in copies:
        copy.wait_send()


def statistics(tiles, peaks, sums, cross):
    lines = lax.axis_size("batch")
    rows = peaks.shape[2]
    vmem = pl.BlockSpec(memory_space=pltpu.VMEM)
    return pl.pallas_call(
        stats_kernel,
        in_specs=[vmem] * 4,
        out_specs=[vmem] * 2,
        out_shape=[
            jax.ShapeDtypeStruct(peaks.shape, jnp.float32),
            jax.ShapeDtypeStruct((8, LANES), jnp.float32),
        ],
        scratch_shapes=[
            pltpu.VMEM((lines, 8, rows), jnp.float32),
            pltpu.SemaphoreType.DMA((lines - 1,)),
            pltpu.SemaphoreType.DMA((lines,)),
        ],
        compiler_params=pltpu.CompilerParams(collective_id=5, has_side_effects=True),
        name="statistics",
    )(tiles, peaks, sums, cross)


def reduce_kernel(
    count,
    grad_ref, bias_ref, note_ref,
    total_ref, bias_out, note_out,
    mine, sibling_land, side_land, line_land, side_sum, line_part, last_land, own_sum,
    land, held, inner_sem, outer_sem, receive_sem,
    tile_land, tile_line, tile_out,
    local_sem, core_send, core_receive, side_send, side_receive, line_send, line_receive,
    last_send, last_receive, bias_send, bias_receive, plane_send, plane_receive, note_send, note_receive,
):
    size = lax.axis_size("seq")
    spot = lax.axis_index("seq")
    place = lax.axis_index("batch")
    core, column, line = plane_place(spot)
    rows = size // 4
    step_rows = total_ref.shape[0] // count // 2
    beside = {"seq": plane_index(core, 1 - column, line)}
    sibling = {"seq": plane_index(1 - core, column, line)}
    across = [{"seq": plane_index(core, column, lax.rem(line + step, rows))} for step in range(1, rows)]
    peers = others("seq")
    planes = others("batch")
    f32 = jnp.float32
    bf16 = jnp.bfloat16
    chips = [
        (step, index, lax.rem(line + step, rows), side)
        for step in range(rows)
        for index, side in enumerate((1 - column, column))
    ]
    sent = []

    def cut(chunk):
        return pl.ds(chunk * step_rows, step_rows)

    loads = {}
    for chunk in range(count):
        for step, index, at, side in chips:
            copy = pltpu.make_async_copy(
                grad_ref.at[:, plane_index(core, side, at), cut(chunk)], mine.at[chunk, step, index],
                local_sem.at[chunk, step, index],
            )
            copy.start()
            loads[chunk, step, index] = copy
    tile_land[spot] = bias_ref[spot]
    greet([{"batch": plane} for plane in planes] + [{"seq": peer} for peer in peers])
    for chunk in range(count):
        for step, index, at, side in chips:
            sent.append(
                push(
                    grad_ref.at[:, plane_index(1 - core, side, at), cut(chunk)], sibling_land.at[chunk, step, index],
                    core_send.at[chunk, step, index], core_receive.at[chunk, step, index], sibling,
                )
            )
    for index, peer in enumerate(peers):
        sent.append(
            push(bias_ref.at[peer], tile_land.at[spot], bias_send.at[index], bias_receive.at[spot], {"seq": peer})
        )
    line_sum = LineSum(
        count, 1, lambda at: own_sum[at],
        land, held, total_ref, inner_sem, outer_sem, receive_sem,
    )

    def pair(chunk):
        for step, index, _, _ in chips:
            loads[chunk, step, index].wait()
            arrived(sibling_land.at[chunk, step, index], core_receive.at[chunk, step, index], sibling)
            mine[chunk, step, index] = (
                mine[chunk, step, index].astype(f32) + sibling_land[chunk, step, index].astype(f32)
            ).astype(bf16)
            if index == 0:
                sent.append(
                    push(
                        mine.at[chunk, step, 0, 0], side_land.at[chunk, step],
                        side_send.at[chunk, step], side_receive.at[chunk, step], beside,
                    )
                )
            if step > 0:
                sent.append(
                    push(
                        mine.at[chunk, step, index, 1], line_land.at[chunk, step - 1, index],
                        line_send.at[chunk, step - 1, index], line_receive.at[chunk, step - 1, index],
                        across[step - 1],
                    )
                )

    def second(chunk):
        begin = chunk * 2 * step_rows
        for step in list(range(1, rows)) + [0]:
            arrived(side_land.at[chunk, step], side_receive.at[chunk, step], beside)
            both = mine[chunk, step, 1, 0].astype(f32) + side_land[chunk, step].astype(f32)
            if step > 0:
                side_sum[chunk, step - 1] = both.astype(bf16)
                sent.append(
                    push(
                        side_sum.at[chunk, step - 1], last_land.at[chunk, step],
                        last_send.at[chunk, step], last_receive.at[chunk, step], across[step - 1],
                    )
                )
            else:
                own_sum[begin : begin + step_rows, :] = both
        for index in range(2):
            both = mine[chunk, 0, index, 1].astype(f32)
            for step in range(1, rows):
                arrived(
                    line_land.at[chunk, step - 1, index], line_receive.at[chunk, step - 1, index], across[-step]
                )
                both += line_land[chunk, step - 1, index].astype(f32)
            if index == 0:
                line_part[chunk] = both.astype(bf16)
                sent.append(
                    push(
                        line_part.at[chunk], last_land.at[chunk, 0],
                        last_send.at[chunk, 0], last_receive.at[chunk, 0], beside,
                    )
                )
            else:
                own_sum[begin + step_rows : begin + 2 * step_rows, :] = both

    def third(chunk):
        begin = chunk * 2 * step_rows
        for step in range(1, rows):
            arrived(last_land.at[chunk, step], last_receive.at[chunk, step], across[-step])
            own_sum[begin : begin + step_rows, :] += last_land[chunk, step].astype(f32)
        arrived(last_land.at[chunk, 0], last_receive.at[chunk, 0], beside)
        own_sum[begin + step_rows : begin + 2 * step_rows, :] += last_land[chunk, 0].astype(f32)
        line_sum.begin([chunk])
        line_sum.gather(chunk)

    def tiles_in_plane():
        for peer in peers:
            arrived(tile_land.at[peer], bias_receive.at[peer], {"seq": peer})
        tile = tile_land[0]
        for source in range(1, size):
            tile += tile_land[source]
        tile_line[place] = tile
        for index, plane in enumerate(planes):
            sent.append(
                push(
                    tile_line.at[place], tile_line.at[place], plane_send.at[index], plane_receive.at[place],
                    {"batch": plane},
                )
            )

    squares = []

    def square(chunk):
        line_sum.spread(chunk)
        for row in range(chunk * 2 * step_rows, (chunk + 1) * 2 * step_rows, 16):
            value = total_ref[row : row + 16, :].astype(f32)
            value = value * value
            for begin in range(0, value.shape[1], LANES):
                block = value[:8, begin : begin + LANES] + value[8:, begin : begin + LANES]
                squares[:] = [block + squares[0]] if squares else [block]

    for time in range(count + 5):
        if time < count:
            pair(time)
        if 0 <= time - 2 < count:
            second(time - 2)
        if 0 <= time - 3 < count:
            third(time - 3)
        if time == count:
            tiles_in_plane()
        if 0 <= time - 5 < count:
            square(time - 5)
    for plane in planes:
        arrived(tile_line.at[plane], plane_receive.at[plane], {"batch": plane})
    tile = tile_line[0]
    for source in range(1, lax.axis_size("batch")):
        tile += tile_line[source]
    bias_out[...] = tile
    head = jnp.sum(squares[0] + tile * tile, axis=0, keepdims=True)
    row8 = lax.broadcasted_iota(jnp.int32, (8, LANES), 0)
    tile_out[...] = jnp.where(row8 == 0, head, note_ref[...])
    note_out[spot] = tile_out[...]
    for index, peer in enumerate(peers):
        sent.append(
            push(tile_out, note_out.at[spot], note_send.at[index], note_receive.at[spot], {"seq": peer})
        )
    for peer in peers:
        arrived(note_out.at[peer], note_receive.at[peer], {"seq": peer})
    for copy in sent:
        copy.wait_send()
    line_sum.finish()


def reduce_gradients(grad, bias, note):
    size = lax.axis_size("seq")
    lines = lax.axis_size("batch")
    _, _, width, depth = grad.shape
    rows = size // 4
    count = min(8, width // 16)
    cut = width // count
    bf16 = jnp.bfloat16
    vmem = pl.BlockSpec(memory_space=pltpu.VMEM)
    dma = pltpu.SemaphoreType.DMA
    near = max(rows - 1, 1)
    return pl.pallas_call(
        functools.partial(reduce_kernel, count),
        in_specs=[pl.BlockSpec(memory_space=pl.ANY), vmem, vmem],
        out_specs=[vmem] * 3,
        out_shape=[
            jax.ShapeDtypeStruct((2 * width, depth), bf16),
            jax.ShapeDtypeStruct(bias.shape[1:], jnp.float32),
            jax.ShapeDtypeStruct((size,) + note.shape, jnp.float32),
        ],
        scratch_shapes=[
            pltpu.VMEM((count, rows, 2, 2, cut, depth), bf16),
            pltpu.VMEM((count, rows, 2, 2, cut, depth), bf16),
            pltpu.VMEM((count, rows, cut, depth), bf16),
            pltpu.VMEM((count, near, 2, cut, depth), bf16),
            pltpu.VMEM((count, near, cut, depth), bf16),
            pltpu.VMEM((count, cut, depth), bf16),
            pltpu.VMEM((count, rows, cut, depth), bf16),
            pltpu.VMEM((2 * width, depth), jnp.float32),
        ] + LineSum.scratch(count, 2 * width, depth) + [
            pltpu.VMEM((size,) + bias.shape[1:], jnp.float32),
            pltpu.VMEM((lines,) + bias.shape[1:], jnp.float32),
            pltpu.VMEM(note.shape, jnp.float32),
            dma((count, rows, 2)),
            dma((count, rows, 2)),
            dma((count, rows, 2)),
            dma((count, rows)),
            dma((count, rows)),
            dma((count, near, 2)),
            dma((count, near, 2)),
            dma((count, rows)),
            dma((count, rows)),
            dma((size - 1,)),
            dma((size,)),
            dma((lines - 1,)),
            dma((lines,)),
            dma((size - 1,)),
            dma((size,)),
        ],
        compiler_params=pltpu.CompilerParams(
            collective_id=6, has_side_effects=True, vmem_limit_bytes=VMEM_BYTES
        ),
        name="reduce_gradients",
    )(grad, bias, note)


def update_kernel(
    total_ref, bias_sum, note_ref, trans_ref, mom1_ref, mom2_ref, trans_bias, mom1_bias, mom2_bias,
    first_out, second_out, weight_out, first_bias, second_bias, weight_bias, result_out,
):
    size = note_ref.shape[0]
    notes = note_ref[0]
    for source in range(1, size):
        notes += note_ref[source]
    sums = jnp.sum(notes, axis=-1, keepdims=True)
    norm = jnp.sqrt(sums[0:1]) / sums[2:3]
    row8 = lax.broadcasted_iota(jnp.int32, (8, LANES), 0)
    result_out[...] = jnp.where(row8 == 0, norm, sums)
    factor = jnp.minimum(1.0, clip_max / (norm + 1e-06)) / sums[2:3]
    for probe in range(2):
        gradient = total_ref[0, probe].astype(jnp.float32) * factor
        first_out[probe], second_out[probe], weight_out[probe] = adam_update(
            trans_ref[probe], gradient, mom1_ref[probe], mom2_ref[probe]
        )
    gradient = bias_sum[0:2, 0 : trans_bias.shape[1]] * factor
    first_bias[...], second_bias[...], weight_bias[...] = adam_update(
        trans_bias[...], gradient, mom1_bias[...], mom2_bias[...]
    )


def update(total, bias_sum, notes, trans, mom1, mom2, trans_bias, mom1_bias, mom2_bias):
    _, width, depth = trans.shape
    count = min(8, width // 16)
    cut = width // count
    f32 = jnp.float32
    whole = lambda part: pl.BlockSpec(part.shape, lambda i: (0,) * part.ndim)
    part = pl.BlockSpec((2, cut, depth), lambda i: (0, i, 0))
    result = pl.BlockSpec((8, LANES), lambda i: (0, 0))
    total = total.reshape(count, 2, cut, depth)
    return pl.pallas_call(
        update_kernel,
        grid=(count,),
        in_specs=[
            pl.BlockSpec((1, 2, cut, depth), lambda i: (i, 0, 0, 0)), whole(bias_sum), whole(notes), part, part, part,
            whole(trans_bias), whole(mom1_bias), whole(mom2_bias),
        ],
        out_specs=[part, part, part, whole(trans_bias), whole(mom1_bias), whole(mom2_bias), result],
        out_shape=[jax.ShapeDtypeStruct(trans.shape, f32)] * 3
        + [jax.ShapeDtypeStruct(trans_bias.shape, f32)] * 3
        + [jax.ShapeDtypeStruct((8, LANES), f32)],
        name="update",
    )(total, bias_sum, notes, trans, mom1, mom2, trans_bias, mom1_bias, mom2_bias)


def body(
    token_ids,
    pos_weights,
    pad_lengths,
    embed_in,
    w_qkv,
    w_out,
    w_fc,
    w_proj,
    norm_gains,
    layer_biases,
    wide_bias,
    unembed,
    trans_weight,
    trans_bias,
    mom1_weight,
    mom2_weight,
    mom1_bias,
    mom2_bias,
):
    bf16 = jnp.bfloat16
    f32 = jnp.float32
    tok_rows = token_ids.shape[1]
    width = embed_in.shape[1]
    vocab_rows = unembed.shape[0]
    n_seq = lax.axis_size("seq")
    n_batch = lax.axis_size("batch")
    batch_index = lax.axis_index("batch")
    seq_index = lax.axis_index("seq")
    head_count = width // HEAD_DIM
    plane_heads = head_count // n_batch
    plane_width = plane_heads * HEAD_DIM
    hidden_rows = w_proj.shape[0]

    half_rot = ROT // 2
    local_places = seq_index * tok_rows + jnp.arange(tok_rows, dtype=jnp.int32)
    frequency = 10000.0 ** (-2.0 * jnp.arange(half_rot, dtype=f32) / ROT)
    angles = local_places.astype(f32)[:, None] * frequency[None, :]
    cosine = jnp.cos(angles)
    sine = jnp.sin(angles)
    still = jnp.zeros((tok_rows, HEAD_DIM - ROT), f32)
    blank = jnp.zeros((tok_rows, half_rot), f32)
    turns = jnp.stack(
        [
            jnp.concatenate([cosine, cosine, still + 1.0], axis=1),
            jnp.concatenate([-sine, blank, still], axis=1),
            jnp.concatenate([blank, sine, still], axis=1),
        ]
    )
    turns = jnp.tile(turns, (1, 1, plane_heads))

    wide = wide_bias[None, :]
    fc = w_fc
    if hidden_rows % LANES:
        fc = jnp.transpose(w_fc.reshape(-1, n_seq, n_batch, hidden_rows), (2, 0, 1, 3))
        fc = fc.reshape(n_batch, -1, n_seq * hidden_rows)
        fc_bias = lax.dynamic_slice_in_dim(
            wide_bias[3 * width :].reshape(n_seq, n_batch, hidden_rows), batch_index, 1, 1
        ).reshape(1, -1)
        wide = jnp.concatenate([wide, fc_bias], axis=1)
    own_width = trans_bias.shape[1]
    tiles, stream_low, joined_w, fc_w, trans_low, out_w, bias_all = front(
        token_ids, pos_weights, pad_lengths, embed_in, w_qkv, fc, trans_weight, w_out, trans_bias
    )
    states, translated, low1, probe_logits = layer(
        stream_low,
        joined_w.reshape(width, 3 * plane_width),
        fc_w.reshape(width, n_seq * hidden_rows),
        w_proj,
        out_w.reshape(plane_width, width),
        trans_low.reshape(width, width),
        trans_weight,
        norm_gains,
        layer_biases,
        wide,
        bias_all,
        turns,
        unembed,
    )
    first, second, peaks, sums_part, cross_part = vocab_forward(states, unembed, probe_logits)
    scales, note = statistics(tiles, peaks, sums_part, cross_part)
    grad, bias_grad = vocab_backward(
        first, second, scales, unembed, translated, stream_low, low1, norm_gains
    )
    bias_grad = jnp.transpose(bias_grad.reshape(2, n_seq, own_width), (1, 0, 2))
    bias_grad = jnp.pad(bias_grad, ((0, 0), (0, 6), (0, LANES - own_width)))
    grad = grad.reshape(2, n_seq, own_width, width)
    first_w, second_w, new_w, first_b, second_b, new_b, result = update(
        *reduce_gradients(grad, bias_grad, note),
        trans_weight, mom1_weight, mom2_weight, trans_bias, mom1_bias, mom2_bias,
    )
    return (result[1, 0], result[2, 0], result[0, 0], first_w, second_w, new_w, first_b, second_b, new_b)


def solution(mesh):
    return jax.shard_map(
        body,
        mesh=mesh,
        in_specs=(
            P("batch", "seq"),
            P("batch", "seq"),
            P("batch"),
            P("batch", None),
            P(("seq", "batch"), None),
            P(("seq", "batch"), None),
            P(("seq", "batch"), None),
            P(("seq", "batch"), None),
            P(),
            P(),
            P(),
            P("batch", None),
            P(None, "seq", None),
            P(None, "seq"),
            P(None, "seq", None),
            P(None, "seq", None),
            P(None, "seq"),
            P(None, "seq"),
        ),
        out_specs=(
            P(),
            P(),
            P(),
            P(None, "seq", None),
            P(None, "seq", None),
            P(None, "seq", None),
            P(None, "seq"),
            P(None, "seq"),
            P(None, "seq"),
        ),
        check_vma=False,
    )
```

```python
import functools
import math

import jax
import jax.numpy as jnp
from jax import lax
from jax.experimental import pallas as pl
from jax.experimental.pallas import tpu as pltpu
from jax.sharding import PartitionSpec as P

HEAD_DIM = 64
ROT = 16
STEP = 10


VOCAB_TILE = 1280
LANES = 128
NEGATIVE = -1e30
VMEM_BYTES = 62 * 1024 * 1024
norm_eps = 1e-05
clip_max = 0.001
beta_one = 0.9
beta_two = 0.999
learn_rate = 0.03
decay_rate = 0.01
adam_eps = 1e-08


def norm_back(values, upstream, gain_row):
    average = jnp.mean(values, axis=-1, keepdims=True)
    centered = values - average
    variance = jnp.mean(centered * centered, axis=-1, keepdims=True)
    inverse = lax.rsqrt(variance + norm_eps)
    unit = centered * inverse
    scaled = upstream * gain_row
    return (
        scaled
        - jnp.mean(scaled, axis=-1, keepdims=True)
        - unit * jnp.mean(scaled * unit, axis=-1, keepdims=True)
    ) * inverse


def adam_update(weight, gradient, earlier, later):
    earlier = beta_one * earlier + (1.0 - beta_one) * gradient
    later = beta_two * later + (1.0 - beta_two) * gradient * gradient
    update = (
        earlier / (1.0 - beta_one**STEP) / (jnp.sqrt(later / (1.0 - beta_two**STEP)) + adam_eps)
    )
    return (earlier, later, weight * (1.0 - learn_rate * decay_rate) - learn_rate * update)


def forward_kernel(vocab, states_ref, table_ref, probe0_ref, probe1_ref, first_ref, second_ref, peaks_ref, sums_ref, cross_ref, turned, left, right, peak):
    step = pl.program_id(0)
    steps = pl.num_programs(0) - 1
    width = table_ref.shape[0]
    half = left.shape[1] // 2
    group = 16
    given = (probe0_ref, probe1_ref)
    last = vocab - (pl.cdiv(vocab, width) - 1) * width
    row = lax.broadcasted_iota(jnp.int32, (group, LANES), 0)

    def reset(part):
        span = slice(part * half, (part + 1) * half)
        peak[:, span] = jnp.full((8, half), NEGATIVE, jnp.float32)
        sums_ref[:, :, span] = jnp.zeros((3, 8, half), jnp.float32)
        cross_ref[:, :, span] = jnp.zeros((2, 8, half), jnp.float32)

    @pl.when(step == 0)
    def _():
        reset(0)
        for state in range(2):
            for part in range(2):
                turned[part, :, state * half : (state + 1) * half] = jnp.transpose(
                    states_ref[2 * state, part * half : (part + 1) * half, :]
                )

    @pl.when(step <= 1)
    def _():
        reset(1)

    def multiply(part, target, state, cut):
        place = slice(state * half, (state + 1) * half)
        at = slice(cut * width // 5, (cut + 1) * width // 5)
        target[at, place] = jnp.dot(
            table_ref[at, :], turned[part, :, place], preferred_element_type=jnp.float32
        )

    def units(part, source, target, tile):
        limit = vocab - tile * width
        blocks = width // group
        result = []
        for lanes in range(half // LANES):
            span = slice(part * half + lanes * LANES, part * half + (lanes + 1) * LANES)
            local = slice(lanes * LANES, (lanes + 1) * LANES)
            held = {}

            def logits(state, block, lanes=lanes):
                at = slice(block * group, (block + 1) * group)
                if state == 1:
                    value = given[part][0, at, lanes * LANES : (lanes + 1) * LANES]
                else:
                    begin = state // 2 * half + lanes * LANES
                    value = source[at, begin : begin + LANES]
                if (block + 1) * group > last:
                    value = jnp.where(row + block * group < limit, value, NEGATIVE)
                return value

            def tops(span=span, held=held, logits=logits):
                held["top"], held["sum"], held["cross"] = [], [], []
                for state in range(3):
                    top = logits(state, 0)
                    for block in range(1, blocks):
                        top = jnp.maximum(top, logits(state, block))
                    before = peak[state : state + 1, span]
                    now = jnp.maximum(before, jnp.max(top, axis=0, keepdims=True))
                    peak[state : state + 1, span] = now
                    peaks_ref[pl.ds(tile, 1), state, span] = now
                    fade = jnp.exp(before - now)
                    held["top"].append(jnp.broadcast_to(now, (group, LANES)))
                    held["sum"].append(sums_ref[state, :, span] * fade)
                    if state == 0:
                        held["cross"] = [cross_ref[other, :, span] * fade for other in range(2)]

            def fold(value):
                return value[:8] + value[8:]

            def powers(begin, end, held=held, logits=logits, local=local, fold=fold):
                for block in range(begin, end):
                    place = slice(block * group, (block + 1) * group)
                    base = logits(0, block)
                    base_exp = jnp.exp(base - held["top"][0])
                    held["sum"][0] += fold(base_exp)
                    target[0, 0, place, local] = base_exp.astype(jnp.bfloat16)
                    for state in range(1, 3):
                        value = logits(state, block)
                        value_exp = jnp.exp(value - held["top"][state])
                        held["sum"][state] += fold(value_exp)
                        target[0, state, place, local] = value_exp.astype(jnp.bfloat16)
                        held["cross"][state - 1] += fold(base_exp * (base - value))

            def finish(span=span, held=held):
                for state in range(3):
                    sums_ref[state, :, span] = held["sum"][state]
                for other in range(2):
                    cross_ref[other, :, span] = held["cross"][other]

            result.append(tops)
            cuts = 10
            for cut in range(cuts):
                result.append(
                    functools.partial(powers, cut * blocks // cuts, (cut + 1) * blocks // cuts)
                )
            result.append(finish)
        return result

    def stage(part, target, work):
        done = 0
        for piece in range(10):
            multiply(part, target, piece // 5, piece % 5)
            upto = (piece + 1) * len(work) // 10
            for unit in work[done:upto]:
                unit()
            done = upto

    before = jnp.maximum(step - 1, 0)

    @pl.when(step < steps)
    def _():
        stage(0, left, units(1, right, second_ref, before))
        stage(1, right, units(0, left, first_ref, step))

    @pl.when(step == steps)
    def _():
        for unit in units(1, right, second_ref, before):
            unit()


def vocab_forward(states, table, given):
    _, rows, depth = states.shape
    vocab = table.shape[0]
    tiles = pl.cdiv(vocab, VOCAB_TILE)
    half = rows // 2
    kept = jax.ShapeDtypeStruct((tiles, 3, VOCAB_TILE, half), jnp.bfloat16)
    block = (1, 3, VOCAB_TILE, half)
    whole = lambda *shape: pl.BlockSpec(shape, lambda i: (0,) * len(shape))
    return pl.pallas_call(
        functools.partial(forward_kernel, vocab),
        grid=(tiles + 1,),
        in_specs=[
            whole(3, rows, depth),
            pl.BlockSpec((VOCAB_TILE, depth), lambda i: (jnp.minimum(i, tiles - 1), 0)),
            pl.BlockSpec((1, VOCAB_TILE, half), lambda i: (jnp.minimum(i, tiles - 1), 0, 0)),
            pl.BlockSpec((1, VOCAB_TILE, half), lambda i: (jnp.maximum(i - 1, 0), 0, 1)),
        ],
        out_specs=[
            pl.BlockSpec(block, lambda i: (jnp.minimum(i, tiles - 1), 0, 0, 0)),
            pl.BlockSpec(block, lambda i: (jnp.maximum(i - 1, 0), 0, 0, 0)),
            whole(tiles, 3, rows),
            whole(3, 8, rows),
            whole(2, 8, rows),
        ],
        out_shape=[
            kept,
            kept,
            jax.ShapeDtypeStruct((tiles, 3, rows), jnp.float32),
            jax.ShapeDtypeStruct((3, 8, rows), jnp.float32),
            jax.ShapeDtypeStruct((2, 8, rows), jnp.float32),
        ],
        scratch_shapes=[
            pltpu.VMEM((2, depth, 2 * half), jnp.bfloat16),
            pltpu.VMEM((VOCAB_TILE, 2 * half), jnp.float32),
            pltpu.VMEM((VOCAB_TILE, 2 * half), jnp.float32),
            pltpu.VMEM((8, rows), jnp.float32),
        ],
        compiler_params=pltpu.CompilerParams(vmem_limit_bytes=VMEM_BYTES),
        cost_estimate=pl.CostEstimate(
            flops=4 * rows * depth * vocab,
            bytes_accessed=2 * vocab * (depth + 5 * rows),
            transcendentals=3 * rows * vocab,
        ),
        name="vocab_forward",
    )(states, table, given, given)


def backward_kernel(
    vocab, first_ref, second_ref, scales_ref, table_ref, moved_ref, low0_ref, low1_ref, gain_ref,
    grad_ref, bias_ref, out_ref, left, right, tail, delta, turned,
):
    step = pl.program_id(0)
    tiles = pl.num_programs(0) - 1
    width, depth = table_ref.shape
    half = first_ref.shape[3]
    piece = 256
    last = vocab - (pl.cdiv(vocab, width) - 1) * width
    whole = last // piece * piece
    tile = jnp.maximum(step - 1, 0)
    limit = vocab - tile * width

    def units(part, source, target, index):
        result = []

        def turn(lanes, block):
            begin = part * half + lanes * LANES
            span = slice(begin, begin + LANES)
            place = slice(block * LANES, (block + 1) * LANES)
            local = slice(lanes * LANES, (lanes + 1) * LANES)
            factors = scales_ref[pl.ds(index, 1), :, span][0]
            base = source[0, 0, place, local].astype(jnp.float32) * factors[0:1]
            for state in range(1, 3):
                value = source[0, state, place, local].astype(jnp.float32) * factors[state : state + 1]
                first = (state - 1) * half + lanes * LANES
                target[first : first + LANES, place] = jnp.transpose(
                    (value - base).astype(jnp.bfloat16)
                )

        for lanes in range(half // LANES):
            for block in range(width // LANES):
                result.append(functools.partial(turn, lanes, block))
        return result

    def multiply(part, source, start):
        place = slice(start, start + piece)
        span = slice(part * half, (part + 1) * half)
        partial = jnp.dot(source[:, whole:], tail[:, place], preferred_element_type=jnp.float32)
        if whole > 0:
            partial += jnp.dot(
                source[:, :whole], table_ref[:whole, place], preferred_element_type=jnp.float32
            )
        for probe in range(2):
            out_ref[probe, span, place] += partial[probe * half : (probe + 1) * half]

    def stage(part, source, work):
        done = 0
        pieces = depth // piece
        for index in range(pieces):
            multiply(part, source, index * piece)
            upto = (index + 1) * len(work) // pieces
            for unit in work[done:upto]:
                unit()
            done = upto

    ahead = jnp.minimum(step, tiles - 1)

    @pl.when(step == 0)
    def _():
        out_ref[...] = jnp.zeros_like(out_ref)
        for unit in units(0, first_ref, left, ahead):
            unit()

    @pl.when(step > 0)
    def _():
        below = lax.broadcasted_iota(jnp.int32, (width - whole, depth), 0) + whole < limit
        tail[...] = jnp.where(below, table_ref[whole:, :], jnp.zeros((), tail.dtype))
        stage(0, left, units(1, second_ref, right, tile))
        stage(1, right, units(0, first_ref, left, ahead))

    @pl.when(step == tiles)
    def _():
        rows = out_ref.shape[1]
        chunk = 32
        block = 256
        for probe in range(2):
            low_ref = (low0_ref, low1_ref)[probe]

            def back(index, total, probe=probe):
                at = pl.ds(pl.multiple_of(index * chunk, chunk), chunk)
                value = norm_back(moved_ref[probe, at, :], out_ref[probe, at, :], gain_ref[2:3, :])
                delta[at, :] = value.astype(jnp.bfloat16)
                return total + jnp.sum(value, axis=0, keepdims=True)

            summed = lax.fori_loop(
                0, rows // chunk, back, jnp.zeros((1, depth), jnp.float32), unroll=4
            )
            if probe == 0:
                bias_ref[...] = jnp.zeros_like(bias_ref)
            own = depth // bias_ref.shape[0]
            for part in range(bias_ref.shape[0]):
                bias_ref[part, probe : probe + 1, 0:own] = summed[:, part * own : (part + 1) * own]
            turned[...] = jnp.transpose(low_ref[...])
            for begin in range(0, depth, block):
                grad_ref[probe, begin : begin + block, :] = jnp.dot(
                    turned[begin : begin + block, :], delta[...], preferred_element_type=jnp.float32
                ).astype(jnp.bfloat16)


def vocab_backward(first, second, scales, table, moved, low0, low1, gains):
    tiles, _, _, half = first.shape
    vocab, depth = table.shape
    rows = 2 * half
    last = vocab - (tiles - 1) * VOCAB_TILE
    block = (1, 3, VOCAB_TILE, half)
    whole = lambda *shape: pl.BlockSpec(shape, lambda i: (0,) * len(shape))
    return pl.pallas_call(
        functools.partial(backward_kernel, vocab),
        grid=(tiles + 1,),
        in_specs=[
            pl.BlockSpec(block, lambda i: (jnp.minimum(i, tiles - 1), 0, 0, 0)),
            pl.BlockSpec(block, lambda i: (jnp.maximum(i - 1, 0), 0, 0, 0)),
            whole(tiles, 3, rows),
            pl.BlockSpec((VOCAB_TILE, depth), lambda i: (jnp.maximum(i - 1, 0), 0)),
            whole(2, rows, depth),
            whole(rows, depth),
            whole(rows, depth),
            whole(*gains.shape),
        ],
        out_specs=[whole(2, depth, depth), whole(lax.axis_size("seq"), 8, LANES)],
        out_shape=[
            jax.ShapeDtypeStruct((2, depth, depth), jnp.bfloat16),
            jax.ShapeDtypeStruct((lax.axis_size("seq"), 8, LANES), jnp.float32),
        ],
        scratch_shapes=[
            pltpu.VMEM((2, rows, depth), jnp.float32),
            pltpu.VMEM((2 * half, VOCAB_TILE), jnp.bfloat16),
            pltpu.VMEM((2 * half, VOCAB_TILE), jnp.bfloat16),
            pltpu.VMEM((VOCAB_TILE - last // 256 * 256, depth), jnp.bfloat16),
            pltpu.VMEM((rows, depth), jnp.bfloat16),
            pltpu.VMEM((depth, rows), jnp.bfloat16),
        ],
        compiler_params=pltpu.CompilerParams(vmem_limit_bytes=VMEM_BYTES),
        cost_estimate=pl.CostEstimate(
            flops=4 * rows * depth * (vocab + depth),
            bytes_accessed=2 * vocab * (depth + 3 * rows),
            transcendentals=0,
        ),
        name="vocab_backward",
    )(first, second, scales, table, moved, low0, low1, gains)


def plane_place(place):
    core = lax.rem(place, 2)
    return core, lax.rem(place // 2, 2), place // 4


def plane_index(core, column, line):
    return (line * 2 + column) * 2 + core


def greet(partners):
    barrier = pltpu.get_barrier_semaphore()
    for partner in partners:
        pl.semaphore_signal(barrier, inc=1, device_id=partner, device_id_type=pl.DeviceIdType.MESH)
    pl.semaphore_wait(barrier, len(partners))


def push(source, target, send, receive, partner):
    copy = pltpu.make_async_remote_copy(
        src_ref=source,
        dst_ref=target,
        send_sem=send,
        recv_sem=receive,
        device_id=partner,
        device_id_type=pl.DeviceIdType.MESH,
    )
    copy.start()
    return copy


def arrived(target, receive, partner):
    pltpu.make_async_remote_copy(
        src_ref=target,
        dst_ref=target,
        send_sem=receive,
        recv_sem=receive,
        device_id=partner,
        device_id_type=pl.DeviceIdType.MESH,
    ).wait_recv()


def departed(source, send, partner):
    pltpu.make_async_remote_copy(
        src_ref=source,
        dst_ref=source,
        send_sem=send,
        recv_sem=send,
        device_id=partner,
        device_id_type=pl.DeviceIdType.MESH,
    ).wait_send()


class LineSum:
    def __init__(self, count, halves, own, land, held, total, inner_sem, outer_sem, receive_sem):
        lines = lax.axis_size("batch")
        rows, depth = held.shape
        self.blocks = count // halves
        place = lax.axis_index("batch")
        near = place < lines // 2
        self.count, self.size, self.columns = count, rows // self.blocks, depth // halves
        self.own, self.land, self.held, self.total = own, land, held, total
        self.inner_sem, self.outer_sem, self.receive_sem = inner_sem, outer_sem, receive_sem
        self.middle = (place == lines // 2 - 1) | (place == lines // 2)
        self.end = (place == 0) | (place == lines - 1)
        self.inner = {"batch": jnp.where(near, place + 1, place - 1)}
        self.outer = {"batch": jnp.where(near, place - 1, place + 1)}
        self.slot = jnp.where(self.middle, 1, 0)

    def rows(self, index):
        return (
            pl.ds(index % self.blocks * self.size, self.size),
            pl.ds(index // self.blocks * self.columns, self.columns),
        )

    def send_in(self, index):
        rows = self.rows(index)
        push(
            self.held.at[*rows],
            self.land.at[self.slot, *rows],
            self.inner_sem.at[index],
            self.receive_sem.at[self.slot, index],
            self.inner,
        )

    def begin(self, indices):
        @pl.when(self.end)
        def _():
            for index in indices:
                rows = self.rows(index)
                self.held[rows] = self.own(rows).astype(jnp.bfloat16)
                self.send_in(index)

    def gather(self, index):
        rows = self.rows(index)

        @pl.when(jnp.logical_not(self.end))
        def _():
            arrived(self.land.at[0, *rows], self.receive_sem.at[0, index], self.outer)
            own = self.own(rows).astype(jnp.float32)
            self.held[rows] = (own + self.land[(0, *rows)].astype(jnp.float32)).astype(jnp.bfloat16)
            self.send_in(index)

    def spread(self, index):
        rows = self.rows(index)

        @pl.when(self.middle)
        def _():
            arrived(self.land.at[1, *rows], self.receive_sem.at[1, index], self.inner)
            both = self.held[rows].astype(jnp.float32) + self.land[(1, *rows)].astype(jnp.float32)
            self.total[rows] = both.astype(jnp.bfloat16)

        @pl.when(jnp.logical_not(self.middle))
        def _():
            arrived(self.total.at[*rows], self.receive_sem.at[2, index], self.inner)

        @pl.when(jnp.logical_not(self.end))
        def _():
            push(
                self.total.at[*rows],
                self.total.at[*rows],
                self.outer_sem.at[index],
                self.receive_sem.at[2, index],
                self.outer,
            )

    def run(self, lag, todo=(), done=0):
        todo = list(todo)
        for index in range(self.count + lag):
            if done <= index < self.count:
                self.gather(index)
            if index >= lag:
                self.spread(index - lag)
            if todo:
                todo.pop(0)()
        for work in todo:
            work()

    def finish(self):
        for index in range(self.count):
            rows = self.rows(index)
            departed(self.held.at[*rows], self.inner_sem.at[index], self.inner)

            @pl.when(jnp.logical_not(self.end))
            def _(rows=rows, index=index):
                departed(self.total.at[*rows], self.outer_sem.at[index], self.outer)

    @staticmethod
    def scratch(count, rows, depth):
        return [
            pltpu.VMEM((2, rows, depth), jnp.bfloat16),
            pltpu.VMEM((rows, depth), jnp.bfloat16),
            pltpu.SemaphoreType.DMA((count,)),
            pltpu.SemaphoreType.DMA((count,)),
            pltpu.SemaphoreType.DMA((3, count)),
        ]


class PlaneGather:
    def __init__(self, views, send_sem, receive_sem):
        self.views, self.send_sem, self.receive_sem = views, send_sem, receive_sem
        self.size = lax.axis_size("seq")
        self.spot = lax.axis_index("seq")
        core, column, line = self.where = plane_place(self.spot)
        self.rows = self.size // 4
        self.beside = plane_index(core, 1 - column, line)
        self.sibling = plane_index(1 - core, column, line)
        lines = [lax.rem(line + step, self.rows) for step in range(1, self.rows)]
        self.across = [plane_index(core, column, at) for at in lines]
        self.corners = [plane_index(core, 1 - column, at) for at in lines]
        self.started = []
        self.used = [0] * len(views)

    def send(self, array, half, slot, target):
        view = self.views[array](half, slot)
        index = self.used[array]
        self.used[array] += 1
        self.started.append(
            push(
                view, view, self.send_sem.at[array, index], self.receive_sem.at[array, 1 if half == 1 else 0, slot],
                {"seq": target},
            )
        )

    def wait(self, array, half, slot):
        arrived(
            self.views[array](half, slot), self.receive_sem.at[array, 1 if half == 1 else 0, slot], {"seq": slot}
        )

    def own(self, array):
        for target in [self.beside] + self.across + [self.sibling]:
            self.send(array, None, self.spot, target)

    def relay_side(self, array):
        self.wait(array, None, self.beside)
        for target in self.across:
            self.send(array, 0, self.beside, target)
        for source in self.across:
            self.wait(array, None, source)
            self.send(array, 1, source, self.beside)
        for source in [self.beside] + self.across:
            self.send(array, None, source, self.sibling)

    def relay_core(self, array):
        for source in self.corners:
            for half in range(2):
                self.wait(array, half, source)
            self.send(array, None, source, self.sibling)

    def receive_core(self, array):
        core, _, line = self.where
        for step in range(self.rows):
            for side in range(2):
                self.wait(array, None, plane_index(1 - core, side, lax.rem(line + step, self.rows)))

    def finish(self):
        for copy in self.started:
            copy.wait_send()

    @staticmethod
    def scratch(arrays):
        size = lax.axis_size("seq")
        dma = pltpu.SemaphoreType.DMA
        return [dma((arrays, 2 * size)), dma((arrays, 2, size))]


def others(axis):
    size = lax.axis_size(axis)
    place = lax.axis_index(axis)
    return [lax.rem(place + step, size) for step in range(1, size)]


def front_kernel(
    count,
    ids_ref, weights_ref, padding_ref, table_ref, mixed_ref, trans_ref, out_ref, trans_bias_ref,
    tiles_out, stream_ref, mixed_out, slab_out, out_out,
    table, column_ids, chosen, picked, tile_ref, slab,
    land, held, inner_sem, outer_sem, receive_sem,
    local_sem, table_sem, tile_send, tile_receive, cross_send, cross_receive, plane_send, plane_receive,
):
    lines = lax.axis_size("batch")
    place = lax.axis_index("batch")
    size = lax.axis_size("seq")
    spot = lax.axis_index("seq")
    planes = others("batch")
    peers = others("seq")
    total_rows, depth = stream_ref.shape
    tokens = tile_ref.shape[1]
    vocab = table_ref.shape[0]
    own_width = trans_ref.shape[1]
    number = spot * lines + place
    goal = {"seq": lax.rem(number, size), "batch": number // size}
    wanted = place * size + spot
    origin = {"seq": wanted // lines, "batch": lax.rem(wanted, lines)}
    stays = number == wanted
    width = VOCAB_TILE
    parts = 2
    cuts = table.shape[0] // width

    def mixed_view(half, slot):
        if half is None:
            return mixed_out.at[slot]
        return mixed_out.at[slot, pl.ds(half * (lines // 2), lines // 2)]

    def slab_view(half, slot):
        if half is None:
            return slab_out.at[slot]
        return slab_out.at[slot, :, pl.ds(half * (depth // 2), depth // 2)]

    plane = PlaneGather([mixed_view, slab_view], plane_send, plane_receive)
    table_copies = [
        pltpu.make_async_copy(
            table_ref.at[pl.ds(cut * width, min(width, vocab - cut * width))],
            table.at[pl.ds(cut * width, min(width, vocab - cut * width))],
            table_sem.at[cut],
        )
        for cut in range(cuts)
    ]
    for copy in table_copies:
        copy.start()
    if table.shape[0] > vocab:
        table[vocab:, :] = jnp.zeros((table.shape[0] - vocab, depth), table.dtype)
    bias = trans_bias_ref[...]
    bias_high = bias.astype(jnp.bfloat16)
    bias_low = (bias - bias_high.astype(jnp.float32)).astype(jnp.bfloat16)
    slab[0:own_width, :] = trans_ref[0].astype(jnp.bfloat16)
    slab[own_width:, :] = jnp.zeros((16, depth), jnp.bfloat16)
    slab[own_width : own_width + 2, 0:own_width] = bias_high
    slab[own_width + 8 : own_width + 10, 0:own_width] = bias_low
    tile_ref[...] = jnp.zeros_like(tile_ref)
    tile_ref[0:1, :] = ids_ref[...]
    tile_ref[1:2, :] = weights_ref[...]
    tile_ref[2:3, :] = jnp.full((1, tokens), padding_ref[0], jnp.int32)
    tiles_out[place] = tile_ref[...]
    slab_copy = pltpu.make_async_copy(slab, slab_out.at[spot], local_sem.at[0])
    slab_copy.start()
    mixed_copy = pltpu.make_async_copy(mixed_ref.at[place], mixed_out.at[spot, place], local_sem.at[1])
    mixed_copy.start()
    out_copy = pltpu.make_async_copy(out_ref, out_out, local_sem.at[2])

    @pl.when(stays)
    def _():
        out_copy.start()

    barrier = pltpu.get_barrier_semaphore()
    for partner in [{"batch": other} for other in planes] + [{"seq": peer} for peer in peers]:
        pl.semaphore_signal(barrier, inc=1, device_id=partner, device_id_type=pl.DeviceIdType.MESH)

    @pl.when(jnp.logical_not(stays))
    def _():
        pl.semaphore_signal(barrier, inc=1, device_id=origin, device_id_type=pl.DeviceIdType.MESH)

    pl.semaphore_wait(barrier, jnp.where(stays, 0, 1) + len(planes) + len(peers))

    sent = [
        push(tile_ref, tiles_out.at[place], tile_send.at[index], tile_receive.at[place], {"batch": other})
        for index, other in enumerate(planes)
    ]
    sent += [
        push(
            mixed_ref.at[other], mixed_out.at[spot, place], cross_send.at[index], cross_receive.at[place],
            {"batch": other},
        )
        for index, other in enumerate(planes)
    ]
    slab_copy.wait()
    plane.own(1)
    out_push = pltpu.make_async_remote_copy(
        src_ref=out_ref, dst_ref=out_out, send_sem=local_sem.at[3],
        recv_sem=local_sem.at[4], device_id=goal, device_id_type=pl.DeviceIdType.MESH,
    )

    @pl.when(jnp.logical_not(stays))
    def _():
        out_push.start()

    for other in planes:
        arrived(tiles_out.at[other], tile_receive.at[other], {"batch": other})
    for sequence in range(lines):
        turned = jnp.transpose(tiles_out[sequence].astype(jnp.float32))
        column_ids[sequence * tokens : (sequence + 1) * tokens, :] = jnp.broadcast_to(
            turned[:, 0:1] - (place * vocab).astype(jnp.float32), (tokens, LANES)
        )
    lane = lax.broadcasted_iota(jnp.int32, (total_rows, LANES), 1)

    def choose(cut):
        for block in range(width // LANES):
            begin = cut * width + block * LANES
            chosen[:, begin : begin + LANES] = jnp.where(
                column_ids[...] == (lane + begin).astype(jnp.float32), 1.0, 0.0
            ).astype(jnp.bfloat16)

    def look(part, cut):
        at = slice(part * (depth // parts), (part + 1) * (depth // parts))
        span = slice(cut * width, (cut + 1) * width)
        if part == 0:
            table_copies[cut].wait()
        found = jnp.dot(chosen[:, span], table[span, at], preferred_element_type=jnp.float32)
        if cut == 0:
            picked[:, at] = found
        else:
            picked[:, at] += found
        if part == 0 and cut + 1 < cuts:
            choose(cut + 1)

    line_sum = LineSum(
        count, parts, lambda at: picked[at],
        land, held, stream_ref, inner_sem, outer_sem, receive_sem,
    )

    def turn():
        mixed_copy.wait()
        for other in planes:
            arrived(mixed_out.at[spot, other], cross_receive.at[other], {"batch": other})
        plane.own(0)

    def turn_out():
        @pl.when(stays)
        def _():
            out_copy.wait()

        @pl.when(jnp.logical_not(stays))
        def _():
            arrived(out_out, local_sem.at[4], origin)

    between = {
        (0, 0): lambda: choose(0),
        (0, 4): lambda: turn(),
        (0, 6): lambda: plane.relay_side(1),
        (1, 4): lambda: plane.relay_core(1),
        (1, 8): lambda: turn_out(),
    }
    for part in range(parts):
        for cut in range(cuts):
            if (part, cut) in between:
                between.pop((part, cut))()
            look(part, cut)
        for work in [between.pop(key) for key in list(between) if key[0] == part]:
            work()
        line_sum.begin(range(part * count // parts, (part + 1) * count // parts))
    todo = [
        lambda: None,
        lambda: None,
        lambda: plane.relay_side(0),
        lambda: plane.receive_core(1),
        lambda: None,
        lambda: None,
        lambda: None,
        lambda: plane.relay_core(0),
        lambda: plane.receive_core(0),
    ]
    line_sum.run(2, todo)
    for copy in sent:
        copy.wait_send()

    @pl.when(jnp.logical_not(stays))
    def _():
        out_push.wait_send()

    plane.finish()
    line_sum.finish()


def front(ids, weights, padding, table, mixed, trans, out, bias):
    size = lax.axis_size("seq")
    lines = lax.axis_size("batch")
    vocab, depth = table.shape
    tokens = ids.shape[1]
    rows = lines * tokens
    count = 8
    vmem = pl.BlockSpec(memory_space=pltpu.VMEM)
    smem = pl.BlockSpec(memory_space=pltpu.SMEM)
    anywhere = pl.BlockSpec(memory_space=pl.ANY)
    dma = pltpu.SemaphoreType.DMA
    bf16 = jnp.bfloat16
    padded = pl.cdiv(vocab, VOCAB_TILE) * VOCAB_TILE
    slab_rows = trans.shape[1] + 16
    return pl.pallas_call(
        functools.partial(front_kernel, count),
        in_specs=[vmem, vmem, smem, anywhere, anywhere, vmem, anywhere, vmem],
        out_specs=[vmem, vmem, anywhere, anywhere, anywhere],
        out_shape=[
            jax.ShapeDtypeStruct((lines, 8, tokens), jnp.int32),
            jax.ShapeDtypeStruct((rows, depth), bf16),
            jax.ShapeDtypeStruct((size,) + mixed.shape, bf16),
            jax.ShapeDtypeStruct((size, slab_rows, depth), bf16),
            jax.ShapeDtypeStruct(out.shape, bf16),
        ],
        scratch_shapes=[
            pltpu.VMEM((padded, depth), bf16),
            pltpu.VMEM((rows, LANES), jnp.float32),
            pltpu.VMEM((rows, padded), bf16),
            pltpu.VMEM((rows, depth), jnp.float32),
            pltpu.VMEM((8, tokens), jnp.int32),
            pltpu.VMEM((slab_rows, depth), bf16),
        ] + LineSum.scratch(count, rows, depth) + [
            dma((5,)),
            dma((padded // VOCAB_TILE,)),
            dma((lines - 1,)),
            dma((lines,)),
            dma((lines - 1,)),
            dma((lines,)),
        ] + PlaneGather.scratch(2),
        compiler_params=pltpu.CompilerParams(
            collective_id=1, has_side_effects=True, vmem_limit_bytes=VMEM_BYTES
        ),
        name="front",
    )(ids, weights, padding, table, mixed, trans, out, bias)


def row_norm(values):
    average = jnp.mean(values, axis=-1, keepdims=True)
    centered = values - average
    variance = jnp.mean(centered * centered, axis=-1, keepdims=True)
    return centered * lax.rsqrt(variance + norm_eps)


def layer_kernel(
    count, heads,
    stream_ref, mixed_ref, proj_ref, out_ref, slab_ref, next_ref,
    gains_ref, offsets_ref, wide_ref, turns_ref, table_ref,
    states_ref, moved_ref, low_ref, logits_ref,
    slab_all, second_trans, trans_bias, fc_bias, hidden, x_attn, x_mlp, spread, gathered, mixed, returned, part,
    land, inner_sem, outer_sem, receive_sem,
    tables, turned, logits, table_sem, logits_sem,
    local_sem, heads_send, heads_receive, rows_send, rows_receive, plane_send, plane_receive,
):
    f32 = jnp.float32
    bf16 = jnp.bfloat16
    lines = lax.axis_size("batch")
    place = lax.axis_index("batch")
    size = lax.axis_size("seq")
    spot = lax.axis_index("seq")
    planes = others("batch")
    peers = others("seq")
    rows, depth = stream_ref.shape
    tokens = rows // lines
    hidden_rows = proj_ref.shape[0]
    fc_width = size * hidden_rows
    plane_width = (mixed_ref.shape[1] - fc_width) // 3
    columns = spread.shape[3]
    groups = plane_width // columns
    head_dim = columns // heads
    own_width = next_ref.shape[1]
    step_rows = 32
    wide_rows = 2 * tokens
    vocab = table_ref.shape[0]
    cut_rows = tables.shape[1]
    cuts = pl.cdiv(vocab, cut_rows)
    sizes = [min(cut_rows, vocab - cut * cut_rows) for cut in range(cuts)]
    loads = [
        pltpu.make_async_copy(
            table_ref.at[pl.ds(cut * cut_rows, sizes[cut])],
            tables.at[cut % 2, pl.ds(0, sizes[cut])],
            table_sem.at[cut % 2],
        )
        for cut in range(cuts)
    ]
    stores = [
        pltpu.make_async_copy(
            logits.at[cut % 2],
            logits_ref.at[cut * cut_rows // VOCAB_TILE, pl.ds(cut * cut_rows % VOCAB_TILE, cut_rows)],
            logits_sem.at[cut % 2],
        )
        for cut in range(cuts)
    ]
    loads[0].start()
    loads[1].start()

    def probe_logits(cut):
        loads[cut].wait()
        if cut >= 2:
            stores[cut - 2].wait()
        logits[cut % 2] = jnp.dot(tables[cut % 2], turned[...], preferred_element_type=f32)
        stores[cut].start()
        if cut + 2 < cuts:
            loads[cut + 2].start()

    spans = (slab_all, second_trans)
    slab_all[spot, 0:hidden_rows, :] = proj_ref[...]
    slab_all[spot, hidden_rows:, :] = out_ref[...]
    second_trans[spot] = next_ref[1].astype(bf16)
    greet([{"batch": plane} for plane in planes] + [{"seq": peer} for peer in peers])
    sent = []

    def view(array):
        def of(half, slot):
            if half is None:
                return spans[array].at[slot]
            return spans[array].at[slot, :, pl.ds(half * (depth // 2), depth // 2)]

        return of

    plane = PlaneGather([view(0), view(1)], plane_send, plane_receive)

    def norms(index, carry):
        at = pl.ds(pl.multiple_of(index * step_rows, step_rows), step_rows)
        unit = row_norm(stream_ref[at, :].astype(f32))
        x_attn[at, :] = (unit * gains_ref[0:1, :] + offsets_ref[0:1, :]).astype(bf16)
        x_mlp[at, :] = (unit * gains_ref[1:2, :] + offsets_ref[1:2, :]).astype(bf16)
        return carry

    lax.fori_loop(0, rows // step_rows, norms, 0, unroll=4)
    half_rot = ROT // 2
    for kind in range(3):
        bias = wide_ref[0:1, pl.ds(pl.multiple_of(kind * depth + place * plane_width, LANES), plane_width)]
        whole = jnp.dot(
            x_attn[...], mixed_ref[:, kind * plane_width : (kind + 1) * plane_width], preferred_element_type=f32
        )
        for sequence in range(lines):
            value = whole[sequence * tokens : (sequence + 1) * tokens] + bias
            if kind < 2:
                value = (
                    value * turns_ref[0]
                    + pltpu.roll(value, plane_width - half_rot, 1) * turns_ref[1]
                    + pltpu.roll(value, half_rot, 1) * turns_ref[2]
                )
            value = value.astype(bf16)
            for group in range(groups):
                spread[sequence * groups + group, kind] = value[:, group * columns : (group + 1) * columns]
    for index, peer in enumerate(peers):
        sent.append(
            push(spread.at[peer], gathered.at[spot], heads_send.at[index], heads_receive.at[spot], {"seq": peer})
        )
    heads_copy = pltpu.make_async_copy(spread.at[spot], gathered.at[spot], local_sem.at[0])
    heads_copy.start()
    plane.own(0)
    for source in range(size):
        at = slice(source * own_width, (source + 1) * own_width)
        for probe in range(2):
            trans_bias[probe : probe + 1, at] = sum(
                slab_ref[source, own_width + 8 * part + probe : own_width + 8 * part + probe + 1, 0:own_width].astype(f32)
                for part in range(2)
            )
        at = slice(source * hidden_rows, (source + 1) * hidden_rows)
        if hidden_rows % LANES:
            begin = wide_ref.shape[1] - fc_width
            fc_bias[:, at] = wide_ref[0:1, begin + source * hidden_rows : begin + (source + 1) * hidden_rows]
        else:
            begin = pl.multiple_of(3 * depth + (source * lines + place) * hidden_rows, LANES)
            fc_bias[:, at] = wide_ref[0:1, pl.ds(begin, hidden_rows)]

    def translate(probe, stream, low, weights, at):
        moved = stream + jnp.dot(low, weights, preferred_element_type=f32) + trans_bias[probe : probe + 1, :]
        moved_ref[probe, at, :] = moved
        states_ref[1 + probe, at, :] = (
            row_norm(moved) * gains_ref[2:3, :] + offsets_ref[4:5, :]
        ).astype(bf16)

    for begin in range(0, rows, wide_rows):
        at = slice(begin, begin + wide_rows)
        low = stream_ref[at, :]
        translate(0, low.astype(f32), low, slab_ref[:, 0:own_width, :].reshape(depth, depth), at)
    turned[...] = jnp.transpose(states_ref[1])
    for begin in range(0, fc_width, 256):
        at = slice(begin, begin + 256)
        for row in range(0, rows, 512):
            span = slice(row, row + 512)
            value = jnp.dot(x_mlp[span, :], mixed_ref[:, 3 * plane_width + begin : 3 * plane_width + begin + 256], preferred_element_type=f32) + fc_bias[:, at]
            hidden[span, at] = (0.5 * value * (1.0 + lax.erf(value * (0.5 ** 0.5)))).astype(bf16)
    plane.relay_side(0)
    heads_copy.wait()
    for peer in peers:
        arrived(gathered.at[peer], heads_receive.at[peer], {"seq": peer})
    length = size * tokens
    block = 2 * tokens
    lane = lax.broadcasted_iota(jnp.int32, (block, columns), 1) // head_dim
    keys = jnp.concatenate([gathered[source, 1] for source in range(size)], axis=0)
    values = jnp.concatenate([gathered[source, 2] for source in range(size)], axis=0)
    for first in range(0, length, block):
        end = first + block
        queries = jnp.concatenate([gathered[first // tokens, 0], gathered[first // tokens + 1, 0]], axis=0)
        allowed = lax.broadcasted_iota(jnp.int32, (block, end), 1) <= (
            lax.broadcasted_iota(jnp.int32, (block, end), 0) + first
        )
        result = None
        for head in range(heads):
            chosen = jnp.where(lane == head, queries, jnp.zeros((), bf16))
            scores = lax.dot_general(
                chosen, keys[:end], (((1,), (1,)), ((), ())), preferred_element_type=f32
            ) * head_dim ** (-0.5)
            scores = jnp.where(allowed, scores, NEGATIVE)
            exponent = jnp.exp(scores - jnp.max(scores, axis=-1, keepdims=True))
            value = jnp.dot(
                exponent.astype(bf16), values[:end], preferred_element_type=f32
            ) / jnp.sum(exponent, axis=-1, keepdims=True)
            result = value if result is None else jnp.where(lane == head, value, result)
        result = result.astype(bf16)
        for index in range(2):
            mixed[first // tokens + index] = result[index * tokens : (index + 1) * tokens]
    for index, peer in enumerate(peers):
        sent.append(
            push(mixed.at[peer], returned.at[spot], rows_send.at[index], rows_receive.at[spot], {"seq": peer})
        )
    rows_copy = pltpu.make_async_copy(mixed.at[spot], returned.at[spot], local_sem.at[1])
    rows_copy.start()
    plane.own(1)
    plane.relay_core(0)
    probe_logits(0)
    probe_logits(1)
    plane.receive_core(0)
    for begin in range(0, depth, 256):
        at = slice(begin, begin + 256)
        part[:, at] = jnp.dot(
            hidden[...], slab_all[:, 0:hidden_rows, at].reshape(fc_width, 256), preferred_element_type=f32
        )
    rows_copy.wait()
    for peer in peers:
        arrived(returned.at[peer], rows_receive.at[peer], {"seq": peer})
    out_w = slab_all[:, hidden_rows:, :].reshape(plane_width, depth)
    for sequence in range(lines):
        at = slice(sequence * tokens, (sequence + 1) * tokens)
        attended = jnp.concatenate(
            [returned[sequence * groups + group] for group in range(groups)], axis=1
        )
        part[at, :] += jnp.dot(attended, out_w, preferred_element_type=f32)
    line_sum = LineSum(
        count, 1, lambda at: part[at],
        land, x_attn, x_mlp, inner_sem, outer_sem, receive_sem,
    )
    line_sum.begin(range(count))
    todo = [functools.partial(probe_logits, cut) for cut in range(2, cuts)]
    todo[4:4] = [lambda: plane.relay_side(1)]
    todo[9:9] = [lambda: plane.relay_core(1)]
    todo[13:13] = [lambda: plane.receive_core(1)]
    line_sum.run(3, todo)

    for begin in range(0, rows, wide_rows):
        at = slice(begin, begin + wide_rows)
        stream = stream_ref[at, :].astype(f32) + x_mlp[at, :].astype(f32) + offsets_ref[2:3, :] + offsets_ref[3:4, :]
        states_ref[0, at, :] = (row_norm(stream) * gains_ref[2:3, :] + offsets_ref[4:5, :]).astype(bf16)
        low = stream.astype(bf16)
        low_ref[at, :] = low
        translate(1, stream, low, second_trans[...].reshape(depth, depth), at)
    for copy in sent:
        copy.wait_send()
    for copy in stores[-2:]:
        copy.wait()
    plane.finish()
    line_sum.finish()


def layer(stream, mixed, proj, out, slab, next_trans, gains, offsets, wide, turns, table):
    size = lax.axis_size("seq")
    lines = lax.axis_size("batch")
    rows, depth = stream.shape
    tokens = rows // lines
    own_heads = depth // HEAD_DIM // size
    columns = own_heads * HEAD_DIM
    count = 16
    fc_width = size * proj.shape[0]
    tiles = pl.cdiv(table.shape[0], VOCAB_TILE)
    bf16 = jnp.bfloat16
    f32 = jnp.float32
    vmem = pl.BlockSpec(memory_space=pltpu.VMEM)
    anywhere = pl.BlockSpec(memory_space=pl.ANY)
    dma = pltpu.SemaphoreType.DMA
    sums = LineSum.scratch(count, rows, depth)
    return pl.pallas_call(
        functools.partial(layer_kernel, count, own_heads),
        in_specs=[vmem] * 10 + [anywhere],
        out_specs=[vmem] * 3 + [anywhere],
        out_shape=[
            jax.ShapeDtypeStruct((3, rows, depth), bf16),
            jax.ShapeDtypeStruct((2, rows, depth), f32),
            jax.ShapeDtypeStruct((rows, depth), bf16),
            jax.ShapeDtypeStruct((tiles, VOCAB_TILE, rows), f32),
        ],
        scratch_shapes=[
            pltpu.VMEM((size, proj.shape[0] + out.shape[0], depth), bf16),
            pltpu.VMEM((size,) + next_trans.shape[1:], bf16),
            pltpu.VMEM((2, depth), f32),
            pltpu.VMEM((1, fc_width), f32),
            pltpu.VMEM((rows, fc_width), bf16),
            pltpu.VMEM((rows, depth), bf16),
            pltpu.VMEM((rows, depth), bf16),
            pltpu.VMEM((size, 3, tokens, columns), bf16),
            pltpu.VMEM((size, 3, tokens, columns), bf16),
            pltpu.VMEM((size, tokens, columns), bf16),
            pltpu.VMEM((size, tokens, columns), bf16),
            pltpu.VMEM((rows, depth), f32),
        ] + sums[:1] + sums[2:] + [
            pltpu.VMEM((2, VOCAB_TILE // 2, depth), bf16),
            pltpu.VMEM((depth, rows), bf16),
            pltpu.VMEM((2, VOCAB_TILE // 2, rows), f32),
            dma((2,)),
            dma((2,)),
            dma((2,)),
            dma((size - 1,)),
            dma((size,)),
            dma((size - 1,)),
            dma((size,)),
        ] + PlaneGather.scratch(2),
        compiler_params=pltpu.CompilerParams(
            collective_id=2, has_side_effects=True, vmem_limit_bytes=VMEM_BYTES
        ),
        name="layer",
    )(stream, mixed, proj, out, slab, next_trans, gains, offsets, wide, turns, table)


def stats_kernel(
    tiles_ref, peaks_ref, sums_ref, cross_ref, scales_ref, note_ref,
    gathered, send_sem, receive_sem,
):
    place = lax.axis_index("batch")
    spot = lax.axis_index("seq")
    size = lax.axis_size("seq")
    planes = others("batch")
    tiles = peaks_ref.shape[0]
    rows = peaks_ref.shape[2]
    lines = gathered.shape[0]
    tokens = rows // lines
    gathered[place, 0:3, :] = peaks_ref[tiles - 1]
    for state in range(3):
        gathered[place, 3 + state : 4 + state, :] = jnp.sum(sums_ref[state], axis=0, keepdims=True)
    for other in range(2):
        gathered[place, 6 + other : 7 + other, :] = jnp.sum(cross_ref[other], axis=0, keepdims=True)
    greet([{"batch": plane} for plane in planes])
    copies = [
        push(gathered.at[place], gathered.at[place], send_sem.at[index], receive_sem.at[place], {"batch": plane})
        for index, plane in enumerate(planes)
    ]
    position = spot * tokens + lax.broadcasted_iota(jnp.int32, (1, tokens), 1)
    weights = jnp.concatenate(
        [
            jnp.where(position < size * tokens - tiles_ref[line, 2:3, :], tiles_ref[line, 1:2, :], 0).astype(jnp.float32)
            for line in range(lines)
        ],
        axis=1,
    )
    for plane in planes:
        arrived(gathered.at[plane], receive_sem.at[plane], {"batch": plane})
    tops = gathered[0, 0:3, :]
    for line in range(1, lines):
        tops = jnp.maximum(tops, gathered[line, 0:3, :])
    sums = jnp.zeros((3, rows), jnp.float32)
    cross = jnp.zeros((2, rows), jnp.float32)
    for line in range(lines):
        fade = jnp.exp(gathered[line, 0:3, :] - tops)
        sums += gathered[line, 3:6, :] * fade
        cross += gathered[line, 6:8, :] * fade[0:1]
    totals = tops + jnp.log(sums)
    diverge = cross / sums[0:1] - totals[0:1] + totals[1:3]
    loss = weights * (diverge[0:1] + diverge[1:2])
    for tile in range(tiles):
        scales_ref[tile] = weights * jnp.exp(peaks_ref[tile] - totals)
    note_ref[...] = jnp.zeros_like(note_ref)
    for line in range(rows // LANES):
        at = slice(line * LANES, (line + 1) * LANES)
        note_ref[1:2, :] += loss[:, at]
        note_ref[2:3, :] += weights[:, at]
    for copy in copies:
        copy.wait_send()


def statistics(tiles, peaks, sums, cross):
    lines = lax.axis_size("batch")
    rows = peaks.shape[2]
    vmem = pl.BlockSpec(memory_space=pltpu.VMEM)
    return pl.pallas_call(
        stats_kernel,
        in_specs=[vmem] * 4,
        out_specs=[vmem] * 2,
        out_shape=[
            jax.ShapeDtypeStruct(peaks.shape, jnp.float32),
            jax.ShapeDtypeStruct((8, LANES), jnp.float32),
        ],
        scratch_shapes=[
            pltpu.VMEM((lines, 8, rows), jnp.float32),
            pltpu.SemaphoreType.DMA((lines - 1,)),
            pltpu.SemaphoreType.DMA((lines,)),
        ],
        compiler_params=pltpu.CompilerParams(collective_id=5, has_side_effects=True),
        name="statistics",
    )(tiles, peaks, sums, cross)


def reduce_kernel(
    count,
    grad_ref, bias_ref, note_ref,
    total_ref, bias_out, note_out,
    mine, sibling_land, side_land, line_land, side_sum, line_part, last_land, own_sum,
    land, held, inner_sem, outer_sem, receive_sem,
    tile_land, tile_line, tile_out,
    local_sem, core_send, core_receive, side_send, side_receive, line_send, line_receive,
    last_send, last_receive, bias_send, bias_receive, plane_send, plane_receive, note_send, note_receive,
):
    size = lax.axis_size("seq")
    spot = lax.axis_index("seq")
    place = lax.axis_index("batch")
    core, column, line = plane_place(spot)
    rows = size // 4
    step_rows = total_ref.shape[0] // count // 2
    beside = {"seq": plane_index(core, 1 - column, line)}
    sibling = {"seq": plane_index(1 - core, column, line)}
    lines_on = [lax.rem(line + step, rows) for step in range(1, rows)]
    across = [{"seq": plane_index(core, column, at)} for at in lines_on]
    peers = others("seq")
    planes = others("batch")
    f32 = jnp.float32
    bf16 = jnp.bfloat16
    sent = []

    def cut(chunk, side):
        return grad_ref.at[:, :, :, side, pl.ds(chunk * step_rows, step_rows)]

    loads = [
        pltpu.make_async_copy(cut(chunk, core), mine.at[chunk], local_sem.at[chunk]) for chunk in range(count)
    ]
    for copy in loads:
        copy.start()
    tile_land[spot] = bias_ref[spot]
    greet([{"batch": plane} for plane in planes] + [{"seq": peer} for peer in peers])
    for chunk in range(count):
        sent.append(
            push(cut(chunk, 1 - core), sibling_land.at[chunk], core_send.at[chunk], core_receive.at[chunk], sibling)
        )
    for index, peer in enumerate(peers):
        sent.append(
            push(bias_ref.at[peer], tile_land.at[spot], bias_send.at[index], bias_receive.at[spot], {"seq": peer})
        )
    line_sum = LineSum(
        count, 1, lambda at: own_sum[at],
        land, held, total_ref, inner_sem, outer_sem, receive_sem,
    )

    def pair(chunk):
        loads[chunk].wait()
        arrived(sibling_land.at[chunk], core_receive.at[chunk], sibling)
        mine[chunk] = (mine[chunk].astype(f32) + sibling_land[chunk].astype(f32)).astype(bf16)
        sent.append(
            push(
                mine.at[chunk, 0, :, 1 - column], side_land.at[chunk],
                side_send.at[chunk], side_receive.at[chunk], beside,
            )
        )
        for index, target in enumerate(across):
            sent.append(
                push(
                    mine.at[chunk, 1, lines_on[index]], line_land.at[chunk, index],
                    line_send.at[chunk, index], line_receive.at[chunk, index], target,
                )
            )

    def second(chunk):
        begin = chunk * 2 * step_rows
        arrived(side_land.at[chunk], side_receive.at[chunk], beside)
        own_sum[begin : begin + step_rows, :] = (
            mine[chunk, 0, line, column].astype(f32) + side_land[chunk, line].astype(f32)
        )
        for index, target in enumerate(across):
            at = lines_on[index]
            side_sum[chunk, index] = (
                mine[chunk, 0, at, column].astype(f32) + side_land[chunk, at].astype(f32)
            ).astype(bf16)
            sent.append(
                push(
                    side_sum.at[chunk, index], last_land.at[chunk, 1 + index],
                    last_send.at[chunk, 1 + index], last_receive.at[chunk, 1 + index], target,
                )
            )
        for index in range(len(across)):
            arrived(line_land.at[chunk, index], line_receive.at[chunk, index], across[-1 - index])
        for side, last in ((1 - column, False), (column, True)):
            both = mine[chunk, 1, line, side].astype(f32)
            for index in range(len(across)):
                both += line_land[chunk, index, side].astype(f32)
            if last:
                own_sum[begin + step_rows : begin + 2 * step_rows, :] = both
            else:
                line_part[chunk] = both.astype(bf16)
                sent.append(
                    push(
                        line_part.at[chunk], last_land.at[chunk, 0],
                        last_send.at[chunk, 0], last_receive.at[chunk, 0], beside,
                    )
                )

    def third(chunk):
        begin = chunk * 2 * step_rows
        for index in range(len(across)):
            arrived(last_land.at[chunk, 1 + index], last_receive.at[chunk, 1 + index], across[-1 - index])
            own_sum[begin : begin + step_rows, :] += last_land[chunk, 1 + index].astype(f32)
        arrived(last_land.at[chunk, 0], last_receive.at[chunk, 0], beside)
        own_sum[begin + step_rows : begin + 2 * step_rows, :] += last_land[chunk, 0].astype(f32)
        line_sum.begin([chunk])
        line_sum.gather(chunk)

    def tiles_in_plane():
        for peer in peers:
            arrived(tile_land.at[peer], bias_receive.at[peer], {"seq": peer})
        tile = tile_land[0]
        for source in range(1, size):
            tile += tile_land[source]
        tile_line[place] = tile
        for index, plane in enumerate(planes):
            sent.append(
                push(
                    tile_line.at[place], tile_line.at[place], plane_send.at[index], plane_receive.at[place],
                    {"batch": plane},
                )
            )

    squares = []

    def square(chunk):
        line_sum.spread(chunk)
        for row in range(chunk * 2 * step_rows, (chunk + 1) * 2 * step_rows, 16):
            value = total_ref[row : row + 16, :].astype(f32)
            value = value * value
            for begin in range(0, value.shape[1], LANES):
                block = value[:8, begin : begin + LANES] + value[8:, begin : begin + LANES]
                squares[:] = [block + squares[0]] if squares else [block]

    for time in range(count + 4):
        if time < count:
            pair(time)
        if 0 <= time - 1 < count:
            second(time - 1)
        if 0 <= time - 2 < count:
            third(time - 2)
        if time == count - 1:
            tiles_in_plane()
        if 0 <= time - 4 < count:
            square(time - 4)
    for plane in planes:
        arrived(tile_line.at[plane], plane_receive.at[plane], {"batch": plane})
    tile = tile_line[0]
    for source in range(1, lax.axis_size("batch")):
        tile += tile_line[source]
    bias_out[...] = tile
    head = jnp.sum(squares[0] + tile * tile, axis=0, keepdims=True)
    row8 = lax.broadcasted_iota(jnp.int32, (8, LANES), 0)
    tile_out[...] = jnp.where(row8 == 0, head, note_ref[...])
    note_out[spot] = tile_out[...]
    for index, peer in enumerate(peers):
        sent.append(
            push(tile_out, note_out.at[spot], note_send.at[index], note_receive.at[spot], {"seq": peer})
        )
    for peer in peers:
        arrived(note_out.at[peer], note_receive.at[peer], {"seq": peer})
    for copy in sent:
        copy.wait_send()
    line_sum.finish()


def reduce_gradients(grad, bias, note):
    size = lax.axis_size("seq")
    lines = lax.axis_size("batch")
    depth = grad.shape[2]
    width = depth // size
    rows = size // 4
    count = 4
    cut = width // count
    bf16 = jnp.bfloat16
    vmem = pl.BlockSpec(memory_space=pltpu.VMEM)
    dma = pltpu.SemaphoreType.DMA
    near = max(rows - 1, 1)
    grad = grad.reshape(2, rows, 2, 2, width, depth)
    return pl.pallas_call(
        functools.partial(reduce_kernel, count),
        in_specs=[pl.BlockSpec(memory_space=pl.ANY), vmem, vmem],
        out_specs=[vmem] * 3,
        out_shape=[
            jax.ShapeDtypeStruct((2 * width, depth), bf16),
            jax.ShapeDtypeStruct(bias.shape[1:], jnp.float32),
            jax.ShapeDtypeStruct((size,) + note.shape, jnp.float32),
        ],
        scratch_shapes=[
            pltpu.VMEM((count, 2, rows, 2, cut, depth), bf16),
            pltpu.VMEM((count, 2, rows, 2, cut, depth), bf16),
            pltpu.VMEM((count, rows, cut, depth), bf16),
            pltpu.VMEM((count, near, 2, cut, depth), bf16),
            pltpu.VMEM((count, near, cut, depth), bf16),
            pltpu.VMEM((count, cut, depth), bf16),
            pltpu.VMEM((count, rows, cut, depth), bf16),
            pltpu.VMEM((2 * width, depth), jnp.float32),
        ] + LineSum.scratch(count, 2 * width, depth) + [
            pltpu.VMEM((size,) + bias.shape[1:], jnp.float32),
            pltpu.VMEM((lines,) + bias.shape[1:], jnp.float32),
            pltpu.VMEM(note.shape, jnp.float32),
            dma((count,)),
            dma((count,)),
            dma((count,)),
            dma((count,)),
            dma((count,)),
            dma((count, near)),
            dma((count, near)),
            dma((count, rows)),
            dma((count, rows)),
            dma((size - 1,)),
            dma((size,)),
            dma((lines - 1,)),
            dma((lines,)),
            dma((size - 1,)),
            dma((size,)),
        ],
        compiler_params=pltpu.CompilerParams(
            collective_id=6, has_side_effects=True, vmem_limit_bytes=VMEM_BYTES
        ),
        name="reduce_gradients",
    )(grad, bias, note)


def update_kernel(
    total_ref, bias_sum, note_ref, trans_ref, mom1_ref, mom2_ref, trans_bias, mom1_bias, mom2_bias,
    first_out, second_out, weight_out, first_bias, second_bias, weight_bias, result_out,
):
    size = note_ref.shape[0]
    notes = note_ref[0]
    for source in range(1, size):
        notes += note_ref[source]
    sums = jnp.sum(notes, axis=-1, keepdims=True)
    norm = jnp.sqrt(sums[0:1]) / sums[2:3]
    row8 = lax.broadcasted_iota(jnp.int32, (8, LANES), 0)
    result_out[...] = jnp.where(row8 == 0, norm, sums)
    factor = jnp.minimum(1.0, clip_max / (norm + 1e-06)) / sums[2:3]
    cut = total_ref.shape[2]
    for chunk in range(total_ref.shape[0]):
        at = slice(chunk * cut, (chunk + 1) * cut)
        for probe in range(2):
            gradient = total_ref[chunk, probe].astype(jnp.float32) * factor
            first_out[probe, at, :], second_out[probe, at, :], weight_out[probe, at, :] = adam_update(
                trans_ref[probe, at, :], gradient, mom1_ref[probe, at, :], mom2_ref[probe, at, :]
            )
    gradient = bias_sum[0:2, 0 : trans_bias.shape[1]] * factor
    first_bias[...], second_bias[...], weight_bias[...] = adam_update(
        trans_bias[...], gradient, mom1_bias[...], mom2_bias[...]
    )


def update(total, bias_sum, notes, trans, mom1, mom2, trans_bias, mom1_bias, mom2_bias):
    _, width, depth = trans.shape
    count = 4
    cut = width // count
    f32 = jnp.float32
    whole = lambda part: pl.BlockSpec(part.shape, lambda i: (0,) * part.ndim)
    part = pl.BlockSpec((2, width, depth), lambda i: (0, 0, 0))
    result = pl.BlockSpec((8, LANES), lambda i: (0, 0))
    total = jnp.reshape(total, (count, 2, cut, depth))
    return pl.pallas_call(
        update_kernel,
        grid=(1,),
        in_specs=[
            pl.BlockSpec((count, 2, cut, depth), lambda i: (0, 0, 0, 0)), whole(bias_sum), whole(notes), part, part, part,
            whole(trans_bias), whole(mom1_bias), whole(mom2_bias),
        ],
        out_specs=[part, part, part, whole(trans_bias), whole(mom1_bias), whole(mom2_bias), result],
        out_shape=[jax.ShapeDtypeStruct(trans.shape, f32)] * 3
        + [jax.ShapeDtypeStruct(trans_bias.shape, f32)] * 3
        + [jax.ShapeDtypeStruct((8, LANES), f32)],
        compiler_params=pltpu.CompilerParams(vmem_limit_bytes=VMEM_BYTES),
        name="update",
    )(total, bias_sum, notes, trans, mom1, mom2, trans_bias, mom1_bias, mom2_bias)


def body(
    token_ids,
    pos_weights,
    pad_lengths,
    embed_in,
    w_qkv,
    w_out,
    w_fc,
    w_proj,
    norm_gains,
    layer_biases,
    wide_bias,
    unembed,
    trans_weight,
    trans_bias,
    mom1_weight,
    mom2_weight,
    mom1_bias,
    mom2_bias,
):
    bf16 = jnp.bfloat16
    f32 = jnp.float32
    tok_rows = token_ids.shape[1]
    width = embed_in.shape[1]
    vocab_rows = unembed.shape[0]
    n_seq = lax.axis_size("seq")
    n_batch = lax.axis_size("batch")
    batch_index = lax.axis_index("batch")
    seq_index = lax.axis_index("seq")
    head_count = width // HEAD_DIM
    plane_heads = head_count // n_batch
    plane_width = plane_heads * HEAD_DIM
    hidden_rows = w_proj.shape[0]

    half_rot = ROT // 2
    local_places = seq_index * tok_rows + jnp.arange(tok_rows, dtype=jnp.int32)
    frequency = 10000.0 ** (-2.0 * jnp.arange(half_rot, dtype=f32) / ROT)
    angles = local_places.astype(f32)[:, None] * frequency[None, :]
    cosine = jnp.cos(angles)
    sine = jnp.sin(angles)
    still = jnp.zeros((tok_rows, HEAD_DIM - ROT), f32)
    blank = jnp.zeros((tok_rows, half_rot), f32)
    turns = jnp.stack(
        [
            jnp.concatenate([cosine, cosine, still + 1.0], axis=1),
            jnp.concatenate([-sine, blank, still], axis=1),
            jnp.concatenate([blank, sine, still], axis=1),
        ]
    )
    turns = jnp.tile(turns, (1, 1, plane_heads))

    wide = wide_bias[None, :]
    if hidden_rows % LANES:
        fc_bias = lax.dynamic_slice_in_dim(
            wide_bias[3 * width :].reshape(n_seq, n_batch, hidden_rows), batch_index, 1, 1
        ).reshape(1, -1)
        wide = jnp.concatenate([wide, fc_bias], axis=1)
    own_rows = w_qkv.shape[0]
    joined_cut = jnp.transpose(w_qkv.reshape(own_rows, 3, n_batch, plane_width), (2, 0, 1, 3))
    fc_cut = jnp.transpose(w_fc.reshape(own_rows, n_seq, n_batch, hidden_rows), (2, 0, 1, 3))
    mixed_cut = jnp.concatenate(
        [joined_cut.reshape(n_batch, own_rows, -1), fc_cut.reshape(n_batch, own_rows, -1)], axis=2
    )
    tiles, stream_low, mixed_w, slab, out_own = front(
        token_ids, pos_weights, pad_lengths, embed_in, mixed_cut, trans_weight, w_out, trans_bias
    )
    states, translated, low1, probe_logits = layer(
        stream_low,
        mixed_w.reshape(width, -1),
        w_proj,
        out_own,
        slab,
        trans_weight,
        norm_gains,
        layer_biases,
        wide,
        turns,
        unembed,
    )
    first, second, peaks, sums_part, cross_part = vocab_forward(states, unembed, probe_logits)
    scales, note = statistics(tiles, peaks, sums_part, cross_part)
    grad, bias_grad = vocab_backward(
        first, second, scales, unembed, translated, stream_low, low1, norm_gains
    )
    first_w, second_w, new_w, first_b, second_b, new_b, result = update(
        *reduce_gradients(grad, bias_grad, note),
        trans_weight, mom1_weight, mom2_weight, trans_bias, mom1_bias, mom2_bias,
    )
    return (result[1, 0], result[2, 0], result[0, 0], first_w, second_w, new_w, first_b, second_b, new_b)


def solution(mesh):
    return jax.shard_map(
        body,
        mesh=mesh,
        in_specs=(
            P("batch", "seq"),
            P("batch", "seq"),
            P("batch"),
            P("batch", None),
            P(("seq", "batch"), None),
            P(("seq", "batch"), None),
            P(("seq", "batch"), None),
            P(("seq", "batch"), None),
            P(),
            P(),
            P(),
            P("batch", None),
            P(None, "seq", None),
            P(None, "seq"),
            P(None, "seq", None),
            P(None, "seq", None),
            P(None, "seq"),
            P(None, "seq"),
        ),
        out_specs=(
            P(),
            P(),
            P(),
            P(None, "seq", None),
            P(None, "seq", None),
            P(None, "seq", None),
            P(None, "seq"),
            P(None, "seq"),
            P(None, "seq"),
        ),
        check_vma=False,
    )
```

```python
import functools
import math

import jax
import jax.numpy as jnp
from jax import lax
from jax.experimental import pallas as pl
from jax.experimental.pallas import tpu as pltpu
from jax.sharding import PartitionSpec as P

HEAD_DIM = 64
ROT = 16
STEP = 10


VOCAB_TILE = 1280
LANES = 128
NEGATIVE = -1e30
VMEM_BYTES = 62 * 1024 * 1024
norm_eps = 1e-05
clip_max = 0.001
beta_one = 0.9
beta_two = 0.999
learn_rate = 0.03
decay_rate = 0.01
adam_eps = 1e-08


def norm_back(values, upstream, gain_row):
    average = jnp.mean(values, axis=-1, keepdims=True)
    centered = values - average
    variance = jnp.mean(centered * centered, axis=-1, keepdims=True)
    inverse = lax.rsqrt(variance + norm_eps)
    unit = centered * inverse
    scaled = upstream * gain_row
    return (
        scaled
        - jnp.mean(scaled, axis=-1, keepdims=True)
        - unit * jnp.mean(scaled * unit, axis=-1, keepdims=True)
    ) * inverse


def adam_update(weight, gradient, earlier, later):
    earlier = beta_one * earlier + (1.0 - beta_one) * gradient
    later = beta_two * later + (1.0 - beta_two) * gradient * gradient
    update = (
        earlier / (1.0 - beta_one**STEP) / (jnp.sqrt(later / (1.0 - beta_two**STEP)) + adam_eps)
    )
    return (earlier, later, weight * (1.0 - learn_rate * decay_rate) - learn_rate * update)


def forward_kernel(vocab, states_ref, table_ref, probe0_ref, probe1_ref, first_ref, second_ref, peaks_ref, sums_ref, cross_ref, turned, left, right, peak, keep_first, keep_second, sems):
    step = pl.program_id(0)
    steps = pl.num_programs(0) - 1
    width = table_ref.shape[0]
    half = left.shape[1] // 2
    group = 16
    given = (probe0_ref, probe1_ref)
    last = vocab - (pl.cdiv(vocab, width) - 1) * width
    row = lax.broadcasted_iota(jnp.int32, (group, LANES), 0)

    def reset(part):
        span = slice(part * half, (part + 1) * half)
        peak[:, span] = jnp.full((8, half), NEGATIVE, jnp.float32)
        sums_ref[:, :, span] = jnp.zeros((3, 8, half), jnp.float32)
        cross_ref[:, :, span] = jnp.zeros((2, 8, half), jnp.float32)

    @pl.when(step == 0)
    def _():
        reset(0)
        for state in range(2):
            for part in range(2):
                turned[part, :, state * half : (state + 1) * half] = jnp.transpose(
                    states_ref[2 * state, part * half : (part + 1) * half, :]
                )

    @pl.when(step <= 1)
    def _():
        reset(1)

    def multiply(part, target, state, cut):
        place = slice(state * half, (state + 1) * half)
        at = slice(cut * width // 5, (cut + 1) * width // 5)
        target[at, place] = jnp.dot(
            table_ref[at, :], turned[part, :, place], preferred_element_type=jnp.float32
        )

    def units(part, source, target, tile):
        limit = vocab - tile * width
        blocks = width // group
        result = []
        for lanes in range(half // LANES):
            span = slice(part * half + lanes * LANES, part * half + (lanes + 1) * LANES)
            local = slice(lanes * LANES, (lanes + 1) * LANES)
            held = {}

            def logits(state, block, lanes=lanes):
                at = slice(block * group, (block + 1) * group)
                if state == 1:
                    value = given[part][0, at, lanes * LANES : (lanes + 1) * LANES]
                else:
                    begin = state // 2 * half + lanes * LANES
                    value = source[at, begin : begin + LANES]
                if (block + 1) * group > last:
                    value = jnp.where(row + block * group < limit, value, NEGATIVE)
                return value

            def tops(span=span, held=held, logits=logits):
                held["top"], held["sum"], held["cross"] = [], [], []
                for state in range(3):
                    top = logits(state, 0)
                    for block in range(1, blocks):
                        top = jnp.maximum(top, logits(state, block))
                    before = peak[state : state + 1, span]
                    now = jnp.maximum(before, jnp.max(top, axis=0, keepdims=True))
                    peak[state : state + 1, span] = now
                    peaks_ref[pl.ds(tile, 1), state, span] = now
                    fade = jnp.exp(before - now)
                    held["top"].append(jnp.broadcast_to(now, (group, LANES)))
                    held["sum"].append(sums_ref[state, :, span] * fade)
                    if state == 0:
                        held["cross"] = [cross_ref[other, :, span] * fade for other in range(2)]

            def fold(value):
                return value[:8] + value[8:]

            def powers(begin, end, held=held, logits=logits, local=local, fold=fold):
                for block in range(begin, end):
                    place = slice(block * group, (block + 1) * group)
                    base = logits(0, block)
                    base_exp = jnp.exp(base - held["top"][0])
                    held["sum"][0] += fold(base_exp)
                    target[0, place, local] = base_exp.astype(jnp.bfloat16)
                    for state in range(1, 3):
                        value = logits(state, block)
                        value_exp = jnp.exp(value - held["top"][state])
                        held["sum"][state] += fold(value_exp)
                        target[state, place, local] = value_exp.astype(jnp.bfloat16)
                        held["cross"][state - 1] += fold(base_exp * (base - value))

            def finish(span=span, held=held):
                for state in range(3):
                    sums_ref[state, :, span] = held["sum"][state]
                for other in range(2):
                    cross_ref[other, :, span] = held["cross"][other]

            result.append(tops)
            cuts = 10
            for cut in range(cuts):
                result.append(
                    functools.partial(powers, cut * blocks // cuts, (cut + 1) * blocks // cuts)
                )
            result.append(finish)
        return result

    def stage(part, target, work):
        done = 0
        for piece in range(10):
            multiply(part, target, piece // 5, piece % 5)
            upto = (piece + 1) * len(work) // 10
            for unit in work[done:upto]:
                unit()
            done = upto

    before = jnp.maximum(step - 1, 0)

    def first_copy(tile):
        return pltpu.make_async_copy(keep_first, first_ref.at[tile], sems.at[0])

    def second_copy(tile):
        return pltpu.make_async_copy(keep_second, second_ref.at[tile], sems.at[1])

    @pl.when(step >= 2)
    def _():
        second_copy(before).wait()

    @pl.when(step < steps)
    def _():
        stage(0, left, units(1, right, keep_second, before))

    @pl.when(step == steps)
    def _():
        for unit in units(1, right, keep_second, before):
            unit()

    @pl.when(step >= 1)
    def _():
        second_copy(before).start()
        first_copy(before).wait()

    @pl.when(step < steps)
    def _():
        stage(1, right, units(0, left, keep_first, step))
        first_copy(step).start()

    @pl.when(step == steps)
    def _():
        second_copy(before).wait()


def vocab_forward(states, table, given):
    _, rows, depth = states.shape
    vocab = table.shape[0]
    tiles = pl.cdiv(vocab, VOCAB_TILE)
    half = rows // 2
    kept = jax.ShapeDtypeStruct((tiles, 3, VOCAB_TILE, half), jnp.bfloat16)
    whole = lambda *shape: pl.BlockSpec(shape, lambda i: (0,) * len(shape))
    return pl.pallas_call(
        functools.partial(forward_kernel, vocab),
        grid=(tiles + 1,),
        in_specs=[
            whole(3, rows, depth),
            pl.BlockSpec((VOCAB_TILE, depth), lambda i: (jnp.minimum(i, tiles - 1), 0)),
            pl.BlockSpec((1, VOCAB_TILE, half), lambda i: (jnp.minimum(i, tiles - 1), 0, 0)),
            pl.BlockSpec((1, VOCAB_TILE, half), lambda i: (jnp.maximum(i - 1, 0), 0, 1)),
        ],
        out_specs=[
            pl.BlockSpec(memory_space=pl.ANY),
            pl.BlockSpec(memory_space=pl.ANY),
            whole(tiles, 3, rows),
            whole(3, 8, rows),
            whole(2, 8, rows),
        ],
        out_shape=[
            kept,
            kept,
            jax.ShapeDtypeStruct((tiles, 3, rows), jnp.float32),
            jax.ShapeDtypeStruct((3, 8, rows), jnp.float32),
            jax.ShapeDtypeStruct((2, 8, rows), jnp.float32),
        ],
        scratch_shapes=[
            pltpu.VMEM((2, depth, 2 * half), jnp.bfloat16),
            pltpu.VMEM((VOCAB_TILE, 2 * half), jnp.float32),
            pltpu.VMEM((VOCAB_TILE, 2 * half), jnp.float32),
            pltpu.VMEM((8, rows), jnp.float32),
            pltpu.VMEM((3, VOCAB_TILE, half), jnp.bfloat16),
            pltpu.VMEM((3, VOCAB_TILE, half), jnp.bfloat16),
            pltpu.SemaphoreType.DMA((2,)),
        ],
        compiler_params=pltpu.CompilerParams(vmem_limit_bytes=VMEM_BYTES),
        cost_estimate=pl.CostEstimate(
            flops=4 * rows * depth * vocab,
            bytes_accessed=2 * vocab * (depth + 5 * rows),
            transcendentals=3 * rows * vocab,
        ),
        name="vocab_forward",
    )(states, table, given, given)


def backward_kernel(
    vocab, first_ref, second_ref, scales_ref, table_ref, moved_ref, low0_ref, low1_ref, gain_ref,
    grad_ref, bias_ref, out_ref, left, right, tail, delta, turned,
):
    step = pl.program_id(0)
    tiles = pl.num_programs(0) - 1
    width, depth = table_ref.shape
    half = first_ref.shape[3]
    piece = 256
    last = vocab - (pl.cdiv(vocab, width) - 1) * width
    whole = last // piece * piece
    tile = jnp.maximum(step - 1, 0)
    limit = vocab - tile * width

    def units(part, source, target, index):
        result = []

        def turn(lanes, block):
            begin = part * half + lanes * LANES
            span = slice(begin, begin + LANES)
            place = slice(block * LANES, (block + 1) * LANES)
            local = slice(lanes * LANES, (lanes + 1) * LANES)
            factors = scales_ref[pl.ds(index, 1), :, span][0]
            base = source[0, 0, place, local].astype(jnp.float32) * factors[0:1]
            for state in range(1, 3):
                value = source[0, state, place, local].astype(jnp.float32) * factors[state : state + 1]
                first = (state - 1) * half + lanes * LANES
                target[first : first + LANES, place] = jnp.transpose(
                    (value - base).astype(jnp.bfloat16)
                )

        for lanes in range(half // LANES):
            for block in range(width // LANES):
                result.append(functools.partial(turn, lanes, block))
        return result

    def multiply(part, source, start):
        place = slice(start, start + piece)
        span = slice(part * half, (part + 1) * half)
        partial = jnp.dot(source[:, whole:], tail[:, place], preferred_element_type=jnp.float32)
        if whole > 0:
            partial += jnp.dot(
                source[:, :whole], table_ref[:whole, place], preferred_element_type=jnp.float32
            )
        for probe in range(2):
            out_ref[probe, span, place] += partial[probe * half : (probe + 1) * half]

    def stage(part, source, work):
        done = 0
        pieces = depth // piece
        for index in range(pieces):
            multiply(part, source, index * piece)
            upto = (index + 1) * len(work) // pieces
            for unit in work[done:upto]:
                unit()
            done = upto

    ahead = jnp.minimum(step, tiles - 1)

    @pl.when(step == 0)
    def _():
        out_ref[...] = jnp.zeros_like(out_ref)
        for unit in units(0, first_ref, left, ahead):
            unit()

    @pl.when(step > 0)
    def _():
        below = lax.broadcasted_iota(jnp.int32, (width - whole, depth), 0) + whole < limit
        tail[...] = jnp.where(below, table_ref[whole:, :], jnp.zeros((), tail.dtype))
        stage(0, left, units(1, second_ref, right, tile))
        stage(1, right, units(0, first_ref, left, ahead))

    @pl.when(step == tiles)
    def _():
        rows = out_ref.shape[1]
        chunk = 32
        block = 256
        for probe in range(2):
            low_ref = (low0_ref, low1_ref)[probe]

            def back(index, total, probe=probe):
                at = pl.ds(pl.multiple_of(index * chunk, chunk), chunk)
                value = norm_back(moved_ref[probe, at, :], out_ref[probe, at, :], gain_ref[2:3, :])
                delta[at, :] = value.astype(jnp.bfloat16)
                return total + jnp.sum(value, axis=0, keepdims=True)

            summed = lax.fori_loop(
                0, rows // chunk, back, jnp.zeros((1, depth), jnp.float32), unroll=4
            )
            if probe == 0:
                bias_ref[...] = jnp.zeros_like(bias_ref)
            own = depth // bias_ref.shape[0]
            for part in range(bias_ref.shape[0]):
                bias_ref[part, probe : probe + 1, 0:own] = summed[:, part * own : (part + 1) * own]
            turned[...] = jnp.transpose(low_ref[...])
            for begin in range(0, depth, block):
                grad_ref[probe, begin : begin + block, :] = jnp.dot(
                    turned[begin : begin + block, :], delta[...], preferred_element_type=jnp.float32
                ).astype(jnp.bfloat16)


def vocab_backward(first, second, scales, table, moved, low0, low1, gains):
    tiles, _, _, half = first.shape
    vocab, depth = table.shape
    rows = 2 * half
    last = vocab - (tiles - 1) * VOCAB_TILE
    block = (1, 3, VOCAB_TILE, half)
    whole = lambda *shape: pl.BlockSpec(shape, lambda i: (0,) * len(shape))
    return pl.pallas_call(
        functools.partial(backward_kernel, vocab),
        grid=(tiles + 1,),
        in_specs=[
            pl.BlockSpec(block, lambda i: (jnp.minimum(i, tiles - 1), 0, 0, 0)),
            pl.BlockSpec(block, lambda i: (jnp.maximum(i - 1, 0), 0, 0, 0)),
            whole(tiles, 3, rows),
            pl.BlockSpec((VOCAB_TILE, depth), lambda i: (jnp.maximum(i - 1, 0), 0)),
            whole(2, rows, depth),
            whole(rows, depth),
            whole(rows, depth),
            whole(*gains.shape),
        ],
        out_specs=[whole(2, depth, depth), whole(lax.axis_size("seq"), 8, LANES)],
        out_shape=[
            jax.ShapeDtypeStruct((2, depth, depth), jnp.bfloat16),
            jax.ShapeDtypeStruct((lax.axis_size("seq"), 8, LANES), jnp.float32),
        ],
        scratch_shapes=[
            pltpu.VMEM((2, rows, depth), jnp.float32),
            pltpu.VMEM((2 * half, VOCAB_TILE), jnp.bfloat16),
            pltpu.VMEM((2 * half, VOCAB_TILE), jnp.bfloat16),
            pltpu.VMEM((VOCAB_TILE - last // 256 * 256, depth), jnp.bfloat16),
            pltpu.VMEM((rows, depth), jnp.bfloat16),
            pltpu.VMEM((depth, rows), jnp.bfloat16),
        ],
        compiler_params=pltpu.CompilerParams(vmem_limit_bytes=VMEM_BYTES),
        cost_estimate=pl.CostEstimate(
            flops=4 * rows * depth * (vocab + depth),
            bytes_accessed=2 * vocab * (depth + 3 * rows),
            transcendentals=0,
        ),
        name="vocab_backward",
    )(first, second, scales, table, moved, low0, low1, gains)


def plane_place(place):
    core = lax.rem(place, 2)
    return core, lax.rem(place // 2, 2), place // 4


def plane_index(core, column, line):
    return (line * 2 + column) * 2 + core


def greet(partners):
    barrier = pltpu.get_barrier_semaphore()
    for partner in partners:
        pl.semaphore_signal(barrier, inc=1, device_id=partner, device_id_type=pl.DeviceIdType.MESH)
    pl.semaphore_wait(barrier, len(partners))


def push(source, target, send, receive, partner):
    copy = pltpu.make_async_remote_copy(
        src_ref=source,
        dst_ref=target,
        send_sem=send,
        recv_sem=receive,
        device_id=partner,
        device_id_type=pl.DeviceIdType.MESH,
    )
    copy.start()
    return copy


def arrived(target, receive, partner):
    pltpu.make_async_remote_copy(
        src_ref=target,
        dst_ref=target,
        send_sem=receive,
        recv_sem=receive,
        device_id=partner,
        device_id_type=pl.DeviceIdType.MESH,
    ).wait_recv()


def departed(source, send, partner):
    pltpu.make_async_remote_copy(
        src_ref=source,
        dst_ref=source,
        send_sem=send,
        recv_sem=send,
        device_id=partner,
        device_id_type=pl.DeviceIdType.MESH,
    ).wait_send()


class LineSum:
    def __init__(self, count, halves, own, land, held, total, inner_sem, outer_sem, receive_sem):
        lines = lax.axis_size("batch")
        rows, depth = held.shape
        self.blocks = count // halves
        place = lax.axis_index("batch")
        near = place < lines // 2
        self.count, self.size, self.columns = count, rows // self.blocks, depth // halves
        self.own, self.land, self.held, self.total = own, land, held, total
        self.inner_sem, self.outer_sem, self.receive_sem = inner_sem, outer_sem, receive_sem
        self.middle = (place == lines // 2 - 1) | (place == lines // 2)
        self.end = (place == 0) | (place == lines - 1)
        self.inner = {"batch": jnp.where(near, place + 1, place - 1)}
        self.outer = {"batch": jnp.where(near, place - 1, place + 1)}
        self.slot = jnp.where(self.middle, 1, 0)

    def rows(self, index):
        return (
            pl.ds(index % self.blocks * self.size, self.size),
            pl.ds(index // self.blocks * self.columns, self.columns),
        )

    def send_in(self, index):
        rows = self.rows(index)
        push(
            self.held.at[*rows],
            self.land.at[self.slot, *rows],
            self.inner_sem.at[index],
            self.receive_sem.at[self.slot, index],
            self.inner,
        )

    def begin(self, indices):
        @pl.when(self.end)
        def _():
            for index in indices:
                rows = self.rows(index)
                self.held[rows] = self.own(rows).astype(jnp.bfloat16)
                self.send_in(index)

    def gather(self, index):
        rows = self.rows(index)

        @pl.when(jnp.logical_not(self.end))
        def _():
            arrived(self.land.at[0, *rows], self.receive_sem.at[0, index], self.outer)
            own = self.own(rows).astype(jnp.float32)
            self.held[rows] = (own + self.land[(0, *rows)].astype(jnp.float32)).astype(jnp.bfloat16)
            self.send_in(index)

    def spread(self, index):
        rows = self.rows(index)

        @pl.when(self.middle)
        def _():
            arrived(self.land.at[1, *rows], self.receive_sem.at[1, index], self.inner)
            both = self.held[rows].astype(jnp.float32) + self.land[(1, *rows)].astype(jnp.float32)
            self.total[rows] = both.astype(jnp.bfloat16)

        @pl.when(jnp.logical_not(self.middle))
        def _():
            arrived(self.total.at[*rows], self.receive_sem.at[2, index], self.inner)

        @pl.when(jnp.logical_not(self.end))
        def _():
            push(
                self.total.at[*rows],
                self.total.at[*rows],
                self.outer_sem.at[index],
                self.receive_sem.at[2, index],
                self.outer,
            )

    def run(self, lag, todo=(), done=0):
        todo = list(todo)
        for index in range(done, self.count + lag):
            if todo:
                todo.pop(0)()
            if index < self.count:
                self.gather(index)
            if index >= lag and index - lag >= done - lag:
                self.spread(index - lag)
        for work in todo:
            work()

    def finish(self):
        for index in range(self.count):
            rows = self.rows(index)
            departed(self.held.at[*rows], self.inner_sem.at[index], self.inner)

            @pl.when(jnp.logical_not(self.end))
            def _(rows=rows, index=index):
                departed(self.total.at[*rows], self.outer_sem.at[index], self.outer)

    @staticmethod
    def scratch(count, rows, depth):
        return [
            pltpu.VMEM((2, rows, depth), jnp.bfloat16),
            pltpu.VMEM((rows, depth), jnp.bfloat16),
            pltpu.SemaphoreType.DMA((count,)),
            pltpu.SemaphoreType.DMA((count,)),
            pltpu.SemaphoreType.DMA((3, count)),
        ]


class PlaneGather:
    def __init__(self, views, send_sem, receive_sem):
        self.views, self.send_sem, self.receive_sem = views, send_sem, receive_sem
        self.size = lax.axis_size("seq")
        self.spot = lax.axis_index("seq")
        core, column, line = self.where = plane_place(self.spot)
        self.rows = self.size // 4
        self.beside = plane_index(core, 1 - column, line)
        self.sibling = plane_index(1 - core, column, line)
        lines = [lax.rem(line + step, self.rows) for step in range(1, self.rows)]
        self.across = [plane_index(core, column, at) for at in lines]
        self.corners = [plane_index(core, 1 - column, at) for at in lines]
        self.started = []
        self.used = [0] * len(views)

    def send(self, array, half, slot, target):
        view = self.views[array](half, slot)
        index = self.used[array]
        self.used[array] += 1
        self.started.append(
            push(
                view, view, self.send_sem.at[array, index], self.receive_sem.at[array, 1 if half == 1 else 0, slot],
                {"seq": target},
            )
        )

    def wait(self, array, half, slot):
        arrived(
            self.views[array](half, slot), self.receive_sem.at[array, 1 if half == 1 else 0, slot], {"seq": slot}
        )

    def own(self, array):
        for target in [self.beside] + self.across + [self.sibling]:
            self.send(array, None, self.spot, target)

    def relay_side(self, array):
        self.wait(array, None, self.beside)
        for target in self.across:
            self.send(array, 0, self.beside, target)
        for source in self.across:
            self.wait(array, None, source)
            self.send(array, 1, source, self.beside)
        for source in [self.beside] + self.across:
            self.send(array, None, source, self.sibling)

    def relay_core(self, array):
        for source in self.corners:
            for half in range(2):
                self.wait(array, half, source)
            self.send(array, None, source, self.sibling)

    def receive_core(self, array):
        core, _, line = self.where
        for step in range(self.rows):
            for side in range(2):
                self.wait(array, None, plane_index(1 - core, side, lax.rem(line + step, self.rows)))

    def finish(self):
        for copy in self.started:
            copy.wait_send()

    @staticmethod
    def scratch(arrays):
        size = lax.axis_size("seq")
        dma = pltpu.SemaphoreType.DMA
        return [dma((arrays, 2 * size)), dma((arrays, 2, size))]


def others(axis):
    size = lax.axis_size(axis)
    place = lax.axis_index(axis)
    return [lax.rem(place + step, size) for step in range(1, size)]


def front_kernel(
    count,
    ids_ref, weights_ref, padding_ref, table_ref, mixed_ref, trans_ref, out_ref, trans_bias_ref,
    tiles_out, stream_ref, mixed_out, slab_out, out_out,
    table, column_ids, chosen, picked, tile_ref, slab,
    land, held, inner_sem, outer_sem, receive_sem,
    local_sem, table_sem, tile_send, tile_receive, cross_send, cross_receive, plane_send, plane_receive,
):
    lines = lax.axis_size("batch")
    place = lax.axis_index("batch")
    size = lax.axis_size("seq")
    spot = lax.axis_index("seq")
    planes = others("batch")
    peers = others("seq")
    total_rows, depth = stream_ref.shape
    tokens = tile_ref.shape[1]
    vocab = table_ref.shape[0]
    own_width = trans_ref.shape[1]
    number = spot * lines + place
    goal = {"seq": lax.rem(number, size), "batch": number // size}
    wanted = place * size + spot
    origin = {"seq": wanted // lines, "batch": lax.rem(wanted, lines)}
    stays = number == wanted
    width = VOCAB_TILE
    parts = 2
    cuts = table.shape[0] // width

    def mixed_view(half, slot):
        if half is None:
            return mixed_out.at[slot]
        return mixed_out.at[slot, pl.ds(half * (lines // 2), lines // 2)]

    def slab_view(half, slot):
        if half is None:
            return slab_out.at[slot]
        return slab_out.at[slot, :, pl.ds(half * (depth // 2), depth // 2)]

    plane = PlaneGather([mixed_view, slab_view], plane_send, plane_receive)
    table_copies = [
        pltpu.make_async_copy(
            table_ref.at[pl.ds(cut * width, min(width, vocab - cut * width))],
            table.at[pl.ds(cut * width, min(width, vocab - cut * width))],
            table_sem.at[cut],
        )
        for cut in range(cuts)
    ]
    for copy in table_copies:
        copy.start()
    if table.shape[0] > vocab:
        table[vocab:, :] = jnp.zeros((table.shape[0] - vocab, depth), table.dtype)
    bias = trans_bias_ref[...]
    bias_high = bias.astype(jnp.bfloat16)
    bias_low = (bias - bias_high.astype(jnp.float32)).astype(jnp.bfloat16)
    slab[0:own_width, :] = trans_ref[0].astype(jnp.bfloat16)
    slab[own_width:, :] = jnp.zeros((16, depth), jnp.bfloat16)
    slab[own_width : own_width + 2, 0:own_width] = bias_high
    slab[own_width + 8 : own_width + 10, 0:own_width] = bias_low
    tile_ref[...] = jnp.zeros_like(tile_ref)
    tile_ref[0:1, :] = ids_ref[...]
    tile_ref[1:2, :] = weights_ref[...]
    tile_ref[2:3, :] = jnp.full((1, tokens), padding_ref[0], jnp.int32)
    tiles_out[place] = tile_ref[...]
    slab_copy = pltpu.make_async_copy(slab, slab_out.at[spot], local_sem.at[0])
    slab_copy.start()
    mixed_copy = pltpu.make_async_copy(mixed_ref.at[place], mixed_out.at[spot, place], local_sem.at[1])
    mixed_copy.start()
    out_copy = pltpu.make_async_copy(out_ref, out_out, local_sem.at[2])

    @pl.when(stays)
    def _():
        out_copy.start()

    barrier = pltpu.get_barrier_semaphore()
    for partner in [{"batch": other} for other in planes] + [{"seq": peer} for peer in peers]:
        pl.semaphore_signal(barrier, inc=1, device_id=partner, device_id_type=pl.DeviceIdType.MESH)

    @pl.when(jnp.logical_not(stays))
    def _():
        pl.semaphore_signal(barrier, inc=1, device_id=origin, device_id_type=pl.DeviceIdType.MESH)

    pl.semaphore_wait(barrier, jnp.where(stays, 0, 1) + len(planes) + len(peers))

    sent = [
        push(tile_ref, tiles_out.at[place], tile_send.at[index], tile_receive.at[place], {"batch": other})
        for index, other in enumerate(planes)
    ]
    sent += [
        push(
            mixed_ref.at[other], mixed_out.at[spot, place], cross_send.at[index], cross_receive.at[place],
            {"batch": other},
        )
        for index, other in enumerate(planes)
    ]
    slab_copy.wait()
    plane.own(1)
    out_push = pltpu.make_async_remote_copy(
        src_ref=out_ref, dst_ref=out_out, send_sem=local_sem.at[3],
        recv_sem=local_sem.at[4], device_id=goal, device_id_type=pl.DeviceIdType.MESH,
    )

    @pl.when(jnp.logical_not(stays))
    def _():
        out_push.start()

    for other in planes:
        arrived(tiles_out.at[other], tile_receive.at[other], {"batch": other})
    for sequence in range(lines):
        turned = jnp.transpose(tiles_out[sequence].astype(jnp.float32))
        column_ids[sequence * tokens : (sequence + 1) * tokens, :] = jnp.broadcast_to(
            turned[:, 0:1] - (place * vocab).astype(jnp.float32), (tokens, LANES)
        )
    lane = lax.broadcasted_iota(jnp.int32, (total_rows, LANES), 1)

    def choose(cut):
        for block in range(width // LANES):
            begin = cut * width + block * LANES
            chosen[:, begin : begin + LANES] = jnp.where(
                column_ids[...] == (lane + begin).astype(jnp.float32), 1.0, 0.0
            ).astype(jnp.bfloat16)

    def look(part, cut):
        at = slice(part * (depth // parts), (part + 1) * (depth // parts))
        span = slice(cut * width, (cut + 1) * width)
        if part == 0:
            table_copies[cut].wait()
        found = jnp.dot(chosen[:, span], table[span, at], preferred_element_type=jnp.float32)
        if cut == 0:
            picked[:, at] = found
        else:
            picked[:, at] += found
        if part == 0 and cut + 1 < cuts:
            choose(cut + 1)

    line_sum = LineSum(
        count, parts, lambda at: picked[at],
        land, held, stream_ref, inner_sem, outer_sem, receive_sem,
    )

    def turn():
        mixed_copy.wait()
        for other in planes:
            arrived(mixed_out.at[spot, other], cross_receive.at[other], {"batch": other})
        plane.own(0)

    def turn_out():
        @pl.when(stays)
        def _():
            out_copy.wait()

        @pl.when(jnp.logical_not(stays))
        def _():
            arrived(out_out, local_sem.at[4], origin)

    between = {
        (0, 0): lambda: choose(0),
        (0, 4): lambda: turn(),
        (0, 6): lambda: plane.relay_side(1),
        (1, 3): lambda: line_sum.gather(0),
        (1, 4): lambda: (line_sum.gather(1), plane.relay_core(1)),
        (1, 6): lambda: (line_sum.gather(2), line_sum.spread(0)),
        (1, 8): lambda: (line_sum.gather(3), line_sum.spread(1)),
        (1, 9): lambda: turn_out(),
    }
    for part in range(parts):
        for cut in range(cuts):
            if (part, cut) in between:
                between.pop((part, cut))()
            look(part, cut)
        for work in [between.pop(key) for key in list(between) if key[0] == part]:
            work()
        line_sum.begin(range(part * count // parts, (part + 1) * count // parts))
    todo = [
        lambda: plane.relay_side(0),
        lambda: plane.receive_core(1),
        lambda: None,
        lambda: None,
        lambda: plane.relay_core(0),
        lambda: None,
        lambda: plane.receive_core(0),
    ]
    line_sum.run(2, todo, 4)
    for copy in sent:
        copy.wait_send()

    @pl.when(jnp.logical_not(stays))
    def _():
        out_push.wait_send()

    plane.finish()
    line_sum.finish()


def front(ids, weights, padding, table, mixed, trans, out, bias):
    size = lax.axis_size("seq")
    lines = lax.axis_size("batch")
    vocab, depth = table.shape
    tokens = ids.shape[1]
    rows = lines * tokens
    count = 8
    vmem = pl.BlockSpec(memory_space=pltpu.VMEM)
    smem = pl.BlockSpec(memory_space=pltpu.SMEM)
    anywhere = pl.BlockSpec(memory_space=pl.ANY)
    dma = pltpu.SemaphoreType.DMA
    bf16 = jnp.bfloat16
    padded = pl.cdiv(vocab, VOCAB_TILE) * VOCAB_TILE
    slab_rows = trans.shape[1] + 16
    return pl.pallas_call(
        functools.partial(front_kernel, count),
        in_specs=[vmem, vmem, smem, anywhere, anywhere, vmem, anywhere, vmem],
        out_specs=[vmem, vmem, anywhere, anywhere, anywhere],
        out_shape=[
            jax.ShapeDtypeStruct((lines, 8, tokens), jnp.int32),
            jax.ShapeDtypeStruct((rows, depth), bf16),
            jax.ShapeDtypeStruct((size,) + mixed.shape, bf16),
            jax.ShapeDtypeStruct((size, slab_rows, depth), bf16),
            jax.ShapeDtypeStruct(out.shape, bf16),
        ],
        scratch_shapes=[
            pltpu.VMEM((padded, depth), bf16),
            pltpu.VMEM((rows, LANES), jnp.float32),
            pltpu.VMEM((rows, padded), bf16),
            pltpu.VMEM((rows, depth), jnp.float32),
            pltpu.VMEM((8, tokens), jnp.int32),
            pltpu.VMEM((slab_rows, depth), bf16),
        ] + LineSum.scratch(count, rows, depth) + [
            dma((5,)),
            dma((padded // VOCAB_TILE,)),
            dma((lines - 1,)),
            dma((lines,)),
            dma((lines - 1,)),
            dma((lines,)),
        ] + PlaneGather.scratch(2),
        compiler_params=pltpu.CompilerParams(
            collective_id=1, has_side_effects=True, vmem_limit_bytes=VMEM_BYTES
        ),
        name="front",
    )(ids, weights, padding, table, mixed, trans, out, bias)


def row_norm(values):
    average = jnp.mean(values, axis=-1, keepdims=True)
    centered = values - average
    variance = jnp.mean(centered * centered, axis=-1, keepdims=True)
    return centered * lax.rsqrt(variance + norm_eps)


def layer_kernel(
    count, heads,
    stream_ref, mixed_ref, proj_ref, out_ref, slab_ref, next_ref,
    gains_ref, offsets_ref, wide_ref, turns_ref, table_ref,
    states_ref, moved_ref, low_ref, logits_ref,
    slab_all, second_trans, trans_bias, fc_bias, hidden, x_attn, x_mlp, spread, gathered, mixed, returned, part,
    land, inner_sem, outer_sem, receive_sem,
    tables, turned, logits, table_sem, logits_sem,
    local_sem, heads_send, heads_receive, rows_send, rows_receive, plane_send, plane_receive,
):
    f32 = jnp.float32
    bf16 = jnp.bfloat16
    lines = lax.axis_size("batch")
    place = lax.axis_index("batch")
    size = lax.axis_size("seq")
    spot = lax.axis_index("seq")
    planes = others("batch")
    peers = others("seq")
    rows, depth = stream_ref.shape
    tokens = rows // lines
    hidden_rows = proj_ref.shape[0]
    fc_width = size * hidden_rows
    plane_width = (mixed_ref.shape[1] - fc_width) // 3
    columns = spread.shape[3]
    groups = plane_width // columns
    head_dim = columns // heads
    own_width = next_ref.shape[1]
    step_rows = 32
    wide_rows = 2 * tokens
    vocab = table_ref.shape[0]
    cut_rows = tables.shape[1]
    cuts = pl.cdiv(vocab, cut_rows)
    sizes = [min(cut_rows, vocab - cut * cut_rows) for cut in range(cuts)]
    loads = [
        pltpu.make_async_copy(
            table_ref.at[pl.ds(cut * cut_rows, sizes[cut])],
            tables.at[cut % 2, pl.ds(0, sizes[cut])],
            table_sem.at[cut % 2],
        )
        for cut in range(cuts)
    ]
    stores = [
        pltpu.make_async_copy(
            logits.at[cut % 2],
            logits_ref.at[cut * cut_rows // VOCAB_TILE, pl.ds(cut * cut_rows % VOCAB_TILE, cut_rows)],
            logits_sem.at[cut % 2],
        )
        for cut in range(cuts)
    ]
    loads[0].start()
    loads[1].start()

    def probe_logits(cut):
        loads[cut].wait()
        if cut >= 2:
            stores[cut - 2].wait()
        logits[cut % 2] = jnp.dot(tables[cut % 2], turned[...], preferred_element_type=f32)
        stores[cut].start()
        if cut + 2 < cuts:
            loads[cut + 2].start()

    spans = (slab_all, second_trans)
    slab_all[spot, 0:hidden_rows, :] = proj_ref[...]
    slab_all[spot, hidden_rows:, :] = out_ref[...]
    second_trans[spot] = next_ref[1].astype(bf16)
    greet([{"batch": plane} for plane in planes] + [{"seq": peer} for peer in peers])
    sent = []

    def view(array):
        def of(half, slot):
            if half is None:
                return spans[array].at[slot]
            return spans[array].at[slot, :, pl.ds(half * (depth // 2), depth // 2)]

        return of

    plane = PlaneGather([view(0), view(1)], plane_send, plane_receive)

    def norms(index, carry):
        at = pl.ds(pl.multiple_of(index * step_rows, step_rows), step_rows)
        unit = row_norm(stream_ref[at, :].astype(f32))
        x_attn[at, :] = (unit * gains_ref[0:1, :] + offsets_ref[0:1, :]).astype(bf16)
        x_mlp[at, :] = (unit * gains_ref[1:2, :] + offsets_ref[1:2, :]).astype(bf16)
        return carry

    lax.fori_loop(0, rows // step_rows, norms, 0, unroll=4)
    half_rot = ROT // 2
    for kind in range(3):
        bias = wide_ref[0:1, pl.ds(pl.multiple_of(kind * depth + place * plane_width, LANES), plane_width)]
        whole = jnp.dot(
            x_attn[...], mixed_ref[:, kind * plane_width : (kind + 1) * plane_width], preferred_element_type=f32
        )
        for sequence in range(lines):
            value = whole[sequence * tokens : (sequence + 1) * tokens] + bias
            if kind < 2:
                value = (
                    value * turns_ref[0]
                    + pltpu.roll(value, plane_width - half_rot, 1) * turns_ref[1]
                    + pltpu.roll(value, half_rot, 1) * turns_ref[2]
                )
            value = value.astype(bf16)
            for group in range(groups):
                spread[sequence * groups + group, kind] = value[:, group * columns : (group + 1) * columns]
    for index, peer in enumerate(peers):
        sent.append(
            push(spread.at[peer], gathered.at[spot], heads_send.at[index], heads_receive.at[spot], {"seq": peer})
        )
    heads_copy = pltpu.make_async_copy(spread.at[spot], gathered.at[spot], local_sem.at[0])
    heads_copy.start()
    plane.own(0)
    for source in range(size):
        at = slice(source * own_width, (source + 1) * own_width)
        for probe in range(2):
            trans_bias[probe : probe + 1, at] = sum(
                slab_ref[source, own_width + 8 * part + probe : own_width + 8 * part + probe + 1, 0:own_width].astype(f32)
                for part in range(2)
            )
        at = slice(source * hidden_rows, (source + 1) * hidden_rows)
        if hidden_rows % LANES:
            begin = wide_ref.shape[1] - fc_width
            fc_bias[:, at] = wide_ref[0:1, begin + source * hidden_rows : begin + (source + 1) * hidden_rows]
        else:
            begin = pl.multiple_of(3 * depth + (source * lines + place) * hidden_rows, LANES)
            fc_bias[:, at] = wide_ref[0:1, pl.ds(begin, hidden_rows)]

    def translate(probe, stream, low, weights, at):
        moved = stream + jnp.dot(low, weights, preferred_element_type=f32) + trans_bias[probe : probe + 1, :]
        moved_ref[probe, at, :] = moved
        states_ref[1 + probe, at, :] = (
            row_norm(moved) * gains_ref[2:3, :] + offsets_ref[4:5, :]
        ).astype(bf16)

    for begin in range(0, rows, wide_rows):
        at = slice(begin, begin + wide_rows)
        low = stream_ref[at, :]
        translate(0, low.astype(f32), low, slab_ref[:, 0:own_width, :].reshape(depth, depth), at)
    turned[...] = jnp.transpose(states_ref[1])
    for begin in range(0, fc_width, 256):
        at = slice(begin, begin + 256)
        for row in range(0, rows, 512):
            span = slice(row, row + 512)
            value = jnp.dot(x_mlp[span, :], mixed_ref[:, 3 * plane_width + begin : 3 * plane_width + begin + 256], preferred_element_type=f32) + fc_bias[:, at]
            hidden[span, at] = (0.5 * value * (1.0 + lax.erf(value * (0.5 ** 0.5)))).astype(bf16)
    plane.relay_side(0)
    heads_copy.wait()
    for peer in peers:
        arrived(gathered.at[peer], heads_receive.at[peer], {"seq": peer})
    length = size * tokens
    block = 2 * tokens
    lane = lax.broadcasted_iota(jnp.int32, (block, columns), 1) // head_dim
    keys = jnp.concatenate([gathered[source, 1] for source in range(size)], axis=0)
    values = jnp.concatenate([gathered[source, 2] for source in range(size)], axis=0)
    for first in range(0, length, block):
        end = first + block
        queries = jnp.concatenate([gathered[first // tokens, 0], gathered[first // tokens + 1, 0]], axis=0)
        allowed = lax.broadcasted_iota(jnp.int32, (block, end), 1) <= (
            lax.broadcasted_iota(jnp.int32, (block, end), 0) + first
        )
        result = None
        for head in range(heads):
            chosen = jnp.where(lane == head, queries, jnp.zeros((), bf16))
            scores = lax.dot_general(
                chosen, keys[:end], (((1,), (1,)), ((), ())), preferred_element_type=f32
            ) * head_dim ** (-0.5)
            scores = jnp.where(allowed, scores, NEGATIVE)
            exponent = jnp.exp(scores - jnp.max(scores, axis=-1, keepdims=True))
            value = jnp.dot(
                exponent.astype(bf16), values[:end], preferred_element_type=f32
            ) / jnp.sum(exponent, axis=-1, keepdims=True)
            result = value if result is None else jnp.where(lane == head, value, result)
        result = result.astype(bf16)
        for index in range(2):
            mixed[first // tokens + index] = result[index * tokens : (index + 1) * tokens]
    for index, peer in enumerate(peers):
        sent.append(
            push(mixed.at[peer], returned.at[spot], rows_send.at[index], rows_receive.at[spot], {"seq": peer})
        )
    rows_copy = pltpu.make_async_copy(mixed.at[spot], returned.at[spot], local_sem.at[1])
    rows_copy.start()
    plane.own(1)
    plane.relay_core(0)
    probe_logits(0)
    probe_logits(1)
    plane.receive_core(0)
    for begin in range(0, depth, 256):
        at = slice(begin, begin + 256)
        part[:, at] = jnp.dot(
            hidden[...], slab_all[:, 0:hidden_rows, at].reshape(fc_width, 256), preferred_element_type=f32
        )
    rows_copy.wait()
    for peer in peers:
        arrived(returned.at[peer], rows_receive.at[peer], {"seq": peer})
    out_w = slab_all[:, hidden_rows:, :].reshape(plane_width, depth)
    for sequence in range(lines):
        at = slice(sequence * tokens, (sequence + 1) * tokens)
        attended = jnp.concatenate(
            [returned[sequence * groups + group] for group in range(groups)], axis=1
        )
        part[at, :] += jnp.dot(attended, out_w, preferred_element_type=f32)
    line_sum = LineSum(
        count, 1, lambda at: part[at],
        land, x_attn, x_mlp, inner_sem, outer_sem, receive_sem,
    )
    line_sum.begin(range(count))
    todo = [functools.partial(probe_logits, cut) for cut in range(2, cuts)]
    todo[4:4] = [lambda: plane.relay_side(1)]
    todo[9:9] = [lambda: plane.relay_core(1)]
    todo[13:13] = [lambda: plane.receive_core(1)]
    line_sum.run(3, todo)

    for begin in range(0, rows, wide_rows):
        at = slice(begin, begin + wide_rows)
        stream = stream_ref[at, :].astype(f32) + x_mlp[at, :].astype(f32) + offsets_ref[2:3, :] + offsets_ref[3:4, :]
        states_ref[0, at, :] = (row_norm(stream) * gains_ref[2:3, :] + offsets_ref[4:5, :]).astype(bf16)
        low = stream.astype(bf16)
        low_ref[at, :] = low
        translate(1, stream, low, second_trans[...].reshape(depth, depth), at)
    for copy in sent:
        copy.wait_send()
    for copy in stores[-2:]:
        copy.wait()
    plane.finish()
    line_sum.finish()


def layer(stream, mixed, proj, out, slab, next_trans, gains, offsets, wide, turns, table):
    size = lax.axis_size("seq")
    lines = lax.axis_size("batch")
    rows, depth = stream.shape
    tokens = rows // lines
    own_heads = depth // HEAD_DIM // size
    columns = own_heads * HEAD_DIM
    count = 16
    fc_width = size * proj.shape[0]
    tiles = pl.cdiv(table.shape[0], VOCAB_TILE)
    bf16 = jnp.bfloat16
    f32 = jnp.float32
    vmem = pl.BlockSpec(memory_space=pltpu.VMEM)
    anywhere = pl.BlockSpec(memory_space=pl.ANY)
    dma = pltpu.SemaphoreType.DMA
    sums = LineSum.scratch(count, rows, depth)
    return pl.pallas_call(
        functools.partial(layer_kernel, count, own_heads),
        in_specs=[vmem] * 10 + [anywhere],
        out_specs=[vmem] * 3 + [anywhere],
        out_shape=[
            jax.ShapeDtypeStruct((3, rows, depth), bf16),
            jax.ShapeDtypeStruct((2, rows, depth), f32),
            jax.ShapeDtypeStruct((rows, depth), bf16),
            jax.ShapeDtypeStruct((tiles, VOCAB_TILE, rows), f32),
        ],
        scratch_shapes=[
            pltpu.VMEM((size, proj.shape[0] + out.shape[0], depth), bf16),
            pltpu.VMEM((size,) + next_trans.shape[1:], bf16),
            pltpu.VMEM((2, depth), f32),
            pltpu.VMEM((1, fc_width), f32),
            pltpu.VMEM((rows, fc_width), bf16),
            pltpu.VMEM((rows, depth), bf16),
            pltpu.VMEM((rows, depth), bf16),
            pltpu.VMEM((size, 3, tokens, columns), bf16),
            pltpu.VMEM((size, 3, tokens, columns), bf16),
            pltpu.VMEM((size, tokens, columns), bf16),
            pltpu.VMEM((size, tokens, columns), bf16),
            pltpu.VMEM((rows, depth), f32),
        ] + sums[:1] + sums[2:] + [
            pltpu.VMEM((2, VOCAB_TILE // 2, depth), bf16),
            pltpu.VMEM((depth, rows), bf16),
            pltpu.VMEM((2, VOCAB_TILE // 2, rows), f32),
            dma((2,)),
            dma((2,)),
            dma((2,)),
            dma((size - 1,)),
            dma((size,)),
            dma((size - 1,)),
            dma((size,)),
        ] + PlaneGather.scratch(2),
        compiler_params=pltpu.CompilerParams(
            collective_id=2, has_side_effects=True, vmem_limit_bytes=VMEM_BYTES
        ),
        name="layer",
    )(stream, mixed, proj, out, slab, next_trans, gains, offsets, wide, turns, table)


def stats_kernel(
    tiles_ref, peaks_ref, sums_ref, cross_ref, scales_ref, note_ref,
    gathered, send_sem, receive_sem,
):
    place = lax.axis_index("batch")
    spot = lax.axis_index("seq")
    size = lax.axis_size("seq")
    planes = others("batch")
    tiles = peaks_ref.shape[0]
    rows = peaks_ref.shape[2]
    lines = gathered.shape[0]
    tokens = rows // lines
    gathered[place, 0:3, :] = peaks_ref[tiles - 1]
    for state in range(3):
        gathered[place, 3 + state : 4 + state, :] = jnp.sum(sums_ref[state], axis=0, keepdims=True)
    for other in range(2):
        gathered[place, 6 + other : 7 + other, :] = jnp.sum(cross_ref[other], axis=0, keepdims=True)
    greet([{"batch": plane} for plane in planes])
    copies = [
        push(gathered.at[place], gathered.at[place], send_sem.at[index], receive_sem.at[place], {"batch": plane})
        for index, plane in enumerate(planes)
    ]
    position = spot * tokens + lax.broadcasted_iota(jnp.int32, (1, tokens), 1)
    weights = jnp.concatenate(
        [
            jnp.where(position < size * tokens - tiles_ref[line, 2:3, :], tiles_ref[line, 1:2, :], 0).astype(jnp.float32)
            for line in range(lines)
        ],
        axis=1,
    )
    for plane in planes:
        arrived(gathered.at[plane], receive_sem.at[plane], {"batch": plane})
    tops = gathered[0, 0:3, :]
    for line in range(1, lines):
        tops = jnp.maximum(tops, gathered[line, 0:3, :])
    sums = jnp.zeros((3, rows), jnp.float32)
    cross = jnp.zeros((2, rows), jnp.float32)
    for line in range(lines):
        fade = jnp.exp(gathered[line, 0:3, :] - tops)
        sums += gathered[line, 3:6, :] * fade
        cross += gathered[line, 6:8, :] * fade[0:1]
    totals = tops + jnp.log(sums)
    diverge = cross / sums[0:1] - totals[0:1] + totals[1:3]
    loss = weights * (diverge[0:1] + diverge[1:2])
    for tile in range(tiles):
        scales_ref[tile] = weights * jnp.exp(peaks_ref[tile] - totals)
    note_ref[...] = jnp.zeros_like(note_ref)
    for line in range(rows // LANES):
        at = slice(line * LANES, (line + 1) * LANES)
        note_ref[1:2, :] += loss[:, at]
        note_ref[2:3, :] += weights[:, at]
    for copy in copies:
        copy.wait_send()


def statistics(tiles, peaks, sums, cross):
    lines = lax.axis_size("batch")
    rows = peaks.shape[2]
    vmem = pl.BlockSpec(memory_space=pltpu.VMEM)
    return pl.pallas_call(
        stats_kernel,
        in_specs=[vmem] * 4,
        out_specs=[vmem] * 2,
        out_shape=[
            jax.ShapeDtypeStruct(peaks.shape, jnp.float32),
            jax.ShapeDtypeStruct((8, LANES), jnp.float32),
        ],
        scratch_shapes=[
            pltpu.VMEM((lines, 8, rows), jnp.float32),
            pltpu.SemaphoreType.DMA((lines - 1,)),
            pltpu.SemaphoreType.DMA((lines,)),
        ],
        compiler_params=pltpu.CompilerParams(collective_id=5, has_side_effects=True),
        name="statistics",
    )(tiles, peaks, sums, cross)


def reduce_kernel(
    count,
    grad_ref, bias_ref, note_ref,
    total_ref, bias_out, note_out,
    mine, sibling_land, side_land, line_land, side_sum, line_part, last_land, own_sum,
    land, held, inner_sem, outer_sem, receive_sem,
    tile_land, tile_line, tile_out,
    local_sem, core_send, core_receive, side_send, side_receive, line_send, line_receive,
    last_send, last_receive, bias_send, bias_receive, plane_send, plane_receive, note_send, note_receive,
):
    size = lax.axis_size("seq")
    spot = lax.axis_index("seq")
    place = lax.axis_index("batch")
    core, column, line = plane_place(spot)
    rows = size // 4
    step_rows = total_ref.shape[0] // count // 2
    beside = {"seq": plane_index(core, 1 - column, line)}
    sibling = {"seq": plane_index(1 - core, column, line)}
    lines_on = [lax.rem(line + step, rows) for step in range(1, rows)]
    across = [{"seq": plane_index(core, column, at)} for at in lines_on]
    peers = others("seq")
    planes = others("batch")
    f32 = jnp.float32
    bf16 = jnp.bfloat16
    sent = []

    def cut(chunk, side):
        return grad_ref.at[:, :, :, side, pl.ds(chunk * step_rows, step_rows)]

    loads = [
        pltpu.make_async_copy(cut(chunk, core), mine.at[chunk], local_sem.at[chunk]) for chunk in range(count)
    ]
    for copy in loads:
        copy.start()
    tile_land[spot] = bias_ref[spot]
    greet([{"batch": plane} for plane in planes] + [{"seq": peer} for peer in peers])
    for chunk in range(count):
        sent.append(
            push(cut(chunk, 1 - core), sibling_land.at[chunk], core_send.at[chunk], core_receive.at[chunk], sibling)
        )
    for index, peer in enumerate(peers):
        sent.append(
            push(bias_ref.at[peer], tile_land.at[spot], bias_send.at[index], bias_receive.at[spot], {"seq": peer})
        )
    line_sum = LineSum(
        count, 1, lambda at: own_sum[at],
        land, held, total_ref, inner_sem, outer_sem, receive_sem,
    )

    def pair(chunk):
        loads[chunk].wait()
        arrived(sibling_land.at[chunk], core_receive.at[chunk], sibling)
        mine[chunk] = (mine[chunk].astype(f32) + sibling_land[chunk].astype(f32)).astype(bf16)
        sent.append(
            push(
                mine.at[chunk, 0, :, 1 - column], side_land.at[chunk],
                side_send.at[chunk], side_receive.at[chunk], beside,
            )
        )
        for index, target in enumerate(across):
            sent.append(
                push(
                    mine.at[chunk, 1, lines_on[index]], line_land.at[chunk, index],
                    line_send.at[chunk, index], line_receive.at[chunk, index], target,
                )
            )

    def second(chunk):
        begin = chunk * 2 * step_rows
        arrived(side_land.at[chunk], side_receive.at[chunk], beside)
        own_sum[begin : begin + step_rows, :] = (
            mine[chunk, 0, line, column].astype(f32) + side_land[chunk, line].astype(f32)
        )
        for index, target in enumerate(across):
            at = lines_on[index]
            side_sum[chunk, index] = (
                mine[chunk, 0, at, column].astype(f32) + side_land[chunk, at].astype(f32)
            ).astype(bf16)
            sent.append(
                push(
                    side_sum.at[chunk, index], last_land.at[chunk, 1 + index],
                    last_send.at[chunk, 1 + index], last_receive.at[chunk, 1 + index], target,
                )
            )
        for index in range(len(across)):
            arrived(line_land.at[chunk, index], line_receive.at[chunk, index], across[-1 - index])
        for side, last in ((1 - column, False), (column, True)):
            both = mine[chunk, 1, line, side].astype(f32)
            for index in range(len(across)):
                both += line_land[chunk, index, side].astype(f32)
            if last:
                own_sum[begin + step_rows : begin + 2 * step_rows, :] = both
            else:
                line_part[chunk] = both.astype(bf16)
                sent.append(
                    push(
                        line_part.at[chunk], last_land.at[chunk, 0],
                        last_send.at[chunk, 0], last_receive.at[chunk, 0], beside,
                    )
                )

    def third(chunk):
        begin = chunk * 2 * step_rows
        for index in range(len(across)):
            arrived(last_land.at[chunk, 1 + index], last_receive.at[chunk, 1 + index], across[-1 - index])
            own_sum[begin : begin + step_rows, :] += last_land[chunk, 1 + index].astype(f32)
        arrived(last_land.at[chunk, 0], last_receive.at[chunk, 0], beside)
        own_sum[begin + step_rows : begin + 2 * step_rows, :] += last_land[chunk, 0].astype(f32)
        line_sum.begin([chunk])
        line_sum.gather(chunk)

    def tiles_in_plane():
        for peer in peers:
            arrived(tile_land.at[peer], bias_receive.at[peer], {"seq": peer})
        tile = tile_land[0]
        for source in range(1, size):
            tile += tile_land[source]
        tile_line[place] = tile
        for index, plane in enumerate(planes):
            sent.append(
                push(
                    tile_line.at[place], tile_line.at[place], plane_send.at[index], plane_receive.at[place],
                    {"batch": plane},
                )
            )

    squares = []

    def square(chunk):
        line_sum.spread(chunk)
        for row in range(chunk * 2 * step_rows, (chunk + 1) * 2 * step_rows, 16):
            value = total_ref[row : row + 16, :].astype(f32)
            value = value * value
            for begin in range(0, value.shape[1], LANES):
                block = value[:8, begin : begin + LANES] + value[8:, begin : begin + LANES]
                squares[:] = [block + squares[0]] if squares else [block]

    for time in range(count + 4):
        if time < count:
            pair(time)
        if 0 <= time - 1 < count:
            second(time - 1)
        if 0 <= time - 2 < count:
            third(time - 2)
        if time == count - 1:
            tiles_in_plane()
        if 0 <= time - 4 < count:
            square(time - 4)
    for plane in planes:
        arrived(tile_line.at[plane], plane_receive.at[plane], {"batch": plane})
    tile = tile_line[0]
    for source in range(1, lax.axis_size("batch")):
        tile += tile_line[source]
    bias_out[...] = tile
    head = jnp.sum(squares[0] + tile * tile, axis=0, keepdims=True)
    row8 = lax.broadcasted_iota(jnp.int32, (8, LANES), 0)
    tile_out[...] = jnp.where(row8 == 0, head, note_ref[...])
    note_out[spot] = tile_out[...]
    for index, peer in enumerate(peers):
        sent.append(
            push(tile_out, note_out.at[spot], note_send.at[index], note_receive.at[spot], {"seq": peer})
        )
    for peer in peers:
        arrived(note_out.at[peer], note_receive.at[peer], {"seq": peer})
    for copy in sent:
        copy.wait_send()
    line_sum.finish()


def reduce_gradients(grad, bias, note):
    size = lax.axis_size("seq")
    lines = lax.axis_size("batch")
    depth = grad.shape[2]
    width = depth // size
    rows = size // 4
    count = 4
    cut = width // count
    bf16 = jnp.bfloat16
    vmem = pl.BlockSpec(memory_space=pltpu.VMEM)
    dma = pltpu.SemaphoreType.DMA
    near = max(rows - 1, 1)
    grad = grad.reshape(2, rows, 2, 2, width, depth)
    return pl.pallas_call(
        functools.partial(reduce_kernel, count),
        in_specs=[pl.BlockSpec(memory_space=pl.ANY), vmem, vmem],
        out_specs=[vmem] * 3,
        out_shape=[
            jax.ShapeDtypeStruct((2 * width, depth), bf16),
            jax.ShapeDtypeStruct(bias.shape[1:], jnp.float32),
            jax.ShapeDtypeStruct((size,) + note.shape, jnp.float32),
        ],
        scratch_shapes=[
            pltpu.VMEM((count, 2, rows, 2, cut, depth), bf16),
            pltpu.VMEM((count, 2, rows, 2, cut, depth), bf16),
            pltpu.VMEM((count, rows, cut, depth), bf16),
            pltpu.VMEM((count, near, 2, cut, depth), bf16),
            pltpu.VMEM((count, near, cut, depth), bf16),
            pltpu.VMEM((count, cut, depth), bf16),
            pltpu.VMEM((count, rows, cut, depth), bf16),
            pltpu.VMEM((2 * width, depth), jnp.float32),
        ] + LineSum.scratch(count, 2 * width, depth) + [
            pltpu.VMEM((size,) + bias.shape[1:], jnp.float32),
            pltpu.VMEM((lines,) + bias.shape[1:], jnp.float32),
            pltpu.VMEM(note.shape, jnp.float32),
            dma((count,)),
            dma((count,)),
            dma((count,)),
            dma((count,)),
            dma((count,)),
            dma((count, near)),
            dma((count, near)),
            dma((count, rows)),
            dma((count, rows)),
            dma((size - 1,)),
            dma((size,)),
            dma((lines - 1,)),
            dma((lines,)),
            dma((size - 1,)),
            dma((size,)),
        ],
        compiler_params=pltpu.CompilerParams(
            collective_id=6, has_side_effects=True, vmem_limit_bytes=VMEM_BYTES
        ),
        name="reduce_gradients",
    )(grad, bias, note)


def update_kernel(
    total_ref, bias_sum, note_ref, trans_ref, mom1_ref, mom2_ref, trans_bias, mom1_bias, mom2_bias,
    first_out, second_out, weight_out, first_bias, second_bias, weight_bias, result_out,
):
    size = note_ref.shape[0]
    notes = note_ref[0]
    for source in range(1, size):
        notes += note_ref[source]
    sums = jnp.sum(notes, axis=-1, keepdims=True)
    norm = jnp.sqrt(sums[0:1]) / sums[2:3]
    row8 = lax.broadcasted_iota(jnp.int32, (8, LANES), 0)
    result_out[...] = jnp.where(row8 == 0, norm, sums)
    factor = jnp.minimum(1.0, clip_max / (norm + 1e-06)) / sums[2:3]
    cut = total_ref.shape[2]
    for chunk in range(total_ref.shape[0]):
        at = slice(chunk * cut, (chunk + 1) * cut)
        for probe in range(2):
            gradient = total_ref[chunk, probe].astype(jnp.float32) * factor
            first_out[probe, at, :], second_out[probe, at, :], weight_out[probe, at, :] = adam_update(
                trans_ref[probe, at, :], gradient, mom1_ref[probe, at, :], mom2_ref[probe, at, :]
            )
    gradient = bias_sum[0:2, 0 : trans_bias.shape[1]] * factor
    first_bias[...], second_bias[...], weight_bias[...] = adam_update(
        trans_bias[...], gradient, mom1_bias[...], mom2_bias[...]
    )


def update(total, bias_sum, notes, trans, mom1, mom2, trans_bias, mom1_bias, mom2_bias):
    _, width, depth = trans.shape
    count = 4
    cut = width // count
    f32 = jnp.float32
    whole = lambda part: pl.BlockSpec(part.shape, lambda i: (0,) * part.ndim)
    part = pl.BlockSpec((2, width, depth), lambda i: (0, 0, 0))
    result = pl.BlockSpec((8, LANES), lambda i: (0, 0))
    total = jnp.reshape(total, (count, 2, cut, depth))
    return pl.pallas_call(
        update_kernel,
        grid=(1,),
        in_specs=[
            pl.BlockSpec((count, 2, cut, depth), lambda i: (0, 0, 0, 0)), whole(bias_sum), whole(notes), part, part, part,
            whole(trans_bias), whole(mom1_bias), whole(mom2_bias),
        ],
        out_specs=[part, part, part, whole(trans_bias), whole(mom1_bias), whole(mom2_bias), result],
        out_shape=[jax.ShapeDtypeStruct(trans.shape, f32)] * 3
        + [jax.ShapeDtypeStruct(trans_bias.shape, f32)] * 3
        + [jax.ShapeDtypeStruct((8, LANES), f32)],
        compiler_params=pltpu.CompilerParams(vmem_limit_bytes=VMEM_BYTES),
        name="update",
    )(total, bias_sum, notes, trans, mom1, mom2, trans_bias, mom1_bias, mom2_bias)


def body(
    token_ids,
    pos_weights,
    pad_lengths,
    embed_in,
    w_qkv,
    w_out,
    w_fc,
    w_proj,
    norm_gains,
    layer_biases,
    wide_bias,
    unembed,
    trans_weight,
    trans_bias,
    mom1_weight,
    mom2_weight,
    mom1_bias,
    mom2_bias,
):
    bf16 = jnp.bfloat16
    f32 = jnp.float32
    tok_rows = token_ids.shape[1]
    width = embed_in.shape[1]
    vocab_rows = unembed.shape[0]
    n_seq = lax.axis_size("seq")
    n_batch = lax.axis_size("batch")
    batch_index = lax.axis_index("batch")
    seq_index = lax.axis_index("seq")
    head_count = width // HEAD_DIM
    plane_heads = head_count // n_batch
    plane_width = plane_heads * HEAD_DIM
    hidden_rows = w_proj.shape[0]

    half_rot = ROT // 2
    local_places = seq_index * tok_rows + jnp.arange(tok_rows, dtype=jnp.int32)
    frequency = 10000.0 ** (-2.0 * jnp.arange(half_rot, dtype=f32) / ROT)
    angles = local_places.astype(f32)[:, None] * frequency[None, :]
    cosine = jnp.cos(angles)
    sine = jnp.sin(angles)
    still = jnp.zeros((tok_rows, HEAD_DIM - ROT), f32)
    blank = jnp.zeros((tok_rows, half_rot), f32)
    turns = jnp.stack(
        [
            jnp.concatenate([cosine, cosine, still + 1.0], axis=1),
            jnp.concatenate([-sine, blank, still], axis=1),
            jnp.concatenate([blank, sine, still], axis=1),
        ]
    )
    turns = jnp.tile(turns, (1, 1, plane_heads))

    wide = wide_bias[None, :]
    if hidden_rows % LANES:
        fc_bias = lax.dynamic_slice_in_dim(
            wide_bias[3 * width :].reshape(n_seq, n_batch, hidden_rows), batch_index, 1, 1
        ).reshape(1, -1)
        wide = jnp.concatenate([wide, fc_bias], axis=1)
    own_rows = w_qkv.shape[0]
    joined_cut = jnp.transpose(w_qkv.reshape(own_rows, 3, n_batch, plane_width), (2, 0, 1, 3))
    fc_cut = jnp.transpose(w_fc.reshape(own_rows, n_seq, n_batch, hidden_rows), (2, 0, 1, 3))
    mixed_cut = jnp.concatenate(
        [joined_cut.reshape(n_batch, own_rows, -1), fc_cut.reshape(n_batch, own_rows, -1)], axis=2
    )
    tiles, stream_low, mixed_w, slab, out_own = front(
        token_ids, pos_weights, pad_lengths, embed_in, mixed_cut, trans_weight, w_out, trans_bias
    )
    states, translated, low1, probe_logits = layer(
        stream_low,
        mixed_w.reshape(width, -1),
        w_proj,
        out_own,
        slab,
        trans_weight,
        norm_gains,
        layer_biases,
        wide,
        turns,
        unembed,
    )
    first, second, peaks, sums_part, cross_part = vocab_forward(states, unembed, probe_logits)
    scales, note = statistics(tiles, peaks, sums_part, cross_part)
    grad, bias_grad = vocab_backward(
        first, second, scales, unembed, translated, stream_low, low1, norm_gains
    )
    first_w, second_w, new_w, first_b, second_b, new_b, result = update(
        *reduce_gradients(grad, bias_grad, note),
        trans_weight, mom1_weight, mom2_weight, trans_bias, mom1_bias, mom2_bias,
    )
    return (result[1, 0], result[2, 0], result[0, 0], first_w, second_w, new_w, first_b, second_b, new_b)


def solution(mesh):
    return jax.shard_map(
        body,
        mesh=mesh,
        in_specs=(
            P("batch", "seq"),
            P("batch", "seq"),
            P("batch"),
            P("batch", None),
            P(("seq", "batch"), None),
            P(("seq", "batch"), None),
            P(("seq", "batch"), None),
            P(("seq", "batch"), None),
            P(),
            P(),
            P(),
            P("batch", None),
            P(None, "seq", None),
            P(None, "seq"),
            P(None, "seq", None),
            P(None, "seq", None),
            P(None, "seq"),
            P(None, "seq"),
        ),
        out_specs=(
            P(),
            P(),
            P(),
            P(None, "seq", None),
            P(None, "seq", None),
            P(None, "seq", None),
            P(None, "seq"),
            P(None, "seq"),
            P(None, "seq"),
        ),
        check_vma=False,
    )
```

```python
import functools
import math

import jax
import jax.numpy as jnp
from jax import lax
from jax.experimental import pallas as pl
from jax.experimental.pallas import tpu as pltpu
from jax.sharding import PartitionSpec as P

HEAD_DIM = 64
ROT = 16
STEP = 10


VOCAB_TILE = 1280
LANES = 128
NEGATIVE = -1e30
VMEM_BYTES = 62 * 1024 * 1024
norm_eps = 1e-05
clip_max = 0.001
beta_one = 0.9
beta_two = 0.999
learn_rate = 0.03
decay_rate = 0.01
adam_eps = 1e-08


def norm_back(values, upstream, gain_row):
    average = jnp.mean(values, axis=-1, keepdims=True)
    centered = values - average
    variance = jnp.mean(centered * centered, axis=-1, keepdims=True)
    inverse = lax.rsqrt(variance + norm_eps)
    unit = centered * inverse
    scaled = upstream * gain_row
    return (
        scaled
        - jnp.mean(scaled, axis=-1, keepdims=True)
        - unit * jnp.mean(scaled * unit, axis=-1, keepdims=True)
    ) * inverse


def adam_update(weight, gradient, earlier, later):
    earlier = beta_one * earlier + (1.0 - beta_one) * gradient
    later = beta_two * later + (1.0 - beta_two) * gradient * gradient
    update = (
        earlier / (1.0 - beta_one**STEP) / (jnp.sqrt(later / (1.0 - beta_two**STEP)) + adam_eps)
    )
    return (earlier, later, weight * (1.0 - learn_rate * decay_rate) - learn_rate * update)


def forward_kernel(vocab, states_ref, table_ref, probe0_ref, probe1_ref, first_ref, second_ref, peaks_ref, sums_ref, cross_ref, turned, left, right, peak):
    step = pl.program_id(0)
    steps = pl.num_programs(0) - 1
    width = table_ref.shape[0]
    half = left.shape[1] // 2
    group = 16
    given = (probe0_ref, probe1_ref)
    last = vocab - (pl.cdiv(vocab, width) - 1) * width
    row = lax.broadcasted_iota(jnp.int32, (group, LANES), 0)

    def reset(part):
        span = slice(part * half, (part + 1) * half)
        peak[:, span] = jnp.full((8, half), NEGATIVE, jnp.float32)
        sums_ref[:, :, span] = jnp.zeros((3, 8, half), jnp.float32)
        cross_ref[:, :, span] = jnp.zeros((2, 8, half), jnp.float32)

    @pl.when(step == 0)
    def _():
        reset(0)
        for state in range(2):
            for part in range(2):
                turned[part, :, state * half : (state + 1) * half] = jnp.transpose(
                    states_ref[2 * state, part * half : (part + 1) * half, :]
                )

    @pl.when(step <= 1)
    def _():
        reset(1)

    def multiply(part, target, state, cut):
        place = slice(state * half, (state + 1) * half)
        at = slice(cut * width // 5, (cut + 1) * width // 5)
        target[at, place] = jnp.dot(
            table_ref[at, :], turned[part, :, place], preferred_element_type=jnp.float32
        )

    def units(part, source, target, tile):
        limit = vocab - tile * width
        blocks = width // group
        result = []
        for lanes in range(half // LANES):
            span = slice(part * half + lanes * LANES, part * half + (lanes + 1) * LANES)
            local = slice(lanes * LANES, (lanes + 1) * LANES)
            held = {}

            def logits(state, block, lanes=lanes):
                at = slice(block * group, (block + 1) * group)
                if state == 1:
                    value = given[part][0, at, lanes * LANES : (lanes + 1) * LANES]
                else:
                    begin = state // 2 * half + lanes * LANES
                    value = source[at, begin : begin + LANES]
                if (block + 1) * group > last:
                    value = jnp.where(row + block * group < limit, value, NEGATIVE)
                return value

            def tops(span=span, held=held, logits=logits):
                held["top"], held["sum"], held["cross"] = [], [], []
                for state in range(3):
                    top = logits(state, 0)
                    for block in range(1, blocks):
                        top = jnp.maximum(top, logits(state, block))
                    before = peak[state : state + 1, span]
                    now = jnp.maximum(before, jnp.max(top, axis=0, keepdims=True))
                    peak[state : state + 1, span] = now
                    peaks_ref[pl.ds(tile, 1), state, span] = now
                    fade = jnp.exp(before - now)
                    held["top"].append(jnp.broadcast_to(now, (group, LANES)))
                    held["sum"].append(sums_ref[state, :, span] * fade)
                    if state == 0:
                        held["cross"] = [cross_ref[other, :, span] * fade for other in range(2)]

            def fold(value):
                return value[:8] + value[8:]

            def powers(begin, end, held=held, logits=logits, local=local, fold=fold):
                for block in range(begin, end):
                    place = slice(block * group, (block + 1) * group)
                    base = logits(0, block)
                    base_exp = jnp.exp(base - held["top"][0])
                    held["sum"][0] += fold(base_exp)
                    target[0, 0, place, local] = base_exp.astype(jnp.bfloat16)
                    for state in range(1, 3):
                        value = logits(state, block)
                        value_exp = jnp.exp(value - held["top"][state])
                        held["sum"][state] += fold(value_exp)
                        target[0, state, place, local] = value_exp.astype(jnp.bfloat16)
                        held["cross"][state - 1] += fold(base_exp * (base - value))

            def finish(span=span, held=held):
                for state in range(3):
                    sums_ref[state, :, span] = held["sum"][state]
                for other in range(2):
                    cross_ref[other, :, span] = held["cross"][other]

            result.append(tops)
            cuts = 10
            for cut in range(cuts):
                result.append(
                    functools.partial(powers, cut * blocks // cuts, (cut + 1) * blocks // cuts)
                )
            result.append(finish)
        return result

    def stage(part, target, work):
        done = 0
        for piece in range(10):
            multiply(part, target, piece // 5, piece % 5)
            upto = (piece + 1) * len(work) // 10
            for unit in work[done:upto]:
                unit()
            done = upto

    before = jnp.maximum(step - 1, 0)

    @pl.when(step < steps)
    def _():
        stage(0, left, units(1, right, second_ref, before))
        stage(1, right, units(0, left, first_ref, step))

    @pl.when(step == steps)
    def _():
        for unit in units(1, right, second_ref, before):
            unit()


def vocab_forward(states, table, given):
    _, rows, depth = states.shape
    vocab = table.shape[0]
    tiles = pl.cdiv(vocab, VOCAB_TILE)
    half = rows // 2
    kept = jax.ShapeDtypeStruct((tiles, 3, VOCAB_TILE, half), jnp.bfloat16)
    block = (1, 3, VOCAB_TILE, half)
    whole = lambda *shape: pl.BlockSpec(shape, lambda i: (0,) * len(shape))
    return pl.pallas_call(
        functools.partial(forward_kernel, vocab),
        grid=(tiles + 1,),
        in_specs=[
            whole(3, rows, depth),
            pl.BlockSpec((VOCAB_TILE, depth), lambda i: (jnp.minimum(i, tiles - 1), 0)),
            pl.BlockSpec((1, VOCAB_TILE, half), lambda i: (jnp.minimum(i, tiles - 1), 0, 0)),
            pl.BlockSpec((1, VOCAB_TILE, half), lambda i: (jnp.maximum(i - 1, 0), 0, 1)),
        ],
        out_specs=[
            pl.BlockSpec(block, lambda i: (jnp.minimum(i, tiles - 1), 0, 0, 0)),
            pl.BlockSpec(block, lambda i: (jnp.maximum(i - 1, 0), 0, 0, 0)),
            whole(tiles, 3, rows),
            whole(3, 8, rows),
            whole(2, 8, rows),
        ],
        out_shape=[
            kept,
            kept,
            jax.ShapeDtypeStruct((tiles, 3, rows), jnp.float32),
            jax.ShapeDtypeStruct((3, 8, rows), jnp.float32),
            jax.ShapeDtypeStruct((2, 8, rows), jnp.float32),
        ],
        scratch_shapes=[
            pltpu.VMEM((2, depth, 2 * half), jnp.bfloat16),
            pltpu.VMEM((VOCAB_TILE, 2 * half), jnp.float32),
            pltpu.VMEM((VOCAB_TILE, 2 * half), jnp.float32),
            pltpu.VMEM((8, rows), jnp.float32),
        ],
        compiler_params=pltpu.CompilerParams(vmem_limit_bytes=VMEM_BYTES),
        cost_estimate=pl.CostEstimate(
            flops=4 * rows * depth * vocab,
            bytes_accessed=2 * vocab * (depth + 5 * rows),
            transcendentals=3 * rows * vocab,
        ),
        name="vocab_forward",
    )(states, table, given, given)


def backward_kernel(
    vocab, first_ref, second_ref, scales_ref, table_ref, moved_ref, low0_ref, low1_ref, gain_ref,
    grad_ref, bias_ref, out_ref, left, right, tail, delta, turned,
):
    step = pl.program_id(0)
    tiles = pl.num_programs(0) - 1
    width, depth = table_ref.shape
    half = first_ref.shape[3]
    piece = 256
    last = vocab - (pl.cdiv(vocab, width) - 1) * width
    whole = last // piece * piece
    tile = jnp.maximum(step - 1, 0)
    limit = vocab - tile * width

    def units(part, source, target, index):
        result = []

        def turn(lanes, block):
            begin = part * half + lanes * LANES
            span = slice(begin, begin + LANES)
            place = slice(block * LANES, (block + 1) * LANES)
            local = slice(lanes * LANES, (lanes + 1) * LANES)
            factors = scales_ref[pl.ds(index, 1), :, span][0]
            base = source[0, 0, place, local].astype(jnp.float32) * factors[0:1]
            for state in range(1, 3):
                value = source[0, state, place, local].astype(jnp.float32) * factors[state : state + 1]
                first = (state - 1) * half + lanes * LANES
                target[first : first + LANES, place] = jnp.transpose(
                    (value - base).astype(jnp.bfloat16)
                )

        for lanes in range(half // LANES):
            for block in range(width // LANES):
                result.append(functools.partial(turn, lanes, block))
        return result

    def multiply(part, source, start):
        place = slice(start, start + piece)
        span = slice(part * half, (part + 1) * half)
        partial = jnp.dot(source[:, whole:], tail[:, place], preferred_element_type=jnp.float32)
        if whole > 0:
            partial += jnp.dot(
                source[:, :whole], table_ref[:whole, place], preferred_element_type=jnp.float32
            )
        for probe in range(2):
            out_ref[probe, span, place] += partial[probe * half : (probe + 1) * half]

    def stage(part, source, work):
        done = 0
        pieces = depth // piece
        for index in range(pieces):
            multiply(part, source, index * piece)
            upto = (index + 1) * len(work) // pieces
            for unit in work[done:upto]:
                unit()
            done = upto

    ahead = jnp.minimum(step, tiles - 1)

    @pl.when(step == 0)
    def _():
        out_ref[...] = jnp.zeros_like(out_ref)
        for unit in units(0, first_ref, left, ahead):
            unit()

    @pl.when(step > 0)
    def _():
        below = lax.broadcasted_iota(jnp.int32, (width - whole, depth), 0) + whole < limit
        tail[...] = jnp.where(below, table_ref[whole:, :], jnp.zeros((), tail.dtype))
        stage(0, left, units(1, second_ref, right, tile))
        stage(1, right, units(0, first_ref, left, ahead))

    @pl.when(step == tiles)
    def _():
        rows = out_ref.shape[1]
        chunk = 32
        block = 256
        for probe in range(2):
            low_ref = (low0_ref, low1_ref)[probe]

            def back(index, total, probe=probe):
                at = pl.ds(pl.multiple_of(index * chunk, chunk), chunk)
                value = norm_back(moved_ref[probe, at, :], out_ref[probe, at, :], gain_ref[2:3, :])
                delta[at, :] = value.astype(jnp.bfloat16)
                return total + jnp.sum(value, axis=0, keepdims=True)

            summed = lax.fori_loop(
                0, rows // chunk, back, jnp.zeros((1, depth), jnp.float32), unroll=4
            )
            if probe == 0:
                bias_ref[...] = jnp.zeros_like(bias_ref)
            own = depth // bias_ref.shape[0]
            for part in range(bias_ref.shape[0]):
                bias_ref[part, probe : probe + 1, 0:own] = summed[:, part * own : (part + 1) * own]
            turned[...] = jnp.transpose(low_ref[...])
            for begin in range(0, depth, block):
                grad_ref[probe, begin : begin + block, :] = jnp.dot(
                    turned[begin : begin + block, :], delta[...], preferred_element_type=jnp.float32
                ).astype(jnp.bfloat16)


def vocab_backward(first, second, scales, table, moved, low0, low1, gains):
    tiles, _, _, half = first.shape
    vocab, depth = table.shape
    rows = 2 * half
    last = vocab - (tiles - 1) * VOCAB_TILE
    block = (1, 3, VOCAB_TILE, half)
    whole = lambda *shape: pl.BlockSpec(shape, lambda i: (0,) * len(shape))
    return pl.pallas_call(
        functools.partial(backward_kernel, vocab),
        grid=(tiles + 1,),
        in_specs=[
            pl.BlockSpec(block, lambda i: (jnp.minimum(i, tiles - 1), 0, 0, 0)),
            pl.BlockSpec(block, lambda i: (jnp.maximum(i - 1, 0), 0, 0, 0)),
            whole(tiles, 3, rows),
            pl.BlockSpec((VOCAB_TILE, depth), lambda i: (jnp.maximum(i - 1, 0), 0)),
            whole(2, rows, depth),
            whole(rows, depth),
            whole(rows, depth),
            whole(*gains.shape),
        ],
        out_specs=[whole(2, depth, depth), whole(lax.axis_size("seq"), 8, LANES)],
        out_shape=[
            jax.ShapeDtypeStruct((2, depth, depth), jnp.bfloat16),
            jax.ShapeDtypeStruct((lax.axis_size("seq"), 8, LANES), jnp.float32),
        ],
        scratch_shapes=[
            pltpu.VMEM((2, rows, depth), jnp.float32),
            pltpu.VMEM((2 * half, VOCAB_TILE), jnp.bfloat16),
            pltpu.VMEM((2 * half, VOCAB_TILE), jnp.bfloat16),
            pltpu.VMEM((VOCAB_TILE - last // 256 * 256, depth), jnp.bfloat16),
            pltpu.VMEM((rows, depth), jnp.bfloat16),
            pltpu.VMEM((depth, rows), jnp.bfloat16),
        ],
        compiler_params=pltpu.CompilerParams(vmem_limit_bytes=VMEM_BYTES),
        cost_estimate=pl.CostEstimate(
            flops=4 * rows * depth * (vocab + depth),
            bytes_accessed=2 * vocab * (depth + 3 * rows),
            transcendentals=0,
        ),
        name="vocab_backward",
    )(first, second, scales, table, moved, low0, low1, gains)


def plane_place(place):
    core = lax.rem(place, 2)
    return core, lax.rem(place // 2, 2), place // 4


def plane_index(core, column, line):
    return (line * 2 + column) * 2 + core


def greet(partners):
    barrier = pltpu.get_barrier_semaphore()
    for partner in partners:
        pl.semaphore_signal(barrier, inc=1, device_id=partner, device_id_type=pl.DeviceIdType.MESH)
    pl.semaphore_wait(barrier, len(partners))


def push(source, target, send, receive, partner):
    copy = pltpu.make_async_remote_copy(
        src_ref=source,
        dst_ref=target,
        send_sem=send,
        recv_sem=receive,
        device_id=partner,
        device_id_type=pl.DeviceIdType.MESH,
    )
    copy.start()
    return copy


def arrived(target, receive, partner):
    pltpu.make_async_remote_copy(
        src_ref=target,
        dst_ref=target,
        send_sem=receive,
        recv_sem=receive,
        device_id=partner,
        device_id_type=pl.DeviceIdType.MESH,
    ).wait_recv()


def departed(source, send, partner):
    pltpu.make_async_remote_copy(
        src_ref=source,
        dst_ref=source,
        send_sem=send,
        recv_sem=send,
        device_id=partner,
        device_id_type=pl.DeviceIdType.MESH,
    ).wait_send()


class LineSum:
    def __init__(self, count, halves, own, land, held, total, inner_sem, outer_sem, receive_sem):
        lines = lax.axis_size("batch")
        rows, depth = held.shape
        self.blocks = count // halves
        place = lax.axis_index("batch")
        near = place < lines // 2
        self.count, self.size, self.columns = count, rows // self.blocks, depth // halves
        self.own, self.land, self.held, self.total = own, land, held, total
        self.inner_sem, self.outer_sem, self.receive_sem = inner_sem, outer_sem, receive_sem
        self.middle = (place == lines // 2 - 1) | (place == lines // 2)
        self.end = (place == 0) | (place == lines - 1)
        self.inner = {"batch": jnp.where(near, place + 1, place - 1)}
        self.outer = {"batch": jnp.where(near, place - 1, place + 1)}
        self.slot = jnp.where(self.middle, 1, 0)

    def rows(self, index):
        return (
            pl.ds(index % self.blocks * self.size, self.size),
            pl.ds(index // self.blocks * self.columns, self.columns),
        )

    def send_in(self, index):
        rows = self.rows(index)
        push(
            self.held.at[*rows],
            self.land.at[self.slot, *rows],
            self.inner_sem.at[index],
            self.receive_sem.at[self.slot, index],
            self.inner,
        )

    def begin(self, indices):
        @pl.when(self.end)
        def _():
            for index in indices:
                rows = self.rows(index)
                self.held[rows] = self.own(rows).astype(jnp.bfloat16)
                self.send_in(index)

    def gather(self, index):
        rows = self.rows(index)

        @pl.when(jnp.logical_not(self.end))
        def _():
            arrived(self.land.at[0, *rows], self.receive_sem.at[0, index], self.outer)
            own = self.own(rows).astype(jnp.float32)
            self.held[rows] = (own + self.land[(0, *rows)].astype(jnp.float32)).astype(jnp.bfloat16)
            self.send_in(index)

    def spread(self, index):
        rows = self.rows(index)

        @pl.when(self.middle)
        def _():
            arrived(self.land.at[1, *rows], self.receive_sem.at[1, index], self.inner)
            both = self.held[rows].astype(jnp.float32) + self.land[(1, *rows)].astype(jnp.float32)
            self.total[rows] = both.astype(jnp.bfloat16)

        @pl.when(jnp.logical_not(self.middle))
        def _():
            arrived(self.total.at[*rows], self.receive_sem.at[2, index], self.inner)

        @pl.when(jnp.logical_not(self.end))
        def _():
            push(
                self.total.at[*rows],
                self.total.at[*rows],
                self.outer_sem.at[index],
                self.receive_sem.at[2, index],
                self.outer,
            )

    def run(self, lag, todo=(), done=0):
        todo = list(todo)
        for index in range(done, self.count + lag):
            if todo:
                todo.pop(0)()
            if index < self.count:
                self.gather(index)
            if index >= lag and index - lag >= done - lag:
                self.spread(index - lag)
        for work in todo:
            work()

    def finish(self):
        for index in range(self.count):
            rows = self.rows(index)
            departed(self.held.at[*rows], self.inner_sem.at[index], self.inner)

            @pl.when(jnp.logical_not(self.end))
            def _(rows=rows, index=index):
                departed(self.total.at[*rows], self.outer_sem.at[index], self.outer)

    @staticmethod
    def scratch(count, rows, depth):
        return [
            pltpu.VMEM((2, rows, depth), jnp.bfloat16),
            pltpu.VMEM((rows, depth), jnp.bfloat16),
            pltpu.SemaphoreType.DMA((count,)),
            pltpu.SemaphoreType.DMA((count,)),
            pltpu.SemaphoreType.DMA((3, count)),
        ]


class PlaneGather:
    def __init__(self, views, send_sem, receive_sem):
        self.views, self.send_sem, self.receive_sem = views, send_sem, receive_sem
        self.size = lax.axis_size("seq")
        self.spot = lax.axis_index("seq")
        core, column, line = self.where = plane_place(self.spot)
        self.rows = self.size // 4
        self.beside = plane_index(core, 1 - column, line)
        self.sibling = plane_index(1 - core, column, line)
        lines = [lax.rem(line + step, self.rows) for step in range(1, self.rows)]
        self.across = [plane_index(core, column, at) for at in lines]
        self.corners = [plane_index(core, 1 - column, at) for at in lines]
        self.started = []
        self.used = [0] * len(views)

    def send(self, array, half, slot, target):
        view = self.views[array](half, slot)
        index = self.used[array]
        self.used[array] += 1
        self.started.append(
            push(
                view, view, self.send_sem.at[array, index], self.receive_sem.at[array, 1 if half == 1 else 0, slot],
                {"seq": target},
            )
        )

    def wait(self, array, half, slot):
        arrived(
            self.views[array](half, slot), self.receive_sem.at[array, 1 if half == 1 else 0, slot], {"seq": slot}
        )

    def own(self, array):
        for target in [self.beside] + self.across + [self.sibling]:
            self.send(array, None, self.spot, target)

    def relay_side(self, array):
        self.wait(array, None, self.beside)
        for target in self.across:
            self.send(array, 0, self.beside, target)
        for source in self.across:
            self.wait(array, None, source)
            self.send(array, 1, source, self.beside)
        for source in [self.beside] + self.across:
            self.send(array, None, source, self.sibling)

    def relay_core(self, array):
        for source in self.corners:
            for half in range(2):
                self.wait(array, half, source)
            self.send(array, None, source, self.sibling)

    def receive_core(self, array):
        core, _, line = self.where
        for step in range(self.rows):
            for side in range(2):
                self.wait(array, None, plane_index(1 - core, side, lax.rem(line + step, self.rows)))

    def finish(self):
        for copy in self.started:
            copy.wait_send()

    @staticmethod
    def scratch(arrays):
        size = lax.axis_size("seq")
        dma = pltpu.SemaphoreType.DMA
        return [dma((arrays, 2 * size)), dma((arrays, 2, size))]


def others(axis):
    size = lax.axis_size(axis)
    place = lax.axis_index(axis)
    return [lax.rem(place + step, size) for step in range(1, size)]


def front_kernel(
    count,
    ids_ref, weights_ref, padding_ref, table_ref, mixed_ref, trans_ref, out_ref, trans_bias_ref,
    tiles_out, stream_ref, mixed_out, slab_out, out_out,
    table, column_ids, chosen, picked, tile_ref, slab,
    land, held, inner_sem, outer_sem, receive_sem,
    local_sem, table_sem, tile_send, tile_receive, cross_send, cross_receive, plane_send, plane_receive,
):
    lines = lax.axis_size("batch")
    place = lax.axis_index("batch")
    size = lax.axis_size("seq")
    spot = lax.axis_index("seq")
    planes = others("batch")
    peers = others("seq")
    total_rows, depth = stream_ref.shape
    tokens = tile_ref.shape[1]
    vocab = table_ref.shape[0]
    own_width = trans_ref.shape[1]
    number = spot * lines + place
    goal = {"seq": lax.rem(number, size), "batch": number // size}
    wanted = place * size + spot
    origin = {"seq": wanted // lines, "batch": lax.rem(wanted, lines)}
    stays = number == wanted
    width = VOCAB_TILE
    parts = 2
    cuts = table.shape[0] // width

    def mixed_view(half, slot):
        if half is None:
            return mixed_out.at[slot]
        return mixed_out.at[slot, pl.ds(half * (lines // 2), lines // 2)]

    def slab_view(half, slot):
        if half is None:
            return slab_out.at[slot]
        return slab_out.at[slot, :, pl.ds(half * (depth // 2), depth // 2)]

    plane = PlaneGather([mixed_view, slab_view], plane_send, plane_receive)
    table_copies = [
        pltpu.make_async_copy(
            table_ref.at[pl.ds(cut * width, min(width, vocab - cut * width))],
            table.at[pl.ds(cut * width, min(width, vocab - cut * width))],
            table_sem.at[cut],
        )
        for cut in range(cuts)
    ]
    for copy in table_copies:
        copy.start()
    if table.shape[0] > vocab:
        table[vocab:, :] = jnp.zeros((table.shape[0] - vocab, depth), table.dtype)
    bias = trans_bias_ref[...]
    bias_high = bias.astype(jnp.bfloat16)
    bias_low = (bias - bias_high.astype(jnp.float32)).astype(jnp.bfloat16)
    slab[0:own_width, :] = trans_ref[0].astype(jnp.bfloat16)
    slab[own_width:, :] = jnp.zeros((16, depth), jnp.bfloat16)
    slab[own_width : own_width + 2, 0:own_width] = bias_high
    slab[own_width + 8 : own_width + 10, 0:own_width] = bias_low
    tile_ref[...] = jnp.zeros_like(tile_ref)
    tile_ref[0:1, :] = ids_ref[...]
    tile_ref[1:2, :] = weights_ref[...]
    tile_ref[2:3, :] = jnp.full((1, tokens), padding_ref[0], jnp.int32)
    tiles_out[place] = tile_ref[...]
    slab_copy = pltpu.make_async_copy(slab, slab_out.at[spot], local_sem.at[0])
    slab_copy.start()
    mixed_copy = pltpu.make_async_copy(mixed_ref.at[place], mixed_out.at[spot, place], local_sem.at[1])
    mixed_copy.start()
    out_copy = pltpu.make_async_copy(out_ref, out_out, local_sem.at[2])

    @pl.when(stays)
    def _():
        out_copy.start()

    barrier = pltpu.get_barrier_semaphore()
    for partner in [{"batch": other} for other in planes] + [{"seq": peer} for peer in peers]:
        pl.semaphore_signal(barrier, inc=1, device_id=partner, device_id_type=pl.DeviceIdType.MESH)

    @pl.when(jnp.logical_not(stays))
    def _():
        pl.semaphore_signal(barrier, inc=1, device_id=origin, device_id_type=pl.DeviceIdType.MESH)

    pl.semaphore_wait(barrier, jnp.where(stays, 0, 1) + len(planes) + len(peers))

    sent = [
        push(tile_ref, tiles_out.at[place], tile_send.at[index], tile_receive.at[place], {"batch": other})
        for index, other in enumerate(planes)
    ]
    sent += [
        push(
            mixed_ref.at[other], mixed_out.at[spot, place], cross_send.at[index], cross_receive.at[place],
            {"batch": other},
        )
        for index, other in enumerate(planes)
    ]
    slab_copy.wait()
    plane.own(1)
    out_push = pltpu.make_async_remote_copy(
        src_ref=out_ref, dst_ref=out_out, send_sem=local_sem.at[3],
        recv_sem=local_sem.at[4], device_id=goal, device_id_type=pl.DeviceIdType.MESH,
    )

    @pl.when(jnp.logical_not(stays))
    def _():
        out_push.start()

    for other in planes:
        arrived(tiles_out.at[other], tile_receive.at[other], {"batch": other})
    for sequence in range(lines):
        turned = jnp.transpose(tiles_out[sequence].astype(jnp.float32))
        column_ids[sequence * tokens : (sequence + 1) * tokens, :] = jnp.broadcast_to(
            turned[:, 0:1] - (place * vocab).astype(jnp.float32), (tokens, LANES)
        )
    lane = lax.broadcasted_iota(jnp.int32, (1, LANES), 1).astype(jnp.float32)

    def choose(cut):
        for block in range(width // LANES):
            begin = cut * width + block * LANES
            chosen[:, begin : begin + LANES] = jnp.where(
                column_ids[...] == lane + float(begin), 1.0, 0.0
            ).astype(jnp.bfloat16)

    def look(part, cut):
        at = slice(part * (depth // parts), (part + 1) * (depth // parts))
        span = slice(cut * width, (cut + 1) * width)
        if part == 0:
            table_copies[cut].wait()
        found = jnp.dot(chosen[:, span], table[span, at], preferred_element_type=jnp.float32)
        if cut == 0:
            picked[:, at] = found
        else:
            picked[:, at] += found
        if part == 0 and cut + 1 < cuts:
            choose(cut + 1)

    line_sum = LineSum(
        count, parts, lambda at: picked[at],
        land, held, stream_ref, inner_sem, outer_sem, receive_sem,
    )

    def turn():
        mixed_copy.wait()
        for other in planes:
            arrived(mixed_out.at[spot, other], cross_receive.at[other], {"batch": other})
        plane.own(0)

    def turn_out():
        @pl.when(stays)
        def _():
            out_copy.wait()

        @pl.when(jnp.logical_not(stays))
        def _():
            arrived(out_out, local_sem.at[4], origin)

    between = {
        (0, 0): lambda: choose(0),
        (0, 4): lambda: turn(),
        (0, 6): lambda: plane.relay_side(1),
        (1, 3): lambda: line_sum.gather(0),
        (1, 4): lambda: (line_sum.gather(1), plane.relay_core(1)),
        (1, 6): lambda: (line_sum.gather(2), line_sum.spread(0)),
        (1, 8): lambda: (line_sum.gather(3), line_sum.spread(1)),
        (1, 9): lambda: turn_out(),
    }
    for part in range(parts):
        for cut in range(cuts):
            if (part, cut) in between:
                between.pop((part, cut))()
            look(part, cut)
        for work in [between.pop(key) for key in list(between) if key[0] == part]:
            work()
        line_sum.begin(range(part * count // parts, (part + 1) * count // parts))
    todo = [
        lambda: plane.relay_side(0),
        lambda: plane.receive_core(1),
        lambda: None,
        lambda: None,
        lambda: plane.relay_core(0),
        lambda: None,
        lambda: plane.receive_core(0),
    ]
    line_sum.run(2, todo, 4)
    for copy in sent:
        copy.wait_send()

    @pl.when(jnp.logical_not(stays))
    def _():
        out_push.wait_send()

    plane.finish()
    line_sum.finish()


def front(ids, weights, padding, table, mixed, trans, out, bias):
    size = lax.axis_size("seq")
    lines = lax.axis_size("batch")
    vocab, depth = table.shape
    tokens = ids.shape[1]
    rows = lines * tokens
    count = 8
    vmem = pl.BlockSpec(memory_space=pltpu.VMEM)
    smem = pl.BlockSpec(memory_space=pltpu.SMEM)
    anywhere = pl.BlockSpec(memory_space=pl.ANY)
    dma = pltpu.SemaphoreType.DMA
    bf16 = jnp.bfloat16
    padded = pl.cdiv(vocab, VOCAB_TILE) * VOCAB_TILE
    slab_rows = trans.shape[1] + 16
    return pl.pallas_call(
        functools.partial(front_kernel, count),
        in_specs=[vmem, vmem, smem, anywhere, anywhere, vmem, anywhere, vmem],
        out_specs=[vmem, vmem, anywhere, anywhere, anywhere],
        out_shape=[
            jax.ShapeDtypeStruct((lines, 8, tokens), jnp.int32),
            jax.ShapeDtypeStruct((rows, depth), bf16),
            jax.ShapeDtypeStruct((size,) + mixed.shape, bf16),
            jax.ShapeDtypeStruct((size, slab_rows, depth), bf16),
            jax.ShapeDtypeStruct(out.shape, bf16),
        ],
        scratch_shapes=[
            pltpu.VMEM((padded, depth), bf16),
            pltpu.VMEM((rows, LANES), jnp.float32),
            pltpu.VMEM((rows, padded), bf16),
            pltpu.VMEM((rows, depth), jnp.float32),
            pltpu.VMEM((8, tokens), jnp.int32),
            pltpu.VMEM((slab_rows, depth), bf16),
        ] + LineSum.scratch(count, rows, depth) + [
            dma((5,)),
            dma((padded // VOCAB_TILE,)),
            dma((lines - 1,)),
            dma((lines,)),
            dma((lines - 1,)),
            dma((lines,)),
        ] + PlaneGather.scratch(2),
        compiler_params=pltpu.CompilerParams(
            collective_id=1, has_side_effects=True, vmem_limit_bytes=VMEM_BYTES
        ),
        name="front",
    )(ids, weights, padding, table, mixed, trans, out, bias)


def row_norm(values):
    average = jnp.mean(values, axis=-1, keepdims=True)
    centered = values - average
    variance = jnp.mean(centered * centered, axis=-1, keepdims=True)
    return centered * lax.rsqrt(variance + norm_eps)


def layer_kernel(
    count, heads,
    stream_ref, mixed_ref, proj_ref, out_ref, slab_ref, next_ref,
    gains_ref, offsets_ref, wide_ref, turns_ref, table_ref,
    states_ref, moved_ref, low_ref, logits_ref,
    slab_all, second_trans, trans_bias, fc_bias, hidden, x_attn, x_mlp, spread, gathered, mixed, returned, part,
    land, inner_sem, outer_sem, receive_sem,
    tables, turned, logits, table_sem, logits_sem,
    local_sem, heads_send, heads_receive, rows_send, rows_receive, plane_send, plane_receive,
):
    f32 = jnp.float32
    bf16 = jnp.bfloat16
    lines = lax.axis_size("batch")
    place = lax.axis_index("batch")
    size = lax.axis_size("seq")
    spot = lax.axis_index("seq")
    planes = others("batch")
    peers = others("seq")
    rows, depth = stream_ref.shape
    tokens = rows // lines
    hidden_rows = proj_ref.shape[0]
    fc_width = size * hidden_rows
    plane_width = (mixed_ref.shape[1] - fc_width) // 3
    columns = spread.shape[3]
    groups = plane_width // columns
    head_dim = columns // heads
    own_width = next_ref.shape[1]
    step_rows = 32
    wide_rows = 2 * tokens
    vocab = table_ref.shape[0]
    cut_rows = tables.shape[1]
    cuts = pl.cdiv(vocab, cut_rows)
    sizes = [min(cut_rows, vocab - cut * cut_rows) for cut in range(cuts)]
    loads = [
        pltpu.make_async_copy(
            table_ref.at[pl.ds(cut * cut_rows, sizes[cut])],
            tables.at[cut % 2, pl.ds(0, sizes[cut])],
            table_sem.at[cut % 2],
        )
        for cut in range(cuts)
    ]
    stores = [
        pltpu.make_async_copy(
            logits.at[cut % 2],
            logits_ref.at[cut * cut_rows // VOCAB_TILE, pl.ds(cut * cut_rows % VOCAB_TILE, cut_rows)],
            logits_sem.at[cut % 2],
        )
        for cut in range(cuts)
    ]
    loads[0].start()
    loads[1].start()

    def probe_logits(cut):
        loads[cut].wait()
        if cut >= 2:
            stores[cut - 2].wait()
        logits[cut % 2] = jnp.dot(tables[cut % 2], turned[...], preferred_element_type=f32)
        stores[cut].start()
        if cut + 2 < cuts:
            loads[cut + 2].start()

    spans = (slab_all, second_trans)
    slab_all[spot, 0:hidden_rows, :] = proj_ref[...]
    slab_all[spot, hidden_rows:, :] = out_ref[...]
    second_trans[spot] = next_ref[1].astype(bf16)
    greet([{"batch": plane} for plane in planes] + [{"seq": peer} for peer in peers])
    sent = []

    def view(array):
        def of(half, slot):
            if half is None:
                return spans[array].at[slot]
            return spans[array].at[slot, :, pl.ds(half * (depth // 2), depth // 2)]

        return of

    plane = PlaneGather([view(0), view(1)], plane_send, plane_receive)

    def norms(index, carry):
        at = pl.ds(pl.multiple_of(index * step_rows, step_rows), step_rows)
        unit = row_norm(stream_ref[at, :].astype(f32))
        x_attn[at, :] = (unit * gains_ref[0:1, :] + offsets_ref[0:1, :]).astype(bf16)
        x_mlp[at, :] = (unit * gains_ref[1:2, :] + offsets_ref[1:2, :]).astype(bf16)
        return carry

    lax.fori_loop(0, rows // step_rows, norms, 0, unroll=4)
    half_rot = ROT // 2
    for kind in range(3):
        bias = wide_ref[0:1, pl.ds(pl.multiple_of(kind * depth + place * plane_width, LANES), plane_width)]
        whole = jnp.dot(
            x_attn[...], mixed_ref[:, kind * plane_width : (kind + 1) * plane_width], preferred_element_type=f32
        )
        for sequence in range(lines):
            value = whole[sequence * tokens : (sequence + 1) * tokens] + bias
            if kind < 2:
                value = (
                    value * turns_ref[0]
                    + pltpu.roll(value, plane_width - half_rot, 1) * turns_ref[1]
                    + pltpu.roll(value, half_rot, 1) * turns_ref[2]
                )
            value = value.astype(bf16)
            for group in range(groups):
                spread[sequence * groups + group, kind] = value[:, group * columns : (group + 1) * columns]
    for index, peer in enumerate(peers):
        sent.append(
            push(spread.at[peer], gathered.at[spot], heads_send.at[index], heads_receive.at[spot], {"seq": peer})
        )
    heads_copy = pltpu.make_async_copy(spread.at[spot], gathered.at[spot], local_sem.at[0])
    heads_copy.start()
    plane.own(0)
    for source in range(size):
        at = slice(source * own_width, (source + 1) * own_width)
        for probe in range(2):
            trans_bias[probe : probe + 1, at] = sum(
                slab_ref[source, own_width + 8 * part + probe : own_width + 8 * part + probe + 1, 0:own_width].astype(f32)
                for part in range(2)
            )
        at = slice(source * hidden_rows, (source + 1) * hidden_rows)
        if hidden_rows % LANES:
            begin = wide_ref.shape[1] - fc_width
            fc_bias[:, at] = wide_ref[0:1, begin + source * hidden_rows : begin + (source + 1) * hidden_rows]
        else:
            begin = pl.multiple_of(3 * depth + (source * lines + place) * hidden_rows, LANES)
            fc_bias[:, at] = wide_ref[0:1, pl.ds(begin, hidden_rows)]

    def translate(probe, stream, low, weights, at):
        moved = stream + jnp.dot(low, weights, preferred_element_type=f32) + trans_bias[probe : probe + 1, :]
        moved_ref[probe, at, :] = moved
        states_ref[1 + probe, at, :] = (
            row_norm(moved) * gains_ref[2:3, :] + offsets_ref[4:5, :]
        ).astype(bf16)

    for begin in range(0, rows, wide_rows):
        at = slice(begin, begin + wide_rows)
        low = stream_ref[at, :]
        translate(0, low.astype(f32), low, slab_ref[:, 0:own_width, :].reshape(depth, depth), at)
    turned[...] = jnp.transpose(states_ref[1])
    for begin in range(0, fc_width, 256):
        at = slice(begin, begin + 256)
        for row in range(0, rows, 512):
            span = slice(row, row + 512)
            value = jnp.dot(x_mlp[span, :], mixed_ref[:, 3 * plane_width + begin : 3 * plane_width + begin + 256], preferred_element_type=f32) + fc_bias[:, at]
            hidden[span, at] = (0.5 * value * (1.0 + lax.erf(value * (0.5 ** 0.5)))).astype(bf16)
    plane.relay_side(0)
    heads_copy.wait()
    for peer in peers:
        arrived(gathered.at[peer], heads_receive.at[peer], {"seq": peer})
    length = size * tokens
    block = 2 * tokens
    lane = lax.broadcasted_iota(jnp.int32, (block, columns), 1) // head_dim
    keys = jnp.concatenate([gathered[source, 1] for source in range(size)], axis=0)
    values = jnp.concatenate([gathered[source, 2] for source in range(size)], axis=0)
    for first in range(0, length, block):
        end = first + block
        queries = jnp.concatenate([gathered[first // tokens, 0], gathered[first // tokens + 1, 0]], axis=0)
        allowed = lax.broadcasted_iota(jnp.int32, (block, end), 1) <= (
            lax.broadcasted_iota(jnp.int32, (block, end), 0) + first
        )
        result = None
        for head in range(heads):
            chosen = jnp.where(lane == head, queries, jnp.zeros((), bf16))
            scores = lax.dot_general(
                chosen, keys[:end], (((1,), (1,)), ((), ())), preferred_element_type=f32
            ) * head_dim ** (-0.5)
            scores = jnp.where(allowed, scores, NEGATIVE)
            exponent = jnp.exp(scores - jnp.max(scores, axis=-1, keepdims=True))
            value = jnp.dot(
                exponent.astype(bf16), values[:end], preferred_element_type=f32
            ) / jnp.sum(exponent, axis=-1, keepdims=True)
            result = value if result is None else jnp.where(lane == head, value, result)
        result = result.astype(bf16)
        for index in range(2):
            mixed[first // tokens + index] = result[index * tokens : (index + 1) * tokens]
    for index, peer in enumerate(peers):
        sent.append(
            push(mixed.at[peer], returned.at[spot], rows_send.at[index], rows_receive.at[spot], {"seq": peer})
        )
    rows_copy = pltpu.make_async_copy(mixed.at[spot], returned.at[spot], local_sem.at[1])
    rows_copy.start()
    plane.own(1)
    plane.relay_core(0)
    probe_logits(0)
    probe_logits(1)
    plane.receive_core(0)
    for begin in range(0, depth, 256):
        at = slice(begin, begin + 256)
        part[:, at] = jnp.dot(
            hidden[...], slab_all[:, 0:hidden_rows, at].reshape(fc_width, 256), preferred_element_type=f32
        )
    rows_copy.wait()
    for peer in peers:
        arrived(returned.at[peer], rows_receive.at[peer], {"seq": peer})
    out_w = slab_all[:, hidden_rows:, :].reshape(plane_width, depth)
    for sequence in range(lines):
        at = slice(sequence * tokens, (sequence + 1) * tokens)
        attended = jnp.concatenate(
            [returned[sequence * groups + group] for group in range(groups)], axis=1
        )
        part[at, :] += jnp.dot(attended, out_w, preferred_element_type=f32)
    line_sum = LineSum(
        count, 1, lambda at: part[at],
        land, x_attn, x_mlp, inner_sem, outer_sem, receive_sem,
    )
    line_sum.begin(range(count))
    todo = [functools.partial(probe_logits, cut) for cut in range(2, cuts)]
    todo[4:4] = [lambda: plane.relay_side(1)]
    todo[9:9] = [lambda: plane.relay_core(1)]
    todo[13:13] = [lambda: plane.receive_core(1)]
    line_sum.run(3, todo)

    for begin in range(0, rows, wide_rows):
        at = slice(begin, begin + wide_rows)
        stream = stream_ref[at, :].astype(f32) + x_mlp[at, :].astype(f32) + offsets_ref[2:3, :] + offsets_ref[3:4, :]
        states_ref[0, at, :] = (row_norm(stream) * gains_ref[2:3, :] + offsets_ref[4:5, :]).astype(bf16)
        low = stream.astype(bf16)
        low_ref[at, :] = low
        translate(1, stream, low, second_trans[...].reshape(depth, depth), at)
    for copy in sent:
        copy.wait_send()
    for copy in stores[-2:]:
        copy.wait()
    plane.finish()
    line_sum.finish()


def layer(stream, mixed, proj, out, slab, next_trans, gains, offsets, wide, turns, table):
    size = lax.axis_size("seq")
    lines = lax.axis_size("batch")
    rows, depth = stream.shape
    tokens = rows // lines
    own_heads = depth // HEAD_DIM // size
    columns = own_heads * HEAD_DIM
    count = 16
    fc_width = size * proj.shape[0]
    tiles = pl.cdiv(table.shape[0], VOCAB_TILE)
    bf16 = jnp.bfloat16
    f32 = jnp.float32
    vmem = pl.BlockSpec(memory_space=pltpu.VMEM)
    anywhere = pl.BlockSpec(memory_space=pl.ANY)
    dma = pltpu.SemaphoreType.DMA
    sums = LineSum.scratch(count, rows, depth)
    return pl.pallas_call(
        functools.partial(layer_kernel, count, own_heads),
        in_specs=[vmem] * 10 + [anywhere],
        out_specs=[vmem] * 3 + [anywhere],
        out_shape=[
            jax.ShapeDtypeStruct((3, rows, depth), bf16),
            jax.ShapeDtypeStruct((2, rows, depth), f32),
            jax.ShapeDtypeStruct((rows, depth), bf16),
            jax.ShapeDtypeStruct((tiles, VOCAB_TILE, rows), f32),
        ],
        scratch_shapes=[
            pltpu.VMEM((size, proj.shape[0] + out.shape[0], depth), bf16),
            pltpu.VMEM((size,) + next_trans.shape[1:], bf16),
            pltpu.VMEM((2, depth), f32),
            pltpu.VMEM((1, fc_width), f32),
            pltpu.VMEM((rows, fc_width), bf16),
            pltpu.VMEM((rows, depth), bf16),
            pltpu.VMEM((rows, depth), bf16),
            pltpu.VMEM((size, 3, tokens, columns), bf16),
            pltpu.VMEM((size, 3, tokens, columns), bf16),
            pltpu.VMEM((size, tokens, columns), bf16),
            pltpu.VMEM((size, tokens, columns), bf16),
            pltpu.VMEM((rows, depth), f32),
        ] + sums[:1] + sums[2:] + [
            pltpu.VMEM((2, VOCAB_TILE // 2, depth), bf16),
            pltpu.VMEM((depth, rows), bf16),
            pltpu.VMEM((2, VOCAB_TILE // 2, rows), f32),
            dma((2,)),
            dma((2,)),
            dma((2,)),
            dma((size - 1,)),
            dma((size,)),
            dma((size - 1,)),
            dma((size,)),
        ] + PlaneGather.scratch(2),
        compiler_params=pltpu.CompilerParams(
            collective_id=2, has_side_effects=True, vmem_limit_bytes=VMEM_BYTES
        ),
        name="layer",
    )(stream, mixed, proj, out, slab, next_trans, gains, offsets, wide, turns, table)


def stats_kernel(
    tiles_ref, peaks_ref, sums_ref, cross_ref, scales_ref, note_ref,
    gathered, send_sem, receive_sem,
):
    place = lax.axis_index("batch")
    spot = lax.axis_index("seq")
    size = lax.axis_size("seq")
    planes = others("batch")
    tiles = peaks_ref.shape[0]
    rows = peaks_ref.shape[2]
    lines = gathered.shape[0]
    tokens = rows // lines
    gathered[place, 0:3, :] = peaks_ref[tiles - 1]
    for state in range(3):
        gathered[place, 3 + state : 4 + state, :] = jnp.sum(sums_ref[state], axis=0, keepdims=True)
    for other in range(2):
        gathered[place, 6 + other : 7 + other, :] = jnp.sum(cross_ref[other], axis=0, keepdims=True)
    greet([{"batch": plane} for plane in planes])
    copies = [
        push(gathered.at[place], gathered.at[place], send_sem.at[index], receive_sem.at[place], {"batch": plane})
        for index, plane in enumerate(planes)
    ]
    position = spot * tokens + lax.broadcasted_iota(jnp.int32, (1, tokens), 1)
    weights = jnp.concatenate(
        [
            jnp.where(position < size * tokens - tiles_ref[line, 2:3, :], tiles_ref[line, 1:2, :], 0).astype(jnp.float32)
            for line in range(lines)
        ],
        axis=1,
    )
    for plane in planes:
        arrived(gathered.at[plane], receive_sem.at[plane], {"batch": plane})
    tops = gathered[0, 0:3, :]
    for line in range(1, lines):
        tops = jnp.maximum(tops, gathered[line, 0:3, :])
    sums = jnp.zeros((3, rows), jnp.float32)
    cross = jnp.zeros((2, rows), jnp.float32)
    for line in range(lines):
        fade = jnp.exp(gathered[line, 0:3, :] - tops)
        sums += gathered[line, 3:6, :] * fade
        cross += gathered[line, 6:8, :] * fade[0:1]
    totals = tops + jnp.log(sums)
    diverge = cross / sums[0:1] - totals[0:1] + totals[1:3]
    loss = weights * (diverge[0:1] + diverge[1:2])
    for tile in range(tiles):
        scales_ref[tile] = weights * jnp.exp(peaks_ref[tile] - totals)
    note_ref[...] = jnp.zeros_like(note_ref)
    for line in range(rows // LANES):
        at = slice(line * LANES, (line + 1) * LANES)
        note_ref[1:2, :] += loss[:, at]
        note_ref[2:3, :] += weights[:, at]
    for copy in copies:
        copy.wait_send()


def statistics(tiles, peaks, sums, cross):
    lines = lax.axis_size("batch")
    rows = peaks.shape[2]
    vmem = pl.BlockSpec(memory_space=pltpu.VMEM)
    return pl.pallas_call(
        stats_kernel,
        in_specs=[vmem] * 4,
        out_specs=[vmem] * 2,
        out_shape=[
            jax.ShapeDtypeStruct(peaks.shape, jnp.float32),
            jax.ShapeDtypeStruct((8, LANES), jnp.float32),
        ],
        scratch_shapes=[
            pltpu.VMEM((lines, 8, rows), jnp.float32),
            pltpu.SemaphoreType.DMA((lines - 1,)),
            pltpu.SemaphoreType.DMA((lines,)),
        ],
        compiler_params=pltpu.CompilerParams(collective_id=5, has_side_effects=True),
        name="statistics",
    )(tiles, peaks, sums, cross)


def reduce_kernel(
    count,
    grad_ref, bias_ref, note_ref,
    total_ref, bias_out, note_out,
    mine, sibling_land, side_land, line_land, side_sum, line_part, last_land, own_sum,
    land, held, inner_sem, outer_sem, receive_sem,
    tile_land, tile_line, tile_out,
    local_sem, core_send, core_receive, side_send, side_receive, line_send, line_receive,
    last_send, last_receive, bias_send, bias_receive, plane_send, plane_receive, note_send, note_receive,
):
    size = lax.axis_size("seq")
    spot = lax.axis_index("seq")
    place = lax.axis_index("batch")
    core, column, line = plane_place(spot)
    rows = size // 4
    step_rows = total_ref.shape[0] // count // 2
    beside = {"seq": plane_index(core, 1 - column, line)}
    sibling = {"seq": plane_index(1 - core, column, line)}
    lines_on = [lax.rem(line + step, rows) for step in range(1, rows)]
    across = [{"seq": plane_index(core, column, at)} for at in lines_on]
    peers = others("seq")
    planes = others("batch")
    f32 = jnp.float32
    bf16 = jnp.bfloat16
    sent = []

    def cut(chunk, side):
        return grad_ref.at[:, :, :, side, pl.ds(chunk * step_rows, step_rows)]

    loads = [
        pltpu.make_async_copy(cut(chunk, core), mine.at[chunk], local_sem.at[chunk]) for chunk in range(count)
    ]
    for copy in loads:
        copy.start()
    tile_land[spot] = bias_ref[spot]
    greet([{"batch": plane} for plane in planes] + [{"seq": peer} for peer in peers])
    for chunk in range(count):
        sent.append(
            push(cut(chunk, 1 - core), sibling_land.at[chunk], core_send.at[chunk], core_receive.at[chunk], sibling)
        )
    for index, peer in enumerate(peers):
        sent.append(
            push(bias_ref.at[peer], tile_land.at[spot], bias_send.at[index], bias_receive.at[spot], {"seq": peer})
        )
    line_sum = LineSum(
        count, 1, lambda at: own_sum[at],
        land, held, total_ref, inner_sem, outer_sem, receive_sem,
    )

    def pair(chunk):
        loads[chunk].wait()
        arrived(sibling_land.at[chunk], core_receive.at[chunk], sibling)
        mine[chunk] = (mine[chunk].astype(f32) + sibling_land[chunk].astype(f32)).astype(bf16)
        sent.append(
            push(
                mine.at[chunk, 0, :, 1 - column], side_land.at[chunk],
                side_send.at[chunk], side_receive.at[chunk], beside,
            )
        )
        for index, target in enumerate(across):
            sent.append(
                push(
                    mine.at[chunk, 1, lines_on[index]], line_land.at[chunk, index],
                    line_send.at[chunk, index], line_receive.at[chunk, index], target,
                )
            )

    def second(chunk):
        begin = chunk * 2 * step_rows
        arrived(side_land.at[chunk], side_receive.at[chunk], beside)
        own_sum[begin : begin + step_rows, :] = (
            mine[chunk, 0, line, column].astype(f32) + side_land[chunk, line].astype(f32)
        )
        for index, target in enumerate(across):
            at = lines_on[index]
            side_sum[chunk, index] = (
                mine[chunk, 0, at, column].astype(f32) + side_land[chunk, at].astype(f32)
            ).astype(bf16)
            sent.append(
                push(
                    side_sum.at[chunk, index], last_land.at[chunk, 1 + index],
                    last_send.at[chunk, 1 + index], last_receive.at[chunk, 1 + index], target,
                )
            )
        for index in range(len(across)):
            arrived(line_land.at[chunk, index], line_receive.at[chunk, index], across[-1 - index])
        for side, last in ((1 - column, False), (column, True)):
            both = mine[chunk, 1, line, side].astype(f32)
            for index in range(len(across)):
                both += line_land[chunk, index, side].astype(f32)
            if last:
                own_sum[begin + step_rows : begin + 2 * step_rows, :] = both
            else:
                line_part[chunk] = both.astype(bf16)
                sent.append(
                    push(
                        line_part.at[chunk], last_land.at[chunk, 0],
                        last_send.at[chunk, 0], last_receive.at[chunk, 0], beside,
                    )
                )

    def third(chunk):
        begin = chunk * 2 * step_rows
        for index in range(len(across)):
            arrived(last_land.at[chunk, 1 + index], last_receive.at[chunk, 1 + index], across[-1 - index])
            own_sum[begin : begin + step_rows, :] += last_land[chunk, 1 + index].astype(f32)
        arrived(last_land.at[chunk, 0], last_receive.at[chunk, 0], beside)
        own_sum[begin + step_rows : begin + 2 * step_rows, :] += last_land[chunk, 0].astype(f32)
        line_sum.begin([chunk])
        line_sum.gather(chunk)

    def tiles_in_plane():
        for peer in peers:
            arrived(tile_land.at[peer], bias_receive.at[peer], {"seq": peer})
        tile = tile_land[0]
        for source in range(1, size):
            tile += tile_land[source]
        tile_line[place] = tile
        for index, plane in enumerate(planes):
            sent.append(
                push(
                    tile_line.at[place], tile_line.at[place], plane_send.at[index], plane_receive.at[place],
                    {"batch": plane},
                )
            )

    squares = []

    def square(chunk):
        line_sum.spread(chunk)
        for row in range(chunk * 2 * step_rows, (chunk + 1) * 2 * step_rows, 16):
            value = total_ref[row : row + 16, :].astype(f32)
            value = value * value
            for begin in range(0, value.shape[1], LANES):
                block = value[:8, begin : begin + LANES] + value[8:, begin : begin + LANES]
                squares[:] = [block + squares[0]] if squares else [block]

    for time in range(count + 4):
        if time < count:
            pair(time)
        if 0 <= time - 1 < count:
            second(time - 1)
        if 0 <= time - 2 < count:
            third(time - 2)
        if time == count - 1:
            tiles_in_plane()
        if 0 <= time - 4 < count:
            square(time - 4)
    for plane in planes:
        arrived(tile_line.at[plane], plane_receive.at[plane], {"batch": plane})
    tile = tile_line[0]
    for source in range(1, lax.axis_size("batch")):
        tile += tile_line[source]
    bias_out[...] = tile
    head = jnp.sum(squares[0] + tile * tile, axis=0, keepdims=True)
    row8 = lax.broadcasted_iota(jnp.int32, (8, LANES), 0)
    tile_out[...] = jnp.where(row8 == 0, head, note_ref[...])
    note_out[spot] = tile_out[...]
    for index, peer in enumerate(peers):
        sent.append(
            push(tile_out, note_out.at[spot], note_send.at[index], note_receive.at[spot], {"seq": peer})
        )
    for peer in peers:
        arrived(note_out.at[peer], note_receive.at[peer], {"seq": peer})
    for copy in sent:
        copy.wait_send()
    line_sum.finish()


def reduce_gradients(grad, bias, note):
    size = lax.axis_size("seq")
    lines = lax.axis_size("batch")
    depth = grad.shape[2]
    width = depth // size
    rows = size // 4
    count = 4
    cut = width // count
    bf16 = jnp.bfloat16
    vmem = pl.BlockSpec(memory_space=pltpu.VMEM)
    dma = pltpu.SemaphoreType.DMA
    near = max(rows - 1, 1)
    grad = grad.reshape(2, rows, 2, 2, width, depth)
    return pl.pallas_call(
        functools.partial(reduce_kernel, count),
        in_specs=[pl.BlockSpec(memory_space=pl.ANY), vmem, vmem],
        out_specs=[vmem] * 3,
        out_shape=[
            jax.ShapeDtypeStruct((2 * width, depth), bf16),
            jax.ShapeDtypeStruct(bias.shape[1:], jnp.float32),
            jax.ShapeDtypeStruct((size,) + note.shape, jnp.float32),
        ],
        scratch_shapes=[
            pltpu.VMEM((count, 2, rows, 2, cut, depth), bf16),
            pltpu.VMEM((count, 2, rows, 2, cut, depth), bf16),
            pltpu.VMEM((count, rows, cut, depth), bf16),
            pltpu.VMEM((count, near, 2, cut, depth), bf16),
            pltpu.VMEM((count, near, cut, depth), bf16),
            pltpu.VMEM((count, cut, depth), bf16),
            pltpu.VMEM((count, rows, cut, depth), bf16),
            pltpu.VMEM((2 * width, depth), jnp.float32),
        ] + LineSum.scratch(count, 2 * width, depth) + [
            pltpu.VMEM((size,) + bias.shape[1:], jnp.float32),
            pltpu.VMEM((lines,) + bias.shape[1:], jnp.float32),
            pltpu.VMEM(note.shape, jnp.float32),
            dma((count,)),
            dma((count,)),
            dma((count,)),
            dma((count,)),
            dma((count,)),
            dma((count, near)),
            dma((count, near)),
            dma((count, rows)),
            dma((count, rows)),
            dma((size - 1,)),
            dma((size,)),
            dma((lines - 1,)),
            dma((lines,)),
            dma((size - 1,)),
            dma((size,)),
        ],
        compiler_params=pltpu.CompilerParams(
            collective_id=6, has_side_effects=True, vmem_limit_bytes=VMEM_BYTES
        ),
        name="reduce_gradients",
    )(grad, bias, note)


def update_kernel(
    total_ref, bias_sum, note_ref, trans_ref, mom1_ref, mom2_ref, trans_bias, mom1_bias, mom2_bias,
    first_out, second_out, weight_out, first_bias, second_bias, weight_bias, result_out,
):
    size = note_ref.shape[0]
    notes = note_ref[0]
    for source in range(1, size):
        notes += note_ref[source]
    sums = jnp.sum(notes, axis=-1, keepdims=True)
    norm = jnp.sqrt(sums[0:1]) / sums[2:3]
    row8 = lax.broadcasted_iota(jnp.int32, (8, LANES), 0)
    result_out[...] = jnp.where(row8 == 0, norm, sums)
    factor = jnp.minimum(1.0, clip_max / (norm + 1e-06)) / sums[2:3]
    cut = total_ref.shape[2]
    for chunk in range(total_ref.shape[0]):
        at = slice(chunk * cut, (chunk + 1) * cut)
        for probe in range(2):
            gradient = total_ref[chunk, probe].astype(jnp.float32) * factor
            first_out[probe, at, :], second_out[probe, at, :], weight_out[probe, at, :] = adam_update(
                trans_ref[probe, at, :], gradient, mom1_ref[probe, at, :], mom2_ref[probe, at, :]
            )
    gradient = bias_sum[0:2, 0 : trans_bias.shape[1]] * factor
    first_bias[...], second_bias[...], weight_bias[...] = adam_update(
        trans_bias[...], gradient, mom1_bias[...], mom2_bias[...]
    )


def update(total, bias_sum, notes, trans, mom1, mom2, trans_bias, mom1_bias, mom2_bias):
    _, width, depth = trans.shape
    count = 4
    cut = width // count
    f32 = jnp.float32
    whole = lambda part: pl.BlockSpec(part.shape, lambda i: (0,) * part.ndim)
    part = pl.BlockSpec((2, width, depth), lambda i: (0, 0, 0))
    result = pl.BlockSpec((8, LANES), lambda i: (0, 0))
    total = jnp.reshape(total, (count, 2, cut, depth))
    return pl.pallas_call(
        update_kernel,
        grid=(1,),
        in_specs=[
            pl.BlockSpec((count, 2, cut, depth), lambda i: (0, 0, 0, 0)), whole(bias_sum), whole(notes), part, part, part,
            whole(trans_bias), whole(mom1_bias), whole(mom2_bias),
        ],
        out_specs=[part, part, part, whole(trans_bias), whole(mom1_bias), whole(mom2_bias), result],
        out_shape=[jax.ShapeDtypeStruct(trans.shape, f32)] * 3
        + [jax.ShapeDtypeStruct(trans_bias.shape, f32)] * 3
        + [jax.ShapeDtypeStruct((8, LANES), f32)],
        compiler_params=pltpu.CompilerParams(vmem_limit_bytes=VMEM_BYTES),
        name="update",
    )(total, bias_sum, notes, trans, mom1, mom2, trans_bias, mom1_bias, mom2_bias)


def body(
    token_ids,
    pos_weights,
    pad_lengths,
    embed_in,
    w_qkv,
    w_out,
    w_fc,
    w_proj,
    norm_gains,
    layer_biases,
    wide_bias,
    unembed,
    trans_weight,
    trans_bias,
    mom1_weight,
    mom2_weight,
    mom1_bias,
    mom2_bias,
):
    bf16 = jnp.bfloat16
    f32 = jnp.float32
    tok_rows = token_ids.shape[1]
    width = embed_in.shape[1]
    vocab_rows = unembed.shape[0]
    n_seq = lax.axis_size("seq")
    n_batch = lax.axis_size("batch")
    batch_index = lax.axis_index("batch")
    seq_index = lax.axis_index("seq")
    head_count = width // HEAD_DIM
    plane_heads = head_count // n_batch
    plane_width = plane_heads * HEAD_DIM
    hidden_rows = w_proj.shape[0]

    half_rot = ROT // 2
    local_places = seq_index * tok_rows + jnp.arange(tok_rows, dtype=jnp.int32)
    frequency = 10000.0 ** (-2.0 * jnp.arange(half_rot, dtype=f32) / ROT)
    angles = local_places.astype(f32)[:, None] * frequency[None, :]
    cosine = jnp.cos(angles)
    sine = jnp.sin(angles)
    still = jnp.zeros((tok_rows, HEAD_DIM - ROT), f32)
    blank = jnp.zeros((tok_rows, half_rot), f32)
    turns = jnp.stack(
        [
            jnp.concatenate([cosine, cosine, still + 1.0], axis=1),
            jnp.concatenate([-sine, blank, still], axis=1),
            jnp.concatenate([blank, sine, still], axis=1),
        ]
    )
    turns = jnp.tile(turns, (1, 1, plane_heads))

    wide = wide_bias[None, :]
    if hidden_rows % LANES:
        fc_bias = lax.dynamic_slice_in_dim(
            wide_bias[3 * width :].reshape(n_seq, n_batch, hidden_rows), batch_index, 1, 1
        ).reshape(1, -1)
        wide = jnp.concatenate([wide, fc_bias], axis=1)
    own_rows = w_qkv.shape[0]
    joined_cut = jnp.transpose(w_qkv.reshape(own_rows, 3, n_batch, plane_width), (2, 0, 1, 3))
    fc_cut = jnp.transpose(w_fc.reshape(own_rows, n_seq, n_batch, hidden_rows), (2, 0, 1, 3))
    mixed_cut = jnp.concatenate(
        [joined_cut.reshape(n_batch, own_rows, -1), fc_cut.reshape(n_batch, own_rows, -1)], axis=2
    )
    tiles, stream_low, mixed_w, slab, out_own = front(
        token_ids, pos_weights, pad_lengths, embed_in, mixed_cut, trans_weight, w_out, trans_bias
    )
    states, translated, low1, probe_logits = layer(
        stream_low,
        mixed_w.reshape(width, -1),
        w_proj,
        out_own,
        slab,
        trans_weight,
        norm_gains,
        layer_biases,
        wide,
        turns,
        unembed,
    )
    first, second, peaks, sums_part, cross_part = vocab_forward(states, unembed, probe_logits)
    scales, note = statistics(tiles, peaks, sums_part, cross_part)
    grad, bias_grad = vocab_backward(
        first, second, scales, unembed, translated, stream_low, low1, norm_gains
    )
    first_w, second_w, new_w, first_b, second_b, new_b, result = update(
        *reduce_gradients(grad, bias_grad, note),
        trans_weight, mom1_weight, mom2_weight, trans_bias, mom1_bias, mom2_bias,
    )
    return (result[1, 0], result[2, 0], result[0, 0], first_w, second_w, new_w, first_b, second_b, new_b)


def solution(mesh):
    return jax.shard_map(
        body,
        mesh=mesh,
        in_specs=(
            P("batch", "seq"),
            P("batch", "seq"),
            P("batch"),
            P("batch", None),
            P(("seq", "batch"), None),
            P(("seq", "batch"), None),
            P(("seq", "batch"), None),
            P(("seq", "batch"), None),
            P(),
            P(),
            P(),
            P("batch", None),
            P(None, "seq", None),
            P(None, "seq"),
            P(None, "seq", None),
            P(None, "seq", None),
            P(None, "seq"),
            P(None, "seq"),
        ),
        out_specs=(
            P(),
            P(),
            P(),
            P(None, "seq", None),
            P(None, "seq", None),
            P(None, "seq", None),
            P(None, "seq"),
            P(None, "seq"),
            P(None, "seq"),
        ),
        check_vma=False,
    )
```
